32 devices in a mesh: nodes: 16 (over z, y, core), grp: 2 (over x).
Axes of the slice: x: 2, y: 2, z: 4, core: 2. Of those that a mesh axis runs over, the one named last changes fastest.
Arguments:
- features: float32 [2, 8192, 1024], P('grp', 'nodes'), may hold values from -6 to 6
- type_mask: int32 [2, 8192], P('grp', 'nodes'), may hold values 0 or 1
- edge_child: int32 [2, 409600], P('grp', 'nodes'), may hold values from 0 to 511
- edge_slot: int32 [2, 409600], P('grp', 'nodes'), may hold values from 0 to 2047, as said below
- edge_weight: int32 [2, 409600], P('grp', 'nodes'), may hold values from 1 to 9
- recv_rows: int32 [2, 16, 16, 128], P('grp', 'nodes'), may hold values from 0 to 511
- board_proj: float32 [1024, 1024], replicated, may hold values from -0.1875 to 0.1875
- neigh_proj: float32 [1024, 1024], replicated, may hold values from -0.1875 to 0.1875
- neigh_bias: float32 [1024], replicated, may hold values from -3 to 3
- combine_proj: float32 [2048, 1024], replicated, may hold values from -0.125 to 0.125
- combine_bias: float32 [1024], replicated, may hold values from -3 to 3
- out_cot: float32 [2, 8192, 1024], P('grp', 'nodes'), as said below
Outputs:
- embedding: float32 [2, 8192, 1024], P('grp', 'nodes')
- penalty: float32 [], replicated
- grad_features: float32 [2, 8192, 1024], P('grp', 'nodes')
- grad_board_proj: float32 [1024, 1024], replicated
- grad_neigh_proj: float32 [1024, 1024], replicated
- grad_neigh_bias: float32 [1024], replicated
- grad_combine_proj: float32 [2048, 1024], replicated
- grad_combine_bias: float32 [1024], replicated
The draws below stay inside these ranges and needn't reach their ends.
Inputs may be any that keep to these rules, and one draw needn't show every extreme that they name: `edge_slot`: each value occurs at least once among the 25600 edges of one device; value s sends to the device s // 128 of the same group. `out_cot`: entries are at most 192 / 16777216 in magnitude.
All inputs are finite; a program needn't handle non-finite values. No bound on the sum of `type_mask` on one device may be relied on, other than what follows from the above.
Results may differ from the reference program's by a relative error of at most 0.0069.
Values may be sent and summed in bfloat16 or wider, within the bound.
A program may use at most 128 MiB of HBM per device.

```python
import math
import jax
import jax.numpy as jnp
import numpy as np
from jax import lax

D = 1024
ROWS = 512
SLOTS = 2048
EDGES = 25600
CAP = 128
NODES = 8192
N_NODES = 16
N_GRP = 2


def draw_edge_slot(key, part):
    key = jax.random.fold_in(key, 3)
    key_perm, key_one, key_two, key_inner = jax.random.split(key, 4)
    shape = (N_GRP * N_NODES, EDGES)
    perm_keys = jax.random.split(key_perm, N_GRP * N_NODES)
    order = jax.vmap(lambda k: jax.random.permutation(k, jnp.arange(EDGES, dtype=jnp.int32)))(perm_keys)
    peer = jnp.minimum(jax.random.randint(key_one, shape, 0, N_NODES), jax.random.randint(key_two, shape, 0, N_NODES))
    inner = jax.random.randint(key_inner, shape, 0, CAP)
    slots = jnp.where(order < SLOTS, order, peer * CAP + inner)
    return slots.reshape(N_GRP, N_NODES * EDGES).astype(jnp.int32)


def draw_out_cot(key, part):
    key = jax.random.fold_in(key, 5)
    factor = 32.0 / (float(D) * float(N_GRP) * float(NODES))
    values = jax.random.truncated_normal(key, -6.0, 6.0, (N_GRP, NODES, D), jnp.float32)
    return (values * factor).astype(jnp.float32)


def plant(drawn, own_key, least, high):
    index_at = [jax.random.randint(jax.random.fold_in(own_key, axis), (), 0, length) for axis, length in enumerate(drawn.shape)]
    longest = drawn.shape.index(max(drawn.shape))
    next_to = index_at[:longest] + [(index_at[longest] + 1) % drawn.shape[longest]] + index_at[longest + 1:]
    return drawn.at[tuple(index_at)].set(least).at[tuple(next_to)].set(high)


def levels(stream_key, extent, cuts, smallest, high):
    level = 1.0
    for dim, blocks in cuts:
        heights = jax.random.uniform(jax.random.fold_in(jax.random.fold_in(stream_key, 6), dim), (blocks,), jnp.float32, smallest / len(cuts), high / len(cuts))
        level = level * jnp.repeat(jnp.exp(heights), extent[dim] // blocks).reshape((-1,) + (1,) * (len(extent) - 1 - dim))
    return level


def cumulative_ranks(count, skew):
    portions = [(1 << 20) // math.isqrt(grade ** skew) + 1 for grade in range(1, count + 1)]
    width = 1 + sum(portions) // (1 << 30)
    return np.cumsum(np.array([max(1, weight // width) for weight in portions]))


def ranked_ids(stream_key, dims, count, lean):
    table = cumulative_ranks(count, lean)
    pick = jax.random.randint(jax.random.fold_in(stream_key, 1), dims, 0, int(table[count - 1]))
    rank = jnp.searchsorted(jnp.asarray(table, jnp.int32), pick, side="right")
    return jax.random.permutation(jax.random.fold_in(stream_key, 2), count)[rank].astype(jnp.int32)


def normal_values(key, shape, scale, limit, shards=(), kind=jnp.bfloat16):
    gain = levels(key, shape, shards, -0.22, 0.18) if shards else 1.0
    result = jax.random.normal(key, shape, jnp.float32) * scale * gain
    return jnp.minimum(jnp.maximum(result, -limit), limit).astype(kind)


def setup_inputs(seed: int = 0) -> dict:
    key_list = jax.random.split(jax.random.key(seed), 13)
    return {
        "features": normal_values(key_list[0], (N_GRP, NODES, D), 1.0, 6.0, ((0, 2), (1, 16)), jnp.float32),
        "type_mask": plant((jax.random.randint(key_list[1], (N_GRP, NODES), 0, 2) < 1).astype(jnp.int32), jax.random.fold_in(key_list[1], 1), 0, 1),
        "edge_child": plant(jax.random.randint(key_list[2], (N_GRP, N_NODES * EDGES), 0, ROWS), jax.random.fold_in(key_list[2], 1), 0, ROWS - 1).astype(jnp.int32),
        "edge_slot": draw_edge_slot(jax.random.fold_in(key_list[12], 71), 0),
        "edge_weight": plant(jax.random.randint(key_list[4], (N_GRP, N_NODES * EDGES), 1, 10), jax.random.fold_in(key_list[4], 1), 1, 9).astype(jnp.int32),
        "recv_rows": plant(ranked_ids(key_list[5], (N_GRP, N_NODES, N_NODES, CAP), ROWS, 2), jax.random.fold_in(key_list[5], 3), 0, ROWS - 1).astype(jnp.int32),
        "board_proj": normal_values(key_list[6], (D, D), D ** -0.5, 0.1875, (), jnp.float32),
        "neigh_proj": normal_values(key_list[7], (D, D), D ** -0.5, 0.1875, (), jnp.float32),
        "neigh_bias": normal_values(key_list[8], (D,), 0.5, 3.0, (), jnp.float32),
        "combine_proj": normal_values(key_list[9], (2 * D, D), (2 * D) ** -0.5, 0.125, (), jnp.float32),
        "combine_bias": normal_values(key_list[10], (D,), 0.5, 3.0, (), jnp.float32),
        "out_cot": draw_out_cot(jax.random.fold_in(key_list[12], 71), 0),
    }


@jax.custom_vjp
def low(v):
    return lax.optimization_barrier(v.astype(jnp.bfloat16)).astype(jnp.float32)

@jax.custom_vjp
def low_back(v):
    return v

def low_keep(v):
    return (low(v), None)

def low_pass(kept, grad):
    return (grad,)

def back_keep(v):
    return (v, None)

def back_low(kept, grad):
    return (low(grad),)
low.defvjp(low_keep, low_pass)
low_back.defvjp(back_keep, back_low)
HIGH = lax.Precision.HIGHEST

def gelu_tanh(v):
    return jax.nn.gelu(v, approximate=True)

def reference(features, type_mask, edge_child, edge_slot, edge_weight, recv_rows, board_proj, neigh_proj, neigh_bias, combine_proj, combine_bias, out_cot):
    boards = jnp.sum(type_mask).astype(jnp.float32)

    def forward(feats, pb, qw, qb, cw, cb):
        pbl = low(pb)
        qwl = low(qw)
        cwl = low(cw)
        loss = jnp.zeros((), jnp.float32)
        board_sq = jnp.zeros((), jnp.float32)
        outs = []
        for group in range(N_GRP):
            xg = feats[group]
            board = (type_mask[group] == 1)[:, None]
            proj = jnp.dot(low(xg), pbl, precision=HIGH)
            hl = low(low_back(jnp.where(board, proj, xg)))
            pre = low_back(jnp.dot(hl, qwl, precision=HIGH) + qb)
            msg = low(gelu_tanh(pre))
            child = edge_child[group].reshape(N_NODES, EDGES)
            slot = edge_slot[group].reshape(N_NODES, EDGES)
            weight = edge_weight[group].reshape(N_NODES, EDGES)
            blocks = msg.reshape(N_NODES, ROWS, D)

            def send_block(pieces):
                kid, place, wgt, block = pieces
                spread = jnp.zeros((SLOTS, ROWS), jnp.float32).at[place, kid].add(wgt.astype(jnp.float32))
                return jnp.dot(spread, block, precision=HIGH)
            slot_vals = low(lax.map(jax.checkpoint(send_block), (child, slot, weight, blocks)))
            totals = jax.vmap(lambda place, wgt: jax.ops.segment_sum(wgt, place, num_segments=SLOTS))(slot, weight)
            owner = jnp.arange(N_NODES, dtype=jnp.int32)[None, :, None] * ROWS
            target = (jnp.transpose(recv_rows[group], (1, 0, 2)) + owner).reshape(-1)
            num = jax.ops.segment_sum(slot_vals.reshape(-1, D), target, num_segments=NODES)
            den = 1.0 + jax.ops.segment_sum(totals.reshape(-1), target, num_segments=NODES).astype(jnp.float32)
            agg = low(low_back(num) / den[:, None])
            zpre = jnp.dot(hl, cwl[:D], precision=HIGH) + jnp.dot(agg, cwl[D:], precision=HIGH) + cb
            zpre = low_back(zpre)
            z = gelu_tanh(zpre)
            ss = lax.optimization_barrier(jnp.sum(z * z, axis=-1))
            emb = z * lax.rsqrt(ss + 1e-06)[:, None]
            outs.append(emb)
            loss = loss + jnp.sum(emb * out_cot[group])
            board_sq = board_sq + jnp.sum(jnp.where(board[:, 0], ss, 0.0))
        pen = board_sq / (D * (1.0 + boards))
        return (loss + pen, (jnp.stack(outs), pen))
    _, pullback, aux = jax.vjp(forward, features, board_proj, neigh_proj, neigh_bias, combine_proj, combine_bias, has_aux=True)
    grads = pullback(jnp.ones((), jnp.float32))
    return (aux[0], aux[1], grads[0], grads[1], grads[2], grads[3], grads[4], grads[5])
```

```python
import functools

import jax
import jax.numpy as jnp
from jax import lax
from jax.experimental import pallas as pl
from jax.experimental.pallas import tpu as pltpu
from jax.sharding import PartitionSpec as P

HIGH = lax.Precision.HIGHEST
MESH = pl.DeviceIdType.MESH
BF16 = jnp.bfloat16
F32 = jnp.float32
F8 = jnp.float8_e4m3fn
MIB = 2**20


def gelu_tanh(v):
    return jax.nn.gelu(v, approximate=True)


def dot_nt(left, right):
    return lax.dot_general(
        left, right, (((1,), (1,)), ((), ())), preferred_element_type=F32
    )


def dot_tn(left, right):
    return lax.dot_general(
        left, right, (((0,), (0,)), ((), ())), preferred_element_type=F32
    )


def spread_kernel(turn, slot_ref, child_ref, weight_ref, out_ref):
    slots, rows = out_ref.shape
    edges = slot_ref.shape[1]
    block = 256
    out_ref[...] = jnp.zeros_like(out_ref)

    @pl.loop(0, edges // turn)
    def _(i):
        at = pl.ds(pl.multiple_of(i * turn, turn), turn)
        slot = slot_ref[:, at].astype(jnp.int16)
        child = child_ref[:, at].astype(jnp.int16)
        weight = weight_ref[:, at].astype(F32).astype(F8)
        right = jnp.where(
            lax.broadcasted_iota(jnp.int16, (rows, turn), 0) == child, weight, jnp.zeros((), F8)
        )
        for first in range(0, slots, block):
            ids = lax.broadcasted_iota(jnp.int16, (block, turn), 0) + jnp.asarray(first, jnp.int16)
            left = jnp.where(ids == slot, jnp.ones((), F8), jnp.zeros((), F8))
            out_ref[pl.ds(first, block), :] += dot_nt(left, right)


def build_spread(place, child, weight, slots, rows):
    edges = place.shape[0]
    return pl.pallas_call(
        functools.partial(spread_kernel, 1024),
        out_shape=jax.ShapeDtypeStruct((slots, rows), F32),
        in_specs=[pl.BlockSpec(memory_space=pltpu.VMEM)] * 3,
        out_specs=pl.BlockSpec(memory_space=pltpu.VMEM),
        compiler_params=pltpu.CompilerParams(vmem_limit_bytes=32 * MIB),
        cost_estimate=pl.CostEstimate(
            flops=2 * edges * slots * rows, bytes_accessed=4 * slots * rows, transcendentals=0
        ),
        name="build_spread",
    )(place.reshape(1, edges), child.reshape(1, edges), weight.reshape(1, edges))


class Place:
    def __init__(self, n_nodes, n_grp):
        node = lax.axis_index("nodes")
        grp = lax.axis_index("grp")
        self.node, self.grp = node, grp
        self.size = {"c": 2, "y": 2, "z": n_nodes // 4, "x": n_grp}
        self.at = {
            "c": lax.rem(node, 2),
            "y": lax.rem(node // 2, 2),
            "z": node // 4,
            "x": grp,
        }

    def member(self, axis, index):
        at = dict(self.at)
        at[axis] = index
        return {"nodes": at["z"] * 4 + at["y"] * 2 + at["c"], "grp": at["x"]}

    def others(self, axis):
        size = self.size[axis]
        for far in range(1, size):
            index = lax.rem(self.at[axis] + far, size)
            yield far - 1, index, self.member(axis, index)


def barrier(place, axes):
    sem = pltpu.get_barrier_semaphore()
    count = 0
    for axis in axes:
        for _, _, device in place.others(axis):
            pl.semaphore_signal(sem, inc=1, device_id=device, device_id_type=MESH)
            count += 1
    pl.semaphore_wait(sem, count)


def add_into(target, first, count, columns, parts, step=16):
    @pl.loop(0, count // step)
    def _(i):
        at = pl.ds(pl.multiple_of(first + i * step, step), step)
        total = target[at, columns].astype(F32)
        for part in parts:
            total += part[pl.ds(pl.multiple_of(i * step, step), step), :].astype(F32)
        target[at, columns] = total.astype(target.dtype)


def reduce_job(place, order, first, rows, grad, out, arrive, land, send, recv, base):
    half = grad.shape[1] // 2
    core = place.at["c"]
    mine = pl.ds(pl.multiple_of(core * half, half), half)
    theirs = pl.ds(pl.multiple_of((1 - core) * half, half), half)
    sem = base
    mate = place.member("c", 1 - core)
    block = pl.ds(first, rows)
    copy = pltpu.make_async_remote_copy(
        src_ref=grad.at[block, theirs],
        dst_ref=arrive,
        send_sem=send.at[sem],
        recv_sem=recv.at[sem],
        device_id=mate,
        device_id_type=MESH,
    )
    copy.start()
    sem += 1
    yield
    copy.wait()
    add_into(grad, first, rows, mine, [arrive])
    begin, length, used = first, rows, 0
    trail = []
    for axis in order:
        size = place.size[axis]
        length //= size
        copies, parts = [], []
        for far, index, device in place.others(axis):
            start = pl.multiple_of(begin + index * length, 16)
            slot = land.at[pl.ds(used, length)]
            used += length
            copy = pltpu.make_async_remote_copy(
                src_ref=grad.at[pl.ds(start, length), mine],
                dst_ref=slot,
                send_sem=send.at[sem],
                recv_sem=recv.at[sem],
                device_id=device,
                device_id_type=MESH,
            )
            copy.start()
            sem += 1
            copies.append(copy)
            parts.append(slot)
        yield
        for copy in copies:
            copy.wait()
        trail.append((axis, begin, length))
        begin = pl.multiple_of(begin + place.at[axis] * length, 16)
        add_into(grad, begin, length, mine, parts)
    at = pl.ds(begin, length)
    out[at, mine] = grad[at, mine]
    for axis, parent, piece in reversed(trail):
        size = place.size[axis]
        start = pl.multiple_of(parent + place.at[axis] * piece, 16)
        own = out.at[pl.ds(start, piece), mine]
        copies = []
        for far, index, device in place.others(axis):
            copy = pltpu.make_async_remote_copy(
                src_ref=own,
                dst_ref=own,
                send_sem=send.at[sem],
                recv_sem=recv.at[sem],
                device_id=device,
                device_id_type=MESH,
            )
            copy.start()
            sem += 1
            copies.append(copy)
        yield
        for copy in copies:
            copy.wait()
    own = out.at[block, mine]
    copy = pltpu.make_async_remote_copy(
        src_ref=own,
        dst_ref=own,
        send_sem=send.at[sem],
        recv_sem=recv.at[sem],
        device_id=mate,
        device_id_type=MESH,
    )
    copy.start()
    yield
    copy.wait()


def job_sems(n_nodes, n_grp):
    return 2 * (1 + (2 - 1) + (n_nodes // 4 - 1) + (n_grp - 1))


def run_jobs(jobs, at_once):
    waiting, running = list(jobs), []
    while waiting or running:
        left = []
        for job in running:
            try:
                next(job)
                left.append(job)
            except StopIteration:
                pass
        for job in waiting[:at_once]:
            next(job)
            left.append(job)
        waiting = waiting[at_once:]
        running = left


def reduce_kernel(n_nodes, n_grp, count, grad_hbm, out_hbm, grad, out, arrive, land, send, recv, sem_in, sem_out):
    place = Place(n_nodes, n_grp)
    rows = grad.shape[0] // count
    loads = []
    for j in range(count):
        at = pl.ds(j * rows, rows)
        load = pltpu.make_async_copy(grad_hbm.at[at], grad.at[at], sem_in.at[j])
        load.start()
        loads.append(load)
    barrier(place, ("c", "x", "y", "z"))
    per_job = job_sems(n_nodes, n_grp)

    def job(j):
        at = pl.ds(j * rows, rows)
        loads[j].wait()
        yield from reduce_job(
            place,
            ("x", "y", "z") if j % 2 == 0 else ("y", "x", "z"),
            j * rows,
            rows,
            grad,
            out,
            arrive.at[at],
            land.at[pl.ds(j * 2 * rows, 2 * rows)],
            send,
            recv,
            j * per_job,
        )
        store = pltpu.make_async_copy(out.at[at], out_hbm.at[at], sem_out.at[j])
        store.start()
        stores.append(store)

    stores = []
    run_jobs([job(j) for j in range(count)], 2)
    for store in stores:
        store.wait()


def all_reduce(grads, n_nodes, n_grp):
    rows, width = grads.shape
    count = max(1, min(8, rows * 2 // (16 * n_nodes * n_grp)))
    sems = count * job_sems(n_nodes, n_grp)
    return pl.pallas_call(
        functools.partial(reduce_kernel, n_nodes, n_grp, count),
        out_shape=jax.ShapeDtypeStruct((rows, width), BF16),
        in_specs=[pl.BlockSpec(memory_space=pl.ANY)],
        out_specs=pl.BlockSpec(memory_space=pl.ANY),
        scratch_shapes=[
            pltpu.VMEM((rows, width), BF16),
            pltpu.VMEM((rows, width), BF16),
            pltpu.VMEM((rows, width // 2), BF16),
            pltpu.VMEM((2 * rows, width // 2), BF16),
            pltpu.SemaphoreType.DMA((sems,)),
            pltpu.SemaphoreType.DMA((sems,)),
            pltpu.SemaphoreType.DMA((count,)),
            pltpu.SemaphoreType.DMA((count,)),
        ],
        compiler_params=pltpu.CompilerParams(
            vmem_limit_bytes=48 * MIB, collective_id=1, has_side_effects=True
        ),
        name="sum_gradients",
    )(grads)


def on_device(
    n_nodes,
    n_grp,
    features,
    type_mask,
    edge_child,
    edge_slot,
    edge_weight,
    recv_rows,
    board_proj,
    neigh_proj,
    neigh_bias,
    combine_proj,
    combine_bias,
    out_cot,
):
    feats = features[0]
    board = (type_mask[0] == 1)[:, None]
    rows, width = feats.shape
    peers = recv_rows.shape[2]
    cap = recv_rows.shape[3]
    slots = peers * cap
    board_count = lax.psum(jnp.sum(type_mask[0]).astype(F32), ("nodes", "grp"))
    scale = 1.0 / (width * (1.0 + board_count))
    spread = build_spread(edge_slot[0], edge_child[0], edge_weight[0], slots, rows)
    totals = jnp.sum(spread, axis=1).astype(jnp.int32).reshape(peers, cap)
    arrived_tot = lax.all_to_all(totals, "nodes", split_axis=0, concat_axis=0, tiled=True)
    pbl = board_proj.astype(BF16)
    qwl = neigh_proj.astype(BF16)
    cwl = combine_proj.astype(BF16)
    featb = feats.astype(BF16)
    proj = jnp.dot(featb, pbl, preferred_element_type=F32)
    hidden = jnp.where(board, proj, feats).astype(BF16)
    pre = jnp.dot(hidden, qwl, preferred_element_type=F32) + neigh_bias
    message, gelu_msg = jax.vjp(gelu_tanh, pre)
    spread_b = spread.astype(BF16)
    slot_sums = jnp.dot(spread_b, message.astype(BF16), preferred_element_type=F32)
    slot_sums = slot_sums.astype(BF16).reshape(peers, cap, width)
    arrived = lax.all_to_all(slot_sums, "nodes", split_axis=0, concat_axis=0, tiled=True)
    targets = recv_rows[0, 0].reshape(-1)
    picker_bool = targets[None, :] == jnp.arange(rows, dtype=jnp.int32)[:, None]
    picker = picker_bool.astype(BF16)
    num = jnp.dot(picker, arrived.reshape(slots, width), preferred_element_type=F32)
    den = 1.0 + jnp.dot(
        picker_bool.astype(F32), arrived_tot.reshape(-1).astype(F32), precision=HIGH
    )
    aggb = (num / den[:, None]).astype(BF16)
    zpre = jnp.dot(hidden, cwl[:width], preferred_element_type=F32)
    zpre = zpre + jnp.dot(aggb, cwl[width:], preferred_element_type=F32) + combine_bias
    zval, gelu_z = jax.vjp(gelu_tanh, zpre)
    sumsq = jnp.sum(zval * zval, axis=1)
    inverse = lax.rsqrt(sumsq + 1e-06)
    embed = zval * inverse[:, None]
    board_sq = jnp.sum(jnp.where(board[:, 0], sumsq, 0.0))
    cot = out_cot[0]
    dz = inverse[:, None] * (cot - embed * jnp.sum(cot * embed, axis=1, keepdims=True))
    dz = dz + jnp.where(board, 2.0 * scale * zval, 0.0)
    dzb = gelu_z(dz)[0].astype(BF16)
    joined = jnp.concatenate([hidden, aggb], axis=1)
    grad_comb = dot_tn(joined, dzb).astype(BF16)
    grad_cbias = jnp.sum(dzb.astype(F32), axis=0)
    dcat = dot_nt(dzb, cwl)
    dnum = (dcat[:, width:] / den[:, None]).astype(BF16)
    back_slots = dot_tn(picker, dnum).astype(BF16).reshape(peers, cap, width)
    returned = lax.all_to_all(back_slots, "nodes", split_axis=0, concat_axis=0, tiled=True)
    dmsg = dot_tn(spread_b, returned.reshape(slots, width))
    dpre = gelu_msg(dmsg)[0].astype(BF16)
    grad_qbias = jnp.sum(dpre.astype(F32), axis=0)
    grad_neigh = dot_tn(hidden, dpre).astype(BF16)
    dhid = (dcat[:, :width] + dot_nt(dpre, qwl)).astype(BF16)
    dproj = jnp.where(board, dhid, jnp.zeros_like(dhid))
    grad_board = dot_tn(featb, dproj).astype(BF16)
    grad_feats = jnp.where(board, dot_nt(dproj, pbl), dhid.astype(F32))
    small = lax.psum(
        jnp.concatenate([grad_qbias, grad_cbias, jnp.full((width,), board_sq)]), ("nodes", "grp")
    )
    penalty = small[2 * width] * scale
    summed = all_reduce(
        jnp.concatenate([grad_comb, grad_neigh, grad_board], axis=0), n_nodes, n_grp
    )
    return (
        embed[None],
        penalty,
        grad_feats[None],
        summed[3 * width :].astype(F32),
        summed[2 * width : 3 * width].astype(F32),
        small[:width],
        summed[: 2 * width].astype(F32),
        small[width : 2 * width],
    )


def solution(mesh):
    in_specs = (
        P("grp", "nodes", None),
        P("grp", "nodes"),
        P("grp", "nodes"),
        P("grp", "nodes"),
        P("grp", "nodes"),
        P("grp", "nodes", None, None),
        P(),
        P(),
        P(),
        P(),
        P(),
        P("grp", "nodes", None),
    )
    out_specs = (P("grp", "nodes", None), P(), P("grp", "nodes", None), P(), P(), P(), P(), P())
    return jax.shard_map(
        functools.partial(on_device, mesh.shape["nodes"], mesh.shape["grp"]),
        mesh=mesh,
        in_specs=in_specs,
        out_specs=out_specs,
        check_vma=False,
    )
```

```python
import functools
import math

import jax
import jax.numpy as jnp
from jax import lax
from jax.experimental import pallas as pl
from jax.experimental.pallas import tpu as pltpu
from jax.sharding import PartitionSpec as P

HIGH = lax.Precision.HIGHEST
MESH = pl.DeviceIdType.MESH
BF16 = jnp.bfloat16
F32 = jnp.float32
F8 = jnp.float8_e4m3fn
MIB = 2**20


def gelu_tanh(v):
    return jax.nn.gelu(v, approximate=True)


def dot_nt(left, right):
    return lax.dot_general(
        left, right, (((1,), (1,)), ((), ())), preferred_element_type=F32
    )


def dot_tn(left, right):
    return lax.dot_general(
        left, right, (((0,), (0,)), ((), ())), preferred_element_type=F32
    )


LINE = 4
CHUNKS = 4


class Place:
    def __init__(self, n_nodes, n_grp):
        layer = n_nodes // LINE
        node = lax.axis_index("nodes")
        grp = lax.axis_index("grp")
        self.node, self.grp = node, grp
        self.size = {"l": layer, "c": 2, "y": layer // 2, "z": LINE, "x": n_grp}
        low = lax.rem(node, layer)
        self.at = {"l": low, "c": lax.rem(low, 2), "y": low // 2, "z": node // layer, "x": grp}

    def member(self, axis, index):
        layer = self.size["l"]
        low, line, grp = self.at["l"], self.at["z"], self.at["x"]
        if axis == "l":
            low = index
        elif axis == "c":
            low = self.at["y"] * 2 + index
        elif axis == "y":
            low = index * 2 + self.at["c"]
        elif axis == "z":
            line = index
        else:
            grp = index
        return {"nodes": line * layer + low, "grp": grp}

    def others(self, axis):
        size = self.size[axis]
        for far in range(1, size):
            index = lax.rem(self.at[axis] + far, size)
            yield far - 1, index, self.member(axis, index)


def remote(src, dst, send, recv, device):
    return pltpu.make_async_remote_copy(
        src_ref=src, dst_ref=dst, send_sem=send, recv_sem=recv, device_id=device, device_id_type=MESH
    )


def barrier(place, axes):
    sem = pltpu.get_barrier_semaphore()
    count = 0
    for axis in axes:
        for _, _, device in place.others(axis):
            pl.semaphore_signal(sem, inc=1, device_id=device, device_id_type=MESH)
            count += 1
    pl.semaphore_wait(sem, count)


def gelu(v):
    t = jnp.tanh(0.7978845608028654 * (v + 0.044715 * (v * v * v)))
    return v * (0.5 * (1.0 + t))


def gelu_slope(v):
    square = v * v
    t = jnp.tanh(0.7978845608028654 * (v + 0.044715 * (v * square)))
    bend = 0.7978845608028654 * (1.0 + 0.134145 * square)
    return 0.5 * (1.0 + t) + 0.5 * v * (1.0 - t * t) * bend


class Share:
    def __init__(self, place, bufs, send, recv):
        self.place, self.send, self.recv = place, send, recv
        self.stages, base = [], 0
        for axis, buf in zip(("l", "z", "x"), bufs):
            self.stages.append((axis, buf, base))
            base += place.size[axis] - 1

    def start(self, stage, value):
        axis, buf, base = self.stages[stage]
        me = self.place.at[axis]
        buf[me] = value
        for far, _, device in self.place.others(axis):
            remote(
                buf.at[me], buf.at[me], self.send.at[base + far], self.recv.at[base + far], device
            ).start()

    def finish(self, stage):
        axis, buf, base = self.stages[stage]
        me = self.place.at[axis]
        for far, _, device in self.place.others(axis):
            remote(
                buf.at[me], buf.at[me], self.send.at[base + far], self.recv.at[base + far], device
            ).wait()
        total = buf[0]
        for i in range(1, self.place.size[axis]):
            total += buf[i]
        return total


def share_sems(n_nodes, n_grp):
    return (n_nodes // LINE - 1) + (LINE - 1) + max(1, n_grp - 1)


def forward_kernel(
    n_nodes,
    n_grp,
    feats_h,
    mask_ref,
    keys_ref,
    targets_ref,
    board_h,
    neigh_h,
    nbias_ref,
    comb_h,
    cbias_ref,
    cot_h,
    embed_h,
    hid_h,
    pre_h,
    featb_h,
    board_b_h,
    neigh_b_h,
    comb1_b_h,
    st_h,
    dnum_h,
    dz_h,
    agg_h,
    stats_ref,
    stage,
    featb,
    hid,
    pre,
    board_b,
    neigh_b,
    comb_b,
    keys,
    msg,
    acc,
    spread,
    spread_t,
    out_slots,
    in_slots,
    out_tot,
    in_tot,
    picker,
    num,
    zval,
    zpre,
    cot,
    agg,
    dz,
    dnum,
    count_l,
    count_z,
    count_x,
    load_sem,
    store_sem,
    key_send,
    key_recv,
    up_send,
    down_send,
    msg_recv,
    slot_send,
    slot_recv,
    tot_send,
    tot_recv,
    count_send,
    count_recv,
):
    place = Place(n_nodes, n_grp)
    z, low = place.at["z"], place.at["l"]
    layer = place.size["l"]
    rows, width = featb.shape
    edges = keys.shape[2]
    layer_slots = spread.shape[1]
    cap = layer_slots // layer
    part = width // CHUNKS
    turn = math.gcd(edges, 1024)
    steps = edges // turn

    sources = [feats_h.at[:]]
    for whole in (board_h, neigh_h, comb_h):
        for first in range(0, whole.shape[0], rows):
            sources.append(whole.at[pl.ds(first, rows)])
    n_stage = stage.shape[0]

    def load(i):
        return pltpu.make_async_copy(sources[i], stage.at[i % n_stage], load_sem.at[i % n_stage])

    for i in range(n_stage):
        load(i).start()
    load_cot = pltpu.make_async_copy(cot_h, cot, load_sem.at[n_stage])
    stores = []

    def store(src, dst):
        copy = pltpu.make_async_copy(src, dst, store_sem.at[len(stores)])
        copy.start()
        stores.append(copy)

    barrier(place, ("l", "z", "x"))
    keys[z] = keys_ref[...]

    def key_copy(far, device):
        return remote(keys.at[z], keys.at[z], key_send.at[far], key_recv.at[far], device)

    for far, _, device in place.others("z"):
        key_copy(far, device).start()
    share = Share(place, (count_l, count_z, count_x), count_send, count_recv)
    mask = mask_ref[...]
    share.start(0, jnp.full((8, 128), jnp.sum(mask)))

    def cast(i, target, first):
        load(i).wait()
        slot = stage.at[i % n_stage]

        @pl.loop(0, rows // 32)
        def _(r):
            at = pl.ds(pl.multiple_of(r * 32, 32), 32)
            to = pl.ds(pl.multiple_of(first + r * 32, 32), 32)
            target[to, :] = slot[at, :].astype(BF16)

    cast(0, featb, 0)
    cast(1, board_b, 0)
    cast(2, board_b, rows)

    @pl.loop(0, CHUNKS)
    def _(k):
        at = pl.ds(pl.multiple_of(k * part, part), part)
        proj = jnp.dot(featb[...], board_b[:, at], preferred_element_type=F32)
        hid[:, at] = jnp.where(mask > 0.5, proj, stage[0, :, at]).astype(BF16)

    cast(3, neigh_b, 0)
    cast(4, neigh_b, rows)
    for i in range(n_stage, len(sources)):
        load(i).start()
    load_cot.start()

    def up_copy(src, k):
        piece = msg.at[src, k]
        index = src * CHUNKS + k
        return remote(
            piece, piece, up_send.at[index], msg_recv.at[index], place.member("z", z + 1)
        )

    def down_copy(src, k):
        piece = msg.at[src, k]
        index = src * CHUNKS + k
        return remote(
            piece, piece, down_send.at[index], msg_recv.at[index], place.member("z", z - 1)
        )

    @pl.loop(0, CHUNKS)
    def _(k):
        at = pl.ds(pl.multiple_of(k * part, part), part)
        value = jnp.dot(hid[...], neigh_b[:, at], preferred_element_type=F32) + nbias_ref[:, at]
        pre[:, at] = value
        msg[z, k] = gelu(value).astype(BF16)

        @pl.when(z < LINE - 1)
        def _():
            up_copy(z, k).start()

        @pl.when(z > 0)
        def _():
            down_copy(z, k).start()

    def forward(s):
        k = lax.rem(s, CHUNKS)
        below = z - 1 - s // CHUNKS
        above = z + 1 + s // CHUNKS

        @pl.when(below >= 0)
        def _():
            up_copy(below, k).wait_recv()

            @pl.when(z < LINE - 1)
            def _():
                up_copy(below, k).start()

        @pl.when(above < LINE)
        def _():
            down_copy(above, k).wait_recv()

            @pl.when(z > 0)
            def _():
                down_copy(above, k).start()

    def tot_copy(src, far, index, device):
        at = (layer - 1) * src + far
        return remote(
            out_tot.at[src, pl.ds(pl.multiple_of(index * cap, cap), cap)],
            in_tot.at[src, pl.ds(pl.multiple_of(low * cap, cap), cap)],
            tot_send.at[at],
            tot_recv.at[at],
            device,
        )

    def finish_spread(src):
        total = acc[...]
        spread[src] = total.astype(BF16)
        spread_t[src] = total.astype(BF16).T
        sums = jnp.sum(total, axis=1, keepdims=True).astype(jnp.int32)
        lane = lax.broadcasted_iota(jnp.int32, (layer_slots, 128), 1)
        digit = jnp.where(
            lane == 0, sums & 255, jnp.where(lane == 1, (sums >> 8) & 255, jnp.where(lane == 2, sums >> 16, 0))
        )
        out_tot[src] = digit.astype(F32).astype(BF16)
        own = pl.ds(pl.multiple_of(low * cap, cap), cap)
        in_tot[src, own] = out_tot[src, own]
        for far, index, device in place.others("l"):
            tot_copy(src, far, index, device).start()

    early = {}
    for s in range(CHUNKS * (LINE - 1)):
        when = int((5.4 * (s + 1) + 3.0) / 0.36)
        if when < LINE * steps:
            early[s] = when

    @pl.loop(0, LINE * steps)
    def _(i):
        which = i // steps
        t = i - which * steps
        src = lax.rem(z + which, LINE)

        @pl.when(t == 0)
        def _():
            acc[...] = jnp.zeros_like(acc)

        for far, index, device in place.others("z"):

            @pl.when(jnp.logical_and(t == 0, which == far + 1))
            def _(far=far):
                remote(
                    keys.at[src], keys.at[src], key_send.at[far], key_recv.at[LINE - 2 - far], device
                ).wait_recv()

        key = keys[src, :, pl.ds(pl.multiple_of(t * turn, turn), turn)]
        weight = (key & 15).astype(F32).astype(F8)
        child = (lax.shift_right_logical(key, 4) & (rows - 1)).astype(jnp.int16)
        shift = 4 + int(math.log2(rows))
        slot = (lax.shift_right_logical(key, shift) - z * layer_slots).astype(jnp.int16)
        right = jnp.where(
            lax.broadcasted_iota(jnp.int16, (rows, turn), 0) == child, weight, jnp.zeros((), F8)
        )
        block = 256
        for first in range(0, layer_slots, block):
            ids = lax.broadcasted_iota(jnp.int16, (block, turn), 0) + jnp.asarray(first, jnp.int16)
            left = jnp.where(ids == slot, jnp.ones((), F8), jnp.zeros((), F8))
            acc[pl.ds(first, block), :] += dot_nt(left, right)

        @pl.when(t == steps - 1)
        def _():
            finish_spread(src)

        for s, when in early.items():

            @pl.when(i == when)
            def _(s=s):
                forward(s)

        @pl.when(i == steps // 2)
        def _():
            share.start(1, share.finish(0))

        @pl.when(i == steps)
        def _():
            share.start(2, share.finish(1))

    boards = share.finish(2)[0:1, 0:1]
    scale = 1.0 / (width * (1.0 + boards))

    def slot_copy(src, k, far, index, device):
        at = (src * CHUNKS + k) * (layer - 1) + far
        return remote(
            out_slots.at[src, k, pl.ds(pl.multiple_of(index * cap, cap), cap)],
            in_slots.at[src, k, pl.ds(pl.multiple_of(low * cap, cap), cap)],
            slot_send.at[at],
            slot_recv.at[at],
            device,
        )

    def piece(src, k):
        out_slots[src, k] = jnp.dot(spread[src], msg[src, k], preferred_element_type=F32).astype(BF16)
        for far, index, device in place.others("l"):
            slot_copy(src, k, far, index, device).start()
        own = pl.ds(pl.multiple_of(low * cap, cap), cap)
        in_slots[src, k, own] = out_slots[src, k, own]

    def pick(src, k):
        for far, index, device in place.others("l"):
            slot_copy(src, k, far, index, device).wait_recv()
        num[k] += jnp.dot(picker[src], in_slots[src, k], preferred_element_type=F32)

    @pl.loop(0, CHUNKS)
    def _(k):
        piece(z, k)

    def both(j, act, k):
        @pl.when(z - 1 - j >= 0)
        def _():
            act(z - 1 - j, k)

        @pl.when(z + 1 + j < LINE)
        def _():
            act(z + 1 + j, k)

    def arrive(j, k):
        s = j * CHUNKS + k
        for done in range(CHUNKS):
            if j * CHUNKS + done not in early:

                @pl.when(k == done)
                def _(done=done):
                    forward(j * CHUNKS + done)

        both(j, piece, k)

    @pl.loop(0, CHUNKS)
    def _(k):
        arrive(0, k)

    num[...] = jnp.zeros_like(num)

    @pl.loop(0, LINE)
    def _(src):
        at = pl.ds(pl.multiple_of(src * layer_slots, layer_slots), layer_slots)
        ids = lax.broadcasted_iota(jnp.int32, (rows, layer_slots), 0)
        picker[src] = jnp.where(ids == targets_ref[:, at], 1.0, 0.0).astype(BF16)

    for i in range(5, 5 + 2 * width // rows):
        cast(i, comb_b, (i - 5) * rows)

    @pl.loop(0, CHUNKS)
    def _(k):
        at = pl.ds(pl.multiple_of(k * part, part), part)
        zpre[:, at] = (
            jnp.dot(hid[...], comb_b[0:width, at], preferred_element_type=F32) + cbias_ref[:, at]
        )

    store(hid, hid_h)
    store(pre, pre_h)
    store(featb, featb_h)
    store(board_b, board_b_h)
    store(neigh_b, neigh_b_h)
    store(comb_b.at[pl.ds(0, width)], comb1_b_h)
    store(spread_t, st_h)

    @pl.loop(0, CHUNKS)
    def _(k):
        pick(z, k)

    for j in range(1, LINE - 1):

        @pl.loop(0, CHUNKS)
        def _(k):
            both(j - 1, pick, k)
            arrive(j, k)

    den_digits = jnp.zeros((rows, 128), F32)
    for src in range(LINE):
        for far, index, device in place.others("l"):
            tot_copy(src, far, index, device).wait_recv()
        den_digits += jnp.dot(picker[src], in_tot[src], preferred_element_type=F32)
    lane = lax.broadcasted_iota(jnp.int32, (rows, 128), 1)
    worth = jnp.where(lane == 0, 1.0, jnp.where(lane == 1, 256.0, jnp.where(lane == 2, 65536.0, 0.0)))
    den = 1.0 + jnp.sum(den_digits * worth, axis=1, keepdims=True)
    load_cot.wait()

    @pl.loop(0, CHUNKS)
    def _(k):
        both(LINE - 2, pick, k)

    @pl.loop(0, CHUNKS)
    def _(k):
        at = pl.ds(pl.multiple_of(k * part, part), part)
        agg[:, at] = (num[k] / den).astype(BF16)

    def dense(k, carry):
        square, along = carry
        at = pl.ds(pl.multiple_of(k * part, part), part)
        value = zpre[:, at] + jnp.dot(
            agg[...], comb_b[width : 2 * width, at], preferred_element_type=F32
        )
        zpre[:, at] = value
        out = gelu(value)
        zval[:, at] = out
        square += jnp.sum(out * out, axis=1, keepdims=True)
        along += jnp.sum(out * cot[:, at], axis=1, keepdims=True)
        return square, along

    zero = jnp.zeros((rows, 1), F32)
    square, along = lax.fori_loop(0, CHUNKS, dense, (zero, zero))
    inverse = lax.rsqrt(square + 1e-06)
    along = along * inverse
    push = jnp.where(mask > 0.5, 2.0 * scale, 0.0)
    stats_ref[...] = jnp.concatenate(
        [
            jnp.full((8, 128), jnp.sum(jnp.where(mask > 0.5, square, 0.0))),
            jnp.broadcast_to(scale, (8, 128)),
        ],
        axis=0,
    )

    @pl.loop(0, CHUNKS)
    def _(k):
        at = pl.ds(pl.multiple_of(k * part, part), part)
        out = zval[:, at]
        emb = out * inverse
        grad = inverse * (cot[:, at] - emb * along) + push * out
        dz[:, at] = (grad * gelu_slope(zpre[:, at])).astype(BF16)
        zval[:, at] = emb

    store(zval, embed_h)
    store(dz, dz_h)
    store(agg, agg_h)

    @pl.loop(0, CHUNKS)
    def _(k):
        at = pl.ds(pl.multiple_of(k * part, part), part)
        back = dot_nt(dz[...], comb_b[pl.ds(pl.multiple_of(width + k * part, part), part), :])
        dnum[:, at] = (back / den).astype(BF16)

    store(dnum, dnum_h)

    for far, _, device in place.others("z"):
        key_copy(far, device).wait_send()

    @pl.loop(0, LINE * CHUNKS)
    def _(i):
        src = i // CHUNKS
        k = lax.rem(i, CHUNKS)

        @pl.when(jnp.logical_and(src <= z, z < LINE - 1))
        def _():
            up_copy(src, k).wait_send()

        @pl.when(jnp.logical_and(src >= z, z > 0))
        def _():
            down_copy(src, k).wait_send()

        for far, index, device in place.others("l"):
            slot_copy(src, k, far, index, device).wait_send()

    for src in range(LINE):
        for far, index, device in place.others("l"):
            tot_copy(src, far, index, device).wait_send()
    for copy in stores:
        copy.wait()


def forward_pass(n_nodes, n_grp, feats, mask, keys, targets, board, neigh, nbias, comb, cbias, cot):
    rows, width = feats.shape
    edges = keys.shape[1]
    layer = n_nodes // LINE
    layer_slots = targets.shape[1] // LINE
    part = width // CHUNKS
    dma = pltpu.SemaphoreType.DMA
    n_stage = 5
    big = pl.BlockSpec(memory_space=pl.ANY)
    small = pl.BlockSpec(memory_space=pltpu.VMEM)

    def hbm(shape, dtype):
        return jax.ShapeDtypeStruct(shape, dtype)

    return pl.pallas_call(
        functools.partial(forward_kernel, n_nodes, n_grp),
        out_shape=[
            hbm((rows, width), F32),
            hbm((rows, width), BF16),
            hbm((rows, width), F32),
            hbm((rows, width), BF16),
            hbm((width, width), BF16),
            hbm((width, width), BF16),
            hbm((width, width), BF16),
            hbm((LINE, rows, layer_slots), BF16),
            hbm((rows, width), BF16),
            hbm((rows, width), BF16),
            hbm((rows, width), BF16),
            hbm((16, 128), F32),
        ],
        in_specs=[big, small, small, small, big, big, small, big, small, big],
        out_specs=[big] * 11 + [small],
        scratch_shapes=[
            pltpu.VMEM((n_stage, rows, width), F32),
            pltpu.VMEM((rows, width), BF16),
            pltpu.VMEM((rows, width), BF16),
            pltpu.VMEM((rows, width), F32),
            pltpu.VMEM((width, width), BF16),
            pltpu.VMEM((width, width), BF16),
            pltpu.VMEM((2 * width, width), BF16),
            pltpu.VMEM((LINE, 1, edges), jnp.int32),
            pltpu.VMEM((LINE, CHUNKS, rows, part), BF16),
            pltpu.VMEM((layer_slots, rows), F32),
            pltpu.VMEM((LINE, layer_slots, rows), BF16),
            pltpu.VMEM((LINE, rows, layer_slots), BF16),
            pltpu.VMEM((LINE, CHUNKS, layer_slots, part), BF16),
            pltpu.VMEM((LINE, CHUNKS, layer_slots, part), BF16),
            pltpu.VMEM((LINE, layer_slots, 128), BF16),
            pltpu.VMEM((LINE, layer_slots, 128), BF16),
            pltpu.VMEM((LINE, rows, layer_slots), BF16),
            pltpu.VMEM((CHUNKS, rows, part), F32),
            pltpu.VMEM((rows, width), F32),
            pltpu.VMEM((rows, width), F32),
            pltpu.VMEM((rows, width), F32),
            pltpu.VMEM((rows, width), BF16),
            pltpu.VMEM((rows, width), BF16),
            pltpu.VMEM((rows, width), BF16),
            pltpu.VMEM((layer, 8, 128), F32),
            pltpu.VMEM((LINE, 8, 128), F32),
            pltpu.VMEM((n_grp, 8, 128), F32),
            dma((n_stage + 1,)),
            dma((11,)),
            dma((LINE - 1,)),
            dma((LINE - 1,)),
            dma((LINE * CHUNKS,)),
            dma((LINE * CHUNKS,)),
            dma((LINE * CHUNKS,)),
            dma((LINE * CHUNKS * (layer - 1),)),
            dma((LINE * CHUNKS * (layer - 1),)),
            dma((LINE * (layer - 1),)),
            dma((LINE * (layer - 1),)),
            dma((share_sems(n_nodes, n_grp),)),
            dma((share_sems(n_nodes, n_grp),)),
        ],
        compiler_params=pltpu.CompilerParams(
            vmem_limit_bytes=60 * MIB, collective_id=2, has_side_effects=True
        ),
        name="forward_pass",
    )(feats, mask, keys, targets, board, neigh, nbias, comb, cbias, cot)


def add_into(target, first, count, columns, parts, step=16):
    @pl.loop(0, count // step)
    def _(i):
        at = pl.ds(pl.multiple_of(first + i * step, step), step)
        total = target[at, columns].astype(F32)
        for part in parts:
            total += part[pl.ds(pl.multiple_of(i * step, step), step), :].astype(F32)
        target[at, columns] = total.astype(target.dtype)


def reduce_job(place, order, first, rows, grad, out, arrive, land, send, recv, base):
    half = grad.shape[1] // 2
    core = place.at["c"]
    mine = pl.ds(pl.multiple_of(core * half, half), half)
    theirs = pl.ds(pl.multiple_of((1 - core) * half, half), half)
    sem = base
    mate = place.member("c", 1 - core)
    block = pl.ds(first, rows)
    copy = pltpu.make_async_remote_copy(
        src_ref=grad.at[block, theirs],
        dst_ref=arrive,
        send_sem=send.at[sem],
        recv_sem=recv.at[sem],
        device_id=mate,
        device_id_type=MESH,
    )
    copy.start()
    sem += 1
    yield
    copy.wait()
    add_into(grad, first, rows, mine, [arrive])
    begin, length, used = first, rows, 0
    trail = []
    for axis in order:
        size = place.size[axis]
        length //= size
        copies, parts = [], []
        for far, index, device in place.others(axis):
            start = pl.multiple_of(begin + index * length, 16)
            slot = land.at[pl.ds(used, length)]
            used += length
            copy = pltpu.make_async_remote_copy(
                src_ref=grad.at[pl.ds(start, length), mine],
                dst_ref=slot,
                send_sem=send.at[sem],
                recv_sem=recv.at[sem],
                device_id=device,
                device_id_type=MESH,
            )
            copy.start()
            sem += 1
            copies.append(copy)
            parts.append(slot)
        yield
        for copy in copies:
            copy.wait()
        trail.append((axis, begin, length))
        begin = pl.multiple_of(begin + place.at[axis] * length, 16)
        add_into(grad, begin, length, mine, parts)
    at = pl.ds(begin, length)
    out[at, mine] = grad[at, mine]
    for axis, parent, piece in reversed(trail):
        size = place.size[axis]
        start = pl.multiple_of(parent + place.at[axis] * piece, 16)
        own = out.at[pl.ds(start, piece), mine]
        copies = []
        for far, index, device in place.others(axis):
            copy = pltpu.make_async_remote_copy(
                src_ref=own,
                dst_ref=own,
                send_sem=send.at[sem],
                recv_sem=recv.at[sem],
                device_id=device,
                device_id_type=MESH,
            )
            copy.start()
            sem += 1
            copies.append(copy)
        yield
        for copy in copies:
            copy.wait()
    own = out.at[block, mine]
    copy = pltpu.make_async_remote_copy(
        src_ref=own,
        dst_ref=own,
        send_sem=send.at[sem],
        recv_sem=recv.at[sem],
        device_id=mate,
        device_id_type=MESH,
    )
    copy.start()
    yield
    copy.wait()


def job_sems(n_nodes, n_grp):
    return 2 * (1 + (n_nodes // LINE // 2 - 1) + (LINE - 1) + (n_grp - 1))


def run_jobs(jobs, at_once):
    waiting, running = list(jobs), []
    while waiting or running:
        left = []
        for job in running:
            try:
                next(job)
                left.append(job)
            except StopIteration:
                pass
        for job in waiting[:at_once]:
            next(job)
            left.append(job)
        waiting = waiting[at_once:]
        running = left


def reduce_kernel(n_nodes, n_grp, count, grad_hbm, out_hbm, grad, out, arrive, land, send, recv, sem_in, sem_out):
    place = Place(n_nodes, n_grp)
    rows = grad.shape[0] // count
    loads = []
    for j in range(count):
        at = pl.ds(j * rows, rows)
        load = pltpu.make_async_copy(grad_hbm.at[at], grad.at[at], sem_in.at[j])
        load.start()
        loads.append(load)
    barrier(place, ("c", "x", "y", "z"))
    per_job = job_sems(n_nodes, n_grp)

    def job(j):
        at = pl.ds(j * rows, rows)
        loads[j].wait()
        yield from reduce_job(
            place,
            ("x", "y", "z") if j % 2 == 0 else ("y", "x", "z"),
            j * rows,
            rows,
            grad,
            out,
            arrive.at[at],
            land.at[pl.ds(j * 2 * rows, 2 * rows)],
            send,
            recv,
            j * per_job,
        )
        store = pltpu.make_async_copy(out.at[at], out_hbm.at[at], sem_out.at[j])
        store.start()
        stores.append(store)

    stores = []
    run_jobs([job(j) for j in range(count)], 2)
    for store in stores:
        store.wait()


def all_reduce(grads, n_nodes, n_grp):
    rows, width = grads.shape
    count = max(1, min(8, rows * 2 // (16 * n_nodes * n_grp)))
    sems = count * job_sems(n_nodes, n_grp)
    return pl.pallas_call(
        functools.partial(reduce_kernel, n_nodes, n_grp, count),
        out_shape=jax.ShapeDtypeStruct((rows, width), BF16),
        in_specs=[pl.BlockSpec(memory_space=pl.ANY)],
        out_specs=pl.BlockSpec(memory_space=pl.ANY),
        scratch_shapes=[
            pltpu.VMEM((rows, width), BF16),
            pltpu.VMEM((rows, width), BF16),
            pltpu.VMEM((rows, width // 2), BF16),
            pltpu.VMEM((2 * rows, width // 2), BF16),
            pltpu.SemaphoreType.DMA((sems,)),
            pltpu.SemaphoreType.DMA((sems,)),
            pltpu.SemaphoreType.DMA((count,)),
            pltpu.SemaphoreType.DMA((count,)),
        ],
        compiler_params=pltpu.CompilerParams(
            vmem_limit_bytes=48 * MIB, collective_id=1, has_side_effects=True
        ),
        name="sum_gradients",
    )(grads)


def on_device(
    n_nodes,
    n_grp,
    features,
    type_mask,
    edge_child,
    edge_slot,
    edge_weight,
    recv_rows,
    board_proj,
    neigh_proj,
    neigh_bias,
    combine_proj,
    combine_bias,
    out_cot,
):
    feats = features[0]
    rows, width = feats.shape
    peers = recv_rows.shape[2]
    cap = recv_rows.shape[3]
    layer = n_nodes // LINE
    slots = peers * cap
    mask = type_mask[0].astype(F32).reshape(rows, 1)
    board = mask > 0.5
    keys = ((edge_slot[0] * rows + edge_child[0]) * 16 + edge_weight[0]).reshape(1, -1)
    targets = recv_rows[0, 0].reshape(1, slots)
    embed, hidden, pre, featb, pbl, qwl, cwl1, spread_t, dnum, dzb, aggb, stats = forward_pass(
        n_nodes,
        n_grp,
        feats,
        mask,
        keys,
        targets,
        board_proj,
        neigh_proj,
        neigh_bias.reshape(1, width),
        combine_proj,
        combine_bias.reshape(1, width),
        out_cot[0],
    )
    board_sq = stats[0, 0]
    scale = stats[8, 0]
    joined = jnp.concatenate([hidden, aggb], axis=1)
    grad_comb = dot_tn(joined, dzb).astype(BF16)
    grad_cbias = jnp.sum(dzb.astype(F32), axis=0)
    picker = (targets[0][None, :] == jnp.arange(rows, dtype=jnp.int32)[:, None]).astype(BF16)
    back_slots = dot_tn(picker, dnum).astype(BF16).reshape(LINE, layer, cap, width)
    layers = [[i * layer + j for j in range(layer)] for i in range(LINE)]
    lines = [[i * layer + j for i in range(LINE)] for j in range(layer)]
    returned = lax.all_to_all(
        back_slots, "nodes", split_axis=1, concat_axis=1, tiled=True, axis_index_groups=layers
    ).reshape(LINE, layer * cap, width)
    partial = jnp.einsum("zcs,zsd->zcd", spread_t, returned, preferred_element_type=F32)
    dmsg = lax.psum_scatter(
        partial, "nodes", scatter_dimension=0, axis_index_groups=lines, tiled=False
    )
    dpre = (dmsg * gelu_slope(pre)).astype(BF16)
    grad_qbias = jnp.sum(dpre.astype(F32), axis=0)
    grad_neigh = dot_tn(hidden, dpre).astype(BF16)
    dhid = (dot_nt(dzb, cwl1) + dot_nt(dpre, qwl)).astype(BF16)
    dproj = jnp.where(board, dhid, jnp.zeros_like(dhid))
    grad_board = dot_tn(featb, dproj).astype(BF16)
    grad_feats = jnp.where(board, dot_nt(dproj, pbl), dhid.astype(F32))
    small = lax.psum(
        jnp.concatenate([grad_qbias, grad_cbias, jnp.full((width,), board_sq)]), ("nodes", "grp")
    )
    penalty = small[2 * width] * scale
    summed = all_reduce(
        jnp.concatenate([grad_comb, grad_neigh, grad_board], axis=0), n_nodes, n_grp
    )
    return (
        embed[None],
        penalty,
        grad_feats[None],
        summed[3 * width :].astype(F32),
        summed[2 * width : 3 * width].astype(F32),
        small[:width],
        summed[: 2 * width].astype(F32),
        small[width : 2 * width],
    )


def solution(mesh):
    in_specs = (
        P("grp", "nodes", None),
        P("grp", "nodes"),
        P("grp", "nodes"),
        P("grp", "nodes"),
        P("grp", "nodes"),
        P("grp", "nodes", None, None),
        P(),
        P(),
        P(),
        P(),
        P(),
        P("grp", "nodes", None),
    )
    out_specs = (P("grp", "nodes", None), P(), P("grp", "nodes", None), P(), P(), P(), P(), P())
    return jax.shard_map(
        functools.partial(on_device, mesh.shape["nodes"], mesh.shape["grp"]),
        mesh=mesh,
        in_specs=in_specs,
        out_specs=out_specs,
        check_vma=False,
    )
```

```python
import functools
import math

import jax
import jax.numpy as jnp
from jax import lax
from jax.experimental import pallas as pl
from jax.experimental.pallas import tpu as pltpu
from jax.sharding import PartitionSpec as P

HIGH = lax.Precision.HIGHEST
MESH = pl.DeviceIdType.MESH
BF16 = jnp.bfloat16
F32 = jnp.float32
F8 = jnp.float8_e4m3fn
MIB = 2**20


def gelu_tanh(v):
    return jax.nn.gelu(v, approximate=True)


def dot_nt(left, right):
    return lax.dot_general(
        left, right, (((1,), (1,)), ((), ())), preferred_element_type=F32
    )


def dot_tn(left, right):
    return lax.dot_general(
        left, right, (((0,), (0,)), ((), ())), preferred_element_type=F32
    )


LINE = 4
CHUNKS = 4
ORDER = ((0, 1, 2, 3), (1, 2, 0, 3))


class Place:
    def __init__(self, n_nodes, n_grp):
        layer = n_nodes // LINE
        node = lax.axis_index("nodes")
        grp = lax.axis_index("grp")
        self.node, self.grp = node, grp
        self.size = {"l": layer, "c": 2, "y": layer // 2, "z": LINE, "x": n_grp}
        low = lax.rem(node, layer)
        self.at = {"l": low, "c": lax.rem(low, 2), "y": low // 2, "z": node // layer, "x": grp}

    def member(self, axis, index):
        layer = self.size["l"]
        low, line, grp = self.at["l"], self.at["z"], self.at["x"]
        if axis == "l":
            low = index
        elif axis == "c":
            low = self.at["y"] * 2 + index
        elif axis == "y":
            low = index * 2 + self.at["c"]
        elif axis == "z":
            line = index
        else:
            grp = index
        return {"nodes": line * layer + low, "grp": grp}

    def others(self, axis):
        size = self.size[axis]
        for far in range(1, size):
            index = lax.rem(self.at[axis] + far, size)
            yield far - 1, index, self.member(axis, index)


def remote(src, dst, send, recv, device):
    return pltpu.make_async_remote_copy(
        src_ref=src, dst_ref=dst, send_sem=send, recv_sem=recv, device_id=device, device_id_type=MESH
    )


def barrier(place, axes):
    sem = pltpu.get_barrier_semaphore()
    count = 0
    for axis in axes:
        for _, _, device in place.others(axis):
            pl.semaphore_signal(sem, inc=1, device_id=device, device_id_type=MESH)
            count += 1
    pl.semaphore_wait(sem, count)


def gelu(v):
    t = jnp.tanh(0.7978845608028654 * (v + 0.044715 * (v * v * v)))
    return v * (0.5 * (1.0 + t))


def gelu_slope(v):
    square = v * v
    t = jnp.tanh(0.7978845608028654 * (v + 0.044715 * (v * square)))
    bend = 0.7978845608028654 * (1.0 + 0.134145 * square)
    return 0.5 * (1.0 + t) + 0.5 * v * (1.0 - t * t) * bend


class Share:
    def __init__(self, place, bufs, send, recv):
        self.place, self.send, self.recv = place, send, recv
        self.stages, base = [], 0
        for axis, buf in zip(("l", "z", "x"), bufs):
            self.stages.append((axis, buf, base))
            base += place.size[axis] - 1

    def start(self, stage, value):
        axis, buf, base = self.stages[stage]
        me = self.place.at[axis]
        buf[me] = value
        for far, _, device in self.place.others(axis):
            remote(
                buf.at[me], buf.at[me], self.send.at[base + far], self.recv.at[base + far], device
            ).start()

    def finish(self, stage):
        axis, buf, base = self.stages[stage]
        me = self.place.at[axis]
        for far, _, device in self.place.others(axis):
            remote(
                buf.at[me], buf.at[me], self.send.at[base + far], self.recv.at[base + far], device
            ).wait()
        total = buf[0]
        for i in range(1, self.place.size[axis]):
            total += buf[i]
        return total


def share_sems(n_nodes, n_grp):
    return (n_nodes // LINE - 1) + (LINE - 1) + max(1, n_grp - 1)


def forward_kernel(
    n_nodes,
    n_grp,
    feats_h,
    mask_ref,
    keys_ref,
    targets_ref,
    board_h,
    neigh_h,
    nbias_ref,
    comb_h,
    cbias_ref,
    cot_h,
    embed_h,
    hid_h,
    pre_h,
    featb_h,
    board_b_h,
    neigh_b_h,
    comb1_b_h,
    st_h,
    dnum_h,
    dz_h,
    agg_h,
    stats_ref,
    stage,
    featb,
    hid,
    pre,
    board_b,
    neigh_b,
    comb_b,
    keys,
    msg,
    acc,
    spread,
    spread_t,
    out_slots,
    in_slots,
    out_tot,
    in_tot,
    picker,
    num,
    zval,
    zpre,
    cot,
    agg,
    dz,
    dnum,
    count_l,
    count_z,
    count_x,
    load_sem,
    store_sem,
    key_send,
    key_recv,
    up_send,
    down_send,
    msg_recv,
    slot_send,
    slot_recv,
    tot_send,
    tot_recv,
    count_send,
    count_recv,
):
    place = Place(n_nodes, n_grp)
    z, low = place.at["z"], place.at["l"]
    layer = place.size["l"]
    rows, width = featb.shape
    edges = keys.shape[2]
    layer_slots = spread.shape[1]
    cap = layer_slots // layer
    part = width // CHUNKS
    turn = math.gcd(edges, 2560)
    steps = edges // turn

    sources = [feats_h.at[:]]
    for whole in (board_h, neigh_h, comb_h):
        for first in range(0, whole.shape[0], rows):
            sources.append(whole.at[pl.ds(first, rows)])
    n_stage = stage.shape[0]

    def load(i):
        return pltpu.make_async_copy(sources[i], stage.at[i % n_stage], load_sem.at[i % n_stage])

    for i in range(n_stage):
        load(i).start()
    load_cot = pltpu.make_async_copy(cot_h, cot, load_sem.at[n_stage])
    stores = []

    def store(src, dst):
        copy = pltpu.make_async_copy(src, dst, store_sem.at[len(stores)])
        copy.start()
        stores.append(copy)

    barrier(place, ("l", "z", "x"))
    keys[z] = keys_ref[...]

    def key_copy(far, device):
        return remote(keys.at[z], keys.at[z], key_send.at[far], key_recv.at[far], device)

    for far, _, device in place.others("z"):
        key_copy(far, device).start()
    share = Share(place, (count_l, count_z, count_x), count_send, count_recv)
    mask = mask_ref[...]
    share.start(0, jnp.full((8, 128), jnp.sum(mask)))

    def cast(i, target, first):
        load(i).wait()
        slot = stage.at[i % n_stage]

        @pl.loop(0, rows // 32)
        def _(r):
            at = pl.ds(pl.multiple_of(r * 32, 32), 32)
            to = pl.ds(pl.multiple_of(first + r * 32, 32), 32)
            target[to, :] = slot[at, :].astype(BF16)

    cast(0, featb, 0)
    cast(1, board_b, 0)
    cast(2, board_b, rows)

    @pl.loop(0, CHUNKS)
    def _(k):
        at = pl.ds(pl.multiple_of(k * part, part), part)
        proj = jnp.dot(featb[...], board_b[:, at], preferred_element_type=F32)
        hid[:, at] = jnp.where(mask > 0.5, proj, stage[0, :, at]).astype(BF16)

    cast(3, neigh_b, 0)
    cast(4, neigh_b, rows)
    for i in range(n_stage, len(sources)):
        load(i).start()
    load_cot.start()

    def up_copy(src, k):
        piece = msg.at[src, k]
        index = src * CHUNKS + k
        return remote(
            piece, piece, up_send.at[index], msg_recv.at[index], place.member("z", z + 1)
        )

    def down_copy(src, k):
        piece = msg.at[src, k]
        index = src * CHUNKS + k
        return remote(
            piece, piece, down_send.at[index], msg_recv.at[index], place.member("z", z - 1)
        )

    @pl.loop(0, CHUNKS)
    def _(k):
        at = pl.ds(pl.multiple_of(k * part, part), part)
        value = jnp.dot(hid[...], neigh_b[:, at], preferred_element_type=F32) + nbias_ref[:, at]
        pre[:, at] = value
        msg[z, k] = gelu(value).astype(BF16)

        @pl.when(z < LINE - 1)
        def _():
            up_copy(z, k).start()

        @pl.when(z > 0)
        def _():
            down_copy(z, k).start()

    def forward(s):
        k = lax.rem(s, CHUNKS)
        below = z - 1 - s // CHUNKS
        above = z + 1 + s // CHUNKS

        @pl.when(below >= 0)
        def _():
            up_copy(below, k).wait_recv()

            @pl.when(z < LINE - 1)
            def _():
                up_copy(below, k).start()

        @pl.when(above < LINE)
        def _():
            down_copy(above, k).wait_recv()

            @pl.when(z > 0)
            def _():
                down_copy(above, k).start()

    def tot_copy(src, far, index, device):
        at = (layer - 1) * src + far
        return remote(
            out_tot.at[src, pl.ds(pl.multiple_of(index * cap, cap), cap)],
            in_tot.at[src, pl.ds(pl.multiple_of(low * cap, cap), cap)],
            tot_send.at[at],
            tot_recv.at[at],
            device,
        )

    def finish_spread(src):
        total = acc[...]
        spread[src] = total.astype(BF16)
        spread_t[src] = total.astype(BF16).T
        sums = jnp.sum(total, axis=1, keepdims=True).astype(jnp.int32)
        lane = lax.broadcasted_iota(jnp.int32, (layer_slots, 128), 1)
        digit = jnp.where(
            lane == 0, sums & 255, jnp.where(lane == 1, (sums >> 8) & 255, jnp.where(lane == 2, sums >> 16, 0))
        )
        out_tot[src] = digit.astype(F32).astype(BF16)
        own = pl.ds(pl.multiple_of(low * cap, cap), cap)
        in_tot[src, own] = out_tot[src, own]
        for far, index, device in place.others("l"):
            tot_copy(src, far, index, device).start()

    def source(which):
        flip = z // 2
        inner = z * (1 - 2 * flip) + (LINE - 1) * flip
        index = ORDER[0][which] * (1 - inner) + ORDER[1][which] * inner
        return index * (1 - 2 * flip) + (LINE - 1) * flip

    def build(which, ticks):
        src = source(which)
        acc[...] = jnp.zeros_like(acc)
        if which > 0:
            far = lax.rem(z - src - 1 + LINE, LINE)
            remote(
                keys.at[src], keys.at[src], key_send.at[0], key_recv.at[far], place.member("z", src)
            ).wait_recv()

        @pl.loop(0, steps)
        def _(t):
            key = keys[src, :, pl.ds(pl.multiple_of(t * turn, turn), turn)]
            weight = (key & 15).astype(F32).astype(F8)
            child = (lax.shift_right_logical(key, 4) & (rows - 1)).astype(jnp.int16)
            shift = 4 + int(math.log2(rows))
            slot = (lax.shift_right_logical(key, shift) - z * layer_slots).astype(jnp.int16)
            right = jnp.where(
                lax.broadcasted_iota(jnp.int16, (rows, turn), 0) == child, weight, jnp.zeros((), F8)
            )
            block = 256
            for first in range(0, layer_slots, block):
                ids = lax.broadcasted_iota(jnp.int16, (block, turn), 0) + jnp.asarray(
                    first, jnp.int16
                )
                left = jnp.where(ids == slot, jnp.ones((), F8), jnp.zeros((), F8))
                acc[pl.ds(first, block), :] += dot_nt(left, right)
            for share_of_loop, act in ticks:

                @pl.when(t == min(steps - 1, int(share_of_loop * steps)))
                def _(act=act):
                    act()

        finish_spread(src)

    def slot_copy(src, k, far, index, device):
        at = (src * CHUNKS + k) * (layer - 1) + far
        return remote(
            out_slots.at[src, k, pl.ds(pl.multiple_of(index * cap, cap), cap)],
            in_slots.at[src, k, pl.ds(pl.multiple_of(low * cap, cap), cap)],
            slot_send.at[at],
            slot_recv.at[at],
            device,
        )

    def piece(src, k):
        out_slots[src, k] = jnp.dot(spread[src], msg[src, k], preferred_element_type=F32).astype(BF16)
        for far, index, device in place.others("l"):
            slot_copy(src, k, far, index, device).start()
        own = pl.ds(pl.multiple_of(low * cap, cap), cap)
        in_slots[src, k, own] = out_slots[src, k, own]

    def pick(src, k):
        for far, index, device in place.others("l"):
            slot_copy(src, k, far, index, device).wait_recv()
        num[k] += jnp.dot(picker[src], in_slots[src, k], preferred_element_type=F32)

    def each(act, which, first, last):
        src = source(which)

        @pl.loop(first, last)
        def _(k):
            act(src, k)

    build(0, [(0.7, lambda: forward(0))])
    each(piece, 0, 0, CHUNKS)

    def second():
        forward(1)
        share.start(1, share.finish(0))

    build(1, [(0.3, second), (0.9, lambda: forward(2))])
    each(piece, 1, 0, CHUNKS - 1)

    def third():
        forward(3)
        share.start(2, share.finish(1))

    build(2, [(0.3, third), (0.9, lambda: forward(4))])
    each(piece, 1, CHUNKS - 1, CHUNKS)
    each(piece, 2, 0, 1)
    build(3, [(0.5, lambda: forward(5)), (0.9, lambda: forward(6))])
    each(piece, 2, 1, 3)

    @pl.loop(0, LINE)
    def _(src):
        at = pl.ds(pl.multiple_of(src * layer_slots, layer_slots), layer_slots)
        ids = lax.broadcasted_iota(jnp.int32, (rows, layer_slots), 0)
        picker[src] = jnp.where(ids == targets_ref[:, at], 1.0, 0.0).astype(BF16)

    num[...] = jnp.zeros_like(num)
    boards = share.finish(2)[0:1, 0:1]
    scale = 1.0 / (width * (1.0 + boards))
    forward(7)
    each(piece, 2, 3, 4)

    for i in range(5, 5 + 2 * width // rows):
        cast(i, comb_b, (i - 5) * rows)

    @pl.loop(0, CHUNKS)
    def _(k):
        at = pl.ds(pl.multiple_of(k * part, part), part)
        zpre[:, at] = (
            jnp.dot(hid[...], comb_b[0:width, at], preferred_element_type=F32) + cbias_ref[:, at]
        )

    store(hid, hid_h)
    store(pre, pre_h)
    store(featb, featb_h)
    store(board_b, board_b_h)
    store(neigh_b, neigh_b_h)
    store(comb_b.at[pl.ds(0, width)], comb1_b_h)
    store(spread_t, st_h)
    each(pick, 0, 0, CHUNKS)
    forward(8)
    each(piece, 3, 0, 1)
    each(pick, 1, 0, CHUNKS)
    forward(9)
    each(piece, 3, 1, 2)
    each(pick, 2, 0, CHUNKS)
    forward(10)
    each(piece, 3, 2, 3)
    each(pick, 3, 0, 1)
    den_digits = jnp.zeros((rows, 128), F32)
    for src in range(LINE):
        for far, index, device in place.others("l"):
            tot_copy(src, far, index, device).wait_recv()
        den_digits += jnp.dot(picker[src], in_tot[src], preferred_element_type=F32)
    lane = lax.broadcasted_iota(jnp.int32, (rows, 128), 1)
    worth = jnp.where(lane == 0, 1.0, jnp.where(lane == 1, 256.0, jnp.where(lane == 2, 65536.0, 0.0)))
    den = 1.0 + jnp.sum(den_digits * worth, axis=1, keepdims=True)
    load_cot.wait()

    forward(11)
    each(piece, 3, 3, 4)
    each(pick, 3, 1, 4)

    @pl.loop(0, CHUNKS)
    def _(k):
        at = pl.ds(pl.multiple_of(k * part, part), part)
        agg[:, at] = (num[k] / den).astype(BF16)

    def dense(k, carry):
        square, along = carry
        at = pl.ds(pl.multiple_of(k * part, part), part)
        value = zpre[:, at] + jnp.dot(
            agg[...], comb_b[width : 2 * width, at], preferred_element_type=F32
        )
        zpre[:, at] = value
        out = gelu(value)
        zval[:, at] = out
        square += jnp.sum(out * out, axis=1, keepdims=True)
        along += jnp.sum(out * cot[:, at], axis=1, keepdims=True)
        return square, along

    zero = jnp.zeros((rows, 1), F32)
    square, along = lax.fori_loop(0, CHUNKS, dense, (zero, zero))
    inverse = lax.rsqrt(square + 1e-06)
    along = along * inverse
    push = jnp.where(mask > 0.5, 2.0 * scale, 0.0)
    stats_ref[...] = jnp.concatenate(
        [
            jnp.full((8, 128), jnp.sum(jnp.where(mask > 0.5, square, 0.0))),
            jnp.broadcast_to(scale, (8, 128)),
        ],
        axis=0,
    )

    @pl.loop(0, CHUNKS)
    def _(k):
        at = pl.ds(pl.multiple_of(k * part, part), part)
        out = zval[:, at]
        emb = out * inverse
        grad = inverse * (cot[:, at] - emb * along) + push * out
        dz[:, at] = (grad * gelu_slope(zpre[:, at])).astype(BF16)
        zval[:, at] = emb

    store(zval, embed_h)
    store(dz, dz_h)
    store(agg, agg_h)

    @pl.loop(0, CHUNKS)
    def _(k):
        at = pl.ds(pl.multiple_of(k * part, part), part)
        back = dot_nt(dz[...], comb_b[pl.ds(pl.multiple_of(width + k * part, part), part), :])
        dnum[:, at] = (back / den).astype(BF16)

    store(dnum, dnum_h)

    for far, _, device in place.others("z"):
        key_copy(far, device).wait_send()

    @pl.loop(0, LINE * CHUNKS)
    def _(i):
        src = i // CHUNKS
        k = lax.rem(i, CHUNKS)

        @pl.when(jnp.logical_and(src <= z, z < LINE - 1))
        def _():
            up_copy(src, k).wait_send()

        @pl.when(jnp.logical_and(src >= z, z > 0))
        def _():
            down_copy(src, k).wait_send()

        for far, index, device in place.others("l"):
            slot_copy(src, k, far, index, device).wait_send()

    for src in range(LINE):
        for far, index, device in place.others("l"):
            tot_copy(src, far, index, device).wait_send()
    for copy in stores:
        copy.wait()


def forward_pass(n_nodes, n_grp, feats, mask, keys, targets, board, neigh, nbias, comb, cbias, cot):
    rows, width = feats.shape
    edges = keys.shape[1]
    layer = n_nodes // LINE
    layer_slots = targets.shape[1] // LINE
    part = width // CHUNKS
    dma = pltpu.SemaphoreType.DMA
    n_stage = 5
    big = pl.BlockSpec(memory_space=pl.ANY)
    small = pl.BlockSpec(memory_space=pltpu.VMEM)

    def hbm(shape, dtype):
        return jax.ShapeDtypeStruct(shape, dtype)

    return pl.pallas_call(
        functools.partial(forward_kernel, n_nodes, n_grp),
        out_shape=[
            hbm((rows, width), F32),
            hbm((rows, width), BF16),
            hbm((rows, width), F32),
            hbm((rows, width), BF16),
            hbm((width, width), BF16),
            hbm((width, width), BF16),
            hbm((width, width), BF16),
            hbm((LINE, rows, layer_slots), BF16),
            hbm((rows, width), BF16),
            hbm((rows, width), BF16),
            hbm((rows, width), BF16),
            hbm((16, 128), F32),
        ],
        in_specs=[big, small, small, small, big, big, small, big, small, big],
        out_specs=[big] * 11 + [small],
        scratch_shapes=[
            pltpu.VMEM((n_stage, rows, width), F32),
            pltpu.VMEM((rows, width), BF16),
            pltpu.VMEM((rows, width), BF16),
            pltpu.VMEM((rows, width), F32),
            pltpu.VMEM((width, width), BF16),
            pltpu.VMEM((width, width), BF16),
            pltpu.VMEM((2 * width, width), BF16),
            pltpu.VMEM((LINE, 1, edges), jnp.int32),
            pltpu.VMEM((LINE, CHUNKS, rows, part), BF16),
            pltpu.VMEM((layer_slots, rows), F32),
            pltpu.VMEM((LINE, layer_slots, rows), BF16),
            pltpu.VMEM((LINE, rows, layer_slots), BF16),
            pltpu.VMEM((LINE, CHUNKS, layer_slots, part), BF16),
            pltpu.VMEM((LINE, CHUNKS, layer_slots, part), BF16),
            pltpu.VMEM((LINE, layer_slots, 128), BF16),
            pltpu.VMEM((LINE, layer_slots, 128), BF16),
            pltpu.VMEM((LINE, rows, layer_slots), BF16),
            pltpu.VMEM((CHUNKS, rows, part), F32),
            pltpu.VMEM((rows, width), F32),
            pltpu.VMEM((rows, width), F32),
            pltpu.VMEM((rows, width), F32),
            pltpu.VMEM((rows, width), BF16),
            pltpu.VMEM((rows, width), BF16),
            pltpu.VMEM((rows, width), BF16),
            pltpu.VMEM((layer, 8, 128), F32),
            pltpu.VMEM((LINE, 8, 128), F32),
            pltpu.VMEM((n_grp, 8, 128), F32),
            dma((n_stage + 1,)),
            dma((11,)),
            dma((LINE - 1,)),
            dma((LINE - 1,)),
            dma((LINE * CHUNKS,)),
            dma((LINE * CHUNKS,)),
            dma((LINE * CHUNKS,)),
            dma((LINE * CHUNKS * (layer - 1),)),
            dma((LINE * CHUNKS * (layer - 1),)),
            dma((LINE * (layer - 1),)),
            dma((LINE * (layer - 1),)),
            dma((share_sems(n_nodes, n_grp),)),
            dma((share_sems(n_nodes, n_grp),)),
        ],
        compiler_params=pltpu.CompilerParams(
            vmem_limit_bytes=60 * MIB, collective_id=2, has_side_effects=True
        ),
        name="forward_pass",
    )(feats, mask, keys, targets, board, neigh, nbias, comb, cbias, cot)


def add_into(target, first, count, columns, parts, step=16):
    @pl.loop(0, count // step)
    def _(i):
        at = pl.ds(pl.multiple_of(first + i * step, step), step)
        total = target[at, columns].astype(F32)
        for part in parts:
            total += part[pl.ds(pl.multiple_of(i * step, step), step), :].astype(F32)
        target[at, columns] = total.astype(target.dtype)


def reduce_job(place, order, first, rows, grad, out, arrive, land, send, recv, base):
    half = grad.shape[1] // 2
    core = place.at["c"]
    mine = pl.ds(pl.multiple_of(core * half, half), half)
    theirs = pl.ds(pl.multiple_of((1 - core) * half, half), half)
    sem = base
    mate = place.member("c", 1 - core)
    block = pl.ds(first, rows)
    copy = pltpu.make_async_remote_copy(
        src_ref=grad.at[block, theirs],
        dst_ref=arrive,
        send_sem=send.at[sem],
        recv_sem=recv.at[sem],
        device_id=mate,
        device_id_type=MESH,
    )
    copy.start()
    sem += 1
    yield
    copy.wait()
    add_into(grad, first, rows, mine, [arrive])
    begin, length, used = first, rows, 0
    trail = []
    for axis in order:
        size = place.size[axis]
        length //= size
        copies, parts = [], []
        for far, index, device in place.others(axis):
            start = pl.multiple_of(begin + index * length, 16)
            slot = land.at[pl.ds(used, length)]
            used += length
            copy = pltpu.make_async_remote_copy(
                src_ref=grad.at[pl.ds(start, length), mine],
                dst_ref=slot,
                send_sem=send.at[sem],
                recv_sem=recv.at[sem],
                device_id=device,
                device_id_type=MESH,
            )
            copy.start()
            sem += 1
            copies.append(copy)
            parts.append(slot)
        yield
        for copy in copies:
            copy.wait()
        trail.append((axis, begin, length))
        begin = pl.multiple_of(begin + place.at[axis] * length, 16)
        add_into(grad, begin, length, mine, parts)
    at = pl.ds(begin, length)
    out[at, mine] = grad[at, mine]
    for axis, parent, piece in reversed(trail):
        size = place.size[axis]
        start = pl.multiple_of(parent + place.at[axis] * piece, 16)
        own = out.at[pl.ds(start, piece), mine]
        copies = []
        for far, index, device in place.others(axis):
            copy = pltpu.make_async_remote_copy(
                src_ref=own,
                dst_ref=own,
                send_sem=send.at[sem],
                recv_sem=recv.at[sem],
                device_id=device,
                device_id_type=MESH,
            )
            copy.start()
            sem += 1
            copies.append(copy)
        yield
        for copy in copies:
            copy.wait()
    own = out.at[block, mine]
    copy = pltpu.make_async_remote_copy(
        src_ref=own,
        dst_ref=own,
        send_sem=send.at[sem],
        recv_sem=recv.at[sem],
        device_id=mate,
        device_id_type=MESH,
    )
    copy.start()
    yield
    copy.wait()


def job_sems(n_nodes, n_grp):
    return 2 * (1 + (n_nodes // LINE // 2 - 1) + (LINE - 1) + (n_grp - 1))


class Line:
    def __init__(self):
        self.running = []

    def add(self, job):
        next(job)
        self.running.append(job)

    def tick(self):
        left = []
        for job in self.running:
            try:
                next(job)
                left.append(job)
            except StopIteration:
                pass
        self.running = left

    def drain(self):
        while self.running:
            self.tick()


def backward_kernel(
    n_nodes,
    n_grp,
    count,
    mask_ref,
    targets_ref,
    stats_ref,
    hid_h,
    pre_h,
    featb_h,
    board_b_h,
    neigh_b_h,
    comb1_b_h,
    st_h,
    dnum_h,
    dz_h,
    agg_h,
    gfeat_h,
    summed_h,
    small_ref,
    hid,
    pre,
    featb,
    board_b,
    neigh_b,
    comb1_b,
    spread_t,
    dnum,
    dz,
    agg,
    picker_t,
    out_slots,
    in_slots,
    chain,
    tmp,
    dpre,
    dh,
    grad,
    out,
    arrive,
    land,
    share_l,
    share_z,
    share_x,
    small,
    load_sem,
    store_sem,
    slot_send,
    slot_recv,
    up_send,
    down_send,
    chain_recv,
    job_send,
    job_recv,
    share_send,
    share_recv,
):
    place = Place(n_nodes, n_grp)
    z, low = place.at["z"], place.at["l"]
    layer = place.size["l"]
    rows, width = hid.shape
    layer_slots = spread_t.shape[2]
    cap = layer_slots // layer
    part = width // CHUNKS

    loads = {}
    for i, (name, src, dst) in enumerate(
        (
            ("dnum", dnum_h, dnum),
            ("hid", hid_h, hid),
            ("agg", agg_h, agg),
            ("dz", dz_h, dz),
            ("spread_t", st_h, spread_t),
            ("comb1_b", comb1_b_h, comb1_b),
            ("pre", pre_h, pre),
            ("neigh_b", neigh_b_h, neigh_b),
            ("featb", featb_h, featb),
            ("board_b", board_b_h, board_b),
        )
    ):
        loads[name] = pltpu.make_async_copy(src, dst, load_sem.at[i])
        loads[name].start()
    barrier(place, ("l", "z", "x"))
    stores = []

    def store(src, dst):
        copy = pltpu.make_async_copy(src, dst, store_sem.at[len(stores)])
        copy.start()
        stores.append(copy)

    mask = mask_ref[...] > 0.5

    def source(which):
        flip = z // 2
        inner = z * (1 - 2 * flip) + (LINE - 1) * flip
        index = ORDER[0][which] * (1 - inner) + ORDER[1][which] * inner
        return index * (1 - 2 * flip) + (LINE - 1) * flip

    def cols(k):
        return pl.ds(pl.multiple_of(k * part, part), part)

    def slot_copy(dst, k, far, index, device):
        at = (dst * CHUNKS + k) * (layer - 1) + far
        return remote(
            out_slots.at[dst, k, pl.ds(pl.multiple_of(index * cap, cap), cap)],
            in_slots.at[dst, k, pl.ds(pl.multiple_of(low * cap, cap), cap)],
            slot_send.at[at],
            slot_recv.at[at],
            device,
        )

    def back(dst, k):
        out_slots[dst, k] = jnp.dot(
            picker_t[dst], dnum[:, cols(k)], preferred_element_type=F32
        ).astype(BF16)
        for far, index, device in place.others("l"):
            slot_copy(dst, k, far, index, device).start()
        own = pl.ds(pl.multiple_of(low * cap, cap), cap)
        in_slots[dst, k, own] = out_slots[dst, k, own]

    def child_sums(dst, k):
        for far, index, device in place.others("l"):
            slot_copy(dst, k, far, index, device).wait_recv()
        tmp[...] = jnp.dot(spread_t[dst], in_slots[dst, k], preferred_element_type=F32)

    def up_copy(dst, k):
        at = dst * CHUNKS + k
        return remote(
            chain.at[dst, k],
            chain.at[dst, k],
            up_send.at[at],
            chain_recv.at[at],
            place.member("z", z + 1),
        )

    def down_copy(dst, k, last):
        slot = LINE if last else dst
        return remote(
            chain.at[dst, k],
            chain.at[slot, k],
            down_send.at[dst * CHUNKS + k],
            chain_recv.at[slot * CHUNKS + k],
            place.member("z", z - 1),
        )

    def arrived(slot, k):
        remote(
            chain.at[slot, k],
            chain.at[slot, k],
            up_send.at[0],
            chain_recv.at[slot * CHUNKS + k],
            place.member("z", lax.rem(z + 1, LINE)),
        ).wait_recv()

    def hand_on(dst, k):
        child_sums(dst, k)

        @pl.when(dst > z)
        def _():
            @pl.when(z > 0)
            def _():
                up_copy(dst, k).wait_recv()
                chain[dst, k] = (chain[dst, k].astype(F32) + tmp[...]).astype(BF16)

            @pl.when(z == 0)
            def _():
                chain[dst, k] = tmp[...].astype(BF16)

            up_copy(dst, k).start()

        @pl.when(dst < z)
        def _():
            @pl.when(z < LINE - 1)
            def _():
                down_copy(dst, k, False).wait_recv()
                chain[dst, k] = (chain[dst, k].astype(F32) + tmp[...]).astype(BF16)

            @pl.when(z == LINE - 1)
            def _():
                chain[dst, k] = tmp[...].astype(BF16)

            @pl.when(dst == z - 1)
            def _():
                down_copy(dst, k, True).start()

            @pl.when(dst < z - 1)
            def _():
                down_copy(dst, k, False).start()

    n_rows = grad.shape[0]
    job_rows = n_rows // count
    per_job = job_sems(n_nodes, n_grp)
    line = Line()

    def job(j):
        at = pl.ds(j * job_rows, job_rows)
        yield from reduce_job(
            place,
            ("x", "y", "z") if j % 2 == 0 else ("y", "x", "z"),
            j * job_rows,
            job_rows,
            grad,
            out,
            arrive.at[at],
            land.at[at],
            job_send,
            job_recv,
            j * per_job,
        )
        store(out.at[at], summed_h.at[at])

    @pl.loop(0, LINE)
    def _(src):
        at = pl.ds(pl.multiple_of(src * layer_slots, layer_slots), layer_slots)
        ids = lax.broadcasted_iota(jnp.int32, (layer_slots, rows), 1)
        picker_t[src] = jnp.where(ids == targets_ref[at, :], 1.0, 0.0).astype(BF16)

    loads["dnum"].wait()

    @pl.loop(0, CHUNKS)
    def _(k):
        for which in (3, 2):
            back(source(which), k)

    @pl.loop(0, CHUNKS)
    def _(k):
        for which in (1, 0):
            back(source(which), k)

    loads["spread_t"].wait()

    def chain_pair(k):
        hand_on(source(3), k)
        hand_on(source(2), k)

    chain_pair(0)
    for name in ("hid", "agg", "dz"):
        loads[name].wait()

    def comb_grad(left, first):
        @pl.loop(0, CHUNKS)
        def _(k):
            grad[pl.ds(first, width), cols(k)] = dot_tn(left[...], dz[:, cols(k)]).astype(BF16)

    comb_grad(hid, 0)
    comb_grad(agg, width)
    small[...] = jnp.zeros_like(small)
    small[1:2, :] = jnp.sum(dz[...].astype(F32), axis=0, keepdims=True)
    small[2:3, :] = jnp.broadcast_to(stats_ref[0:1, 0:1], (1, width))
    waiting = [job(j) for j in range(count)]
    half = count // 2

    def advance():
        line.tick()
        if len(waiting) > count - half:
            line.add(waiting.pop(0))

    advance()
    chain_pair(1)
    advance()
    loads["comb1_b"].wait()

    @pl.loop(0, CHUNKS)
    def _(k):
        dh[:, cols(k)] = dot_nt(dz[...], comb1_b[cols(k), :])

    for k in range(2, CHUNKS):
        chain_pair(k)
        advance()
    for k in range(CHUNKS):
        hand_on(source(1), k)
        advance()
    for name in ("pre", "neigh_b", "featb", "board_b"):
        loads[name].wait()

    def own(k):
        child_sums(z, k)

        @pl.when(z > 0)
        def _():
            arrived(z, k)
            tmp[...] += chain[z, k].astype(F32)

        @pl.when(z < LINE - 1)
        def _():
            arrived(LINE, k)
            tmp[...] += chain[LINE, k].astype(F32)

        down = (tmp[...] * gelu_slope(pre[:, cols(k)])).astype(BF16)
        dpre[:, cols(k)] = down
        small[0:1, cols(k)] = jnp.sum(down.astype(F32), axis=0, keepdims=True)
        grad[pl.ds(2 * width, width), cols(k)] = dot_tn(hid[...], down).astype(BF16)
        dh[...] += dot_nt(down, neigh_b[:, cols(k)])

    for k in range(CHUNKS):
        own(k)
        advance()
    while len(waiting) > count - half:
        advance()

    def tail_job():
        if waiting:
            line.add(waiting.pop(0))

    quarter = (count - half) // 2
    for _ in range(quarter):
        tail_job()
    share = Share(place, (share_l, share_z, share_x), share_send, share_recv)
    share.start(0, small[...])
    last = dh[...].astype(BF16)
    dpre[...] = jnp.where(mask, last, jnp.zeros_like(last))
    pre[...] = last.astype(F32)

    @pl.loop(0, CHUNKS)
    def _(k):
        grad[pl.ds(3 * width, width), cols(k)] = dot_tn(featb[...], dpre[:, cols(k)]).astype(BF16)

    line.tick()
    while waiting:
        tail_job()
    share.start(1, share.finish(0))

    @pl.loop(0, CHUNKS)
    def _(k):
        pre[:, cols(k)] = jnp.where(
            mask, dot_nt(dpre[...], board_b[cols(k), :]), pre[:, cols(k)]
        )

    store(pre, gfeat_h)
    line.tick()
    share.start(2, share.finish(1))
    line.tick()
    small_ref[...] = share.finish(2)
    line.drain()

    @pl.loop(0, LINE * CHUNKS)
    def _(i):
        dst = i // CHUNKS
        k = lax.rem(i, CHUNKS)

        @pl.when(dst > z)
        def _():
            up_copy(dst, k).wait_send()

        @pl.when(dst < z)
        def _():
            down_copy(dst, k, False).wait_send()

        for far, index, device in place.others("l"):
            slot_copy(dst, k, far, index, device).wait_send()

    for copy in stores:
        copy.wait()


def backward_pass(n_nodes, n_grp, mask, targets, stats, hid, pre, featb, board_b, neigh_b, comb1_b, st, dnum, dz, agg):
    rows, width = hid.shape
    layer = n_nodes // LINE
    layer_slots = st.shape[2]
    part = width // CHUNKS
    n_rows = 4 * width
    count = max(2, min(8, n_rows * 2 // (16 * n_nodes * n_grp)))
    dma = pltpu.SemaphoreType.DMA
    big = pl.BlockSpec(memory_space=pl.ANY)
    vmem = pl.BlockSpec(memory_space=pltpu.VMEM)
    sems = count * job_sems(n_nodes, n_grp)
    pieces = LINE * CHUNKS
    return pl.pallas_call(
        functools.partial(backward_kernel, n_nodes, n_grp, count),
        out_shape=[
            jax.ShapeDtypeStruct((rows, width), F32),
            jax.ShapeDtypeStruct((n_rows, width), BF16),
            jax.ShapeDtypeStruct((8, width), F32),
        ],
        in_specs=[vmem, vmem, vmem] + [big] * 10,
        out_specs=[big, big, vmem],
        scratch_shapes=[
            pltpu.VMEM((rows, width), BF16),
            pltpu.VMEM((rows, width), F32),
            pltpu.VMEM((rows, width), BF16),
            pltpu.VMEM((width, width), BF16),
            pltpu.VMEM((width, width), BF16),
            pltpu.VMEM((width, width), BF16),
            pltpu.VMEM((LINE, rows, layer_slots), BF16),
            pltpu.VMEM((rows, width), BF16),
            pltpu.VMEM((rows, width), BF16),
            pltpu.VMEM((rows, width), BF16),
            pltpu.VMEM((LINE, layer_slots, rows), BF16),
            pltpu.VMEM((LINE, CHUNKS, layer_slots, part), BF16),
            pltpu.VMEM((LINE, CHUNKS, layer_slots, part), BF16),
            pltpu.VMEM((LINE + 1, CHUNKS, rows, part), BF16),
            pltpu.VMEM((rows, part), F32),
            pltpu.VMEM((rows, width), BF16),
            pltpu.VMEM((rows, width), F32),
            pltpu.VMEM((n_rows, width), BF16),
            pltpu.VMEM((n_rows, width), BF16),
            pltpu.VMEM((n_rows, width // 2), BF16),
            pltpu.VMEM((n_rows, width // 2), BF16),
            pltpu.VMEM((layer, 8, width), F32),
            pltpu.VMEM((LINE, 8, width), F32),
            pltpu.VMEM((n_grp, 8, width), F32),
            pltpu.VMEM((8, width), F32),
            dma((10,)),
            dma((count + 1,)),
            dma((pieces * (layer - 1),)),
            dma((pieces * (layer - 1),)),
            dma((pieces,)),
            dma((pieces,)),
            dma((pieces + CHUNKS,)),
            dma((sems,)),
            dma((sems,)),
            dma((share_sems(n_nodes, n_grp),)),
            dma((share_sems(n_nodes, n_grp),)),
        ],
        compiler_params=pltpu.CompilerParams(
            vmem_limit_bytes=62 * MIB, collective_id=3, has_side_effects=True
        ),
        name="backward_pass",
    )(mask, targets, stats, hid, pre, featb, board_b, neigh_b, comb1_b, st, dnum, dz, agg)


def on_device(
    n_nodes,
    n_grp,
    features,
    type_mask,
    edge_child,
    edge_slot,
    edge_weight,
    recv_rows,
    board_proj,
    neigh_proj,
    neigh_bias,
    combine_proj,
    combine_bias,
    out_cot,
):
    feats = features[0]
    rows, width = feats.shape
    peers = recv_rows.shape[2]
    cap = recv_rows.shape[3]
    slots = peers * cap
    mask = type_mask[0].astype(F32).reshape(rows, 1)
    keys = ((edge_slot[0] * rows + edge_child[0]) * 16 + edge_weight[0]).reshape(1, -1)
    targets = recv_rows[0, 0].reshape(1, slots)
    embed, hidden, pre, featb, pbl, qwl, cwl1, spread_t, dnum, dzb, aggb, stats = forward_pass(
        n_nodes,
        n_grp,
        feats,
        mask,
        keys,
        targets,
        board_proj,
        neigh_proj,
        neigh_bias.reshape(1, width),
        combine_proj,
        combine_bias.reshape(1, width),
        out_cot[0],
    )
    grad_feats, summed, small = backward_pass(
        n_nodes,
        n_grp,
        mask,
        targets.reshape(slots, 1),
        stats,
        hidden,
        pre,
        featb,
        pbl,
        qwl,
        cwl1,
        spread_t,
        dnum,
        dzb,
        aggb,
    )
    penalty = small[2, 0] * stats[8, 0]
    return (
        embed[None],
        penalty,
        grad_feats[None],
        summed[3 * width :].astype(F32),
        summed[2 * width : 3 * width].astype(F32),
        small[0],
        summed[: 2 * width].astype(F32),
        small[1],
    )


def solution(mesh):
    in_specs = (
        P("grp", "nodes", None),
        P("grp", "nodes"),
        P("grp", "nodes"),
        P("grp", "nodes"),
        P("grp", "nodes"),
        P("grp", "nodes", None, None),
        P(),
        P(),
        P(),
        P(),
        P(),
        P("grp", "nodes", None),
    )
    out_specs = (P("grp", "nodes", None), P(), P("grp", "nodes", None), P(), P(), P(), P(), P())
    return jax.shard_map(
        functools.partial(on_device, mesh.shape["nodes"], mesh.shape["grp"]),
        mesh=mesh,
        in_specs=in_specs,
        out_specs=out_specs,
        check_vma=False,
    )
```

```python
import functools
import math

import jax
import jax.numpy as jnp
from jax import lax
from jax.experimental import pallas as pl
from jax.experimental.pallas import tpu as pltpu
from jax.sharding import PartitionSpec as P

HIGH = lax.Precision.HIGHEST
MESH = pl.DeviceIdType.MESH
BF16 = jnp.bfloat16
F32 = jnp.float32
F8 = jnp.float8_e4m3fn
MIB = 2**20


def gelu_tanh(v):
    return jax.nn.gelu(v, approximate=True)


def dot_nt(left, right):
    return lax.dot_general(
        left, right, (((1,), (1,)), ((), ())), preferred_element_type=F32
    )


def dot_tn(left, right):
    return lax.dot_general(
        left, right, (((0,), (0,)), ((), ())), preferred_element_type=F32
    )


LINE = 4
CHUNKS = 4
FORWARD = (
    "m0", "m1", "m2", "m3", "Y00", "Y01", "Y02", "Y03", "Z0", "f00", "p00", "p01", "p02", "p03",
    "Y10", "P1", "Y11", "f01", "Y12", "f02", "Y13", "Z1", "p10", "p11", "p12", "Y20", "P2", "Y21",
    "f03", "Y22", "Y23", "f10", "Z2", "p13", "p20", "Y30", "Y31", "f11", "Y32", "Y33", "f12", "Z3",
    "p21", "p22", "G0", "P3", "f13", "p23", "D0", "D1", "D2", "D3", "X0", "R0", "i00", "i01",
    "i02", "i03", "f20", "p30", "i10", "i11", "i12", "i13", "f21", "p31", "i20", "i21", "i22",
    "i23", "f22", "p32", "i30", "d0", "a0", "f23", "p33", "i31", "a1", "i32", "a2", "i33",
)
ORDER = ((0, 1, 2, 3), (1, 2, 0, 3))


class Place:
    def __init__(self, n_nodes, n_grp):
        layer = n_nodes // LINE
        node = lax.axis_index("nodes")
        grp = lax.axis_index("grp")
        self.node, self.grp = node, grp
        self.size = {"l": layer, "c": 2, "y": layer // 2, "z": LINE, "x": n_grp}
        low = lax.rem(node, layer)
        self.at = {"l": low, "c": lax.rem(low, 2), "y": low // 2, "z": node // layer, "x": grp}

    def member(self, axis, index):
        layer = self.size["l"]
        low, line, grp = self.at["l"], self.at["z"], self.at["x"]
        if axis == "l":
            low = index
        elif axis == "c":
            low = self.at["y"] * 2 + index
        elif axis == "y":
            low = index * 2 + self.at["c"]
        elif axis == "z":
            line = index
        else:
            grp = index
        return {"nodes": line * layer + low, "grp": grp}

    def others(self, axis):
        size = self.size[axis]
        for far in range(1, size):
            index = lax.rem(self.at[axis] + far, size)
            yield far - 1, index, self.member(axis, index)


def remote(src, dst, send, recv, device):
    return pltpu.make_async_remote_copy(
        src_ref=src, dst_ref=dst, send_sem=send, recv_sem=recv, device_id=device, device_id_type=MESH
    )


def barrier(place, axes):
    sem = pltpu.get_barrier_semaphore()
    count = 0
    for axis in axes:
        for _, _, device in place.others(axis):
            pl.semaphore_signal(sem, inc=1, device_id=device, device_id_type=MESH)
            count += 1
    pl.semaphore_wait(sem, count)


def column_of(row_ref):
    row = row_ref[...].astype(F32)
    return jnp.broadcast_to(row, (128, row.shape[1])).T[:, 0:1]


def gelu(v):
    t = jnp.tanh(0.7978845608028654 * (v + 0.044715 * (v * v * v)))
    return v * (0.5 * (1.0 + t))


def gelu_slope(v):
    square = v * v
    t = jnp.tanh(0.7978845608028654 * (v + 0.044715 * (v * square)))
    bend = 0.7978845608028654 * (1.0 + 0.134145 * square)
    return 0.5 * (1.0 + t) + 0.5 * v * (1.0 - t * t) * bend


class Share:
    def __init__(self, place, bufs, send, recv):
        self.place, self.send, self.recv = place, send, recv
        self.stages, base = [], 0
        for axis, buf in zip(("l", "z", "x"), bufs):
            self.stages.append((axis, buf, base))
            base += place.size[axis] - 1

    def start(self, stage, value):
        axis, buf, base = self.stages[stage]
        me = self.place.at[axis]
        buf[me] = value
        for far, _, device in self.place.others(axis):
            remote(
                buf.at[me], buf.at[me], self.send.at[base + far], self.recv.at[base + far], device
            ).start()

    def finish(self, stage):
        axis, buf, base = self.stages[stage]
        me = self.place.at[axis]
        for far, _, device in self.place.others(axis):
            remote(
                buf.at[me], buf.at[me], self.send.at[base + far], self.recv.at[base + far], device
            ).wait()
        total = buf[0]
        for i in range(1, self.place.size[axis]):
            total += buf[i]
        return total


def share_sems(n_nodes, n_grp):
    return (n_nodes // LINE - 1) + (LINE - 1) + max(1, n_grp - 1)


def forward_kernel(
    n_nodes,
    n_grp,
    feats_h,
    mask_ref,
    place_ref,
    child_ref,
    weight_ref,
    targets_ref,
    board_h,
    neigh_h,
    nbias_ref,
    comb_h,
    cbias_ref,
    cot_h,
    embed_h,
    hid_h,
    pre_h,
    featb_h,
    board_b_h,
    neigh_b_h,
    comb1_b_h,
    st_h,
    dnum_h,
    dz_h,
    agg_h,
    stats_ref,
    stage,
    featb,
    hid,
    pre,
    board_b,
    neigh_b,
    comb_b,
    keys,
    msg,
    acc,
    spread,
    spread_t,
    out_slots,
    in_slots,
    out_tot,
    in_tot,
    picker,
    num,
    zval,
    zpre,
    cot,
    agg,
    dz,
    dnum,
    den_ref,
    scale_ref,
    count_l,
    count_z,
    count_x,
    load_sem,
    store_sem,
    key_send,
    key_recv,
    up_send,
    down_send,
    msg_recv,
    slot_send,
    slot_recv,
    tot_send,
    tot_recv,
    count_send,
    count_recv,
):
    place = Place(n_nodes, n_grp)
    z, low = place.at["z"], place.at["l"]
    layer = place.size["l"]
    rows, width = featb.shape
    edges = place_ref.shape[1]
    half = edges // 2
    layer_slots = spread.shape[1]
    cap = layer_slots // layer
    part = width // CHUNKS
    turn = math.gcd(half, 6400)
    steps = edges // turn

    sources = [feats_h.at[:]]
    for whole in (board_h, neigh_h, comb_h):
        for first in range(0, whole.shape[0], rows):
            sources.append(whole.at[pl.ds(first, rows)])
    n_stage = stage.shape[0]

    def load(i):
        return pltpu.make_async_copy(sources[i], stage.at[i % n_stage], load_sem.at[i % n_stage])

    for i in range(n_stage):
        load(i).start()
    load_cot = pltpu.make_async_copy(cot_h, cot, load_sem.at[n_stage])
    stores = []

    def store(src, dst):
        copy = pltpu.make_async_copy(src, dst, store_sem.at[len(stores)])
        copy.start()
        stores.append(copy)

    barrier(place, ("l", "z", "x"))
    keys[z, :, pl.ds(0, edges)] = place_ref[...] * 65536 + child_ref[...]
    keys[z, :, pl.ds(edges, half)] = (
        weight_ref[:, pl.ds(half, half)] * 65536 + weight_ref[:, pl.ds(0, half)]
    )

    def key_copy(far, device):
        return remote(keys.at[z], keys.at[z], key_send.at[far], key_recv.at[far], device)

    for far, _, device in place.others("z"):
        key_copy(far, device).start()
    share = Share(place, (count_l, count_z, count_x), count_send, count_recv)
    mask = column_of(mask_ref)
    share.start(0, jnp.full((8, 128), jnp.sum(mask)))

    def cast(i, target, first):
        load(i).wait()
        slot = stage.at[i % n_stage]

        @pl.loop(0, rows // 32)
        def _(r):
            at = pl.ds(pl.multiple_of(r * 32, 32), 32)
            to = pl.ds(pl.multiple_of(first + r * 32, 32), 32)
            target[to, :] = slot[at, :].astype(BF16)

    cast(0, featb, 0)
    cast(1, board_b, 0)
    cast(2, board_b, rows)

    @pl.loop(0, CHUNKS)
    def _(k):
        at = pl.ds(pl.multiple_of(k * part, part), part)
        proj = jnp.dot(featb[...], board_b[:, at], preferred_element_type=F32)
        hid[:, at] = jnp.where(mask > 0.5, proj, stage[0, :, at]).astype(BF16)

    cast(3, neigh_b, 0)
    cast(4, neigh_b, rows)
    for i in range(n_stage, len(sources)):
        load(i).start()
    load_cot.start()

    def up_copy(src, k):
        piece = msg.at[src, k]
        index = src * CHUNKS + k
        return remote(
            piece, piece, up_send.at[index], msg_recv.at[index], place.member("z", z + 1)
        )

    def down_copy(src, k):
        piece = msg.at[src, k]
        index = src * CHUNKS + k
        return remote(
            piece, piece, down_send.at[index], msg_recv.at[index], place.member("z", z - 1)
        )

    def message(k):
        at = pl.ds(k * part, part)
        value = jnp.dot(hid[...], neigh_b[:, at], preferred_element_type=F32) + nbias_ref[:, at]
        pre[:, at] = value
        msg[z, k] = gelu(value).astype(BF16)

        @pl.when(z < LINE - 1)
        def _():
            up_copy(z, k).start()

        @pl.when(z > 0)
        def _():
            down_copy(z, k).start()

    def forward(j, k):
        below = z - 1 - j
        above = z + 1 + j

        @pl.when(below >= 0)
        def _():
            up_copy(below, k).wait_recv()

            @pl.when(z < LINE - 1)
            def _():
                up_copy(below, k).start()

        @pl.when(above < LINE)
        def _():
            down_copy(above, k).wait_recv()

            @pl.when(z > 0)
            def _():
                down_copy(above, k).start()

    def tot_copy(src, far, index, device):
        at = (layer - 1) * src + far
        return remote(
            out_tot.at[src, pl.ds(pl.multiple_of(index * cap, cap), cap)],
            in_tot.at[src, pl.ds(pl.multiple_of(low * cap, cap), cap)],
            tot_send.at[at],
            tot_recv.at[at],
            device,
        )

    def finish_spread(src):
        total = acc[...]
        spread[src] = total.astype(BF16)
        spread_t[src] = total.astype(BF16).T
        sums = jnp.sum(total, axis=1, keepdims=True).astype(jnp.int32)
        lane = lax.broadcasted_iota(jnp.int32, (layer_slots, 128), 1)
        digit = jnp.where(
            lane == 0, sums & 255, jnp.where(lane == 1, (sums >> 8) & 255, jnp.where(lane == 2, sums >> 16, 0))
        )
        out_tot[src] = digit.astype(F32).astype(BF16)
        own = pl.ds(pl.multiple_of(low * cap, cap), cap)
        in_tot[src, own] = out_tot[src, own]
        for far, index, device in place.others("l"):
            tot_copy(src, far, index, device).start()

    def source(which):
        flip = z // 2
        inner = z * (1 - 2 * flip) + (LINE - 1) * flip
        index = ORDER[0][which] * (1 - inner) + ORDER[1][which] * inner
        return index * (1 - 2 * flip) + (LINE - 1) * flip

    def build(which, ticks):
        src = source(which)
        acc[...] = jnp.zeros_like(acc)
        if which > 0:
            far = lax.rem(z - src - 1 + LINE, LINE)
            remote(
                keys.at[src], keys.at[src], key_send.at[0], key_recv.at[far], place.member("z", src)
            ).wait_recv()

        @pl.loop(0, steps)
        def _(t):
            second = t // (steps // 2)
            key = keys[src, :, pl.ds(pl.multiple_of(t * turn, turn), turn)]
            start = edges + (t - second * (steps // 2)) * turn
            pair = keys[src, :, pl.ds(pl.multiple_of(start, turn), turn)]
            weight = (lax.shift_right_logical(pair, second * 16) & 65535).astype(F32).astype(F8)
            child = (key & 65535).astype(jnp.int16)
            slot = (lax.shift_right_logical(key, 16) - z * layer_slots).astype(jnp.int16)
            right = jnp.where(
                lax.broadcasted_iota(jnp.int16, (rows, turn), 0) == child, weight, jnp.zeros((), F8)
            )
            block = 256
            for first in range(0, layer_slots, block):
                ids = lax.broadcasted_iota(jnp.int16, (block, turn), 0) + jnp.asarray(
                    first, jnp.int16
                )
                left = jnp.where(ids == slot, jnp.ones((), F8), jnp.zeros((), F8))
                acc[pl.ds(first, block), :] += dot_nt(left, right)
            for at, acts in enumerate(ticks):
                if acts:

                    @pl.when(t == at)
                    def _(acts=acts):
                        for act in acts:
                            act()

        finish_spread(src)

    def slot_copy(src, k, far, index, device):
        at = (src * CHUNKS + k) * (layer - 1) + far
        return remote(
            out_slots.at[src, k, pl.ds(pl.multiple_of(index * cap, cap), cap)],
            in_slots.at[src, k, pl.ds(pl.multiple_of(low * cap, cap), cap)],
            slot_send.at[at],
            slot_recv.at[at],
            device,
        )

    def piece(src, k):
        out_slots[src, k] = jnp.dot(spread[src], msg[src, k], preferred_element_type=F32).astype(BF16)
        for far, index, device in place.others("l"):
            slot_copy(src, k, far, index, device).start()
        own = pl.ds(pl.multiple_of(low * cap, cap), cap)
        in_slots[src, k, own] = out_slots[src, k, own]

    def pick(src, k):
        for far, index, device in place.others("l"):
            slot_copy(src, k, far, index, device).wait_recv()
        num[k] += jnp.dot(picker[src], in_slots[src, k], preferred_element_type=F32)

    def make_picker():
        @pl.loop(0, LINE)
        def _(src):
            at = pl.ds(pl.multiple_of(src * layer_slots, layer_slots), layer_slots)
            ids = lax.broadcasted_iota(jnp.int32, (rows, layer_slots), 0)
            picker[src] = jnp.where(ids == targets_ref[:, at], 1.0, 0.0).astype(BF16)

        num[...] = jnp.zeros_like(num)

    def comb_piece(i):
        for j in range(i, 2 * width // rows, CHUNKS):
            cast(5 + j, comb_b, j * rows)

    def self_part():
        @pl.loop(0, CHUNKS)
        def _(k):
            at = pl.ds(pl.multiple_of(k * part, part), part)
            zpre[:, at] = (
                jnp.dot(hid[...], comb_b[0:width, at], preferred_element_type=F32)
                + cbias_ref[:, at]
            )

    def results():
        store(hid, hid_h)
        store(pre, pre_h)
        store(featb, featb_h)
        store(board_b, board_b_h)
        store(neigh_b, neigh_b_h)
        store(comb_b.at[pl.ds(0, width)], comb1_b_h)
        store(spread_t, st_h)

    def totals():
        digits = jnp.zeros((rows, 128), F32)
        for src in range(LINE):
            for far, index, device in place.others("l"):
                tot_copy(src, far, index, device).wait_recv()
            digits += jnp.dot(picker[src], in_tot[src], preferred_element_type=F32)
        lane = lax.broadcasted_iota(jnp.int32, (rows, 128), 1)
        worth = jnp.where(
            lane == 0, 1.0, jnp.where(lane == 1, 256.0, jnp.where(lane == 2, 65536.0, 0.0))
        )
        den_ref[...] = jnp.broadcast_to(
            1.0 + jnp.sum(digits * worth, axis=1, keepdims=True), (rows, 128)
        )

    def neighbours(k):
        at = pl.ds(k * part, part)
        agg[:, at] = (num[k] / den_ref[:, 0:1]).astype(BF16)
        if k < CHUNKS - 1:

            @pl.loop(0, CHUNKS)
            def _(n):
                to = pl.ds(pl.multiple_of(n * part, part), part)
                zpre[:, to] += jnp.dot(
                    agg[:, at], comb_b[pl.ds(width + k * part, part), to], preferred_element_type=F32
                )

    def step_share(stage):
        if stage in (1, 2):
            share.start(stage, share.finish(stage - 1))
        elif stage == 3:
            boards = share.finish(2)
            scale_ref[...] = 1.0 / (width * (1.0 + boards))

    acts = {
        "P": step_share,
        "m": message,
        "f": forward,
        "p": lambda which, k: piece(source(which), k),
        "i": lambda which, k: pick(source(which), k),
        "G": lambda _: make_picker(),
        "D": comb_piece,
        "X": lambda _: self_part(),
        "R": lambda _: results(),
        "d": lambda _: totals(),
        "a": neighbours,
    }

    def act(step):
        acts[step[0]](*(int(c) for c in step[1:]))

    ticks = None
    for step in FORWARD:
        if step[0] == "Y":
            if ticks is None:
                ticks = [[] for _ in range(steps)]
            now = min(int(step[2]), steps - 1)
        elif step[0] == "Z":
            build(int(step[1]), ticks)
            ticks = None
        elif ticks is not None:
            ticks[now].append(functools.partial(act, step))
        else:
            act(step)

    neighbours(CHUNKS - 1)
    load_cot.wait()
    den = den_ref[:, 0:1]
    scale = scale_ref[0:1, 0:1]
    last = pl.ds(width - part, part)

    def dense(k, carry):
        square, along = carry
        at = pl.ds(pl.multiple_of(k * part, part), part)
        value = zpre[:, at] + jnp.dot(
            agg[:, last], comb_b[pl.ds(2 * width - part, part), at], preferred_element_type=F32
        )
        zpre[:, at] = value
        out = gelu(value)
        zval[:, at] = out
        square += jnp.sum(out * out, axis=1, keepdims=True)
        along += jnp.sum(out * cot[:, at], axis=1, keepdims=True)
        return square, along

    zero = jnp.zeros((rows, 1), F32)
    square, along = lax.fori_loop(0, CHUNKS, dense, (zero, zero))
    inverse = lax.rsqrt(square + 1e-06)
    along = along * inverse
    push = jnp.where(mask > 0.5, 2.0 * scale, 0.0)
    stats_ref[...] = jnp.concatenate(
        [
            jnp.full((8, 128), jnp.sum(jnp.where(mask > 0.5, square, 0.0))),
            jnp.broadcast_to(scale, (8, 128)),
        ],
        axis=0,
    )

    @pl.loop(0, CHUNKS)
    def _(k):
        at = pl.ds(pl.multiple_of(k * part, part), part)
        out = zval[:, at]
        emb = out * inverse
        grad = inverse * (cot[:, at] - emb * along) + push * out
        dz[:, at] = (grad * gelu_slope(zpre[:, at])).astype(BF16)
        zval[:, at] = emb

    store(zval, embed_h)
    store(dz, dz_h)
    store(agg, agg_h)

    @pl.loop(0, CHUNKS)
    def _(k):
        at = pl.ds(pl.multiple_of(k * part, part), part)
        back = dot_nt(dz[...], comb_b[pl.ds(pl.multiple_of(width + k * part, part), part), :])
        dnum[:, at] = (back / den).astype(BF16)

    store(dnum, dnum_h)

    for far, _, device in place.others("z"):
        key_copy(far, device).wait_send()

    @pl.loop(0, LINE * CHUNKS)
    def _(i):
        src = i // CHUNKS
        k = lax.rem(i, CHUNKS)

        @pl.when(jnp.logical_and(src <= z, z < LINE - 1))
        def _():
            up_copy(src, k).wait_send()

        @pl.when(jnp.logical_and(src >= z, z > 0))
        def _():
            down_copy(src, k).wait_send()

        for far, index, device in place.others("l"):
            slot_copy(src, k, far, index, device).wait_send()

    for src in range(LINE):
        for far, index, device in place.others("l"):
            tot_copy(src, far, index, device).wait_send()
    for copy in stores:
        copy.wait()


def forward_pass(n_nodes, n_grp, feats, mask, edges_of, targets, board, neigh, nbias, comb, cbias, cot):
    rows, width = feats.shape
    edges = edges_of[0].shape[1]
    layer = n_nodes // LINE
    layer_slots = targets.shape[1] // LINE
    part = width // CHUNKS
    dma = pltpu.SemaphoreType.DMA
    n_stage = 5
    big = pl.BlockSpec(memory_space=pl.ANY)
    small = pl.BlockSpec(memory_space=pltpu.VMEM)

    def hbm(shape, dtype):
        return jax.ShapeDtypeStruct(shape, dtype)

    return pl.pallas_call(
        functools.partial(forward_kernel, n_nodes, n_grp),
        out_shape=[
            hbm((rows, width), F32),
            hbm((rows, width), BF16),
            hbm((rows, width), F32),
            hbm((rows, width), BF16),
            hbm((width, width), BF16),
            hbm((width, width), BF16),
            hbm((width, width), BF16),
            hbm((LINE, rows, layer_slots), BF16),
            hbm((rows, width), BF16),
            hbm((rows, width), BF16),
            hbm((rows, width), BF16),
            hbm((16, 128), F32),
        ],
        in_specs=[big] + [small] * 5 + [big, big, small, big, small, big],
        out_specs=[big] * 11 + [small],
        scratch_shapes=[
            pltpu.VMEM((n_stage, rows, width), F32),
            pltpu.VMEM((rows, width), BF16),
            pltpu.VMEM((rows, width), BF16),
            pltpu.VMEM((rows, width), F32),
            pltpu.VMEM((width, width), BF16),
            pltpu.VMEM((width, width), BF16),
            pltpu.VMEM((2 * width, width), BF16),
            pltpu.VMEM((LINE, 1, edges + edges // 2), jnp.int32),
            pltpu.VMEM((LINE, CHUNKS, rows, part), BF16),
            pltpu.VMEM((layer_slots, rows), F32),
            pltpu.VMEM((LINE, layer_slots, rows), BF16),
            pltpu.VMEM((LINE, rows, layer_slots), BF16),
            pltpu.VMEM((LINE, CHUNKS, layer_slots, part), BF16),
            pltpu.VMEM((LINE, CHUNKS, layer_slots, part), BF16),
            pltpu.VMEM((LINE, layer_slots, 128), BF16),
            pltpu.VMEM((LINE, layer_slots, 128), BF16),
            pltpu.VMEM((LINE, rows, layer_slots), BF16),
            pltpu.VMEM((CHUNKS, rows, part), F32),
            pltpu.VMEM((rows, width), F32),
            pltpu.VMEM((rows, width), F32),
            pltpu.VMEM((rows, width), F32),
            pltpu.VMEM((rows, width), BF16),
            pltpu.VMEM((rows, width), BF16),
            pltpu.VMEM((rows, width), BF16),
            pltpu.VMEM((rows, 128), F32),
            pltpu.VMEM((8, 128), F32),
            pltpu.VMEM((layer, 8, 128), F32),
            pltpu.VMEM((LINE, 8, 128), F32),
            pltpu.VMEM((n_grp, 8, 128), F32),
            dma((n_stage + 1,)),
            dma((11,)),
            dma((LINE - 1,)),
            dma((LINE - 1,)),
            dma((LINE * CHUNKS,)),
            dma((LINE * CHUNKS,)),
            dma((LINE * CHUNKS,)),
            dma((LINE * CHUNKS * (layer - 1),)),
            dma((LINE * CHUNKS * (layer - 1),)),
            dma((LINE * (layer - 1),)),
            dma((LINE * (layer - 1),)),
            dma((share_sems(n_nodes, n_grp),)),
            dma((share_sems(n_nodes, n_grp),)),
        ],
        compiler_params=pltpu.CompilerParams(
            vmem_limit_bytes=60 * MIB, collective_id=2, has_side_effects=True
        ),
        name="forward_pass",
    )(feats, mask, *edges_of, targets, board, neigh, nbias, comb, cbias, cot)


def add_into(target, first, count, columns, parts, step=16):
    @pl.loop(0, count // step)
    def _(i):
        at = pl.ds(pl.multiple_of(first + i * step, step), step)
        total = target[at, columns].astype(F32)
        for part in parts:
            total += part[pl.ds(pl.multiple_of(i * step, step), step), :].astype(F32)
        target[at, columns] = total.astype(target.dtype)


def reduce_job(place, order, grad, out, region, arrive, land, send, recv, base):
    first, rows, left, columns = region
    half = columns // 2
    core = place.at["c"]
    mine = pl.ds(pl.multiple_of(left + core * half, half), half)
    theirs = pl.ds(pl.multiple_of(left + (1 - core) * half, half), half)
    sem = base
    mate = place.member("c", 1 - core)
    block = pl.ds(first, rows)
    copy = remote(grad.at[block, theirs], arrive, send.at[sem], recv.at[sem], mate)
    copy.start()
    sem += 1
    yield
    copy.wait()
    add_into(grad, first, rows, mine, [arrive])
    begin, length, used = first, rows, 0
    trail = []
    for axis in order:
        size = place.size[axis]
        length //= size
        copies, parts = [], []
        for far, index, device in place.others(axis):
            start = pl.multiple_of(begin + index * length, 16)
            slot = land.at[pl.ds(used, length)]
            used += length
            copy = remote(
                grad.at[pl.ds(start, length), mine], slot, send.at[sem], recv.at[sem], device
            )
            copy.start()
            sem += 1
            copies.append(copy)
            parts.append(slot)
        yield
        for copy in copies:
            copy.wait()
        trail.append((axis, begin, length))
        begin = pl.multiple_of(begin + place.at[axis] * length, 16)
        add_into(grad, begin, length, mine, parts)
    at = pl.ds(begin, length)
    out[at, mine] = grad[at, mine]
    for axis, parent, piece in reversed(trail):
        start = pl.multiple_of(parent + place.at[axis] * piece, 16)
        own = out.at[pl.ds(start, piece), mine]
        copies = []
        for far, index, device in place.others(axis):
            copy = remote(own, own, send.at[sem], recv.at[sem], device)
            copy.start()
            sem += 1
            copies.append(copy)
        yield
        for copy in copies:
            copy.wait()
    own = out.at[block, mine]
    copy = remote(own, own, send.at[sem], recv.at[sem], mate)
    copy.start()
    yield
    copy.wait()


def job_sems(n_nodes, n_grp):
    return 2 * (1 + (n_nodes // LINE // 2 - 1) + (LINE - 1) + (n_grp - 1))


JOBS = {
    kind[0] + str(i): kind + str(i) for kind, count in (("comb", 4), ("neigh", 4), ("board", 2)) for i in range(count)
}
BACKWARD = (
    "B0", "B1", "W0", "30", "20", "G0", "B2", "31", "10", "c2", "B3", "c1", "S0", "c3", "c0", "32",
    "c0", "11", "c2", "c1", "O0", "n0", "c3", "21", "33", "n0", "22", "23", "c2", "c1", "12", "O1",
    "n1", "13", "n0", "c0", "n1", "n0", "O2", "n2", "n2", "c3", "c1", "O3", "n3", "n1", "E0", "H1",
    "b1", "n2", "H0", "b0", "c2", "n3", "n0", "b1", "c1", "b0", "c2", "c1", "n0", "c0", "b1", "P0",
    "c2", "n2", "c3", "c1", "b0", "n0", "c0", "n2", "c2", "c3", "b0", "c0", "F0", "n2", "c1", "b1",
    "c3", "n0", "c0", "b0", "n3", "b1", "c3", "n1", "b0", "c1", "n2", "n3", "b1", "n1", "n3", "b0",
    "n1", "n3", "P1", "b1", "c0", "c2", "n3", "c3", "b0", "n1", "n3", "n2", "c0", "b1", "c3", "n3",
    "b0", "P2", "n1", "n0", "c2", "P3", "n2", "b1", "n1",
)


def gradient_regions(n_nodes, n_grp, width):
    pieces = n_nodes * n_grp // 2
    x_first, y_first = ("x", "y", "z"), ("y", "x", "z")
    regions = {}
    count = max(1, min(4, 2 * width // (16 * pieces)))
    n_rows = 2 * width // count
    for j in range(count):
        regions[f"comb{j}"] = (j * n_rows, n_rows, 0, width, x_first)
    if width % (16 * pieces) == 0:
        part = width // CHUNKS
        for k in range(CHUNKS):
            regions[f"neigh{k}"] = (2 * width, width, k * part, part, x_first if k % 2 else y_first)
        count = max(1, min(2, width // (16 * pieces)))
        n_rows = width // count
        for j in range(count):
            order = x_first if j % 2 == 0 else y_first
            regions[f"board{j}"] = (3 * width + j * n_rows, n_rows, 0, width, order)
    else:
        regions["board0"] = (2 * width, 2 * width, 0, width, x_first)
    return regions


def backward_kernel(
    n_nodes,
    n_grp,
    mask_ref,
    targets_ref,
    stats_ref,
    hid_h,
    pre_h,
    featb_h,
    board_b_h,
    neigh_b_h,
    comb1_b_h,
    st_h,
    dnum_h,
    dz_h,
    agg_h,
    gfeat_h,
    summed_h,
    small_ref,
    hid,
    pre,
    featb,
    board_b,
    neigh_b,
    comb1_b,
    spread_t,
    dnum,
    dz,
    agg,
    picker_t,
    out_slots,
    in_slots,
    chain,
    tmp,
    dpre,
    dh,
    grad,
    out,
    arrive,
    land,
    share_l,
    share_z,
    share_x,
    small,
    load_sem,
    store_sem,
    slot_send,
    slot_recv,
    up_send,
    down_send,
    chain_recv,
    job_send,
    job_recv,
    share_send,
    share_recv,
):
    place = Place(n_nodes, n_grp)
    z, low = place.at["z"], place.at["l"]
    layer = place.size["l"]
    rows, width = hid.shape
    layer_slots = spread_t.shape[2]
    cap = layer_slots // layer
    part = width // CHUNKS

    loads = {}
    for i, (name, src, dst) in enumerate(
        (
            ("dnum", dnum_h, dnum),
            ("hid", hid_h, hid),
            ("agg", agg_h, agg),
            ("dz", dz_h, dz),
            ("spread_t", st_h, spread_t),
            ("comb1_b", comb1_b_h, comb1_b),
            ("pre", pre_h, pre),
            ("neigh_b", neigh_b_h, neigh_b),
            ("featb", featb_h, featb),
            ("board_b", board_b_h, board_b),
        )
    ):
        loads[name] = pltpu.make_async_copy(src, dst, load_sem.at[i])
        loads[name].start()
    barrier(place, ("l", "z", "x"))
    stores = []

    def store(src, dst):
        copy = pltpu.make_async_copy(src, dst, store_sem.at[len(stores)])
        copy.start()
        stores.append(copy)

    mask = column_of(mask_ref) > 0.5

    def source(which):
        flip = z // 2
        inner = z * (1 - 2 * flip) + (LINE - 1) * flip
        index = ORDER[0][which] * (1 - inner) + ORDER[1][which] * inner
        return index * (1 - 2 * flip) + (LINE - 1) * flip

    def cols(k):
        return pl.ds(pl.multiple_of(k * part, part), part)

    def slot_copy(dst, k, far, index, device):
        at = (dst * CHUNKS + k) * (layer - 1) + far
        return remote(
            out_slots.at[dst, k, pl.ds(pl.multiple_of(index * cap, cap), cap)],
            in_slots.at[dst, k, pl.ds(pl.multiple_of(low * cap, cap), cap)],
            slot_send.at[at],
            slot_recv.at[at],
            device,
        )

    def back(dst, k):
        out_slots[dst, k] = jnp.dot(
            picker_t[dst], dnum[:, cols(k)], preferred_element_type=F32
        ).astype(BF16)
        for far, index, device in place.others("l"):
            slot_copy(dst, k, far, index, device).start()
        own = pl.ds(pl.multiple_of(low * cap, cap), cap)
        in_slots[dst, k, own] = out_slots[dst, k, own]

    def child_sums(dst, k):
        for far, index, device in place.others("l"):
            slot_copy(dst, k, far, index, device).wait_recv()
        tmp[...] = jnp.dot(spread_t[dst], in_slots[dst, k], preferred_element_type=F32)

    def up_copy(dst, k):
        at = dst * CHUNKS + k
        return remote(
            chain.at[dst, k],
            chain.at[dst, k],
            up_send.at[at],
            chain_recv.at[at],
            place.member("z", z + 1),
        )

    def down_copy(dst, k, last):
        slot = LINE if last else dst
        return remote(
            chain.at[dst, k],
            chain.at[slot, k],
            down_send.at[dst * CHUNKS + k],
            chain_recv.at[slot * CHUNKS + k],
            place.member("z", z - 1),
        )

    def arrived(slot, k):
        remote(
            chain.at[slot, k],
            chain.at[slot, k],
            up_send.at[0],
            chain_recv.at[slot * CHUNKS + k],
            place.member("z", lax.rem(z + 1, LINE)),
        ).wait_recv()

    def hand_on(dst, k):
        child_sums(dst, k)

        @pl.when(dst > z)
        def _():
            @pl.when(z > 0)
            def _():
                up_copy(dst, k).wait_recv()
                chain[dst, k] = (chain[dst, k].astype(F32) + tmp[...]).astype(BF16)

            @pl.when(z == 0)
            def _():
                chain[dst, k] = tmp[...].astype(BF16)

            up_copy(dst, k).start()

        @pl.when(dst < z)
        def _():
            @pl.when(z < LINE - 1)
            def _():
                down_copy(dst, k, False).wait_recv()
                chain[dst, k] = (chain[dst, k].astype(F32) + tmp[...]).astype(BF16)

            @pl.when(z == LINE - 1)
            def _():
                chain[dst, k] = tmp[...].astype(BF16)

            @pl.when(dst == z - 1)
            def _():
                down_copy(dst, k, True).start()

            @pl.when(dst < z - 1)
            def _():
                down_copy(dst, k, False).start()

    regions = gradient_regions(n_nodes, n_grp, width)
    per_job = job_sems(n_nodes, n_grp)

    def job(name):
        first, n_rows, left, columns, order = regions[name]
        rows_at, cols_at = pl.ds(first, n_rows), pl.ds(left, columns)
        land_at = pl.ds(left // 2, columns // 2)
        yield from reduce_job(
            place,
            order,
            grad,
            out,
            (first, n_rows, left, columns),
            arrive.at[rows_at, land_at],
            land.at[rows_at, land_at],
            job_send,
            job_recv,
            list(regions).index(name) * per_job,
        )
        store(out.at[rows_at, cols_at], summed_h.at[rows_at, cols_at])

    jobs = {name: job(name) for name in regions}

    def step_job(name, last=False):
        if name in jobs and (last or name != "board0" or "board1" in regions):
            try:
                next(jobs[name])
            except StopIteration:
                del jobs[name]

    @pl.loop(0, LINE)
    def _(src):
        at = pl.ds(pl.multiple_of(src * layer_slots, layer_slots), layer_slots)
        ids = lax.broadcasted_iota(jnp.int32, (rows, layer_slots), 0)
        picker_t[src] = jnp.where(ids == targets_ref[:, at], 1.0, 0.0).astype(BF16).T

    loads["dnum"].wait()

    def back_all(k):
        for which in (3, 2, 1, 0):
            back(source(which), k)

    def comb_grad(left, first):
        @pl.loop(0, CHUNKS)
        def _(k):
            grad[pl.ds(first, width), cols(k)] = dot_tn(left[...], dz[:, cols(k)]).astype(BF16)

    def own(k):
        child_sums(z, k)

        @pl.when(z > 0)
        def _():
            arrived(z, k)
            tmp[...] += chain[z, k].astype(F32)

        @pl.when(z < LINE - 1)
        def _():
            arrived(LINE, k)
            tmp[...] += chain[LINE, k].astype(F32)

        down = (tmp[...] * gelu_slope(pre[:, cols(k)])).astype(BF16)
        dpre[:, cols(k)] = down
        small[0:1, cols(k)] = jnp.sum(down.astype(F32), axis=0, keepdims=True)
        dh[...] += dot_nt(down, neigh_b[:, cols(k)])

    def neigh_grad(k):
        grad[pl.ds(2 * width, width), cols(k)] = dot_tn(hid[...], dpre[:, cols(k)]).astype(BF16)

    def comb_grads():
        for name in ("hid", "agg", "dz", "comb1_b"):
            loads[name].wait()
        comb_grad(hid, 0)
        comb_grad(agg, width)

    def self_part():
        small[...] = jnp.zeros_like(small)
        small[1:2, :] = jnp.sum(dz[...].astype(F32), axis=0, keepdims=True)
        small[2:3, :] = jnp.broadcast_to(stats_ref[0:1, 0:1], (1, width))

        @pl.loop(0, CHUNKS)
        def _(k):
            dh[:, cols(k)] = dot_nt(dz[...], comb1_b[cols(k), :])

        for name in ("pre", "neigh_b", "featb", "board_b"):
            loads[name].wait()

    def own_and_grad(k):
        own(k)
        neigh_grad(k)

    def end_of_line():
        last = dh[...].astype(BF16)
        dpre[...] = jnp.where(mask, last, jnp.zeros_like(last))
        pre[...] = last.astype(F32)

    def board_grad(i):
        half = width // 2
        grad[pl.ds(3 * width + i * half, half), :] = dot_tn(
            featb[:, i * half : (i + 1) * half], dpre[...]
        ).astype(BF16)

    def feature_grad():
        @pl.loop(0, CHUNKS)
        def _(k):
            pre[:, cols(k)] = jnp.where(
                mask, dot_nt(dpre[...], board_b[cols(k), :]), pre[:, cols(k)]
            )

        store(pre, gfeat_h)

    share = Share(place, (share_l, share_z, share_x), share_send, share_recv)

    def step_share(stage):
        if stage == 0:
            share.start(0, small[...])
        elif stage < 3:
            share.start(stage, share.finish(stage - 1))
        else:
            small_ref[...] = share.finish(2)

    acts = {
        "B": back_all,
        "W": lambda _: loads["spread_t"].wait(),
        "G": lambda _: comb_grads(),
        "S": lambda _: self_part(),
        "O": own_and_grad,
        "E": lambda _: end_of_line(),
        "H": board_grad,
        "F": lambda _: feature_grad(),
        "P": step_share,
        "3": lambda k: hand_on(source(3), k),
        "2": lambda k: hand_on(source(2), k),
        "1": lambda k: hand_on(source(1), k),
    }
    for step in BACKWARD:
        if step in JOBS:
            step_job(JOBS[step])
        else:
            acts[step[0]](int(step[1]))
    while jobs:
        for name in list(jobs):
            step_job(name, last=True)

    @pl.loop(0, LINE * CHUNKS)
    def _(i):
        dst = i // CHUNKS
        k = lax.rem(i, CHUNKS)

        @pl.when(dst > z)
        def _():
            up_copy(dst, k).wait_send()

        @pl.when(dst < z)
        def _():
            down_copy(dst, k, False).wait_send()

        for far, index, device in place.others("l"):
            slot_copy(dst, k, far, index, device).wait_send()

    for copy in stores:
        copy.wait()


def backward_pass(n_nodes, n_grp, mask, targets, stats, hid, pre, featb, board_b, neigh_b, comb1_b, st, dnum, dz, agg):
    rows, width = hid.shape
    layer = n_nodes // LINE
    layer_slots = st.shape[2]
    part = width // CHUNKS
    n_rows = 4 * width
    count = len(gradient_regions(n_nodes, n_grp, width))
    dma = pltpu.SemaphoreType.DMA
    big = pl.BlockSpec(memory_space=pl.ANY)
    vmem = pl.BlockSpec(memory_space=pltpu.VMEM)
    sems = count * job_sems(n_nodes, n_grp)
    pieces = LINE * CHUNKS
    return pl.pallas_call(
        functools.partial(backward_kernel, n_nodes, n_grp),
        out_shape=[
            jax.ShapeDtypeStruct((rows, width), F32),
            jax.ShapeDtypeStruct((n_rows, width), BF16),
            jax.ShapeDtypeStruct((8, width), F32),
        ],
        in_specs=[vmem, vmem, vmem] + [big] * 10,
        out_specs=[big, big, vmem],
        scratch_shapes=[
            pltpu.VMEM((rows, width), BF16),
            pltpu.VMEM((rows, width), F32),
            pltpu.VMEM((rows, width), BF16),
            pltpu.VMEM((width, width), BF16),
            pltpu.VMEM((width, width), BF16),
            pltpu.VMEM((width, width), BF16),
            pltpu.VMEM((LINE, rows, layer_slots), BF16),
            pltpu.VMEM((rows, width), BF16),
            pltpu.VMEM((rows, width), BF16),
            pltpu.VMEM((rows, width), BF16),
            pltpu.VMEM((LINE, layer_slots, rows), BF16),
            pltpu.VMEM((LINE, CHUNKS, layer_slots, part), BF16),
            pltpu.VMEM((LINE, CHUNKS, layer_slots, part), BF16),
            pltpu.VMEM((LINE + 1, CHUNKS, rows, part), BF16),
            pltpu.VMEM((rows, part), F32),
            pltpu.VMEM((rows, width), BF16),
            pltpu.VMEM((rows, width), F32),
            pltpu.VMEM((n_rows, width), BF16),
            pltpu.VMEM((n_rows, width), BF16),
            pltpu.VMEM((n_rows, width // 2), BF16),
            pltpu.VMEM((n_rows, width // 2), BF16),
            pltpu.VMEM((layer, 8, width), F32),
            pltpu.VMEM((LINE, 8, width), F32),
            pltpu.VMEM((n_grp, 8, width), F32),
            pltpu.VMEM((8, width), F32),
            dma((10,)),
            dma((count + 1,)),
            dma((pieces * (layer - 1),)),
            dma((pieces * (layer - 1),)),
            dma((pieces,)),
            dma((pieces,)),
            dma((pieces + CHUNKS,)),
            dma((sems,)),
            dma((sems,)),
            dma((share_sems(n_nodes, n_grp),)),
            dma((share_sems(n_nodes, n_grp),)),
        ],
        compiler_params=pltpu.CompilerParams(
            vmem_limit_bytes=62 * MIB, collective_id=3, has_side_effects=True
        ),
        name="backward_pass",
    )(mask, targets, stats, hid, pre, featb, board_b, neigh_b, comb1_b, st, dnum, dz, agg)


def unpack_kernel(blocks, joined_ref, embed_in, gfeat_in, comb_ref, neigh_ref, board_ref, embed, gfeat, sem):
    step = pl.program_id(0)
    moves = [
        pltpu.make_async_copy(embed_in, embed, sem.at[0]),
        pltpu.make_async_copy(gfeat_in, gfeat, sem.at[1]),
    ]

    @pl.when(step == 0)
    def _():
        for move in moves:
            move.start()

    value = joined_ref[...].astype(F32)
    for target, first, count in ((comb_ref, 0, 2), (neigh_ref, 2, 1), (board_ref, 3, 1)):

        @pl.when(jnp.logical_and(step >= first * blocks, step < (first + count) * blocks))
        def _(target=target):
            target[...] = value

    @pl.when(step == 4 * blocks - 1)
    def _():
        for move in moves:
            move.wait()


def unpack(joined, embed, gfeat):
    width = joined.shape[1]
    rows = math.gcd(width, 256)
    blocks = width // rows
    big = pl.BlockSpec(memory_space=pl.ANY)

    def block(first, count):
        return pl.BlockSpec(
            (rows, width), lambda i: (jnp.clip(i - first * blocks, 0, count * blocks - 1), 0)
        )

    return pl.pallas_call(
        functools.partial(unpack_kernel, blocks),
        grid=(4 * blocks,),
        out_shape=[
            jax.ShapeDtypeStruct((2 * width, width), F32),
            jax.ShapeDtypeStruct((width, width), F32),
            jax.ShapeDtypeStruct((width, width), F32),
            jax.ShapeDtypeStruct(embed.shape, F32),
            jax.ShapeDtypeStruct(gfeat.shape, F32),
        ],
        in_specs=[pl.BlockSpec((rows, width), lambda i: (i, 0)), big, big],
        out_specs=[block(0, 2), block(2, 1), block(3, 1), big, big],
        scratch_shapes=[pltpu.SemaphoreType.DMA((2,))],
        compiler_params=pltpu.CompilerParams(vmem_limit_bytes=32 * MIB),
        name="unpack",
    )(joined, embed, gfeat)


def on_device(
    n_nodes,
    n_grp,
    features,
    type_mask,
    edge_child,
    edge_slot,
    edge_weight,
    recv_rows,
    board_proj,
    neigh_proj,
    neigh_bias,
    combine_proj,
    combine_bias,
    out_cot,
):
    feats = features[0]
    rows, width = feats.shape
    peers = recv_rows.shape[2]
    cap = recv_rows.shape[3]
    slots = peers * cap
    targets = recv_rows[0, 0].reshape(1, slots)
    embed, hidden, pre, featb, pbl, qwl, cwl1, spread_t, dnum, dzb, aggb, stats = forward_pass(
        n_nodes,
        n_grp,
        feats,
        type_mask,
        (edge_slot, edge_child, edge_weight),
        targets,
        board_proj,
        neigh_proj,
        neigh_bias.reshape(1, width),
        combine_proj,
        combine_bias.reshape(1, width),
        out_cot[0],
    )
    grad_feats, summed, small = backward_pass(
        n_nodes,
        n_grp,
        type_mask,
        targets,
        stats,
        hidden,
        pre,
        featb,
        pbl,
        qwl,
        cwl1,
        spread_t,
        dnum,
        dzb,
        aggb,
    )
    penalty = small[2, 0] * stats[8, 0]
    grad_comb, grad_neigh, grad_board, embed, grad_feats = unpack(summed, embed, grad_feats)
    return (
        embed[None],
        penalty,
        grad_feats[None],
        grad_board,
        grad_neigh,
        small[0],
        grad_comb,
        small[1],
    )


def solution(mesh):
    in_specs = (
        P("grp", "nodes", None),
        P("grp", "nodes"),
        P("grp", "nodes"),
        P("grp", "nodes"),
        P("grp", "nodes"),
        P("grp", "nodes", None, None),
        P(),
        P(),
        P(),
        P(),
        P(),
        P("grp", "nodes", None),
    )
    out_specs = (P("grp", "nodes", None), P(), P("grp", "nodes", None), P(), P(), P(), P(), P())
    return jax.shard_map(
        functools.partial(on_device, mesh.shape["nodes"], mesh.shape["grp"]),
        mesh=mesh,
        in_specs=in_specs,
        out_specs=out_specs,
        check_vma=False,
    )
```

```python
import functools
import math

import jax
import jax.numpy as jnp
from jax import lax
from jax.experimental import pallas as pl
from jax.experimental.pallas import tpu as pltpu
from jax.sharding import PartitionSpec as P

HIGH = lax.Precision.HIGHEST
MESH = pl.DeviceIdType.MESH
BF16 = jnp.bfloat16
F32 = jnp.float32
F8 = jnp.float8_e4m3fn
MIB = 2**20


def gelu_tanh(v):
    return jax.nn.gelu(v, approximate=True)


def dot_nt(left, right):
    return lax.dot_general(
        left, right, (((1,), (1,)), ((), ())), preferred_element_type=F32
    )


def dot_tn(left, right):
    return lax.dot_general(
        left, right, (((0,), (0,)), ((), ())), preferred_element_type=F32
    )


LINE = 4
CHUNKS = 4
FORWARD = (
    "m0", "m1", "m2", "m3", "Y00", "Y01", "Y02", "Y03", "Z0", "f00", "p00", "p01", "p02", "p03",
    "Y10", "P1", "Y11", "f01", "Y12", "f02", "Y13", "Z1", "p10", "p11", "p12", "Y20", "P2", "Y21",
    "f03", "Y22", "Y23", "f10", "Z2", "p13", "p20", "Y30", "Y31", "f11", "Y32", "Y33", "f12", "Z3",
    "p21", "p22", "G0", "P3", "f13", "p23", "D0", "D1", "D2", "D3", "X0", "R0", "i00", "i01",
    "i02", "i03", "f20", "p30", "i10", "i11", "i12", "i13", "f21", "p31", "i20", "i21", "i22",
    "i23", "f22", "p32", "i30", "d0", "a0", "f23", "p33", "i31", "a1", "i32", "a2", "i33",
)
ORDER = ((0, 1, 2, 3), (1, 2, 0, 3))


class Place:
    def __init__(self, n_nodes, n_grp):
        layer = n_nodes // LINE
        node = lax.axis_index("nodes")
        grp = lax.axis_index("grp")
        self.node, self.grp = node, grp
        self.size = {"l": layer, "c": 2, "y": layer // 2, "z": LINE, "x": n_grp}
        low = lax.rem(node, layer)
        self.at = {"l": low, "c": lax.rem(low, 2), "y": low // 2, "z": node // layer, "x": grp}

    def member(self, axis, index):
        layer = self.size["l"]
        low, line, grp = self.at["l"], self.at["z"], self.at["x"]
        if axis == "l":
            low = index
        elif axis == "c":
            low = self.at["y"] * 2 + index
        elif axis == "y":
            low = index * 2 + self.at["c"]
        elif axis == "z":
            line = index
        else:
            grp = index
        return {"nodes": line * layer + low, "grp": grp}

    def others(self, axis):
        size = self.size[axis]
        for far in range(1, size):
            index = lax.rem(self.at[axis] + far, size)
            yield far - 1, index, self.member(axis, index)


def remote(src, dst, send, recv, device):
    return pltpu.make_async_remote_copy(
        src_ref=src, dst_ref=dst, send_sem=send, recv_sem=recv, device_id=device, device_id_type=MESH
    )


def barrier(place, axes, meanwhile=None):
    sem = pltpu.get_barrier_semaphore()
    count = 0
    for axis in axes:
        for _, _, device in place.others(axis):
            pl.semaphore_signal(sem, inc=1, device_id=device, device_id_type=MESH)
            count += 1
    if meanwhile is not None:
        meanwhile()
    pl.semaphore_wait(sem, count)


def column_of(row_ref):
    row = row_ref[...].astype(F32)
    return jnp.broadcast_to(row, (128, row.shape[1])).T[:, 0:1]


def gelu(v):
    t = jnp.tanh(0.7978845608028654 * (v + 0.044715 * (v * v * v)))
    return v * (0.5 * (1.0 + t))


def gelu_slope(v):
    square = v * v
    t = jnp.tanh(0.7978845608028654 * (v + 0.044715 * (v * square)))
    bend = 0.7978845608028654 * (1.0 + 0.134145 * square)
    return 0.5 * (1.0 + t) + 0.5 * v * (1.0 - t * t) * bend


class Share:
    def __init__(self, place, bufs, send, recv):
        self.place, self.send, self.recv = place, send, recv
        self.stages, base = [], 0
        for axis, buf in zip(("l", "z", "x"), bufs):
            self.stages.append((axis, buf, base))
            base += place.size[axis] - 1

    def start(self, stage, value):
        axis, buf, base = self.stages[stage]
        me = self.place.at[axis]
        buf[me] = value
        for far, _, device in self.place.others(axis):
            remote(
                buf.at[me], buf.at[me], self.send.at[base + far], self.recv.at[base + far], device
            ).start()

    def finish(self, stage):
        axis, buf, base = self.stages[stage]
        me = self.place.at[axis]
        for far, _, device in self.place.others(axis):
            remote(
                buf.at[me], buf.at[me], self.send.at[base + far], self.recv.at[base + far], device
            ).wait()
        total = buf[0]
        for i in range(1, self.place.size[axis]):
            total += buf[i]
        return total


def share_sems(n_nodes, n_grp):
    return (n_nodes // LINE - 1) + (LINE - 1) + max(1, n_grp - 1)


def forward_kernel(
    n_nodes,
    n_grp,
    feats_h,
    mask_ref,
    place_ref,
    child_ref,
    weight_ref,
    targets_ref,
    board_h,
    neigh_h,
    nbias_ref,
    comb_h,
    cbias_ref,
    cot_h,
    embed_h,
    hid_h,
    pre_h,
    featb_h,
    board_b_h,
    neigh_b_h,
    comb1_b_h,
    st_h,
    dnum_h,
    dz_h,
    agg_h,
    stats_ref,
    stage,
    featb,
    hid,
    pre,
    board_b,
    neigh_b,
    comb_b,
    keys,
    msg,
    acc,
    spread,
    spread_t,
    out_slots,
    in_slots,
    out_tot,
    in_tot,
    picker,
    num,
    zval,
    zpre,
    cot,
    agg,
    dz,
    dnum,
    den_ref,
    scale_ref,
    count_l,
    count_z,
    count_x,
    load_sem,
    store_sem,
    key_send,
    key_recv,
    up_send,
    down_send,
    msg_recv,
    slot_send,
    slot_recv,
    tot_send,
    tot_recv,
    count_send,
    count_recv,
):
    place = Place(n_nodes, n_grp)
    z, low = place.at["z"], place.at["l"]
    layer = place.size["l"]
    rows, width = featb.shape
    edges = place_ref.shape[1]
    half = edges // 2
    layer_slots = spread.shape[1]
    cap = layer_slots // layer
    part = width // CHUNKS
    turn = math.gcd(half, 6400)
    steps = edges // turn

    sources = [feats_h.at[:]]
    for whole in (board_h, neigh_h, comb_h):
        for first in range(0, whole.shape[0], rows):
            sources.append(whole.at[pl.ds(first, rows)])
    n_stage = stage.shape[0]

    def load(i):
        return pltpu.make_async_copy(sources[i], stage.at[i % n_stage], load_sem.at[i % n_stage])

    for i in range(n_stage):
        load(i).start()
    load_cot = pltpu.make_async_copy(cot_h, cot, load_sem.at[n_stage])
    stores = []

    def store(src, dst):
        copy = pltpu.make_async_copy(src, dst, store_sem.at[len(stores)])
        copy.start()
        stores.append(copy)

    barrier(place, ("l", "z", "x"))
    keys[z, :, pl.ds(0, edges)] = place_ref[...] * 65536 + child_ref[...]
    keys[z, :, pl.ds(edges, half)] = (
        weight_ref[:, pl.ds(half, half)] * 65536 + weight_ref[:, pl.ds(0, half)]
    )

    def key_copy(far, device):
        return remote(keys.at[z], keys.at[z], key_send.at[far], key_recv.at[far], device)

    for far, _, device in place.others("z"):
        key_copy(far, device).start()
    share = Share(place, (count_l, count_z, count_x), count_send, count_recv)
    mask = column_of(mask_ref)
    share.start(0, jnp.full((8, 128), jnp.sum(mask)))

    def cast(i, target, first):
        load(i).wait()
        slot = stage.at[i % n_stage]

        @pl.loop(0, rows // 32)
        def _(r):
            at = pl.ds(pl.multiple_of(r * 32, 32), 32)
            to = pl.ds(pl.multiple_of(first + r * 32, 32), 32)
            target[to, :] = slot[at, :].astype(BF16)

    cast(0, featb, 0)
    cast(1, board_b, 0)
    cast(2, board_b, rows)

    @pl.loop(0, CHUNKS)
    def _(k):
        at = pl.ds(pl.multiple_of(k * part, part), part)
        proj = jnp.dot(featb[...], board_b[:, at], preferred_element_type=F32)
        hid[:, at] = jnp.where(mask > 0.5, proj, stage[0, :, at]).astype(BF16)

    cast(3, neigh_b, 0)
    cast(4, neigh_b, rows)
    for i in range(n_stage, len(sources)):
        load(i).start()
    load_cot.start()

    def up_copy(src, k):
        piece = msg.at[src, k]
        index = src * CHUNKS + k
        return remote(
            piece, piece, up_send.at[index], msg_recv.at[index], place.member("z", z + 1)
        )

    def down_copy(src, k):
        piece = msg.at[src, k]
        index = src * CHUNKS + k
        return remote(
            piece, piece, down_send.at[index], msg_recv.at[index], place.member("z", z - 1)
        )

    def message(k):
        at = pl.ds(k * part, part)
        value = jnp.dot(hid[...], neigh_b[:, at], preferred_element_type=F32) + nbias_ref[:, at]
        pre[:, at] = value
        msg[z, k] = gelu(value).astype(BF16)

        @pl.when(z < LINE - 1)
        def _():
            up_copy(z, k).start()

        @pl.when(z > 0)
        def _():
            down_copy(z, k).start()

    def forward(j, k):
        below = z - 1 - j
        above = z + 1 + j

        @pl.when(below >= 0)
        def _():
            up_copy(below, k).wait_recv()

            @pl.when(z < LINE - 1)
            def _():
                up_copy(below, k).start()

        @pl.when(above < LINE)
        def _():
            down_copy(above, k).wait_recv()

            @pl.when(z > 0)
            def _():
                down_copy(above, k).start()

    def tot_copy(src, far, index, device):
        at = (layer - 1) * src + far
        return remote(
            out_tot.at[src, pl.ds(pl.multiple_of(index * cap, cap), cap)],
            in_tot.at[src, pl.ds(pl.multiple_of(low * cap, cap), cap)],
            tot_send.at[at],
            tot_recv.at[at],
            device,
        )

    def finish_spread(src):
        total = acc[...]
        spread[src] = total.astype(BF16)
        spread_t[src] = total.astype(BF16).T
        sums = jnp.sum(total, axis=1, keepdims=True).astype(jnp.int32)
        lane = lax.broadcasted_iota(jnp.int32, (layer_slots, 128), 1)
        digit = jnp.where(
            lane == 0, sums & 255, jnp.where(lane == 1, (sums >> 8) & 255, jnp.where(lane == 2, sums >> 16, 0))
        )
        out_tot[src] = digit.astype(F32).astype(BF16)
        own = pl.ds(pl.multiple_of(low * cap, cap), cap)
        in_tot[src, own] = out_tot[src, own]
        for far, index, device in place.others("l"):
            tot_copy(src, far, index, device).start()

    def source(which):
        flip = z // 2
        inner = z * (1 - 2 * flip) + (LINE - 1) * flip
        index = ORDER[0][which] * (1 - inner) + ORDER[1][which] * inner
        return index * (1 - 2 * flip) + (LINE - 1) * flip

    def build(which, ticks):
        src = source(which)
        acc[...] = jnp.zeros_like(acc)
        if which > 0:
            far = lax.rem(z - src - 1 + LINE, LINE)
            remote(
                keys.at[src], keys.at[src], key_send.at[0], key_recv.at[far], place.member("z", src)
            ).wait_recv()

        @pl.loop(0, steps)
        def _(t):
            second = t // (steps // 2)
            key = keys[src, :, pl.ds(pl.multiple_of(t * turn, turn), turn)]
            start = edges + (t - second * (steps // 2)) * turn
            pair = keys[src, :, pl.ds(pl.multiple_of(start, turn), turn)]
            weight = (lax.shift_right_logical(pair, second * 16) & 65535).astype(F32).astype(F8)
            child = (key & 65535).astype(jnp.int16)
            slot = (lax.shift_right_logical(key, 16) - z * layer_slots).astype(jnp.int16)
            right = jnp.where(
                lax.broadcasted_iota(jnp.int16, (rows, turn), 0) == child, weight, jnp.zeros((), F8)
            )
            block = 256
            for first in range(0, layer_slots, block):
                ids = lax.broadcasted_iota(jnp.int16, (block, turn), 0) + jnp.asarray(
                    first, jnp.int16
                )
                left = jnp.where(ids == slot, jnp.ones((), F8), jnp.zeros((), F8))
                acc[pl.ds(first, block), :] += dot_nt(left, right)
            for at, acts in enumerate(ticks):
                if acts:

                    @pl.when(t == at)
                    def _(acts=acts):
                        for act in acts:
                            act()

        finish_spread(src)

    def slot_copy(src, k, far, index, device):
        at = (src * CHUNKS + k) * (layer - 1) + far
        return remote(
            out_slots.at[src, k, pl.ds(pl.multiple_of(index * cap, cap), cap)],
            in_slots.at[src, k, pl.ds(pl.multiple_of(low * cap, cap), cap)],
            slot_send.at[at],
            slot_recv.at[at],
            device,
        )

    def piece(src, k):
        out_slots[src, k] = jnp.dot(spread[src], msg[src, k], preferred_element_type=F32).astype(BF16)
        for far, index, device in place.others("l"):
            slot_copy(src, k, far, index, device).start()
        own = pl.ds(pl.multiple_of(low * cap, cap), cap)
        in_slots[src, k, own] = out_slots[src, k, own]

    def pick(src, k):
        for far, index, device in place.others("l"):
            slot_copy(src, k, far, index, device).wait_recv()
        num[k] += jnp.dot(picker[src], in_slots[src, k], preferred_element_type=F32)

    def make_picker():
        @pl.loop(0, LINE)
        def _(src):
            at = pl.ds(pl.multiple_of(src * layer_slots, layer_slots), layer_slots)
            ids = lax.broadcasted_iota(jnp.int32, (rows, layer_slots), 0)
            picker[src] = jnp.where(ids == targets_ref[:, at], 1.0, 0.0).astype(BF16)

        num[...] = jnp.zeros_like(num)

    def comb_piece(i):
        for j in range(i, 2 * width // rows, CHUNKS):
            cast(5 + j, comb_b, j * rows)

    def self_part():
        @pl.loop(0, CHUNKS)
        def _(k):
            at = pl.ds(pl.multiple_of(k * part, part), part)
            zpre[:, at] = (
                jnp.dot(hid[...], comb_b[0:width, at], preferred_element_type=F32)
                + cbias_ref[:, at]
            )

    def results():
        store(hid, hid_h)
        store(pre, pre_h)
        store(featb, featb_h)
        store(board_b, board_b_h)
        store(neigh_b, neigh_b_h)
        store(comb_b.at[pl.ds(0, width)], comb1_b_h)
        store(spread_t, st_h)

    def totals():
        digits = jnp.zeros((rows, 128), F32)
        for src in range(LINE):
            for far, index, device in place.others("l"):
                tot_copy(src, far, index, device).wait_recv()
            digits += jnp.dot(picker[src], in_tot[src], preferred_element_type=F32)
        lane = lax.broadcasted_iota(jnp.int32, (rows, 128), 1)
        worth = jnp.where(
            lane == 0, 1.0, jnp.where(lane == 1, 256.0, jnp.where(lane == 2, 65536.0, 0.0))
        )
        den_ref[...] = jnp.broadcast_to(
            1.0 + jnp.sum(digits * worth, axis=1, keepdims=True), (rows, 128)
        )

    def neighbours(k):
        at = pl.ds(k * part, part)
        agg[:, at] = (num[k] / den_ref[:, 0:1]).astype(BF16)
        if k < CHUNKS - 1:

            @pl.loop(0, CHUNKS)
            def _(n):
                to = pl.ds(pl.multiple_of(n * part, part), part)
                zpre[:, to] += jnp.dot(
                    agg[:, at], comb_b[pl.ds(width + k * part, part), to], preferred_element_type=F32
                )

    def step_share(stage):
        if stage in (1, 2):
            share.start(stage, share.finish(stage - 1))
        elif stage == 3:
            boards = share.finish(2)
            scale_ref[...] = 1.0 / (width * (1.0 + boards))

    acts = {
        "P": step_share,
        "m": message,
        "f": forward,
        "p": lambda which, k: piece(source(which), k),
        "i": lambda which, k: pick(source(which), k),
        "G": lambda _: make_picker(),
        "D": comb_piece,
        "X": lambda _: self_part(),
        "R": lambda _: results(),
        "d": lambda _: totals(),
        "a": neighbours,
    }

    def act(step):
        acts[step[0]](*(int(c) for c in step[1:]))

    ticks = None
    for step in FORWARD:
        if step[0] == "Y":
            if ticks is None:
                ticks = [[] for _ in range(steps)]
            now = min(int(step[2]), steps - 1)
        elif step[0] == "Z":
            build(int(step[1]), ticks)
            ticks = None
        elif ticks is not None:
            ticks[now].append(functools.partial(act, step))
        else:
            act(step)

    neighbours(CHUNKS - 1)
    load_cot.wait()
    den = den_ref[:, 0:1]
    scale = scale_ref[0:1, 0:1]
    last = pl.ds(width - part, part)

    def dense(k, carry):
        square, along = carry
        at = pl.ds(pl.multiple_of(k * part, part), part)
        value = zpre[:, at] + jnp.dot(
            agg[:, last], comb_b[pl.ds(2 * width - part, part), at], preferred_element_type=F32
        )
        zpre[:, at] = value
        out = gelu(value)
        zval[:, at] = out
        square += jnp.sum(out * out, axis=1, keepdims=True)
        along += jnp.sum(out * cot[:, at], axis=1, keepdims=True)
        return square, along

    zero = jnp.zeros((rows, 1), F32)
    square, along = lax.fori_loop(0, CHUNKS, dense, (zero, zero))
    inverse = lax.rsqrt(square + 1e-06)
    along = along * inverse
    push = jnp.where(mask > 0.5, 2.0 * scale, 0.0)
    stats_ref[...] = jnp.concatenate(
        [
            jnp.full((8, 128), jnp.sum(jnp.where(mask > 0.5, square, 0.0))),
            jnp.broadcast_to(scale, (8, 128)),
        ],
        axis=0,
    )

    @pl.loop(0, CHUNKS)
    def _(k):
        at = pl.ds(pl.multiple_of(k * part, part), part)
        out = zval[:, at]
        emb = out * inverse
        grad = inverse * (cot[:, at] - emb * along) + push * out
        dz[:, at] = (grad * gelu_slope(zpre[:, at])).astype(BF16)
        zval[:, at] = emb

    store(zval, embed_h)
    store(dz, dz_h)
    store(agg, agg_h)

    @pl.loop(0, CHUNKS)
    def _(k):
        at = pl.ds(pl.multiple_of(k * part, part), part)
        back = dot_nt(dz[...], comb_b[pl.ds(pl.multiple_of(width + k * part, part), part), :])
        dnum[:, at] = (back / den).astype(BF16)

    store(dnum, dnum_h)

    for far, _, device in place.others("z"):
        key_copy(far, device).wait_send()

    @pl.loop(0, LINE * CHUNKS)
    def _(i):
        src = i // CHUNKS
        k = lax.rem(i, CHUNKS)

        @pl.when(jnp.logical_and(src <= z, z < LINE - 1))
        def _():
            up_copy(src, k).wait_send()

        @pl.when(jnp.logical_and(src >= z, z > 0))
        def _():
            down_copy(src, k).wait_send()

        for far, index, device in place.others("l"):
            slot_copy(src, k, far, index, device).wait_send()

    for src in range(LINE):
        for far, index, device in place.others("l"):
            tot_copy(src, far, index, device).wait_send()
    for copy in stores:
        copy.wait()


def forward_pass(n_nodes, n_grp, feats, mask, edges_of, targets, board, neigh, nbias, comb, cbias, cot):
    rows, width = feats.shape
    edges = edges_of[0].shape[1]
    layer = n_nodes // LINE
    layer_slots = targets.shape[1] // LINE
    part = width // CHUNKS
    dma = pltpu.SemaphoreType.DMA
    n_stage = 5
    big = pl.BlockSpec(memory_space=pl.ANY)
    small = pl.BlockSpec(memory_space=pltpu.VMEM)

    def hbm(shape, dtype):
        return jax.ShapeDtypeStruct(shape, dtype)

    return pl.pallas_call(
        functools.partial(forward_kernel, n_nodes, n_grp),
        out_shape=[
            hbm((rows, width), F32),
            hbm((rows, width), BF16),
            hbm((rows, width), F32),
            hbm((rows, width), BF16),
            hbm((width, width), BF16),
            hbm((width, width), BF16),
            hbm((width, width), BF16),
            hbm((LINE, rows, layer_slots), BF16),
            hbm((rows, width), BF16),
            hbm((rows, width), BF16),
            hbm((rows, width), BF16),
            hbm((16, 128), F32),
        ],
        in_specs=[big] + [small] * 5 + [big, big, small, big, small, big],
        out_specs=[big] * 11 + [small],
        scratch_shapes=[
            pltpu.VMEM((n_stage, rows, width), F32),
            pltpu.VMEM((rows, width), BF16),
            pltpu.VMEM((rows, width), BF16),
            pltpu.VMEM((rows, width), F32),
            pltpu.VMEM((width, width), BF16),
            pltpu.VMEM((width, width), BF16),
            pltpu.VMEM((2 * width, width), BF16),
            pltpu.VMEM((LINE, 1, edges + edges // 2), jnp.int32),
            pltpu.VMEM((LINE, CHUNKS, rows, part), BF16),
            pltpu.VMEM((layer_slots, rows), F32),
            pltpu.VMEM((LINE, layer_slots, rows), BF16),
            pltpu.VMEM((LINE, rows, layer_slots), BF16),
            pltpu.VMEM((LINE, CHUNKS, layer_slots, part), BF16),
            pltpu.VMEM((LINE, CHUNKS, layer_slots, part), BF16),
            pltpu.VMEM((LINE, layer_slots, 128), BF16),
            pltpu.VMEM((LINE, layer_slots, 128), BF16),
            pltpu.VMEM((LINE, rows, layer_slots), BF16),
            pltpu.VMEM((CHUNKS, rows, part), F32),
            pltpu.VMEM((rows, width), F32),
            pltpu.VMEM((rows, width), F32),
            pltpu.VMEM((rows, width), F32),
            pltpu.VMEM((rows, width), BF16),
            pltpu.VMEM((rows, width), BF16),
            pltpu.VMEM((rows, width), BF16),
            pltpu.VMEM((rows, 128), F32),
            pltpu.VMEM((8, 128), F32),
            pltpu.VMEM((layer, 8, 128), F32),
            pltpu.VMEM((LINE, 8, 128), F32),
            pltpu.VMEM((n_grp, 8, 128), F32),
            dma((n_stage + 1,)),
            dma((11,)),
            dma((LINE - 1,)),
            dma((LINE - 1,)),
            dma((LINE * CHUNKS,)),
            dma((LINE * CHUNKS,)),
            dma((LINE * CHUNKS,)),
            dma((LINE * CHUNKS * (layer - 1),)),
            dma((LINE * CHUNKS * (layer - 1),)),
            dma((LINE * (layer - 1),)),
            dma((LINE * (layer - 1),)),
            dma((share_sems(n_nodes, n_grp),)),
            dma((share_sems(n_nodes, n_grp),)),
        ],
        compiler_params=pltpu.CompilerParams(
            vmem_limit_bytes=60 * MIB, collective_id=2, has_side_effects=True
        ),
        name="forward_pass",
    )(feats, mask, *edges_of, targets, board, neigh, nbias, comb, cbias, cot)


def add_into(target, first, count, columns, parts, step=16):
    @pl.loop(0, count // step)
    def _(i):
        at = pl.ds(pl.multiple_of(first + i * step, step), step)
        total = target[at, columns].astype(F32)
        for part in parts:
            total += part[pl.ds(pl.multiple_of(i * step, step), step), :].astype(F32)
        target[at, columns] = total.astype(target.dtype)


def reduce_job(place, order, grad, region, arrive, land, send, recv, free, base):
    def release(axis, at):
        for _, _, device in place.others(axis):
            pl.semaphore_signal(free.at[at], inc=1, device_id=device, device_id_type=MESH)

    first, rows, left, columns = region
    half = columns // 2
    core = place.at["c"]
    mine = pl.ds(pl.multiple_of(left + core * half, half), half)
    theirs = pl.ds(pl.multiple_of(left + (1 - core) * half, half), half)
    sem = base
    mate = place.member("c", 1 - core)
    block = pl.ds(first, rows)
    copy = remote(grad.at[block, theirs], arrive, send.at[sem], recv.at[sem], mate)
    copy.start()
    sem += 1
    yield
    copy.wait()
    release("c", base)
    add_into(grad, first, rows, mine, [arrive])
    begin, length, used = first, rows, 0
    trail = []
    for axis in order:
        size = place.size[axis]
        length //= size
        copies, parts = [], []
        for far, index, device in place.others(axis):
            start = pl.multiple_of(begin + index * length, 16)
            slot = land.at[pl.ds(used, length)]
            used += length
            copy = remote(
                grad.at[pl.ds(start, length), mine], slot, send.at[sem], recv.at[sem], device
            )
            copy.start()
            sem += 1
            copies.append(copy)
            parts.append(slot)
        yield
        for copy in copies:
            copy.wait()
        trail.append((axis, begin, length))
        release(axis, base + len(trail))
        begin = pl.multiple_of(begin + place.at[axis] * length, 16)
        add_into(grad, begin, length, mine, parts)
    for stage in range(len(trail), 0, -1):
        axis, parent, piece = trail[stage - 1]
        pl.semaphore_wait(free.at[base + stage], place.size[axis] - 1)
        start = pl.multiple_of(parent + place.at[axis] * piece, 16)
        own = grad.at[pl.ds(start, piece), mine]
        copies = []
        for far, index, device in place.others(axis):
            copy = remote(own, own, send.at[sem], recv.at[sem], device)
            copy.start()
            sem += 1
            copies.append(copy)
        yield
        for copy in copies:
            copy.wait()
    pl.semaphore_wait(free.at[base], 1)
    own = grad.at[block, mine]
    copy = remote(own, own, send.at[sem], recv.at[sem], mate)
    copy.start()
    yield
    copy.wait()


def job_sems(n_nodes, n_grp):
    return 2 * (1 + (n_nodes // LINE // 2 - 1) + (LINE - 1) + (n_grp - 1))


JOBS = {
    kind[0] + str(i): kind + str(i) for kind, count in (("comb", 4), ("neigh", 4), ("board", 2)) for i in range(count)
}
BACKWARD = (
    "B0", "B1", "W0", "30", "20", "G0", "B2", "31", "10", "c2", "B3", "c1", "S0", "c3", "c0", "32",
    "c0", "11", "c2", "c1", "O0", "n0", "c3", "21", "33", "n0", "22", "23", "c2", "c1", "12", "O1",
    "n1", "13", "n0", "c0", "n1", "n0", "O2", "n2", "n2", "c3", "c1", "O3", "n3", "n1", "E0", "H1",
    "b1", "n2", "H0", "b0", "c2", "n3", "n0", "b1", "c1", "b0", "c2", "c1", "n0", "c0", "b1", "P0",
    "c2", "n2", "c3", "c1", "b0", "n0", "c0", "n2", "c2", "c3", "b0", "c0", "F0", "n2", "c1", "b1",
    "c3", "n0", "c0", "b0", "n3", "b1", "c3", "n1", "b0", "c1", "n2", "n3", "b1", "n1", "n3", "b0",
    "n1", "n3", "P1", "b1", "c0", "c2", "n3", "c3", "b0", "n1", "n3", "n2", "c0", "b1", "c3", "n3",
    "b0", "P2", "n1", "n0", "c2", "P3", "n2", "b1", "n1",
)


def gradient_regions(n_nodes, n_grp, width):
    pieces = n_nodes * n_grp // 2
    x_first, y_first = ("x", "y", "z"), ("y", "x", "z")
    regions = {}
    count = max(1, min(4, 2 * width // (16 * pieces)))
    n_rows = 2 * width // count
    for j in range(count):
        regions[f"comb{j}"] = (j * n_rows, n_rows, 0, width, x_first)
    if width % (16 * pieces) == 0:
        part = width // CHUNKS
        for k in range(CHUNKS):
            regions[f"neigh{k}"] = (2 * width, width, k * part, part, x_first if k % 2 else y_first)
        count = max(1, min(2, width // (16 * pieces)))
        n_rows = width // count
        for j in range(count):
            order = x_first if j % 2 == 0 else y_first
            regions[f"board{j}"] = (3 * width + j * n_rows, n_rows, 0, width, order)
    else:
        regions["board0"] = (2 * width, 2 * width, 0, width, x_first)
    return regions


def backward_kernel(
    n_nodes,
    n_grp,
    mask_ref,
    targets_ref,
    stats_ref,
    hid_h,
    pre_h,
    featb_h,
    board_b_h,
    neigh_b_h,
    comb1_b_h,
    st_h,
    dnum_h,
    dz_h,
    agg_h,
    gfeat_h,
    summed_h,
    small_ref,
    hid,
    pre,
    featb,
    board_b,
    neigh_b,
    comb1_b,
    spread_t,
    dnum,
    dz,
    agg,
    picker_t,
    out_slots,
    in_slots,
    chain,
    tmp,
    dpre,
    dh,
    grad,
    arrive,
    land,
    share_l,
    share_z,
    share_x,
    small,
    load_sem,
    store_sem,
    slot_send,
    slot_recv,
    up_send,
    down_send,
    chain_recv,
    job_send,
    job_recv,
    job_free,
    share_send,
    share_recv,
):
    place = Place(n_nodes, n_grp)
    z, low = place.at["z"], place.at["l"]
    layer = place.size["l"]
    rows, width = hid.shape
    layer_slots = spread_t.shape[2]
    cap = layer_slots // layer
    part = width // CHUNKS

    loads = {}
    for i, (name, src, dst) in enumerate(
        (
            ("dnum", dnum_h, dnum),
            ("hid", hid_h, hid),
            ("agg", agg_h, agg),
            ("dz", dz_h, dz),
            ("spread_t", st_h, spread_t),
            ("comb1_b", comb1_b_h, comb1_b),
            ("pre", pre_h, pre),
            ("neigh_b", neigh_b_h, neigh_b),
            ("featb", featb_h, featb),
            ("board_b", board_b_h, board_b),
        )
    ):
        loads[name] = pltpu.make_async_copy(src, dst, load_sem.at[i])
        loads[name].start()
    def make_pickers():
        @pl.loop(0, LINE)
        def _(src):
            at = pl.ds(pl.multiple_of(src * layer_slots, layer_slots), layer_slots)
            ids = lax.broadcasted_iota(jnp.int32, (rows, layer_slots), 0)
            picker_t[src] = jnp.where(ids == targets_ref[:, at], 1.0, 0.0).astype(BF16).T

    barrier(place, ("l", "z", "x"), make_pickers)
    stores = []

    def store(src, dst):
        copy = pltpu.make_async_copy(src, dst, store_sem.at[len(stores)])
        copy.start()
        stores.append(copy)

    mask = column_of(mask_ref) > 0.5

    def source(which):
        flip = z // 2
        inner = z * (1 - 2 * flip) + (LINE - 1) * flip
        index = ORDER[0][which] * (1 - inner) + ORDER[1][which] * inner
        return index * (1 - 2 * flip) + (LINE - 1) * flip

    def cols(k):
        return pl.ds(pl.multiple_of(k * part, part), part)

    def slot_copy(dst, k, far, index, device):
        at = (dst * CHUNKS + k) * (layer - 1) + far
        return remote(
            out_slots.at[dst, k, pl.ds(pl.multiple_of(index * cap, cap), cap)],
            in_slots.at[dst, k, pl.ds(pl.multiple_of(low * cap, cap), cap)],
            slot_send.at[at],
            slot_recv.at[at],
            device,
        )

    def back(dst, k):
        out_slots[dst, k] = jnp.dot(
            picker_t[dst], dnum[:, cols(k)], preferred_element_type=F32
        ).astype(BF16)
        for far, index, device in place.others("l"):
            slot_copy(dst, k, far, index, device).start()
        own = pl.ds(pl.multiple_of(low * cap, cap), cap)
        in_slots[dst, k, own] = out_slots[dst, k, own]

    def child_sums(dst, k):
        for far, index, device in place.others("l"):
            slot_copy(dst, k, far, index, device).wait_recv()
        tmp[...] = jnp.dot(spread_t[dst], in_slots[dst, k], preferred_element_type=F32)

    def up_copy(dst, k):
        at = dst * CHUNKS + k
        return remote(
            chain.at[dst, k],
            chain.at[dst, k],
            up_send.at[at],
            chain_recv.at[at],
            place.member("z", z + 1),
        )

    def down_copy(dst, k, last):
        slot = LINE if last else dst
        return remote(
            chain.at[dst, k],
            chain.at[slot, k],
            down_send.at[dst * CHUNKS + k],
            chain_recv.at[slot * CHUNKS + k],
            place.member("z", z - 1),
        )

    def arrived(slot, k):
        remote(
            chain.at[slot, k],
            chain.at[slot, k],
            up_send.at[0],
            chain_recv.at[slot * CHUNKS + k],
            place.member("z", lax.rem(z + 1, LINE)),
        ).wait_recv()

    def hand_on(dst, k):
        child_sums(dst, k)

        @pl.when(dst > z)
        def _():
            @pl.when(z > 0)
            def _():
                up_copy(dst, k).wait_recv()
                chain[dst, k] = (chain[dst, k].astype(F32) + tmp[...]).astype(BF16)

            @pl.when(z == 0)
            def _():
                chain[dst, k] = tmp[...].astype(BF16)

            up_copy(dst, k).start()

        @pl.when(dst < z)
        def _():
            @pl.when(z < LINE - 1)
            def _():
                down_copy(dst, k, False).wait_recv()
                chain[dst, k] = (chain[dst, k].astype(F32) + tmp[...]).astype(BF16)

            @pl.when(z == LINE - 1)
            def _():
                chain[dst, k] = tmp[...].astype(BF16)

            @pl.when(dst == z - 1)
            def _():
                down_copy(dst, k, True).start()

            @pl.when(dst < z - 1)
            def _():
                down_copy(dst, k, False).start()

    regions = gradient_regions(n_nodes, n_grp, width)
    per_job = job_sems(n_nodes, n_grp)

    def job(name):
        first, n_rows, left, columns, order = regions[name]
        rows_at, cols_at = pl.ds(first, n_rows), pl.ds(left, columns)
        land_at = pl.ds(left // 2, columns // 2)
        yield from reduce_job(
            place,
            order,
            grad,
            (first, n_rows, left, columns),
            arrive.at[rows_at, land_at],
            land.at[rows_at, land_at],
            job_send,
            job_recv,
            job_free,
            list(regions).index(name) * per_job,
        )
        store(grad.at[rows_at, cols_at], summed_h.at[rows_at, cols_at])

    jobs = {name: job(name) for name in regions}

    def step_job(name, last=False):
        if name in jobs and (last or name != "board0" or "board1" in regions):
            try:
                next(jobs[name])
            except StopIteration:
                del jobs[name]

    loads["dnum"].wait()

    def back_all(k):
        for which in (3, 2, 1, 0):
            back(source(which), k)

    def comb_grad(left, first):
        @pl.loop(0, CHUNKS)
        def _(k):
            grad[pl.ds(first, width), cols(k)] = dot_tn(left[...], dz[:, cols(k)]).astype(BF16)

    def own(k):
        child_sums(z, k)

        @pl.when(z > 0)
        def _():
            arrived(z, k)
            tmp[...] += chain[z, k].astype(F32)

        @pl.when(z < LINE - 1)
        def _():
            arrived(LINE, k)
            tmp[...] += chain[LINE, k].astype(F32)

        down = (tmp[...] * gelu_slope(pre[:, cols(k)])).astype(BF16)
        dpre[:, cols(k)] = down
        small[0:1, cols(k)] = jnp.sum(down.astype(F32), axis=0, keepdims=True)
        dh[...] += dot_nt(down, neigh_b[:, cols(k)])

    def neigh_grad(k):
        grad[pl.ds(2 * width, width), cols(k)] = dot_tn(hid[...], dpre[:, cols(k)]).astype(BF16)

    def comb_grads():
        for name in ("hid", "agg", "dz", "comb1_b"):
            loads[name].wait()
        comb_grad(hid, 0)
        comb_grad(agg, width)

    def self_part():
        small[...] = jnp.zeros_like(small)
        small[1:2, :] = jnp.sum(dz[...].astype(F32), axis=0, keepdims=True)
        small[2:3, :] = jnp.broadcast_to(stats_ref[0:1, 0:1], (1, width))

        @pl.loop(0, CHUNKS)
        def _(k):
            dh[:, cols(k)] = dot_nt(dz[...], comb1_b[cols(k), :])

        for name in ("pre", "neigh_b", "featb", "board_b"):
            loads[name].wait()

    def own_and_grad(k):
        own(k)
        neigh_grad(k)

    def end_of_line():
        last = dh[...].astype(BF16)
        dpre[...] = jnp.where(mask, last, jnp.zeros_like(last))
        pre[...] = last.astype(F32)

    def board_grad(i):
        half = width // 2
        grad[pl.ds(3 * width + i * half, half), :] = dot_tn(
            featb[:, i * half : (i + 1) * half], dpre[...]
        ).astype(BF16)

    def feature_grad():
        @pl.loop(0, CHUNKS)
        def _(k):
            pre[:, cols(k)] = jnp.where(
                mask, dot_nt(dpre[...], board_b[cols(k), :]), pre[:, cols(k)]
            )

        store(pre, gfeat_h)

    share = Share(place, (share_l, share_z, share_x), share_send, share_recv)

    def step_share(stage):
        if stage == 0:
            share.start(0, small[...])
        elif stage < 3:
            share.start(stage, share.finish(stage - 1))
        else:
            row = lax.broadcasted_iota(jnp.int32, small_ref.shape, 0)
            small_ref[...] = share.finish(2) * jnp.where(row == 2, stats_ref[8:9, 0:1], 1.0)

    acts = {
        "B": back_all,
        "W": lambda _: loads["spread_t"].wait(),
        "G": lambda _: comb_grads(),
        "S": lambda _: self_part(),
        "O": own_and_grad,
        "E": lambda _: end_of_line(),
        "H": board_grad,
        "F": lambda _: feature_grad(),
        "P": step_share,
        "3": lambda k: hand_on(source(3), k),
        "2": lambda k: hand_on(source(2), k),
        "1": lambda k: hand_on(source(1), k),
    }
    for step in BACKWARD:
        if step in JOBS:
            step_job(JOBS[step])
        else:
            acts[step[0]](int(step[1]))
    while jobs:
        for name in list(jobs):
            step_job(name, last=True)

    @pl.loop(0, LINE * CHUNKS)
    def _(i):
        dst = i // CHUNKS
        k = lax.rem(i, CHUNKS)

        @pl.when(dst > z)
        def _():
            up_copy(dst, k).wait_send()

        @pl.when(dst < z)
        def _():
            down_copy(dst, k, False).wait_send()

        for far, index, device in place.others("l"):
            slot_copy(dst, k, far, index, device).wait_send()

    for copy in stores:
        copy.wait()


def backward_pass(n_nodes, n_grp, mask, targets, stats, hid, pre, featb, board_b, neigh_b, comb1_b, st, dnum, dz, agg):
    rows, width = hid.shape
    layer = n_nodes // LINE
    layer_slots = st.shape[2]
    part = width // CHUNKS
    n_rows = 4 * width
    count = len(gradient_regions(n_nodes, n_grp, width))
    dma = pltpu.SemaphoreType.DMA
    big = pl.BlockSpec(memory_space=pl.ANY)
    vmem = pl.BlockSpec(memory_space=pltpu.VMEM)
    sems = count * job_sems(n_nodes, n_grp)
    pieces = LINE * CHUNKS
    return pl.pallas_call(
        functools.partial(backward_kernel, n_nodes, n_grp),
        out_shape=[
            jax.ShapeDtypeStruct((rows, width), F32),
            jax.ShapeDtypeStruct((n_rows, width), BF16),
            jax.ShapeDtypeStruct((8, width), F32),
        ],
        in_specs=[vmem, vmem, vmem] + [big] * 10,
        out_specs=[big, big, vmem],
        scratch_shapes=[
            pltpu.VMEM((rows, width), BF16),
            pltpu.VMEM((rows, width), F32),
            pltpu.VMEM((rows, width), BF16),
            pltpu.VMEM((width, width), BF16),
            pltpu.VMEM((width, width), BF16),
            pltpu.VMEM((width, width), BF16),
            pltpu.VMEM((LINE, rows, layer_slots), BF16),
            pltpu.VMEM((rows, width), BF16),
            pltpu.VMEM((rows, width), BF16),
            pltpu.VMEM((rows, width), BF16),
            pltpu.VMEM((LINE, layer_slots, rows), BF16),
            pltpu.VMEM((LINE, CHUNKS, layer_slots, part), BF16),
            pltpu.VMEM((LINE, CHUNKS, layer_slots, part), BF16),
            pltpu.VMEM((LINE + 1, CHUNKS, rows, part), BF16),
            pltpu.VMEM((rows, part), F32),
            pltpu.VMEM((rows, width), BF16),
            pltpu.VMEM((rows, width), F32),
            pltpu.VMEM((n_rows, width), BF16),
            pltpu.VMEM((n_rows, width // 2), BF16),
            pltpu.VMEM((n_rows, width // 2), BF16),
            pltpu.VMEM((layer, 8, width), F32),
            pltpu.VMEM((LINE, 8, width), F32),
            pltpu.VMEM((n_grp, 8, width), F32),
            pltpu.VMEM((8, width), F32),
            dma((10,)),
            dma((count + 1,)),
            dma((pieces * (layer - 1),)),
            dma((pieces * (layer - 1),)),
            dma((pieces,)),
            dma((pieces,)),
            dma((pieces + CHUNKS,)),
            dma((sems,)),
            dma((sems,)),
            pltpu.SemaphoreType.REGULAR((sems,)),
            dma((share_sems(n_nodes, n_grp),)),
            dma((share_sems(n_nodes, n_grp),)),
        ],
        compiler_params=pltpu.CompilerParams(
            vmem_limit_bytes=62 * MIB, collective_id=3, has_side_effects=True
        ),
        name="backward_pass",
    )(mask, targets, stats, hid, pre, featb, board_b, neigh_b, comb1_b, st, dnum, dz, agg)


def unpack_kernel(
    blocks,
    joined_ref,
    small_ref,
    embed_in,
    gfeat_in,
    comb_ref,
    neigh_ref,
    board_ref,
    nbias_ref,
    cbias_ref,
    penalty_ref,
    embed,
    gfeat,
    sem,
):
    step = pl.program_id(0)
    moves = [
        pltpu.make_async_copy(embed_in, embed, sem.at[0]),
        pltpu.make_async_copy(gfeat_in, gfeat, sem.at[1]),
    ]

    @pl.when(step == 0)
    def _():
        for move in moves:
            move.start()
        nbias_ref[...] = small_ref[0:1, :]
        cbias_ref[...] = small_ref[1:2, :]
        penalty_ref[...] = small_ref[2:3, 0:1]

    value = joined_ref[...].astype(F32)
    for target, first, count in ((comb_ref, 0, 2), (neigh_ref, 2, 1), (board_ref, 3, 1)):

        @pl.when(jnp.logical_and(step >= first * blocks, step < (first + count) * blocks))
        def _(target=target):
            target[...] = value

    @pl.when(step == 4 * blocks - 1)
    def _():
        for move in moves:
            move.wait()


def unpack(joined, small, embed, gfeat):
    width = joined.shape[1]
    rows = math.gcd(width, 256)
    blocks = width // rows
    big = pl.BlockSpec(memory_space=pl.ANY)

    def block(first, count):
        return pl.BlockSpec(
            (rows, width), lambda i: (jnp.clip(i - first * blocks, 0, count * blocks - 1), 0)
        )

    def whole(shape):
        return pl.BlockSpec(shape, lambda i: (0, 0))

    return pl.pallas_call(
        functools.partial(unpack_kernel, blocks),
        grid=(4 * blocks,),
        out_shape=[
            jax.ShapeDtypeStruct((2 * width, width), F32),
            jax.ShapeDtypeStruct((width, width), F32),
            jax.ShapeDtypeStruct((width, width), F32),
            jax.ShapeDtypeStruct((1, width), F32),
            jax.ShapeDtypeStruct((1, width), F32),
            jax.ShapeDtypeStruct((1, 1), F32),
            jax.ShapeDtypeStruct(embed.shape, F32),
            jax.ShapeDtypeStruct(gfeat.shape, F32),
        ],
        in_specs=[pl.BlockSpec((rows, width), lambda i: (i, 0)), whole(small.shape), big, big],
        out_specs=[block(0, 2), block(2, 1), block(3, 1)]
        + [whole((1, width)), whole((1, width)), whole((1, 1)), big, big],
        scratch_shapes=[pltpu.SemaphoreType.DMA((2,))],
        compiler_params=pltpu.CompilerParams(vmem_limit_bytes=60 * MIB),
        name="unpack",
    )(joined, small, embed, gfeat)


def on_device(
    n_nodes,
    n_grp,
    features,
    type_mask,
    edge_child,
    edge_slot,
    edge_weight,
    recv_rows,
    board_proj,
    neigh_proj,
    neigh_bias,
    combine_proj,
    combine_bias,
    out_cot,
):
    feats = features[0]
    rows, width = feats.shape
    peers = recv_rows.shape[2]
    cap = recv_rows.shape[3]
    slots = peers * cap
    targets = recv_rows[0, 0].reshape(1, slots)
    embed, hidden, pre, featb, pbl, qwl, cwl1, spread_t, dnum, dzb, aggb, stats = forward_pass(
        n_nodes,
        n_grp,
        feats,
        type_mask,
        (edge_slot, edge_child, edge_weight),
        targets,
        board_proj,
        neigh_proj,
        neigh_bias.reshape(1, width),
        combine_proj,
        combine_bias.reshape(1, width),
        out_cot[0],
    )
    grad_feats, summed, small = backward_pass(
        n_nodes,
        n_grp,
        type_mask,
        targets,
        stats,
        hidden,
        pre,
        featb,
        pbl,
        qwl,
        cwl1,
        spread_t,
        dnum,
        dzb,
        aggb,
    )
    grad_comb, grad_neigh, grad_board, grad_nbias, grad_cbias, penalty, embed, grad_feats = unpack(
        summed, small, embed, grad_feats
    )
    return (
        embed[None],
        penalty[0, 0],
        grad_feats[None],
        grad_board,
        grad_neigh,
        grad_nbias[0],
        grad_comb,
        grad_cbias[0],
    )


def solution(mesh):
    in_specs = (
        P("grp", "nodes", None),
        P("grp", "nodes"),
        P("grp", "nodes"),
        P("grp", "nodes"),
        P("grp", "nodes"),
        P("grp", "nodes", None, None),
        P(),
        P(),
        P(),
        P(),
        P(),
        P("grp", "nodes", None),
    )
    out_specs = (P("grp", "nodes", None), P(), P("grp", "nodes", None), P(), P(), P(), P(), P())
    return jax.shard_map(
        functools.partial(on_device, mesh.shape["nodes"], mesh.shape["grp"]),
        mesh=mesh,
        in_specs=in_specs,
        out_specs=out_specs,
        check_vma=False,
    )
```

```python
import functools
import math

import jax
import jax.numpy as jnp
from jax import lax
from jax.experimental import pallas as pl
from jax.experimental.pallas import tpu as pltpu
from jax.sharding import PartitionSpec as P

HIGH = lax.Precision.HIGHEST
MESH = pl.DeviceIdType.MESH
BF16 = jnp.bfloat16
F32 = jnp.float32
F8 = jnp.float8_e4m3fn
MIB = 2**20


def gelu_tanh(v):
    return jax.nn.gelu(v, approximate=True)


def dot_nt(left, right):
    return lax.dot_general(
        left, right, (((1,), (1,)), ((), ())), preferred_element_type=F32
    )


def dot_tn(left, right):
    return lax.dot_general(
        left, right, (((0,), (0,)), ((), ())), preferred_element_type=F32
    )


LINE = 4
CHUNKS = 4
FORWARD = (
    "m0", "m1", "m2", "m3", "Y00", "Y01", "Y02", "Y03", "Z0", "f00", "p00", "p01", "p02", "p03",
    "Y10", "P1", "Y11", "f01", "Y12", "f02", "Y13", "Z1", "p10", "p11", "p12", "Y20", "P2", "Y21",
    "f03", "Y22", "Y23", "f10", "Z2", "p13", "p20", "Y30", "Y31", "f11", "Y32", "Y33", "f12", "Z3",
    "p21", "p22", "G0", "P3", "f13", "p23", "D0", "D1", "D2", "D3", "X0", "R0", "i00", "i01",
    "i02", "i03", "f20", "p30", "i10", "i11", "i12", "i13", "f21", "p31", "i20", "i21", "i22",
    "i23", "f22", "p32", "i30", "d0", "a0", "f23", "p33", "i31", "a1", "i32", "a2", "i33",
)
ORDER = ((0, 1, 2, 3), (1, 2, 0, 3))


class Place:
    def __init__(self, n_nodes, n_grp):
        layer = n_nodes // LINE
        node = lax.axis_index("nodes")
        grp = lax.axis_index("grp")
        self.node, self.grp = node, grp
        self.size = {"l": layer, "c": 2, "y": layer // 2, "z": LINE, "x": n_grp}
        low = lax.rem(node, layer)
        self.at = {"l": low, "c": lax.rem(low, 2), "y": low // 2, "z": node // layer, "x": grp}

    def member(self, axis, index):
        layer = self.size["l"]
        low, line, grp = self.at["l"], self.at["z"], self.at["x"]
        if axis == "l":
            low = index
        elif axis == "c":
            low = self.at["y"] * 2 + index
        elif axis == "y":
            low = index * 2 + self.at["c"]
        elif axis == "z":
            line = index
        else:
            grp = index
        return {"nodes": line * layer + low, "grp": grp}

    def others(self, axis):
        size = self.size[axis]
        for far in range(1, size):
            index = lax.rem(self.at[axis] + far, size)
            yield far - 1, index, self.member(axis, index)


def remote(src, dst, send, recv, device):
    return pltpu.make_async_remote_copy(
        src_ref=src, dst_ref=dst, send_sem=send, recv_sem=recv, device_id=device, device_id_type=MESH
    )


def barrier(place, axes, meanwhile=None):
    sem = pltpu.get_barrier_semaphore()
    count = 0
    for axis in axes:
        for _, _, device in place.others(axis):
            pl.semaphore_signal(sem, inc=1, device_id=device, device_id_type=MESH)
            count += 1
    if meanwhile is not None:
        meanwhile()
    pl.semaphore_wait(sem, count)


def column_of(row_ref):
    row = row_ref[...].astype(F32)
    return jnp.broadcast_to(row, (128, row.shape[1])).T[:, 0:1]


def gelu(v):
    t = jnp.tanh(0.7978845608028654 * (v + 0.044715 * (v * v * v)))
    return v * (0.5 * (1.0 + t))


def gelu_slope(v):
    square = v * v
    t = jnp.tanh(0.7978845608028654 * (v + 0.044715 * (v * square)))
    bend = 0.7978845608028654 * (1.0 + 0.134145 * square)
    return 0.5 * (1.0 + t) + 0.5 * v * (1.0 - t * t) * bend


class Share:
    def __init__(self, place, bufs, send, recv):
        self.place, self.send, self.recv = place, send, recv
        self.stages, base = [], 0
        for axis, buf in zip(("l", "z", "x"), bufs):
            self.stages.append((axis, buf, base))
            base += place.size[axis] - 1

    def start(self, stage, value):
        axis, buf, base = self.stages[stage]
        me = self.place.at[axis]
        buf[me] = value
        for far, _, device in self.place.others(axis):
            remote(
                buf.at[me], buf.at[me], self.send.at[base + far], self.recv.at[base + far], device
            ).start()

    def finish(self, stage):
        axis, buf, base = self.stages[stage]
        me = self.place.at[axis]
        for far, _, device in self.place.others(axis):
            remote(
                buf.at[me], buf.at[me], self.send.at[base + far], self.recv.at[base + far], device
            ).wait()
        total = buf[0]
        for i in range(1, self.place.size[axis]):
            total += buf[i]
        return total


def share_sems(n_nodes, n_grp):
    return (n_nodes // LINE - 1) + (LINE - 1) + max(1, n_grp - 1)


def forward_kernel(
    n_nodes,
    n_grp,
    feats_h,
    mask_ref,
    place_ref,
    child_ref,
    weight_ref,
    targets_ref,
    board_h,
    neigh_h,
    nbias_ref,
    comb_h,
    cbias_ref,
    cot_h,
    embed_h,
    hid_h,
    pre_h,
    featb_h,
    board_b_h,
    neigh_b_h,
    comb1_b_h,
    st_h,
    dnum_h,
    dz_h,
    agg_h,
    stats_ref,
    stage,
    featb,
    hid,
    pre,
    board_b,
    neigh_b,
    comb_b,
    keys,
    msg,
    acc,
    spread,
    spread_t,
    out_slots,
    in_slots,
    out_tot,
    in_tot,
    picker,
    num,
    zval,
    zpre,
    cot,
    agg,
    dz,
    dnum,
    den_ref,
    scale_ref,
    count_l,
    count_z,
    count_x,
    load_sem,
    store_sem,
    key_send,
    key_recv,
    up_send,
    down_send,
    msg_recv,
    slot_send,
    slot_recv,
    tot_send,
    tot_recv,
    count_send,
    count_recv,
):
    place = Place(n_nodes, n_grp)
    z, low = place.at["z"], place.at["l"]
    layer = place.size["l"]
    rows, width = featb.shape
    edges = place_ref.shape[1]
    half = edges // 2
    layer_slots = spread.shape[1]
    cap = layer_slots // layer
    part = width // CHUNKS
    turn = math.gcd(half, 6400)
    steps = edges // turn

    sources = [feats_h.at[:]]
    for whole in (board_h, neigh_h, comb_h):
        for first in range(0, whole.shape[0], rows):
            sources.append(whole.at[pl.ds(first, rows)])
    n_stage = stage.shape[0]

    def load(i):
        return pltpu.make_async_copy(sources[i], stage.at[i % n_stage], load_sem.at[i % n_stage])

    for i in range(n_stage):
        load(i).start()
    load_cot = pltpu.make_async_copy(cot_h, cot, load_sem.at[n_stage])
    stores = []

    def store(src, dst):
        copy = pltpu.make_async_copy(src, dst, store_sem.at[len(stores)])
        copy.start()
        stores.append(copy)

    barrier(place, ("l", "z", "x"))
    keys[z, :, pl.ds(0, edges)] = place_ref[...] * 65536 + child_ref[...]
    keys[z, :, pl.ds(edges, half)] = (
        weight_ref[:, pl.ds(half, half)] * 65536 + weight_ref[:, pl.ds(0, half)]
    )

    def key_copy(far, device):
        return remote(keys.at[z], keys.at[z], key_send.at[far], key_recv.at[far], device)

    for far, _, device in place.others("z"):
        key_copy(far, device).start()
    share = Share(place, (count_l, count_z, count_x), count_send, count_recv)
    mask = column_of(mask_ref)
    share.start(0, jnp.full((8, 128), jnp.sum(mask)))

    def cast(i, target, first):
        load(i).wait()
        slot = stage.at[i % n_stage]

        @pl.loop(0, rows // 32)
        def _(r):
            at = pl.ds(pl.multiple_of(r * 32, 32), 32)
            to = pl.ds(pl.multiple_of(first + r * 32, 32), 32)
            target[to, :] = slot[at, :].astype(BF16)

    cast(0, featb, 0)
    cast(1, board_b, 0)
    cast(2, board_b, rows)

    @pl.loop(0, CHUNKS)
    def _(k):
        at = pl.ds(pl.multiple_of(k * part, part), part)
        proj = jnp.dot(featb[...], board_b[:, at], preferred_element_type=F32)
        hid[:, at] = jnp.where(mask > 0.5, proj, stage[0, :, at]).astype(BF16)

    cast(3, neigh_b, 0)
    cast(4, neigh_b, rows)
    for i in range(n_stage, len(sources)):
        load(i).start()
    load_cot.start()

    def up_copy(src, k):
        piece = msg.at[src, k]
        index = src * CHUNKS + k
        return remote(
            piece, piece, up_send.at[index], msg_recv.at[index], place.member("z", z + 1)
        )

    def down_copy(src, k):
        piece = msg.at[src, k]
        index = src * CHUNKS + k
        return remote(
            piece, piece, down_send.at[index], msg_recv.at[index], place.member("z", z - 1)
        )

    def message(k):
        at = pl.ds(k * part, part)
        value = jnp.dot(hid[...], neigh_b[:, at], preferred_element_type=F32) + nbias_ref[:, at]
        pre[:, at] = value
        msg[z, k] = gelu(value).astype(BF16)

        @pl.when(z < LINE - 1)
        def _():
            up_copy(z, k).start()

        @pl.when(z > 0)
        def _():
            down_copy(z, k).start()

    def forward(j, k):
        below = z - 1 - j
        above = z + 1 + j

        @pl.when(below >= 0)
        def _():
            up_copy(below, k).wait_recv()

            @pl.when(z < LINE - 1)
            def _():
                up_copy(below, k).start()

        @pl.when(above < LINE)
        def _():
            down_copy(above, k).wait_recv()

            @pl.when(z > 0)
            def _():
                down_copy(above, k).start()

    def tot_copy(src, far, index, device):
        at = (layer - 1) * src + far
        return remote(
            out_tot.at[src, pl.ds(pl.multiple_of(index * cap, cap), cap)],
            in_tot.at[src, pl.ds(pl.multiple_of(low * cap, cap), cap)],
            tot_send.at[at],
            tot_recv.at[at],
            device,
        )

    def finish_spread(src):
        total = acc[...]
        spread[src] = total.astype(BF16)
        spread_t[src] = total.astype(BF16).T
        sums = jnp.sum(total, axis=1, keepdims=True).astype(jnp.int32)
        lane = lax.broadcasted_iota(jnp.int32, (layer_slots, 128), 1)
        digit = jnp.where(
            lane == 0, sums & 255, jnp.where(lane == 1, (sums >> 8) & 255, jnp.where(lane == 2, sums >> 16, 0))
        )
        out_tot[src] = digit.astype(F32).astype(BF16)
        own = pl.ds(pl.multiple_of(low * cap, cap), cap)
        in_tot[src, own] = out_tot[src, own]
        for far, index, device in place.others("l"):
            tot_copy(src, far, index, device).start()

    def source(which):
        flip = z // 2
        inner = z * (1 - 2 * flip) + (LINE - 1) * flip
        index = ORDER[0][which] * (1 - inner) + ORDER[1][which] * inner
        return index * (1 - 2 * flip) + (LINE - 1) * flip

    def build(which, ticks):
        src = source(which)
        acc[...] = jnp.zeros_like(acc)
        if which > 0:
            far = lax.rem(z - src - 1 + LINE, LINE)
            remote(
                keys.at[src], keys.at[src], key_send.at[0], key_recv.at[far], place.member("z", src)
            ).wait_recv()

        @pl.loop(0, steps)
        def _(t):
            second = t // (steps // 2)
            key = keys[src, :, pl.ds(pl.multiple_of(t * turn, turn), turn)]
            start = edges + (t - second * (steps // 2)) * turn
            pair = keys[src, :, pl.ds(pl.multiple_of(start, turn), turn)]
            weight = (lax.shift_right_logical(pair, second * 16) & 65535).astype(F32).astype(F8)
            child = (key & 65535).astype(jnp.int16)
            slot = (lax.shift_right_logical(key, 16) - z * layer_slots).astype(jnp.int16)
            right = jnp.where(
                lax.broadcasted_iota(jnp.int16, (rows, turn), 0) == child, weight, jnp.zeros((), F8)
            )
            block = 256
            for first in range(0, layer_slots, block):
                ids = lax.broadcasted_iota(jnp.int16, (block, turn), 0) + jnp.asarray(
                    first, jnp.int16
                )
                left = jnp.where(ids == slot, jnp.ones((), F8), jnp.zeros((), F8))
                acc[pl.ds(first, block), :] += dot_nt(left, right)
            for at, acts in enumerate(ticks):
                if acts:

                    @pl.when(t == at)
                    def _(acts=acts):
                        for act in acts:
                            act()

        finish_spread(src)

    def slot_copy(src, k, far, index, device):
        at = (src * CHUNKS + k) * (layer - 1) + far
        return remote(
            out_slots.at[src, k, pl.ds(pl.multiple_of(index * cap, cap), cap)],
            in_slots.at[src, k, pl.ds(pl.multiple_of(low * cap, cap), cap)],
            slot_send.at[at],
            slot_recv.at[at],
            device,
        )

    def piece(src, k):
        out_slots[src, k] = jnp.dot(spread[src], msg[src, k], preferred_element_type=F32).astype(BF16)
        for far, index, device in place.others("l"):
            slot_copy(src, k, far, index, device).start()
        own = pl.ds(pl.multiple_of(low * cap, cap), cap)
        in_slots[src, k, own] = out_slots[src, k, own]

    def pick(src, k):
        for far, index, device in place.others("l"):
            slot_copy(src, k, far, index, device).wait_recv()
        num[k] += jnp.dot(picker[src], in_slots[src, k], preferred_element_type=F32)

    def make_picker():
        @pl.loop(0, LINE)
        def _(src):
            at = pl.ds(pl.multiple_of(src * layer_slots, layer_slots), layer_slots)
            ids = lax.broadcasted_iota(jnp.int32, (rows, layer_slots), 0)
            picker[src] = jnp.where(ids == targets_ref[:, at], 1.0, 0.0).astype(BF16)

        num[...] = jnp.zeros_like(num)

    def comb_piece(i):
        for j in range(i, 2 * width // rows, CHUNKS):
            cast(5 + j, comb_b, j * rows)

    def self_part():
        @pl.loop(0, CHUNKS)
        def _(k):
            at = pl.ds(pl.multiple_of(k * part, part), part)
            zpre[:, at] = (
                jnp.dot(hid[...], comb_b[0:width, at], preferred_element_type=F32)
                + cbias_ref[:, at]
            )

    def results():
        store(hid, hid_h)
        store(pre, pre_h)
        store(featb, featb_h)
        store(board_b, board_b_h)
        store(neigh_b, neigh_b_h)
        store(comb_b.at[pl.ds(0, width)], comb1_b_h)
        store(spread_t, st_h)

    def totals():
        digits = jnp.zeros((rows, 128), F32)
        for src in range(LINE):
            for far, index, device in place.others("l"):
                tot_copy(src, far, index, device).wait_recv()
            digits += jnp.dot(picker[src], in_tot[src], preferred_element_type=F32)
        lane = lax.broadcasted_iota(jnp.int32, (rows, 128), 1)
        worth = jnp.where(
            lane == 0, 1.0, jnp.where(lane == 1, 256.0, jnp.where(lane == 2, 65536.0, 0.0))
        )
        den_ref[...] = jnp.broadcast_to(
            1.0 + jnp.sum(digits * worth, axis=1, keepdims=True), (rows, 128)
        )

    def neighbours(k):
        at = pl.ds(k * part, part)
        agg[:, at] = (num[k] / den_ref[:, 0:1]).astype(BF16)
        if k < CHUNKS - 1:

            @pl.loop(0, CHUNKS)
            def _(n):
                to = pl.ds(pl.multiple_of(n * part, part), part)
                zpre[:, to] += jnp.dot(
                    agg[:, at], comb_b[pl.ds(width + k * part, part), to], preferred_element_type=F32
                )

    def step_share(stage):
        if stage in (1, 2):
            share.start(stage, share.finish(stage - 1))
        elif stage == 3:
            boards = share.finish(2)
            scale_ref[...] = 1.0 / (width * (1.0 + boards))

    acts = {
        "P": step_share,
        "m": message,
        "f": forward,
        "p": lambda which, k: piece(source(which), k),
        "i": lambda which, k: pick(source(which), k),
        "G": lambda _: make_picker(),
        "D": comb_piece,
        "X": lambda _: self_part(),
        "R": lambda _: results(),
        "d": lambda _: totals(),
        "a": neighbours,
    }

    def act(step):
        acts[step[0]](*(int(c) for c in step[1:]))

    ticks = None
    for step in FORWARD:
        if step[0] == "Y":
            if ticks is None:
                ticks = [[] for _ in range(steps)]
            now = min(int(step[2]), steps - 1)
        elif step[0] == "Z":
            build(int(step[1]), ticks)
            ticks = None
        elif ticks is not None:
            ticks[now].append(functools.partial(act, step))
        else:
            act(step)

    neighbours(CHUNKS - 1)
    load_cot.wait()
    den = den_ref[:, 0:1]
    scale = scale_ref[0:1, 0:1]
    last = pl.ds(width - part, part)

    def dense(k, carry):
        square, along = carry
        at = pl.ds(pl.multiple_of(k * part, part), part)
        value = zpre[:, at] + jnp.dot(
            agg[:, last], comb_b[pl.ds(2 * width - part, part), at], preferred_element_type=F32
        )
        zpre[:, at] = value
        out = gelu(value)
        zval[:, at] = out
        square += jnp.sum(out * out, axis=1, keepdims=True)
        along += jnp.sum(out * cot[:, at], axis=1, keepdims=True)
        return square, along

    zero = jnp.zeros((rows, 1), F32)
    square, along = lax.fori_loop(0, CHUNKS, dense, (zero, zero))
    inverse = lax.rsqrt(square + 1e-06)
    along = along * inverse
    push = jnp.where(mask > 0.5, 2.0 * scale, 0.0)
    stats_ref[...] = jnp.concatenate(
        [
            jnp.full((8, 128), jnp.sum(jnp.where(mask > 0.5, square, 0.0))),
            jnp.broadcast_to(scale, (8, 128)),
        ],
        axis=0,
    )

    @pl.loop(0, CHUNKS)
    def _(k):
        at = pl.ds(pl.multiple_of(k * part, part), part)
        out = zval[:, at]
        emb = out * inverse
        grad = inverse * (cot[:, at] - emb * along) + push * out
        dz[:, at] = (grad * gelu_slope(zpre[:, at])).astype(BF16)
        zval[:, at] = emb

    store(zval, embed_h)
    store(dz, dz_h)
    store(agg, agg_h)

    @pl.loop(0, CHUNKS)
    def _(k):
        at = pl.ds(pl.multiple_of(k * part, part), part)
        back = dot_nt(dz[...], comb_b[pl.ds(pl.multiple_of(width + k * part, part), part), :])
        dnum[:, at] = (back / den).astype(BF16)

    store(dnum, dnum_h)

    for far, _, device in place.others("z"):
        key_copy(far, device).wait_send()

    @pl.loop(0, LINE * CHUNKS)
    def _(i):
        src = i // CHUNKS
        k = lax.rem(i, CHUNKS)

        @pl.when(jnp.logical_and(src <= z, z < LINE - 1))
        def _():
            up_copy(src, k).wait_send()

        @pl.when(jnp.logical_and(src >= z, z > 0))
        def _():
            down_copy(src, k).wait_send()

        for far, index, device in place.others("l"):
            slot_copy(src, k, far, index, device).wait_send()

    for src in range(LINE):
        for far, index, device in place.others("l"):
            tot_copy(src, far, index, device).wait_send()
    for copy in stores:
        copy.wait()


def forward_pass(n_nodes, n_grp, feats, mask, edges_of, targets, board, neigh, nbias, comb, cbias, cot):
    rows, width = feats.shape
    edges = edges_of[0].shape[1]
    layer = n_nodes // LINE
    layer_slots = targets.shape[1] // LINE
    part = width // CHUNKS
    dma = pltpu.SemaphoreType.DMA
    n_stage = 5
    big = pl.BlockSpec(memory_space=pl.ANY)
    small = pl.BlockSpec(memory_space=pltpu.VMEM)

    def hbm(shape, dtype):
        return jax.ShapeDtypeStruct(shape, dtype)

    return pl.pallas_call(
        functools.partial(forward_kernel, n_nodes, n_grp),
        out_shape=[
            hbm((rows, width), F32),
            hbm((rows, width), BF16),
            hbm((rows, width), F32),
            hbm((rows, width), BF16),
            hbm((width, width), BF16),
            hbm((width, width), BF16),
            hbm((width, width), BF16),
            hbm((LINE, rows, layer_slots), BF16),
            hbm((rows, width), BF16),
            hbm((rows, width), BF16),
            hbm((rows, width), BF16),
            hbm((16, 128), F32),
        ],
        in_specs=[big] + [small] * 5 + [big, big, small, big, small, big],
        out_specs=[big] * 11 + [small],
        scratch_shapes=[
            pltpu.VMEM((n_stage, rows, width), F32),
            pltpu.VMEM((rows, width), BF16),
            pltpu.VMEM((rows, width), BF16),
            pltpu.VMEM((rows, width), F32),
            pltpu.VMEM((width, width), BF16),
            pltpu.VMEM((width, width), BF16),
            pltpu.VMEM((2 * width, width), BF16),
            pltpu.VMEM((LINE, 1, edges + edges // 2), jnp.int32),
            pltpu.VMEM((LINE, CHUNKS, rows, part), BF16),
            pltpu.VMEM((layer_slots, rows), F32),
            pltpu.VMEM((LINE, layer_slots, rows), BF16),
            pltpu.VMEM((LINE, rows, layer_slots), BF16),
            pltpu.VMEM((LINE, CHUNKS, layer_slots, part), BF16),
            pltpu.VMEM((LINE, CHUNKS, layer_slots, part), BF16),
            pltpu.VMEM((LINE, layer_slots, 128), BF16),
            pltpu.VMEM((LINE, layer_slots, 128), BF16),
            pltpu.VMEM((LINE, rows, layer_slots), BF16),
            pltpu.VMEM((CHUNKS, rows, part), F32),
            pltpu.VMEM((rows, width), F32),
            pltpu.VMEM((rows, width), F32),
            pltpu.VMEM((rows, width), F32),
            pltpu.VMEM((rows, width), BF16),
            pltpu.VMEM((rows, width), BF16),
            pltpu.VMEM((rows, width), BF16),
            pltpu.VMEM((rows, 128), F32),
            pltpu.VMEM((8, 128), F32),
            pltpu.VMEM((layer, 8, 128), F32),
            pltpu.VMEM((LINE, 8, 128), F32),
            pltpu.VMEM((n_grp, 8, 128), F32),
            dma((n_stage + 1,)),
            dma((11,)),
            dma((LINE - 1,)),
            dma((LINE - 1,)),
            dma((LINE * CHUNKS,)),
            dma((LINE * CHUNKS,)),
            dma((LINE * CHUNKS,)),
            dma((LINE * CHUNKS * (layer - 1),)),
            dma((LINE * CHUNKS * (layer - 1),)),
            dma((LINE * (layer - 1),)),
            dma((LINE * (layer - 1),)),
            dma((share_sems(n_nodes, n_grp),)),
            dma((share_sems(n_nodes, n_grp),)),
        ],
        compiler_params=pltpu.CompilerParams(
            vmem_limit_bytes=60 * MIB, collective_id=2, has_side_effects=True
        ),
        name="forward_pass",
    )(feats, mask, *edges_of, targets, board, neigh, nbias, comb, cbias, cot)


def add_into(target, first, count, columns, parts, step=16):
    @pl.loop(0, count // step)
    def _(i):
        at = pl.ds(pl.multiple_of(first + i * step, step), step)
        total = target[at, columns].astype(F32)
        for part in parts:
            total += part[pl.ds(pl.multiple_of(i * step, step), step), :].astype(F32)
        target[at, columns] = total.astype(target.dtype)


def reduce_job(place, order, grad, region, arrive, land, last, send, recv, free, base):
    def release(axis, at):
        for _, _, device in place.others(axis):
            pl.semaphore_signal(free.at[at], inc=1, device_id=device, device_id_type=MESH)

    first, rows, left, columns = region
    half = columns // 2
    core = place.at["c"]
    mine = pl.ds(pl.multiple_of(left + core * half, half), half)
    theirs = pl.ds(pl.multiple_of(left + (1 - core) * half, half), half)
    sem = base
    mate = place.member("c", 1 - core)
    block = pl.ds(first, rows)
    copy = remote(grad.at[block, theirs], arrive, send.at[sem], recv.at[sem], mate)
    copy.start()
    sem += 1
    yield
    copy.wait()
    release("c", base)
    add_into(grad, first, rows, mine, [arrive])
    begin, length, used = first, rows, 0
    trail = []
    for axis in order:
        size = place.size[axis]
        length //= size
        copies, parts = [], []
        for far, index, device in place.others(axis):
            start = pl.multiple_of(begin + index * length, 16)
            slot = land.at[pl.ds(used, length)]
            used += length
            copy = remote(
                grad.at[pl.ds(start, length), mine], slot, send.at[sem], recv.at[sem], device
            )
            copy.start()
            sem += 1
            copies.append(copy)
            parts.append(slot)
        yield
        for copy in copies:
            copy.wait()
        trail.append((axis, begin, length))
        if len(trail) < len(order):
            release(axis, base + len(trail))
        begin = pl.multiple_of(begin + place.at[axis] * length, 16)
        add_into(grad, begin, length, mine, parts)
    axis, parent, piece = trail[-1]
    here = pl.ds(pl.multiple_of(place.at[axis] * piece, 16), piece)
    last[here] = grad[pl.ds(begin, piece), mine]
    copies = []
    for far, index, device in place.others(axis):
        copy = remote(last.at[here], last.at[here], send.at[sem], recv.at[sem], device)
        copy.start()
        sem += 1
        copies.append(copy)
    yield
    for copy in copies:
        copy.wait()
    size = piece * place.size[axis]
    grad[pl.ds(pl.multiple_of(parent, 16), size), mine] = last[pl.ds(0, size)]
    for stage in range(len(trail) - 1, 0, -1):
        axis, parent, piece = trail[stage - 1]
        pl.semaphore_wait(free.at[base + stage], place.size[axis] - 1)
        start = pl.multiple_of(parent + place.at[axis] * piece, 16)
        own = grad.at[pl.ds(start, piece), mine]
        copies = []
        for far, index, device in place.others(axis):
            copy = remote(own, own, send.at[sem], recv.at[sem], device)
            copy.start()
            sem += 1
            copies.append(copy)
        yield
        for copy in copies:
            copy.wait()
    pl.semaphore_wait(free.at[base], 1)
    own = grad.at[block, mine]
    copy = remote(own, own, send.at[sem], recv.at[sem], mate)
    copy.start()
    yield
    copy.wait()


def job_sems(n_nodes, n_grp):
    return 2 * (1 + (n_nodes // LINE // 2 - 1) + (LINE - 1) + (n_grp - 1))


JOBS = {
    kind[0] + str(i): kind + str(i) for kind, count in (("comb", 4), ("neigh", 4), ("board", 2)) for i in range(count)
}
BACKWARD = (
    "B0", "B1", "W0", "30", "20", "G0", "B2", "31", "10", "c2", "B3", "c1", "S0", "c3", "c0", "32",
    "c0", "11", "c2", "c1", "O0", "n0", "c3", "21", "33", "n0", "22", "23", "c2", "c1", "12", "O1",
    "n1", "13", "n0", "c0", "n1", "n0", "O2", "n2", "n2", "c3", "c1", "O3", "n3", "n1", "E0", "H1",
    "b1", "n2", "H0", "b0", "c2", "n3", "n0", "b1", "c1", "b0", "c2", "c1", "n0", "c0", "b1", "P0",
    "c2", "n2", "c3", "c1", "b0", "n0", "c0", "n2", "c2", "c3", "b0", "c0", "F0", "n2", "c1", "b1",
    "c3", "n0", "c0", "b0", "n3", "b1", "c3", "n1", "b0", "c1", "n2", "n3", "b1", "n1", "n3", "b0",
    "n1", "n3", "P1", "b1", "c0", "c2", "n3", "c3", "b0", "n1", "n3", "n2", "c0", "b1", "c3", "n3",
    "b0", "P2", "n1", "n0", "c2", "P3", "n2", "b1", "n1",
)


def gradient_regions(n_nodes, n_grp, width):
    pieces = n_nodes * n_grp // 2
    x_first, y_first = ("x", "y", "z"), ("y", "x", "z")
    regions = {}
    count = max(1, min(4, 2 * width // (16 * pieces)))
    n_rows = 2 * width // count
    for j in range(count):
        regions[f"comb{j}"] = (j * n_rows, n_rows, 0, width, x_first)
    if width % (16 * pieces) == 0:
        part = width // CHUNKS
        for k in range(CHUNKS):
            regions[f"neigh{k}"] = (2 * width, width, k * part, part, x_first if k % 2 else y_first)
        count = max(1, min(2, width // (16 * pieces)))
        n_rows = width // count
        for j in range(count):
            order = x_first if j % 2 == 0 else y_first
            regions[f"board{j}"] = (3 * width + j * n_rows, n_rows, 0, width, order)
    else:
        regions["board0"] = (2 * width, 2 * width, 0, width, x_first)
    return regions


def backward_kernel(
    n_nodes,
    n_grp,
    mask_ref,
    targets_ref,
    stats_ref,
    hid_h,
    pre_h,
    featb_h,
    board_b_h,
    neigh_b_h,
    comb1_b_h,
    st_h,
    dnum_h,
    dz_h,
    agg_h,
    gfeat_h,
    summed_h,
    small_ref,
    hid,
    pre,
    featb,
    board_b,
    neigh_b,
    comb1_b,
    spread_t,
    dnum,
    dz,
    agg,
    picker_t,
    out_slots,
    in_slots,
    chain,
    tmp,
    dpre,
    dh,
    grad,
    arrive,
    land,
    gather,
    share_l,
    share_z,
    share_x,
    small,
    load_sem,
    store_sem,
    slot_send,
    slot_recv,
    up_send,
    down_send,
    chain_recv,
    job_send,
    job_recv,
    job_free,
    share_send,
    share_recv,
):
    place = Place(n_nodes, n_grp)
    z, low = place.at["z"], place.at["l"]
    layer = place.size["l"]
    rows, width = hid.shape
    layer_slots = spread_t.shape[2]
    cap = layer_slots // layer
    part = width // CHUNKS

    loads = {}
    for i, (name, src, dst) in enumerate(
        (
            ("dnum", dnum_h, dnum),
            ("hid", hid_h, hid),
            ("agg", agg_h, agg),
            ("dz", dz_h, dz),
            ("spread_t", st_h, spread_t),
            ("comb1_b", comb1_b_h, comb1_b),
            ("pre", pre_h, pre),
            ("neigh_b", neigh_b_h, neigh_b),
            ("featb", featb_h, featb),
            ("board_b", board_b_h, board_b),
        )
    ):
        loads[name] = pltpu.make_async_copy(src, dst, load_sem.at[i])
        loads[name].start()
    def make_pickers():
        @pl.loop(0, LINE)
        def _(src):
            at = pl.ds(pl.multiple_of(src * layer_slots, layer_slots), layer_slots)
            ids = lax.broadcasted_iota(jnp.int32, (rows, layer_slots), 0)
            picker_t[src] = jnp.where(ids == targets_ref[:, at], 1.0, 0.0).astype(BF16).T

    barrier(place, ("l", "z", "x"), make_pickers)
    stores = []

    def store(src, dst):
        copy = pltpu.make_async_copy(src, dst, store_sem.at[len(stores)])
        copy.start()
        stores.append(copy)

    mask = column_of(mask_ref) > 0.5

    def source(which):
        flip = z // 2
        inner = z * (1 - 2 * flip) + (LINE - 1) * flip
        index = ORDER[0][which] * (1 - inner) + ORDER[1][which] * inner
        return index * (1 - 2 * flip) + (LINE - 1) * flip

    def cols(k):
        return pl.ds(pl.multiple_of(k * part, part), part)

    def slot_copy(dst, k, far, index, device):
        at = (dst * CHUNKS + k) * (layer - 1) + far
        return remote(
            out_slots.at[dst, k, pl.ds(pl.multiple_of(index * cap, cap), cap)],
            in_slots.at[dst, k, pl.ds(pl.multiple_of(low * cap, cap), cap)],
            slot_send.at[at],
            slot_recv.at[at],
            device,
        )

    def back(dst, k):
        out_slots[dst, k] = jnp.dot(
            picker_t[dst], dnum[:, cols(k)], preferred_element_type=F32
        ).astype(BF16)
        for far, index, device in place.others("l"):
            slot_copy(dst, k, far, index, device).start()
        own = pl.ds(pl.multiple_of(low * cap, cap), cap)
        in_slots[dst, k, own] = out_slots[dst, k, own]

    def child_sums(dst, k):
        for far, index, device in place.others("l"):
            slot_copy(dst, k, far, index, device).wait_recv()
        tmp[...] = jnp.dot(spread_t[dst], in_slots[dst, k], preferred_element_type=F32)

    def up_copy(dst, k):
        at = dst * CHUNKS + k
        return remote(
            chain.at[dst, k],
            chain.at[dst, k],
            up_send.at[at],
            chain_recv.at[at],
            place.member("z", z + 1),
        )

    def down_copy(dst, k, last):
        slot = LINE if last else dst
        return remote(
            chain.at[dst, k],
            chain.at[slot, k],
            down_send.at[dst * CHUNKS + k],
            chain_recv.at[slot * CHUNKS + k],
            place.member("z", z - 1),
        )

    def arrived(slot, k):
        remote(
            chain.at[slot, k],
            chain.at[slot, k],
            up_send.at[0],
            chain_recv.at[slot * CHUNKS + k],
            place.member("z", lax.rem(z + 1, LINE)),
        ).wait_recv()

    def hand_on(dst, k):
        child_sums(dst, k)

        @pl.when(dst > z)
        def _():
            @pl.when(z > 0)
            def _():
                up_copy(dst, k).wait_recv()
                chain[dst, k] = (chain[dst, k].astype(F32) + tmp[...]).astype(BF16)

            @pl.when(z == 0)
            def _():
                chain[dst, k] = tmp[...].astype(BF16)

            up_copy(dst, k).start()

        @pl.when(dst < z)
        def _():
            @pl.when(z < LINE - 1)
            def _():
                down_copy(dst, k, False).wait_recv()
                chain[dst, k] = (chain[dst, k].astype(F32) + tmp[...]).astype(BF16)

            @pl.when(z == LINE - 1)
            def _():
                chain[dst, k] = tmp[...].astype(BF16)

            @pl.when(dst == z - 1)
            def _():
                down_copy(dst, k, True).start()

            @pl.when(dst < z - 1)
            def _():
                down_copy(dst, k, False).start()

    regions = gradient_regions(n_nodes, n_grp, width)
    per_job = job_sems(n_nodes, n_grp)

    def job(name):
        first, n_rows, left, columns, order = regions[name]
        rows_at, cols_at = pl.ds(first, n_rows), pl.ds(left, columns)
        land_at = pl.ds(left // 2, columns // 2)
        yield from reduce_job(
            place,
            order,
            grad,
            (first, n_rows, left, columns),
            arrive.at[rows_at, land_at],
            land.at[rows_at, land_at],
            gather.at[pl.ds(first // 4, n_rows // 4), land_at],
            job_send,
            job_recv,
            job_free,
            list(regions).index(name) * per_job,
        )
        store(grad.at[rows_at, cols_at], summed_h.at[rows_at, cols_at])

    jobs = {name: job(name) for name in regions}

    def step_job(name, last=False):
        if name in jobs and (last or name != "board0" or "board1" in regions):
            try:
                next(jobs[name])
            except StopIteration:
                del jobs[name]

    loads["dnum"].wait()

    def back_all(k):
        for which in (3, 2, 1, 0):
            back(source(which), k)

    def comb_grad(left, first):
        @pl.loop(0, CHUNKS)
        def _(k):
            grad[pl.ds(first, width), cols(k)] = dot_tn(left[...], dz[:, cols(k)]).astype(BF16)

    def own(k):
        child_sums(z, k)

        @pl.when(z > 0)
        def _():
            arrived(z, k)
            tmp[...] += chain[z, k].astype(F32)

        @pl.when(z < LINE - 1)
        def _():
            arrived(LINE, k)
            tmp[...] += chain[LINE, k].astype(F32)

        down = (tmp[...] * gelu_slope(pre[:, cols(k)])).astype(BF16)
        dpre[:, cols(k)] = down
        small[0:1, cols(k)] = jnp.sum(down.astype(F32), axis=0, keepdims=True)
        dh[...] += dot_nt(down, neigh_b[:, cols(k)])

    def neigh_grad(k):
        grad[pl.ds(2 * width, width), cols(k)] = dot_tn(hid[...], dpre[:, cols(k)]).astype(BF16)

    def comb_grads():
        for name in ("hid", "agg", "dz", "comb1_b"):
            loads[name].wait()
        comb_grad(hid, 0)
        comb_grad(agg, width)

    def self_part():
        small[...] = jnp.zeros_like(small)
        small[1:2, :] = jnp.sum(dz[...].astype(F32), axis=0, keepdims=True)
        small[2:3, :] = jnp.broadcast_to(stats_ref[0:1, 0:1], (1, width))

        @pl.loop(0, CHUNKS)
        def _(k):
            dh[:, cols(k)] = dot_nt(dz[...], comb1_b[cols(k), :])

        for name in ("pre", "neigh_b", "featb", "board_b"):
            loads[name].wait()

    def own_and_grad(k):
        own(k)
        neigh_grad(k)

    def end_of_line():
        last = dh[...].astype(BF16)
        dpre[...] = jnp.where(mask, last, jnp.zeros_like(last))
        pre[...] = last.astype(F32)

    def board_grad(i):
        half = width // 2
        grad[pl.ds(3 * width + i * half, half), :] = dot_tn(
            featb[:, i * half : (i + 1) * half], dpre[...]
        ).astype(BF16)

    def feature_grad():
        @pl.loop(0, CHUNKS)
        def _(k):
            pre[:, cols(k)] = jnp.where(
                mask, dot_nt(dpre[...], board_b[cols(k), :]), pre[:, cols(k)]
            )

        store(pre, gfeat_h)

    share = Share(place, (share_l, share_z, share_x), share_send, share_recv)

    def step_share(stage):
        if stage == 0:
            share.start(0, small[...])
        elif stage < 3:
            share.start(stage, share.finish(stage - 1))
        else:
            row = lax.broadcasted_iota(jnp.int32, small_ref.shape, 0)
            small_ref[...] = share.finish(2) * jnp.where(row == 2, stats_ref[8:9, 0:1], 1.0)

    acts = {
        "B": back_all,
        "W": lambda _: loads["spread_t"].wait(),
        "G": lambda _: comb_grads(),
        "S": lambda _: self_part(),
        "O": own_and_grad,
        "E": lambda _: end_of_line(),
        "H": board_grad,
        "F": lambda _: feature_grad(),
        "P": step_share,
        "3": lambda k: hand_on(source(3), k),
        "2": lambda k: hand_on(source(2), k),
        "1": lambda k: hand_on(source(1), k),
    }
    for step in BACKWARD:
        if step in JOBS:
            step_job(JOBS[step])
        else:
            acts[step[0]](int(step[1]))
    while jobs:
        for name in list(jobs):
            step_job(name, last=True)

    @pl.loop(0, LINE * CHUNKS)
    def _(i):
        dst = i // CHUNKS
        k = lax.rem(i, CHUNKS)

        @pl.when(dst > z)
        def _():
            up_copy(dst, k).wait_send()

        @pl.when(dst < z)
        def _():
            down_copy(dst, k, False).wait_send()

        for far, index, device in place.others("l"):
            slot_copy(dst, k, far, index, device).wait_send()

    for copy in stores:
        copy.wait()


def backward_pass(n_nodes, n_grp, mask, targets, stats, hid, pre, featb, board_b, neigh_b, comb1_b, st, dnum, dz, agg):
    rows, width = hid.shape
    layer = n_nodes // LINE
    layer_slots = st.shape[2]
    part = width // CHUNKS
    n_rows = 4 * width
    count = len(gradient_regions(n_nodes, n_grp, width))
    dma = pltpu.SemaphoreType.DMA
    big = pl.BlockSpec(memory_space=pl.ANY)
    vmem = pl.BlockSpec(memory_space=pltpu.VMEM)
    sems = count * job_sems(n_nodes, n_grp)
    pieces = LINE * CHUNKS
    return pl.pallas_call(
        functools.partial(backward_kernel, n_nodes, n_grp),
        out_shape=[
            jax.ShapeDtypeStruct((rows, width), F32),
            jax.ShapeDtypeStruct((n_rows, width), BF16),
            jax.ShapeDtypeStruct((8, width), F32),
        ],
        in_specs=[vmem, vmem, vmem] + [big] * 10,
        out_specs=[big, big, vmem],
        scratch_shapes=[
            pltpu.VMEM((rows, width), BF16),
            pltpu.VMEM((rows, width), F32),
            pltpu.VMEM((rows, width), BF16),
            pltpu.VMEM((width, width), BF16),
            pltpu.VMEM((width, width), BF16),
            pltpu.VMEM((width, width), BF16),
            pltpu.VMEM((LINE, rows, layer_slots), BF16),
            pltpu.VMEM((rows, width), BF16),
            pltpu.VMEM((rows, width), BF16),
            pltpu.VMEM((rows, width), BF16),
            pltpu.VMEM((LINE, layer_slots, rows), BF16),
            pltpu.VMEM((LINE, CHUNKS, layer_slots, part), BF16),
            pltpu.VMEM((LINE, CHUNKS, layer_slots, part), BF16),
            pltpu.VMEM((LINE + 1, CHUNKS, rows, part), BF16),
            pltpu.VMEM((rows, part), F32),
            pltpu.VMEM((rows, width), BF16),
            pltpu.VMEM((rows, width), F32),
            pltpu.VMEM((n_rows, width), BF16),
            pltpu.VMEM((n_rows, width // 2), BF16),
            pltpu.VMEM((n_rows, width // 2), BF16),
            pltpu.VMEM((n_rows // 4, width // 2), BF16),
            pltpu.VMEM((layer, 8, width), F32),
            pltpu.VMEM((LINE, 8, width), F32),
            pltpu.VMEM((n_grp, 8, width), F32),
            pltpu.VMEM((8, width), F32),
            dma((10,)),
            dma((count + 1,)),
            dma((pieces * (layer - 1),)),
            dma((pieces * (layer - 1),)),
            dma((pieces,)),
            dma((pieces,)),
            dma((pieces + CHUNKS,)),
            dma((sems,)),
            dma((sems,)),
            pltpu.SemaphoreType.REGULAR((sems,)),
            dma((share_sems(n_nodes, n_grp),)),
            dma((share_sems(n_nodes, n_grp),)),
        ],
        compiler_params=pltpu.CompilerParams(
            vmem_limit_bytes=62 * MIB, collective_id=3, has_side_effects=True
        ),
        name="backward_pass",
    )(mask, targets, stats, hid, pre, featb, board_b, neigh_b, comb1_b, st, dnum, dz, agg)


def unpack_kernel(
    rows, joined, small_ref, comb, neigh, board, nbias_ref, cbias_ref, penalty_ref, low, wide, load_sem, store_sem
):
    width = joined.shape[1]
    blocks = joined.shape[0] // rows

    def load(i):
        at = pl.ds(i * rows, rows)
        return pltpu.make_async_copy(joined.at[at], low.at[at], load_sem.at[i])

    def store(i):
        first = i * rows
        if first < 2 * width:
            target = comb.at[pl.ds(first, rows)]
        elif first < 3 * width:
            target = neigh.at[pl.ds(first - 2 * width, rows)]
        else:
            target = board.at[pl.ds(first - 3 * width, rows)]
        return pltpu.make_async_copy(wide.at[pl.ds(first, rows)], target, store_sem.at[i])

    for i in range(blocks):
        load(i).start()
    nbias_ref[...] = small_ref[0:1, :]
    cbias_ref[...] = small_ref[1:2, :]
    penalty_ref[...] = small_ref[2:3, 0:1]
    for i in range(blocks):
        load(i).wait()

        @pl.loop(0, rows // 32)
        def _(r, i=i):
            at = pl.ds(pl.multiple_of(i * rows + r * 32, 32), 32)
            wide[at, :] = low[at, :].astype(F32)

        store(i).start()
    for i in range(blocks):
        store(i).wait()


def unpack(joined, small):
    n_rows, width = joined.shape
    rows = math.gcd(width, 256)
    big = pl.BlockSpec(memory_space=pl.ANY)
    vmem = pl.BlockSpec(memory_space=pltpu.VMEM)
    dma = pltpu.SemaphoreType.DMA
    return pl.pallas_call(
        functools.partial(unpack_kernel, rows),
        out_shape=[
            jax.ShapeDtypeStruct((2 * width, width), F32),
            jax.ShapeDtypeStruct((width, width), F32),
            jax.ShapeDtypeStruct((width, width), F32),
            jax.ShapeDtypeStruct((1, width), F32),
            jax.ShapeDtypeStruct((1, width), F32),
            jax.ShapeDtypeStruct((1, 1), F32),
        ],
        in_specs=[big, vmem],
        out_specs=[big] * 3 + [vmem] * 3,
        scratch_shapes=[
            pltpu.VMEM((n_rows, width), BF16),
            pltpu.VMEM((n_rows, width), F32),
            dma((n_rows // rows,)),
            dma((n_rows // rows,)),
        ],
        compiler_params=pltpu.CompilerParams(vmem_limit_bytes=60 * MIB),
        name="unpack",
    )(joined, small)


def on_device(
    n_nodes,
    n_grp,
    features,
    type_mask,
    edge_child,
    edge_slot,
    edge_weight,
    recv_rows,
    board_proj,
    neigh_proj,
    neigh_bias,
    combine_proj,
    combine_bias,
    out_cot,
):
    feats = features[0]
    rows, width = feats.shape
    peers = recv_rows.shape[2]
    cap = recv_rows.shape[3]
    slots = peers * cap
    targets = recv_rows[0, 0].reshape(1, slots)
    embed, hidden, pre, featb, pbl, qwl, cwl1, spread_t, dnum, dzb, aggb, stats = forward_pass(
        n_nodes,
        n_grp,
        feats,
        type_mask,
        (edge_slot, edge_child, edge_weight),
        targets,
        board_proj,
        neigh_proj,
        neigh_bias.reshape(1, width),
        combine_proj,
        combine_bias.reshape(1, width),
        out_cot[0],
    )
    grad_feats, summed, small = backward_pass(
        n_nodes,
        n_grp,
        type_mask,
        targets,
        stats,
        hidden,
        pre,
        featb,
        pbl,
        qwl,
        cwl1,
        spread_t,
        dnum,
        dzb,
        aggb,
    )
    grad_comb, grad_neigh, grad_board, grad_nbias, grad_cbias, penalty = unpack(summed, small)
    return (
        embed[None],
        penalty[0, 0],
        grad_feats[None],
        grad_board,
        grad_neigh,
        grad_nbias[0],
        grad_comb,
        grad_cbias[0],
    )


def solution(mesh):
    in_specs = (
        P("grp", "nodes", None),
        P("grp", "nodes"),
        P("grp", "nodes"),
        P("grp", "nodes"),
        P("grp", "nodes"),
        P("grp", "nodes", None, None),
        P(),
        P(),
        P(),
        P(),
        P(),
        P("grp", "nodes", None),
    )
    out_specs = (P("grp", "nodes", None), P(), P("grp", "nodes", None), P(), P(), P(), P(), P())
    return jax.shard_map(
        functools.partial(on_device, mesh.shape["nodes"], mesh.shape["grp"]),
        mesh=mesh,
        in_specs=in_specs,
        out_specs=out_specs,
        check_vma=False,
    )
```

```python
import functools
import math

import jax
import jax.numpy as jnp
from jax import lax
from jax.experimental import pallas as pl
from jax.experimental.pallas import tpu as pltpu
from jax.sharding import PartitionSpec as P

HIGH = lax.Precision.HIGHEST
MESH = pl.DeviceIdType.MESH
BF16 = jnp.bfloat16
F32 = jnp.float32
F8 = jnp.float8_e4m3fn
MIB = 2**20


def gelu_tanh(v):
    return jax.nn.gelu(v, approximate=True)


def dot_nt(left, right):
    return lax.dot_general(
        left, right, (((1,), (1,)), ((), ())), preferred_element_type=F32
    )


def dot_tn(left, right):
    return lax.dot_general(
        left, right, (((0,), (0,)), ((), ())), preferred_element_type=F32
    )


LINE = 4
CHUNKS = 4
FORWARD = (
    "m0", "m1", "m2", "m3", "Y00", "Y01", "Y02", "Y03", "Z0", "f00", "p00", "p01", "p02", "p03",
    "Y10", "P1", "Y11", "f01", "Y12", "f02", "Y13", "Z1", "p10", "p11", "p12", "Y20", "P2", "Y21",
    "f03", "Y22", "Y23", "f10", "Z2", "p13", "p20", "Y30", "Y31", "f11", "Y32", "Y33", "f12", "Z3",
    "p21", "p22", "G0", "P3", "f13", "p23", "D0", "D1", "D2", "D3", "X0", "R0", "i00", "i01",
    "i02", "i03", "f20", "p30", "i10", "i11", "i12", "i13", "f21", "p31", "i20", "i21", "i22",
    "i23", "f22", "p32", "i30", "d0", "a0", "f23", "p33", "i31", "a1", "i32", "a2", "i33",
)
ORDER = ((0, 1, 2, 3), (1, 2, 0, 3))


class Place:
    def __init__(self, n_nodes, n_grp):
        layer = n_nodes // LINE
        node = lax.axis_index("nodes")
        grp = lax.axis_index("grp")
        self.node, self.grp = node, grp
        self.size = {"l": layer, "c": 2, "y": layer // 2, "z": LINE, "x": n_grp}
        low = lax.rem(node, layer)
        self.at = {"l": low, "c": lax.rem(low, 2), "y": low // 2, "z": node // layer, "x": grp}

    def member(self, axis, index):
        layer = self.size["l"]
        low, line, grp = self.at["l"], self.at["z"], self.at["x"]
        if axis == "l":
            low = index
        elif axis == "c":
            low = self.at["y"] * 2 + index
        elif axis == "y":
            low = index * 2 + self.at["c"]
        elif axis == "z":
            line = index
        else:
            grp = index
        return {"nodes": line * layer + low, "grp": grp}

    def others(self, axis):
        size = self.size[axis]
        for far in range(1, size):
            index = lax.rem(self.at[axis] + far, size)
            yield far - 1, index, self.member(axis, index)


def remote(src, dst, send, recv, device):
    return pltpu.make_async_remote_copy(
        src_ref=src, dst_ref=dst, send_sem=send, recv_sem=recv, device_id=device, device_id_type=MESH
    )


def barrier(place, axes, meanwhile=None):
    sem = pltpu.get_barrier_semaphore()
    count = 0
    for axis in axes:
        for _, _, device in place.others(axis):
            pl.semaphore_signal(sem, inc=1, device_id=device, device_id_type=MESH)
            count += 1
    if meanwhile is not None:
        meanwhile()
    pl.semaphore_wait(sem, count)


def column_of(row_ref):
    row = row_ref[...].astype(F32)
    return jnp.broadcast_to(row, (128, row.shape[1])).T[:, 0:1]


def gelu(v):
    t = jnp.tanh(0.7978845608028654 * (v + 0.044715 * (v * v * v)))
    return v * (0.5 * (1.0 + t))


def gelu_slope(v):
    square = v * v
    t = jnp.tanh(0.7978845608028654 * (v + 0.044715 * (v * square)))
    bend = 0.7978845608028654 * (1.0 + 0.134145 * square)
    return 0.5 * (1.0 + t) + 0.5 * v * (1.0 - t * t) * bend


class Share:
    def __init__(self, place, bufs, send, recv):
        self.place, self.send, self.recv = place, send, recv
        self.stages, base = [], 0
        for axis, buf in zip(("l", "z", "x"), bufs):
            self.stages.append((axis, buf, base))
            base += place.size[axis] - 1

    def start(self, stage, value):
        axis, buf, base = self.stages[stage]
        me = self.place.at[axis]
        buf[me] = value
        for far, _, device in self.place.others(axis):
            remote(
                buf.at[me], buf.at[me], self.send.at[base + far], self.recv.at[base + far], device
            ).start()

    def finish(self, stage):
        axis, buf, base = self.stages[stage]
        me = self.place.at[axis]
        for far, _, device in self.place.others(axis):
            remote(
                buf.at[me], buf.at[me], self.send.at[base + far], self.recv.at[base + far], device
            ).wait()
        total = buf[0]
        for i in range(1, self.place.size[axis]):
            total += buf[i]
        return total


def run_ticks(t, ticks):
    for at, acts in enumerate(ticks):
        if acts:

            @pl.when(t == at)
            def _(acts=acts):
                for act in acts:
                    act()


def run_order(order, steps, build, act):
    ticks = None
    for name in order:
        if name[0] == "Y":
            if ticks is None:
                ticks = [[] for _ in range(steps)]
            now = min(int(name[2]), steps - 1)
        elif name[0] == "Z":
            build(int(name[1]), ticks)
            ticks = None
        elif ticks is not None:
            ticks[now].append(functools.partial(act, name))
        else:
            act(name)


def share_sems(n_nodes, n_grp):
    return (n_nodes // LINE - 1) + (LINE - 1) + max(1, n_grp - 1)


def forward_kernel(
    n_nodes,
    n_grp,
    feats_h,
    mask_ref,
    place_ref,
    child_ref,
    weight_ref,
    targets_ref,
    board_h,
    neigh_h,
    nbias_ref,
    comb_h,
    cbias_ref,
    cot_h,
    embed_h,
    hid_h,
    pre_h,
    featb_h,
    board_b_h,
    neigh_b_h,
    comb1_b_h,
    st_h,
    dnum_h,
    dz_h,
    agg_h,
    stats_ref,
    stage,
    featb,
    hid,
    pre,
    board_b,
    neigh_b,
    comb_b,
    keys,
    msg,
    acc,
    spread,
    spread_t,
    out_slots,
    in_slots,
    out_tot,
    in_tot,
    picker,
    num,
    zval,
    zpre,
    cot,
    agg,
    dz,
    dnum,
    den_ref,
    scale_ref,
    count_l,
    count_z,
    count_x,
    load_sem,
    store_sem,
    key_send,
    key_recv,
    up_send,
    down_send,
    msg_recv,
    slot_send,
    slot_recv,
    tot_send,
    tot_recv,
    count_send,
    count_recv,
):
    place = Place(n_nodes, n_grp)
    z, low = place.at["z"], place.at["l"]
    layer = place.size["l"]
    rows, width = featb.shape
    edges = place_ref.shape[1]
    half = edges // 2
    layer_slots = spread.shape[1]
    cap = layer_slots // layer
    part = width // CHUNKS
    turn = math.gcd(half, 6400)
    steps = edges // turn

    sources = [feats_h.at[:]]
    for whole in (board_h, neigh_h, comb_h):
        for first in range(0, whole.shape[0], rows):
            sources.append(whole.at[pl.ds(first, rows)])
    n_stage = stage.shape[0]

    def load(i):
        return pltpu.make_async_copy(sources[i], stage.at[i % n_stage], load_sem.at[i % n_stage])

    for i in range(n_stage):
        load(i).start()
    load_cot = pltpu.make_async_copy(cot_h, cot, load_sem.at[n_stage])
    stores = []

    def store(src, dst):
        copy = pltpu.make_async_copy(src, dst, store_sem.at[len(stores)])
        copy.start()
        stores.append(copy)

    barrier(place, ("l", "z", "x"))
    keys[z, :, pl.ds(0, edges)] = place_ref[...] * 65536 + child_ref[...]
    keys[z, :, pl.ds(edges, half)] = (
        weight_ref[:, pl.ds(half, half)] * 65536 + weight_ref[:, pl.ds(0, half)]
    )

    def key_copy(far, device):
        return remote(keys.at[z], keys.at[z], key_send.at[far], key_recv.at[far], device)

    for far, _, device in place.others("z"):
        key_copy(far, device).start()
    share = Share(place, (count_l, count_z, count_x), count_send, count_recv)
    mask = column_of(mask_ref)
    share.start(0, jnp.full((8, 128), jnp.sum(mask)))

    def cast(i, target, first):
        load(i).wait()
        slot = stage.at[i % n_stage]

        @pl.loop(0, rows // 32)
        def _(r):
            at = pl.ds(pl.multiple_of(r * 32, 32), 32)
            to = pl.ds(pl.multiple_of(first + r * 32, 32), 32)
            target[to, :] = slot[at, :].astype(BF16)

    cast(0, featb, 0)
    cast(1, board_b, 0)
    cast(2, board_b, rows)

    @pl.loop(0, CHUNKS)
    def _(k):
        at = pl.ds(pl.multiple_of(k * part, part), part)
        proj = jnp.dot(featb[...], board_b[:, at], preferred_element_type=F32)
        hid[:, at] = jnp.where(mask > 0.5, proj, stage[0, :, at]).astype(BF16)

    cast(3, neigh_b, 0)
    cast(4, neigh_b, rows)
    for i in range(n_stage, len(sources)):
        load(i).start()
    load_cot.start()

    def up_copy(src, k):
        piece = msg.at[src, k]
        index = src * CHUNKS + k
        return remote(
            piece, piece, up_send.at[index], msg_recv.at[index], place.member("z", z + 1)
        )

    def down_copy(src, k):
        piece = msg.at[src, k]
        index = src * CHUNKS + k
        return remote(
            piece, piece, down_send.at[index], msg_recv.at[index], place.member("z", z - 1)
        )

    def message(k):
        at = pl.ds(k * part, part)
        value = jnp.dot(hid[...], neigh_b[:, at], preferred_element_type=F32) + nbias_ref[:, at]
        pre[:, at] = value
        msg[z, k] = gelu(value).astype(BF16)

        @pl.when(z < LINE - 1)
        def _():
            up_copy(z, k).start()

        @pl.when(z > 0)
        def _():
            down_copy(z, k).start()

    def forward(j, k):
        below = z - 1 - j
        above = z + 1 + j

        @pl.when(below >= 0)
        def _():
            up_copy(below, k).wait_recv()

            @pl.when(z < LINE - 1)
            def _():
                up_copy(below, k).start()

        @pl.when(above < LINE)
        def _():
            down_copy(above, k).wait_recv()

            @pl.when(z > 0)
            def _():
                down_copy(above, k).start()

    def tot_copy(src, far, index, device):
        at = (layer - 1) * src + far
        return remote(
            out_tot.at[src, pl.ds(pl.multiple_of(index * cap, cap), cap)],
            in_tot.at[src, pl.ds(pl.multiple_of(low * cap, cap), cap)],
            tot_send.at[at],
            tot_recv.at[at],
            device,
        )

    def finish_spread(src):
        total = acc[...]
        spread[src] = total.astype(BF16)
        spread_t[src] = total.astype(BF16).T
        sums = jnp.sum(total, axis=1, keepdims=True).astype(jnp.int32)
        lane = lax.broadcasted_iota(jnp.int32, (layer_slots, 128), 1)
        digit = jnp.where(
            lane == 0, sums & 255, jnp.where(lane == 1, (sums >> 8) & 255, jnp.where(lane == 2, sums >> 16, 0))
        )
        out_tot[src] = digit.astype(F32).astype(BF16)
        own = pl.ds(pl.multiple_of(low * cap, cap), cap)
        in_tot[src, own] = out_tot[src, own]
        for far, index, device in place.others("l"):
            tot_copy(src, far, index, device).start()

    def source(which):
        flip = z // 2
        inner = z * (1 - 2 * flip) + (LINE - 1) * flip
        index = ORDER[0][which] * (1 - inner) + ORDER[1][which] * inner
        return index * (1 - 2 * flip) + (LINE - 1) * flip

    def build(which, ticks):
        src = source(which)
        acc[...] = jnp.zeros_like(acc)
        if which > 0:
            far = lax.rem(z - src - 1 + LINE, LINE)
            remote(
                keys.at[src], keys.at[src], key_send.at[0], key_recv.at[far], place.member("z", src)
            ).wait_recv()

        @pl.loop(0, steps)
        def _(t):
            second = t // (steps // 2)
            key = keys[src, :, pl.ds(pl.multiple_of(t * turn, turn), turn)]
            start = edges + (t - second * (steps // 2)) * turn
            pair = keys[src, :, pl.ds(pl.multiple_of(start, turn), turn)]
            weight = (lax.shift_right_logical(pair, second * 16) & 65535).astype(F32).astype(F8)
            child = (key & 65535).astype(jnp.int16)
            slot = (lax.shift_right_logical(key, 16) - z * layer_slots).astype(jnp.int16)
            right = jnp.where(
                lax.broadcasted_iota(jnp.int16, (rows, turn), 0) == child, weight, jnp.zeros((), F8)
            )
            block = 256
            for first in range(0, layer_slots, block):
                ids = lax.broadcasted_iota(jnp.int16, (block, turn), 0) + jnp.asarray(
                    first, jnp.int16
                )
                left = jnp.where(ids == slot, jnp.ones((), F8), jnp.zeros((), F8))
                acc[pl.ds(first, block), :] += dot_nt(left, right)
            run_ticks(t, ticks)

        finish_spread(src)

    def slot_copy(src, k, far, index, device):
        at = (src * CHUNKS + k) * (layer - 1) + far
        return remote(
            out_slots.at[src, k, pl.ds(pl.multiple_of(index * cap, cap), cap)],
            in_slots.at[src, k, pl.ds(pl.multiple_of(low * cap, cap), cap)],
            slot_send.at[at],
            slot_recv.at[at],
            device,
        )

    def piece(src, k):
        out_slots[src, k] = jnp.dot(spread[src], msg[src, k], preferred_element_type=F32).astype(BF16)
        for far, index, device in place.others("l"):
            slot_copy(src, k, far, index, device).start()
        own = pl.ds(pl.multiple_of(low * cap, cap), cap)
        in_slots[src, k, own] = out_slots[src, k, own]

    def pick(src, k):
        for far, index, device in place.others("l"):
            slot_copy(src, k, far, index, device).wait_recv()
        num[k] += jnp.dot(picker[src], in_slots[src, k], preferred_element_type=F32)

    def make_picker():
        @pl.loop(0, LINE)
        def _(src):
            at = pl.ds(pl.multiple_of(src * layer_slots, layer_slots), layer_slots)
            ids = lax.broadcasted_iota(jnp.int32, (rows, layer_slots), 0)
            picker[src] = jnp.where(ids == targets_ref[:, at], 1.0, 0.0).astype(BF16)

        num[...] = jnp.zeros_like(num)

    def comb_piece(i):
        for j in range(i, 2 * width // rows, CHUNKS):
            cast(5 + j, comb_b, j * rows)

    def self_part():
        @pl.loop(0, CHUNKS)
        def _(k):
            at = pl.ds(pl.multiple_of(k * part, part), part)
            zpre[:, at] = (
                jnp.dot(hid[...], comb_b[0:width, at], preferred_element_type=F32)
                + cbias_ref[:, at]
            )

    def results():
        store(hid, hid_h)
        store(pre, pre_h)
        store(featb, featb_h)
        store(board_b, board_b_h)
        store(neigh_b, neigh_b_h)
        store(comb_b.at[pl.ds(0, width)], comb1_b_h)
        store(spread_t, st_h)

    def totals():
        digits = jnp.zeros((rows, 128), F32)
        for src in range(LINE):
            for far, index, device in place.others("l"):
                tot_copy(src, far, index, device).wait_recv()
            digits += jnp.dot(picker[src], in_tot[src], preferred_element_type=F32)
        lane = lax.broadcasted_iota(jnp.int32, (rows, 128), 1)
        worth = jnp.where(
            lane == 0, 1.0, jnp.where(lane == 1, 256.0, jnp.where(lane == 2, 65536.0, 0.0))
        )
        den_ref[...] = jnp.broadcast_to(
            1.0 + jnp.sum(digits * worth, axis=1, keepdims=True), (rows, 128)
        )

    def neighbours(k):
        at = pl.ds(k * part, part)
        agg[:, at] = (num[k] / den_ref[:, 0:1]).astype(BF16)
        if k < CHUNKS - 1:

            @pl.loop(0, CHUNKS)
            def _(n):
                to = pl.ds(pl.multiple_of(n * part, part), part)
                zpre[:, to] += jnp.dot(
                    agg[:, at], comb_b[pl.ds(width + k * part, part), to], preferred_element_type=F32
                )

    def step_share(stage):
        if stage in (1, 2):
            share.start(stage, share.finish(stage - 1))
        elif stage == 3:
            boards = share.finish(2)
            scale_ref[...] = 1.0 / (width * (1.0 + boards))

    acts = {
        "P": step_share,
        "m": message,
        "f": forward,
        "p": lambda which, k: piece(source(which), k),
        "i": lambda which, k: pick(source(which), k),
        "G": lambda _: make_picker(),
        "D": comb_piece,
        "X": lambda _: self_part(),
        "R": lambda _: results(),
        "d": lambda _: totals(),
        "a": neighbours,
    }

    def act(step):
        acts[step[0]](*(int(c) for c in step[1:]))

    run_order(FORWARD, steps, build, act)
    neighbours(CHUNKS - 1)
    load_cot.wait()
    den = den_ref[:, 0:1]
    scale = scale_ref[0:1, 0:1]
    last = pl.ds(width - part, part)

    def dense(k, carry):
        square, along = carry
        at = pl.ds(pl.multiple_of(k * part, part), part)
        value = zpre[:, at] + jnp.dot(
            agg[:, last], comb_b[pl.ds(2 * width - part, part), at], preferred_element_type=F32
        )
        zpre[:, at] = value
        out = gelu(value)
        zval[:, at] = out
        square += jnp.sum(out * out, axis=1, keepdims=True)
        along += jnp.sum(out * cot[:, at], axis=1, keepdims=True)
        return square, along

    zero = jnp.zeros((rows, 1), F32)
    square, along = lax.fori_loop(0, CHUNKS, dense, (zero, zero))
    inverse = lax.rsqrt(square + 1e-06)
    along = along * inverse
    push = jnp.where(mask > 0.5, 2.0 * scale, 0.0)
    stats_ref[...] = jnp.concatenate(
        [
            jnp.full((8, 128), jnp.sum(jnp.where(mask > 0.5, square, 0.0))),
            jnp.broadcast_to(scale, (8, 128)),
        ],
        axis=0,
    )

    @pl.loop(0, CHUNKS)
    def _(k):
        at = pl.ds(pl.multiple_of(k * part, part), part)
        out = zval[:, at]
        emb = out * inverse
        grad = inverse * (cot[:, at] - emb * along) + push * out
        dz[:, at] = (grad * gelu_slope(zpre[:, at])).astype(BF16)
        zval[:, at] = emb

    store(zval, embed_h)
    store(dz, dz_h)
    store(agg, agg_h)

    @pl.loop(0, CHUNKS)
    def _(k):
        at = pl.ds(pl.multiple_of(k * part, part), part)
        back = dot_nt(dz[...], comb_b[pl.ds(pl.multiple_of(width + k * part, part), part), :])
        dnum[:, at] = (back / den).astype(BF16)

    store(dnum, dnum_h)

    for far, _, device in place.others("z"):
        key_copy(far, device).wait_send()

    @pl.loop(0, LINE * CHUNKS)
    def _(i):
        src = i // CHUNKS
        k = lax.rem(i, CHUNKS)

        @pl.when(jnp.logical_and(src <= z, z < LINE - 1))
        def _():
            up_copy(src, k).wait_send()

        @pl.when(jnp.logical_and(src >= z, z > 0))
        def _():
            down_copy(src, k).wait_send()

        for far, index, device in place.others("l"):
            slot_copy(src, k, far, index, device).wait_send()

    for src in range(LINE):
        for far, index, device in place.others("l"):
            tot_copy(src, far, index, device).wait_send()
    for copy in stores:
        copy.wait()


def forward_pass(n_nodes, n_grp, feats, mask, edges_of, targets, board, neigh, nbias, comb, cbias, cot):
    rows, width = feats.shape
    edges = edges_of[0].shape[1]
    layer = n_nodes // LINE
    layer_slots = targets.shape[1] // LINE
    part = width // CHUNKS
    dma = pltpu.SemaphoreType.DMA
    n_stage = 5
    big = pl.BlockSpec(memory_space=pl.ANY)
    small = pl.BlockSpec(memory_space=pltpu.VMEM)

    def hbm(shape, dtype):
        return jax.ShapeDtypeStruct(shape, dtype)

    return pl.pallas_call(
        functools.partial(forward_kernel, n_nodes, n_grp),
        out_shape=[
            hbm((rows, width), F32),
            hbm((rows, width), BF16),
            hbm((rows, width), F32),
            hbm((rows, width), BF16),
            hbm((width, width), BF16),
            hbm((width, width), BF16),
            hbm((width, width), BF16),
            hbm((LINE, rows, layer_slots), BF16),
            hbm((rows, width), BF16),
            hbm((rows, width), BF16),
            hbm((rows, width), BF16),
            hbm((16, 128), F32),
        ],
        in_specs=[big] + [small] * 5 + [big, big, small, big, small, big],
        out_specs=[big] * 11 + [small],
        scratch_shapes=[
            pltpu.VMEM((n_stage, rows, width), F32),
            pltpu.VMEM((rows, width), BF16),
            pltpu.VMEM((rows, width), BF16),
            pltpu.VMEM((rows, width), F32),
            pltpu.VMEM((width, width), BF16),
            pltpu.VMEM((width, width), BF16),
            pltpu.VMEM((2 * width, width), BF16),
            pltpu.VMEM((LINE, 1, edges + edges // 2), jnp.int32),
            pltpu.VMEM((LINE, CHUNKS, rows, part), BF16),
            pltpu.VMEM((layer_slots, rows), F32),
            pltpu.VMEM((LINE, layer_slots, rows), BF16),
            pltpu.VMEM((LINE, rows, layer_slots), BF16),
            pltpu.VMEM((LINE, CHUNKS, layer_slots, part), BF16),
            pltpu.VMEM((LINE, CHUNKS, layer_slots, part), BF16),
            pltpu.VMEM((LINE, layer_slots, 128), BF16),
            pltpu.VMEM((LINE, layer_slots, 128), BF16),
            pltpu.VMEM((LINE, rows, layer_slots), BF16),
            pltpu.VMEM((CHUNKS, rows, part), F32),
            pltpu.VMEM((rows, width), F32),
            pltpu.VMEM((rows, width), F32),
            pltpu.VMEM((rows, width), F32),
            pltpu.VMEM((rows, width), BF16),
            pltpu.VMEM((rows, width), BF16),
            pltpu.VMEM((rows, width), BF16),
            pltpu.VMEM((rows, 128), F32),
            pltpu.VMEM((8, 128), F32),
            pltpu.VMEM((layer, 8, 128), F32),
            pltpu.VMEM((LINE, 8, 128), F32),
            pltpu.VMEM((n_grp, 8, 128), F32),
            dma((n_stage + 1,)),
            dma((11,)),
            dma((LINE - 1,)),
            dma((LINE - 1,)),
            dma((LINE * CHUNKS,)),
            dma((LINE * CHUNKS,)),
            dma((LINE * CHUNKS,)),
            dma((LINE * CHUNKS * (layer - 1),)),
            dma((LINE * CHUNKS * (layer - 1),)),
            dma((LINE * (layer - 1),)),
            dma((LINE * (layer - 1),)),
            dma((share_sems(n_nodes, n_grp),)),
            dma((share_sems(n_nodes, n_grp),)),
        ],
        compiler_params=pltpu.CompilerParams(
            vmem_limit_bytes=60 * MIB, collective_id=2, has_side_effects=True
        ),
        name="forward_pass",
    )(feats, mask, *edges_of, targets, board, neigh, nbias, comb, cbias, cot)


def add_into(target, first, count, columns, parts, step=16):
    @pl.loop(0, count // step)
    def _(i):
        at = pl.ds(pl.multiple_of(first + i * step, step), step)
        total = target[at, columns].astype(F32)
        for part in parts:
            total += part[pl.ds(pl.multiple_of(i * step, step), step), :].astype(F32)
        target[at, columns] = total.astype(target.dtype)


def reduce_job(place, order, grad, region, arrive, land, last, send, recv, free, base):
    first, rows, left, columns = region
    half = columns // 2
    core = place.at["c"]
    mine = pl.ds(pl.multiple_of(left + core * half, half), half)
    theirs = pl.ds(pl.multiple_of(left + (1 - core) * half, half), half)
    mate = place.member("c", 1 - core)
    block = pl.ds(first, rows)
    sems = iter(range(base, base + send.shape[0]))

    def lay(src, dst, device):
        sem = next(sems)
        return remote(src, dst, send.at[sem], recv.at[sem], device)

    across = lay(grad.at[block, theirs], arrive, mate)
    down = []
    begin, length, used = first, rows, 0
    for axis in order:
        length //= place.size[axis]
        copies, parts, devices = [], [], []
        for far, index, device in place.others(axis):
            start = pl.multiple_of(begin + index * length, 16)
            slot = land.at[pl.ds(used, length)]
            used += length
            copies.append(lay(grad.at[pl.ds(start, length), mine], slot, device))
            parts.append(slot)
            devices.append(device)
        parent = begin
        begin = pl.multiple_of(begin + place.at[axis] * length, 16)
        down.append((axis, parent, begin, length, copies, parts, devices))
    axis, parent, begin, length, _, _, devices = down[-1]
    here = pl.ds(pl.multiple_of(place.at[axis] * length, 16), length)
    whole = pl.ds(pl.multiple_of(parent, 16), length * place.size[axis])
    end = [lay(last.at[here], last.at[here], device) for device in devices]
    up = []
    for stage in range(len(down) - 1, 0, -1):
        axis, _, start, piece, _, _, devices = down[stage - 1]
        own = grad.at[pl.ds(start, piece), mine]
        up.append((stage, len(devices), [lay(own, own, device) for device in devices]))
    own = grad.at[block, mine]
    back = lay(own, own, mate)
    yield

    def release(at, devices):
        for device in devices:
            pl.semaphore_signal(free.at[base + at], inc=1, device_id=device, device_id_type=MESH)

    across.start()
    yield
    across.wait()
    release(0, [mate])
    add_into(grad, first, rows, mine, [arrive])
    for stage, (_, _, begin, length, copies, parts, devices) in enumerate(down):
        for copy in copies:
            copy.start()
        yield
        for copy in copies:
            copy.wait()
        if stage < len(down) - 1:
            release(stage + 1, devices)
        add_into(grad, begin, length, mine, parts)
    last[here] = grad[pl.ds(begin, length), mine]
    for copy in end:
        copy.start()
    yield
    for copy in end:
        copy.wait()
    grad[whole, mine] = last[pl.ds(0, whole.size)]
    for stage, count, copies in up:
        pl.semaphore_wait(free.at[base + stage], count)
        for copy in copies:
            copy.start()
        yield
        for copy in copies:
            copy.wait()
    pl.semaphore_wait(free.at[base], 1)
    back.start()
    yield
    back.wait()


def job_sems(n_nodes, n_grp):
    return 2 * (1 + (n_nodes // LINE // 2 - 1) + (LINE - 1) + (n_grp - 1))


AHEAD = 2
BEHIND = CHUNKS - AHEAD
JOBS = {
    kind[0] + str(i): kind + str(i) for kind, count in (("comb", 4), ("neigh", 4), ("board", 2)) for i in range(count)
}
BACKWARD = (
    "l0", "A1", "G0", "B2", "c3", "A0", "L1", "W0", "Y10", "f01", "Y11", "B3", "q00", "Y12", "f00",
    "c3", "c2", "32", "S0", "Y13", "c2", "c0", "f11", "L2", "33", "L3", "c3", "22", "Y14", "c1",
    "Z1", "q01", "Y20", "q11", "c2", "c3", "12", "Y21", "c1", "f10", "Y22", "q20", "q10", "c3",
    "c0", "23", "Y23", "q21", "O2", "f21", "Y24", "c2", "c3", "Z2", "n2", "Y30", "13", "n2", "f20",
    "q30", "Y31", "q31", "Y32", "Y33", "c2", "n2", "c3", "O3", "n3", "Y34", "n2", "c2", "Z3", "c0",
    "c1", "n3", "O1", "n2", "n1", "c2", "O0", "n3", "n0", "c0", "E0", "H1", "b1", "n0", "n2", "c1",
    "H0", "n1", "c0", "b0", "b1", "n0", "b0", "n3", "n0", "c0", "c1", "n1", "b1", "n3", "n0", "b0",
    "c1", "c2", "c0", "n1", "c3", "b1", "n3", "b0", "n2", "n0", "c2", "c1", "b1", "n1", "b0", "n0",
    "n2", "b1", "P0", "n3", "n1", "c0", "b0", "b1", "c1", "n0", "n2", "P1", "n1", "b0", "F0", "n0",
    "c0", "n1", "n3", "c1", "n3", "b1", "b0", "P2", "c3", "P3", "b1", "n1", "b0",
)


def gradient_regions(n_nodes, n_grp, width):
    pieces = n_nodes * n_grp // 2
    x_first, y_first = ("x", "y", "z"), ("y", "x", "z")
    regions = {}
    count = max(1, min(4, 2 * width // (16 * pieces)))
    n_rows = 2 * width // count
    for j in range(count):
        regions[f"comb{j}"] = (j * n_rows, n_rows, 0, width, x_first)
    if width % (16 * pieces) == 0:
        part = width // CHUNKS
        for k in range(CHUNKS):
            regions[f"neigh{k}"] = (2 * width, width, k * part, part, x_first if k % 2 else y_first)
        count = max(1, min(2, width // (16 * pieces)))
        n_rows = width // count
        for j in range(count):
            order = x_first if j % 2 == 0 else y_first
            regions[f"board{j}"] = (3 * width + j * n_rows, n_rows, 0, width, order)
    else:
        regions["board0"] = (2 * width, 2 * width, 0, width, x_first)
    return regions


def backward_kernel(
    n_nodes,
    n_grp,
    mask_ref,
    targets_ref,
    stats_ref,
    place_h,
    child_h,
    weight_h,
    hid_h,
    pre_h,
    featb_h,
    board_b_h,
    neigh_b_h,
    comb1_b_h,
    st_h,
    dnum_h,
    dz_h,
    agg_h,
    gfeat_h,
    summed_h,
    small_ref,
    hid,
    pre,
    featb,
    board_b,
    neigh_b,
    comb1_b,
    spread_t,
    dnum,
    dz,
    agg,
    picker_t,
    picker_l,
    lines,
    edge_place,
    edge_child,
    edge_weight,
    acc,
    own_t,
    parents,
    out_slots,
    in_slots,
    chain,
    tmp,
    dpre,
    dh,
    grad,
    arrive,
    land,
    gather,
    share_l,
    share_z,
    share_x,
    small,
    load_sem,
    store_sem,
    slot_send,
    slot_recv,
    up_send,
    down_send,
    chain_recv,
    line_send,
    line_recv,
    parent_up,
    parent_down,
    parent_recv,
    job_send,
    job_recv,
    job_free,
    share_send,
    share_recv,
):
    place = Place(n_nodes, n_grp)
    z, low = place.at["z"], place.at["l"]
    layer = place.size["l"]
    rows, width = hid.shape
    layer_slots = spread_t.shape[2]
    cap = layer_slots // layer
    part = width // CHUNKS

    loads = {}
    for i, (name, src, dst) in enumerate(
        (
            ("dnum", dnum_h, dnum),
            ("hid", hid_h, hid),
            ("agg", agg_h, agg),
            ("dz", dz_h, dz),
            ("spread_t", st_h, spread_t),
            ("comb1_b", comb1_b_h, comb1_b),
            ("pre", pre_h, pre),
            ("neigh_b", neigh_b_h, neigh_b),
            ("featb", featb_h, featb),
            ("board_b", board_b_h, board_b),
            ("place", place_h, edge_place),
            ("child", child_h, edge_child),
            ("weight", weight_h, edge_weight),
        )
    ):
        loads[name] = pltpu.make_async_copy(src, dst, load_sem.at[i])
        loads[name].start()
    def make_pickers():
        @pl.loop(0, LINE)
        def _(src):
            at = pl.ds(pl.multiple_of(src * layer_slots, layer_slots), layer_slots)
            ids = lax.broadcasted_iota(jnp.int32, (rows, layer_slots), 0)
            picker_t[src] = jnp.where(ids == targets_ref[:, at], 1.0, 0.0).astype(BF16).T

    barrier(place, ("l", "z", "x"), make_pickers)
    stores = []

    def store(src, dst):
        copy = pltpu.make_async_copy(src, dst, store_sem.at[len(stores)])
        copy.start()
        stores.append(copy)

    mask = column_of(mask_ref) > 0.5

    def source(which):
        flip = z // 2
        inner = z * (1 - 2 * flip) + (LINE - 1) * flip
        index = ORDER[0][which] * (1 - inner) + ORDER[1][which] * inner
        return index * (1 - 2 * flip) + (LINE - 1) * flip

    def cols(k):
        return pl.ds(pl.multiple_of(k * part, part), part)

    def slot_copy(dst, k, far, index, device):
        at = (dst * CHUNKS + k) * (layer - 1) + far
        return remote(
            out_slots.at[dst, k, pl.ds(pl.multiple_of(index * cap, cap), cap)],
            in_slots.at[dst, k, pl.ds(pl.multiple_of(low * cap, cap), cap)],
            slot_send.at[at],
            slot_recv.at[at],
            device,
        )

    def back(dst, k):
        out_slots[dst, k] = jnp.dot(
            picker_t[dst], dnum[:, cols(k)], preferred_element_type=F32
        ).astype(BF16)
        for far, index, device in place.others("l"):
            slot_copy(dst, k, far, index, device).start()
        own = pl.ds(pl.multiple_of(low * cap, cap), cap)
        in_slots[dst, k, own] = out_slots[dst, k, own]

    def child_sums(dst, k):
        for far, index, device in place.others("l"):
            slot_copy(dst, k, far, index, device).wait_recv()
        tmp[...] = jnp.dot(spread_t[dst], in_slots[dst, k], preferred_element_type=F32)

    def up_copy(dst, k):
        k = k - AHEAD
        at = dst * BEHIND + k
        return remote(
            chain.at[dst, k],
            chain.at[dst, k],
            up_send.at[at],
            chain_recv.at[at],
            place.member("z", z + 1),
        )

    def down_copy(dst, k, last):
        slot = LINE if last else dst
        k = k - AHEAD
        return remote(
            chain.at[dst, k],
            chain.at[slot, k],
            down_send.at[dst * BEHIND + k],
            chain_recv.at[slot * BEHIND + k],
            place.member("z", z - 1),
        )

    def arrived(slot, k):
        k = k - AHEAD
        remote(
            chain.at[slot, k],
            chain.at[slot, k],
            up_send.at[0],
            chain_recv.at[slot * BEHIND + k],
            place.member("z", lax.rem(z + 1, LINE)),
        ).wait_recv()

    def hand_on(dst, k):
        child_sums(dst, k)

        @pl.when(dst > z)
        def _():
            @pl.when(z > 0)
            def _():
                up_copy(dst, k).wait_recv()
                chain[dst, k - AHEAD] = (chain[dst, k - AHEAD].astype(F32) + tmp[...]).astype(BF16)

            @pl.when(z == 0)
            def _():
                chain[dst, k - AHEAD] = tmp[...].astype(BF16)

            up_copy(dst, k).start()

        @pl.when(dst < z)
        def _():
            @pl.when(z < LINE - 1)
            def _():
                down_copy(dst, k, False).wait_recv()
                chain[dst, k - AHEAD] = (chain[dst, k - AHEAD].astype(F32) + tmp[...]).astype(BF16)

            @pl.when(z == LINE - 1)
            def _():
                chain[dst, k - AHEAD] = tmp[...].astype(BF16)

            @pl.when(dst == z - 1)
            def _():
                down_copy(dst, k, True).start()

            @pl.when(dst < z - 1)
            def _():
                down_copy(dst, k, False).start()

    regions = gradient_regions(n_nodes, n_grp, width)
    per_job = job_sems(n_nodes, n_grp)

    def job(name):
        first, n_rows, left, columns, order = regions[name]
        rows_at, cols_at = pl.ds(first, n_rows), pl.ds(left, columns)
        land_at = pl.ds(left // 2, columns // 2)
        yield from reduce_job(
            place,
            order,
            grad,
            (first, n_rows, left, columns),
            arrive.at[rows_at, land_at],
            land.at[rows_at, land_at],
            gather.at[pl.ds(first // 4, n_rows // 4), land_at],
            job_send,
            job_recv,
            job_free,
            list(regions).index(name) * per_job,
        )
        store(grad.at[rows_at, cols_at], summed_h.at[rows_at, cols_at])

    jobs = {name: job(name) for name in regions}
    for lay_out in jobs.values():
        next(lay_out)

    def step_job(name, last=False):
        if name in jobs and (last or name != "board0" or "board1" in regions):
            try:
                next(jobs[name])
            except StopIteration:
                del jobs[name]

    loads["dnum"].wait()

    def back_all(k):
        for which in (3, 2, 1, 0):
            back(source(which), k)

    def comb_grad(left, first):
        @pl.loop(0, CHUNKS)
        def _(k):
            grad[pl.ds(first, width), cols(k)] = dot_tn(left[...], dz[:, cols(k)]).astype(BF16)

    def line_targets():
        lines[z] = targets_ref[:, pl.ds(pl.multiple_of(z * layer_slots, layer_slots), layer_slots)]
        for far, index, device in place.others("z"):
            at = pl.ds(pl.multiple_of(index * layer_slots, layer_slots), layer_slots)
            remote(
                targets_ref.at[:, at], lines.at[z], line_send.at[far], line_recv.at[far], device
            ).start()

    def line_picker(which):
        src = source(which)
        far = lax.rem(z - src - 1 + LINE, LINE)
        remote(
            lines.at[src], lines.at[src], line_send.at[0], line_recv.at[far], place.member("z", src)
        ).wait_recv()
        ids = lax.broadcasted_iota(jnp.int32, (rows, layer_slots), 0)
        picker_l[src] = jnp.where(ids == lines[src], 1.0, 0.0).astype(BF16).T

    def parent_copy(src, k, sems, to):
        piece = parents.at[src, k]
        at = src * AHEAD + k
        return remote(piece, piece, sems.at[at], parent_recv.at[at], place.member("z", to))

    def parent_send(k):
        parents[z, k] = dnum[:, cols(k)]

        @pl.when(z < LINE - 1)
        def _():
            parent_copy(z, k, parent_up, z + 1).start()

        @pl.when(z > 0)
        def _():
            parent_copy(z, k, parent_down, z - 1).start()

    def parent_forward(j, k):
        below = z - 1 - j
        above = z + 1 + j

        @pl.when(below >= 0)
        def _():
            parent_copy(below, k, parent_up, z + 1).wait_recv()

            @pl.when(z < LINE - 1)
            def _():
                parent_copy(below, k, parent_up, z + 1).start()

        @pl.when(above < LINE)
        def _():
            parent_copy(above, k, parent_down, z - 1).wait_recv()

            @pl.when(z > 0)
            def _():
                parent_copy(above, k, parent_down, z - 1).start()

    def parent_slots(which, k):
        src = source(which)
        choose = picker_t[z] if which == 0 else picker_l[src]
        out_slots[src, k] = jnp.dot(choose, parents[src, k], preferred_element_type=F32).astype(
            BF16
        )
        for far, index, device in place.others("l"):
            slot_copy(src, k, far, index, device).start()
        own = pl.ds(pl.multiple_of(low * cap, cap), cap)
        in_slots[src, k, own] = out_slots[src, k, own]

    edges = edge_place.shape[1]
    turn = math.gcd(edges, 5120)
    steps = edges // turn

    def build_own(which, ticks):
        src = source(which)
        if which == 1:
            for name in ("place", "child", "weight"):
                loads[name].wait()
        acc[...] = jnp.zeros_like(acc)

        @pl.loop(0, steps)
        def _(t):
            at = pl.ds(pl.multiple_of(t * turn, turn), turn)
            slot = (edge_place[:, at] - src * layer_slots).astype(jnp.int16)
            child = edge_child[:, at].astype(jnp.int16)
            weight = edge_weight[:, at].astype(F32).astype(F8)
            right = jnp.where(
                lax.broadcasted_iota(jnp.int16, (layer_slots, turn), 0) == slot,
                jnp.ones((), F8),
                jnp.zeros((), F8),
            )
            block = 256
            for first in range(0, rows, block):
                ids = lax.broadcasted_iota(jnp.int16, (block, turn), 0) + jnp.asarray(
                    first, jnp.int16
                )
                left = jnp.where(ids == child, weight, jnp.zeros((), F8))
                acc[pl.ds(first, block), :] += dot_nt(left, right)
            run_ticks(t, ticks)

        own_t[src] = acc[...].astype(BF16)

    def own(k):
        if k < AHEAD:
            for which in range(LINE):
                src = source(which)
                for far, index, device in place.others("l"):
                    slot_copy(src, k, far, index, device).wait_recv()
                weights = spread_t[z] if which == 0 else own_t[src]
                value = jnp.dot(weights, in_slots[src, k], preferred_element_type=F32)
                if which == 0:
                    tmp[...] = value
                else:
                    tmp[...] += value
        else:
            child_sums(z, k)

            @pl.when(z > 0)
            def _():
                arrived(z, k)
                tmp[...] += chain[z, k - AHEAD].astype(F32)

            @pl.when(z < LINE - 1)
            def _():
                arrived(LINE, k)
                tmp[...] += chain[LINE, k - AHEAD].astype(F32)

        down = (tmp[...] * gelu_slope(pre[:, cols(k)])).astype(BF16)
        dpre[:, cols(k)] = down
        small[0:1, cols(k)] = jnp.sum(down.astype(F32), axis=0, keepdims=True)
        dh[...] += dot_nt(down, neigh_b[:, cols(k)])

    def neigh_grad(k):
        grad[pl.ds(2 * width, width), cols(k)] = dot_tn(hid[...], dpre[:, cols(k)]).astype(BF16)

    def comb_grads():
        for name in ("hid", "agg", "dz", "comb1_b"):
            loads[name].wait()
        comb_grad(hid, 0)
        comb_grad(agg, width)

    def self_part():
        small[...] = jnp.zeros_like(small)
        small[1:2, :] = jnp.sum(dz[...].astype(F32), axis=0, keepdims=True)
        small[2:3, :] = jnp.broadcast_to(stats_ref[0:1, 0:1], (1, width))

        @pl.loop(0, CHUNKS)
        def _(k):
            dh[:, cols(k)] = dot_nt(dz[...], comb1_b[cols(k), :])

        for name in ("pre", "neigh_b", "featb", "board_b"):
            loads[name].wait()

    def own_and_grad(k):
        own(k)
        neigh_grad(k)

    def end_of_line():
        last = dh[...].astype(BF16)
        dpre[...] = jnp.where(mask, last, jnp.zeros_like(last))
        pre[...] = last.astype(F32)

    def board_grad(i):
        half = width // 2
        grad[pl.ds(3 * width + i * half, half), :] = dot_tn(
            featb[:, i * half : (i + 1) * half], dpre[...]
        ).astype(BF16)

    def feature_grad():
        @pl.loop(0, CHUNKS)
        def _(k):
            pre[:, cols(k)] = jnp.where(
                mask, dot_nt(dpre[...], board_b[cols(k), :]), pre[:, cols(k)]
            )

        store(pre, gfeat_h)

    share = Share(place, (share_l, share_z, share_x), share_send, share_recv)

    def step_share(stage):
        if stage == 0:
            share.start(0, small[...])
        elif stage < 3:
            share.start(stage, share.finish(stage - 1))
        else:
            row = lax.broadcasted_iota(jnp.int32, small_ref.shape, 0)
            small_ref[...] = share.finish(2) * jnp.where(row == 2, stats_ref[8:9, 0:1], 1.0)

    acts = {
        "l": lambda _: line_targets(),
        "L": line_picker,
        "A": parent_send,
        "f": parent_forward,
        "q": parent_slots,
        "B": back_all,
        "W": lambda _: loads["spread_t"].wait(),
        "G": lambda _: comb_grads(),
        "S": lambda _: self_part(),
        "O": own_and_grad,
        "E": lambda _: end_of_line(),
        "H": board_grad,
        "F": lambda _: feature_grad(),
        "P": step_share,
        "3": lambda k: hand_on(source(3), k),
        "2": lambda k: hand_on(source(2), k),
        "1": lambda k: hand_on(source(1), k),
    }
    def act(name):
        if name in JOBS:
            step_job(JOBS[name])
        else:
            acts[name[0]](*(int(c) for c in name[1:]))

    run_order(BACKWARD, steps, build_own, act)
    while jobs:
        for name in list(jobs):
            step_job(name, last=True)

    for far, index, device in place.others("z"):
        remote(lines.at[z], lines.at[z], line_send.at[far], line_recv.at[far], device).wait_send()

    @pl.loop(0, LINE * CHUNKS)
    def _(i):
        dst = i // CHUNKS
        k = lax.rem(i, CHUNKS)

        @pl.when(k < AHEAD)
        def _():
            @pl.when(jnp.logical_and(dst <= z, z < LINE - 1))
            def _():
                parent_copy(dst, k, parent_up, z + 1).wait_send()

            @pl.when(jnp.logical_and(dst >= z, z > 0))
            def _():
                parent_copy(dst, k, parent_down, z - 1).wait_send()

        @pl.when(k >= AHEAD)
        def _():
            @pl.when(dst > z)
            def _():
                up_copy(dst, k).wait_send()

            @pl.when(dst < z)
            def _():
                down_copy(dst, k, False).wait_send()

        for far, index, device in place.others("l"):
            slot_copy(dst, k, far, index, device).wait_send()

    for copy in stores:
        copy.wait()


def backward_pass(n_nodes, n_grp, mask, targets, stats, edges_of, hid, pre, featb, board_b, neigh_b, comb1_b, st, dnum, dz, agg):
    rows, width = hid.shape
    edges = edges_of[0].shape[1]
    layer = n_nodes // LINE
    layer_slots = st.shape[2]
    part = width // CHUNKS
    n_rows = 4 * width
    count = len(gradient_regions(n_nodes, n_grp, width))
    dma = pltpu.SemaphoreType.DMA
    big = pl.BlockSpec(memory_space=pl.ANY)
    vmem = pl.BlockSpec(memory_space=pltpu.VMEM)
    sems = count * job_sems(n_nodes, n_grp)
    pieces = LINE * CHUNKS
    return pl.pallas_call(
        functools.partial(backward_kernel, n_nodes, n_grp),
        out_shape=[
            jax.ShapeDtypeStruct((rows, width), F32),
            jax.ShapeDtypeStruct((n_rows, width), BF16),
            jax.ShapeDtypeStruct((8, width), F32),
        ],
        in_specs=[vmem, vmem, vmem] + [big] * 13,
        out_specs=[big, big, vmem],
        scratch_shapes=[
            pltpu.VMEM((rows, width), BF16),
            pltpu.VMEM((rows, width), F32),
            pltpu.VMEM((rows, width), BF16),
            pltpu.VMEM((width, width), BF16),
            pltpu.VMEM((width, width), BF16),
            pltpu.VMEM((width, width), BF16),
            pltpu.VMEM((LINE, rows, layer_slots), BF16),
            pltpu.VMEM((rows, width), BF16),
            pltpu.VMEM((rows, width), BF16),
            pltpu.VMEM((rows, width), BF16),
            pltpu.VMEM((LINE, layer_slots, rows), BF16),
            pltpu.VMEM((LINE, layer_slots, rows), BF16),
            pltpu.VMEM((LINE, 1, layer_slots), jnp.int32),
            pltpu.VMEM((1, edges), jnp.int32),
            pltpu.VMEM((1, edges), jnp.int32),
            pltpu.VMEM((1, edges), jnp.int32),
            pltpu.VMEM((rows, layer_slots), F32),
            pltpu.VMEM((LINE, rows, layer_slots), BF16),
            pltpu.VMEM((LINE, AHEAD, rows, part), BF16),
            pltpu.VMEM((LINE, CHUNKS, layer_slots, part), BF16),
            pltpu.VMEM((LINE, CHUNKS, layer_slots, part), BF16),
            pltpu.VMEM((LINE + 1, BEHIND, rows, part), BF16),
            pltpu.VMEM((rows, part), F32),
            pltpu.VMEM((rows, width), BF16),
            pltpu.VMEM((rows, width), F32),
            pltpu.VMEM((n_rows, width), BF16),
            pltpu.VMEM((n_rows, width // 2), BF16),
            pltpu.VMEM((n_rows, width // 2), BF16),
            pltpu.VMEM((n_rows // 4, width // 2), BF16),
            pltpu.VMEM((layer, 8, width), F32),
            pltpu.VMEM((LINE, 8, width), F32),
            pltpu.VMEM((n_grp, 8, width), F32),
            pltpu.VMEM((8, width), F32),
            dma((13,)),
            dma((count + 1,)),
            dma((pieces * (layer - 1),)),
            dma((pieces * (layer - 1),)),
            dma((LINE * BEHIND,)),
            dma((LINE * BEHIND,)),
            dma(((LINE + 1) * BEHIND,)),
            dma((LINE - 1,)),
            dma((LINE - 1,)),
            dma((LINE * AHEAD,)),
            dma((LINE * AHEAD,)),
            dma((LINE * AHEAD,)),
            dma((sems,)),
            dma((sems,)),
            pltpu.SemaphoreType.REGULAR((sems,)),
            dma((share_sems(n_nodes, n_grp),)),
            dma((share_sems(n_nodes, n_grp),)),
        ],
        compiler_params=pltpu.CompilerParams(
            vmem_limit_bytes=62 * MIB, collective_id=3, has_side_effects=True
        ),
        name="backward_pass",
    )(mask, targets, stats, *edges_of, hid, pre, featb, board_b, neigh_b, comb1_b, st, dnum, dz, agg)


def unpack_kernel(
    rows, joined, small_ref, comb, neigh, board, nbias_ref, cbias_ref, penalty_ref, low, wide, load_sem, store_sem
):
    width = joined.shape[1]
    blocks = joined.shape[0] // rows

    def load(i):
        at = pl.ds(i * rows, rows)
        return pltpu.make_async_copy(joined.at[at], low.at[at], load_sem.at[i])

    def store(i):
        first = i * rows
        if first < 2 * width:
            target = comb.at[pl.ds(first, rows)]
        elif first < 3 * width:
            target = neigh.at[pl.ds(first - 2 * width, rows)]
        else:
            target = board.at[pl.ds(first - 3 * width, rows)]
        return pltpu.make_async_copy(wide.at[pl.ds(first, rows)], target, store_sem.at[i])

    for i in range(blocks):
        load(i).start()
    nbias_ref[...] = small_ref[0:1, :]
    cbias_ref[...] = small_ref[1:2, :]
    penalty_ref[...] = small_ref[2:3, 0:1]
    for i in range(blocks):
        load(i).wait()

        @pl.loop(0, rows // 32)
        def _(r, i=i):
            at = pl.ds(pl.multiple_of(i * rows + r * 32, 32), 32)
            wide[at, :] = low[at, :].astype(F32)

        store(i).start()
    for i in range(blocks):
        store(i).wait()


def unpack(joined, small):
    n_rows, width = joined.shape
    rows = math.gcd(width, 256)
    big = pl.BlockSpec(memory_space=pl.ANY)
    vmem = pl.BlockSpec(memory_space=pltpu.VMEM)
    dma = pltpu.SemaphoreType.DMA
    return pl.pallas_call(
        functools.partial(unpack_kernel, rows),
        out_shape=[
            jax.ShapeDtypeStruct((2 * width, width), F32),
            jax.ShapeDtypeStruct((width, width), F32),
            jax.ShapeDtypeStruct((width, width), F32),
            jax.ShapeDtypeStruct((1, width), F32),
            jax.ShapeDtypeStruct((1, width), F32),
            jax.ShapeDtypeStruct((1, 1), F32),
        ],
        in_specs=[big, vmem],
        out_specs=[big] * 3 + [vmem] * 3,
        scratch_shapes=[
            pltpu.VMEM((n_rows, width), BF16),
            pltpu.VMEM((n_rows, width), F32),
            dma((n_rows // rows,)),
            dma((n_rows // rows,)),
        ],
        compiler_params=pltpu.CompilerParams(vmem_limit_bytes=60 * MIB),
        name="unpack",
    )(joined, small)


def on_device(
    n_nodes,
    n_grp,
    features,
    type_mask,
    edge_child,
    edge_slot,
    edge_weight,
    recv_rows,
    board_proj,
    neigh_proj,
    neigh_bias,
    combine_proj,
    combine_bias,
    out_cot,
):
    feats = features[0]
    rows, width = feats.shape
    peers = recv_rows.shape[2]
    cap = recv_rows.shape[3]
    slots = peers * cap
    targets = recv_rows[0, 0].reshape(1, slots)
    embed, hidden, pre, featb, pbl, qwl, cwl1, spread_t, dnum, dzb, aggb, stats = forward_pass(
        n_nodes,
        n_grp,
        feats,
        type_mask,
        (edge_slot, edge_child, edge_weight),
        targets,
        board_proj,
        neigh_proj,
        neigh_bias.reshape(1, width),
        combine_proj,
        combine_bias.reshape(1, width),
        out_cot[0],
    )
    grad_feats, summed, small = backward_pass(
        n_nodes,
        n_grp,
        type_mask,
        targets,
        stats,
        (edge_slot, edge_child, edge_weight),
        hidden,
        pre,
        featb,
        pbl,
        qwl,
        cwl1,
        spread_t,
        dnum,
        dzb,
        aggb,
    )
    grad_comb, grad_neigh, grad_board, grad_nbias, grad_cbias, penalty = unpack(summed, small)
    return (
        embed[None],
        penalty[0, 0],
        grad_feats[None],
        grad_board,
        grad_neigh,
        grad_nbias[0],
        grad_comb,
        grad_cbias[0],
    )


def solution(mesh):
    in_specs = (
        P("grp", "nodes", None),
        P("grp", "nodes"),
        P("grp", "nodes"),
        P("grp", "nodes"),
        P("grp", "nodes"),
        P("grp", "nodes", None, None),
        P(),
        P(),
        P(),
        P(),
        P(),
        P("grp", "nodes", None),
    )
    out_specs = (P("grp", "nodes", None), P(), P("grp", "nodes", None), P(), P(), P(), P(), P())
    return jax.shard_map(
        functools.partial(on_device, mesh.shape["nodes"], mesh.shape["grp"]),
        mesh=mesh,
        in_specs=in_specs,
        out_specs=out_specs,
        check_vma=False,
    )
```

```python
import functools
import math

import jax
import jax.numpy as jnp
from jax import lax
from jax.experimental import pallas as pl
from jax.experimental.pallas import tpu as pltpu
from jax.sharding import PartitionSpec as P

HIGH = lax.Precision.HIGHEST
MESH = pl.DeviceIdType.MESH
BF16 = jnp.bfloat16
F32 = jnp.float32
F8 = jnp.float8_e4m3fn
MIB = 2**20


def gelu_tanh(v):
    return jax.nn.gelu(v, approximate=True)


def dot_nt(left, right):
    return lax.dot_general(
        left, right, (((1,), (1,)), ((), ())), preferred_element_type=F32
    )


def dot_tn(left, right):
    return lax.dot_general(
        left, right, (((0,), (0,)), ((), ())), preferred_element_type=F32
    )


LINE = 4
CHUNKS = 4
FORWARD = (
    "m0", "m1", "m2", "m3", "Y00", "Y01", "Y02", "Y03", "Z0", "f00", "p00", "p01", "p02", "p03",
    "Y10", "P1", "Y11", "f01", "Y12", "f02", "Y13", "Z1", "p10", "p11", "p12", "Y20", "P2", "Y21",
    "f03", "Y22", "Y23", "f10", "Z2", "p13", "p20", "Y30", "Y31", "f11", "Y32", "Y33", "f12", "Z3",
    "p21", "p22", "G0", "P3", "f13", "p23", "D0", "D1", "D2", "D3", "X0", "R0", "i00", "i01",
    "i02", "i03", "f20", "p30", "i10", "i11", "i12", "i13", "f21", "p31", "i20", "i21", "i22",
    "i23", "f22", "p32", "i30", "d0", "a0", "f23", "p33", "i31", "a1", "i32", "a2", "i33",
)
ORDER = ((0, 1, 2, 3), (1, 2, 0, 3))


class Place:
    def __init__(self, n_nodes, n_grp):
        layer = n_nodes // LINE
        node = lax.axis_index("nodes")
        grp = lax.axis_index("grp")
        self.node, self.grp = node, grp
        self.size = {"l": layer, "c": 2, "y": layer // 2, "z": LINE, "x": n_grp}
        low = lax.rem(node, layer)
        self.at = {"l": low, "c": lax.rem(low, 2), "y": low // 2, "z": node // layer, "x": grp}

    def member(self, axis, index):
        layer = self.size["l"]
        low, line, grp = self.at["l"], self.at["z"], self.at["x"]
        if axis == "l":
            low = index
        elif axis == "c":
            low = self.at["y"] * 2 + index
        elif axis == "y":
            low = index * 2 + self.at["c"]
        elif axis == "z":
            line = index
        else:
            grp = index
        return {"nodes": line * layer + low, "grp": grp}

    def others(self, axis):
        size = self.size[axis]
        for far in range(1, size):
            index = lax.rem(self.at[axis] + far, size)
            yield far - 1, index, self.member(axis, index)


def remote(src, dst, send, recv, device):
    return pltpu.make_async_remote_copy(
        src_ref=src, dst_ref=dst, send_sem=send, recv_sem=recv, device_id=device, device_id_type=MESH
    )


def barrier(place, axes, meanwhile=None):
    sem = pltpu.get_barrier_semaphore()
    count = 0
    for axis in axes:
        for _, _, device in place.others(axis):
            pl.semaphore_signal(sem, inc=1, device_id=device, device_id_type=MESH)
            count += 1
    if meanwhile is not None:
        meanwhile()
    pl.semaphore_wait(sem, count)


def column_of(row_ref):
    row = row_ref[...]
    return jnp.broadcast_to(row, (128, row.shape[1])).T[:, 0:1]


def gelu(v):
    t = jnp.tanh(0.7978845608028654 * (v + 0.044715 * (v * v * v)))
    return v * (0.5 * (1.0 + t))


def gelu_slope(v):
    square = v * v
    t = jnp.tanh(0.7978845608028654 * (v + 0.044715 * (v * square)))
    bend = 0.7978845608028654 * (1.0 + 0.134145 * square)
    return 0.5 * (1.0 + t) + 0.5 * v * (1.0 - t * t) * bend


class Share:
    def __init__(self, place, bufs, send, recv):
        self.place, self.send, self.recv = place, send, recv
        self.stages, base = [], 0
        for axis, buf in zip(("l", "z", "x"), bufs):
            self.stages.append((axis, buf, base))
            base += place.size[axis] - 1

    def start(self, stage, value):
        axis, buf, base = self.stages[stage]
        me = self.place.at[axis]
        buf[me] = value
        for far, _, device in self.place.others(axis):
            remote(
                buf.at[me], buf.at[me], self.send.at[base + far], self.recv.at[base + far], device
            ).start()

    def finish(self, stage):
        axis, buf, base = self.stages[stage]
        me = self.place.at[axis]
        for far, _, device in self.place.others(axis):
            remote(
                buf.at[me], buf.at[me], self.send.at[base + far], self.recv.at[base + far], device
            ).wait()
        total = buf[0]
        for i in range(1, self.place.size[axis]):
            total += buf[i]
        return total


def run_ticks(t, ticks):
    for at, acts in enumerate(ticks):
        if acts:

            @pl.when(t == at)
            def _(acts=acts):
                for act in acts:
                    act()


def run_order(order, steps, build, act):
    ticks = None
    for name in order:
        if name[0] == "Y":
            if ticks is None:
                ticks = [[] for _ in range(steps)]
            now = min(int(name[2]), steps - 1)
        elif name[0] == "Z":
            build(int(name[1]), ticks)
            ticks = None
        elif ticks is not None:
            ticks[now].append(functools.partial(act, name))
        else:
            act(name)


def share_sems(n_nodes, n_grp):
    return (n_nodes // LINE - 1) + (LINE - 1) + max(1, n_grp - 1)


def forward_kernel(
    n_nodes,
    n_grp,
    feats_h,
    mask_ref,
    place_ref,
    child_ref,
    weight_ref,
    targets_ref,
    board_h,
    neigh_h,
    nbias_ref,
    comb_h,
    cbias_ref,
    cot_h,
    embed_h,
    hid_h,
    pre_h,
    featb_h,
    board_b_h,
    neigh_b_h,
    comb1_b_h,
    st_h,
    dnum_h,
    dz_h,
    agg_h,
    stats_ref,
    stage,
    featb,
    hid,
    pre,
    board_b,
    neigh_b,
    comb_b,
    keys,
    msg,
    acc,
    spread,
    spread_t,
    out_slots,
    in_slots,
    out_tot,
    in_tot,
    picker,
    num,
    zval,
    zpre,
    cot,
    agg,
    dz,
    dnum,
    den_ref,
    scale_ref,
    count_l,
    count_z,
    count_x,
    load_sem,
    store_sem,
    key_send,
    key_recv,
    up_send,
    down_send,
    msg_recv,
    slot_send,
    slot_recv,
    tot_send,
    tot_recv,
    count_send,
    count_recv,
):
    place = Place(n_nodes, n_grp)
    z, low = place.at["z"], place.at["l"]
    layer = place.size["l"]
    rows, width = featb.shape
    edges = place_ref.shape[1]
    half = edges // 2
    layer_slots = spread.shape[1]
    cap = layer_slots // layer
    part = width // CHUNKS
    turn = math.gcd(half, 6400)
    steps = edges // turn

    sources = [feats_h.at[:]]
    for whole in (board_h, neigh_h, comb_h):
        for first in range(0, whole.shape[0], rows):
            sources.append(whole.at[pl.ds(first, rows)])
    n_stage = stage.shape[0]

    def load(i):
        return pltpu.make_async_copy(sources[i], stage.at[i % n_stage], load_sem.at[i % n_stage])

    for i in range(n_stage):
        load(i).start()
    load_cot = pltpu.make_async_copy(cot_h, cot, load_sem.at[n_stage])
    stores = []

    def store(src, dst):
        copy = pltpu.make_async_copy(src, dst, store_sem.at[len(stores)])
        copy.start()
        stores.append(copy)

    barrier(place, ("l", "z", "x"))
    keys[z, :, pl.ds(0, edges)] = place_ref[...] * 65536 + child_ref[...]
    keys[z, :, pl.ds(edges, half)] = (
        weight_ref[:, pl.ds(half, half)] * 65536 + weight_ref[:, pl.ds(0, half)]
    )

    def key_copy(far, device):
        return remote(keys.at[z], keys.at[z], key_send.at[far], key_recv.at[far], device)

    for far, _, device in place.others("z"):
        key_copy(far, device).start()
    share = Share(place, (count_l, count_z, count_x), count_send, count_recv)
    mask = column_of(mask_ref)
    share.start(0, jnp.full((8, 128), jnp.sum(mask)))

    def cast(i, target, first):
        load(i).wait()
        slot = stage.at[i % n_stage]

        @pl.loop(0, rows // 32)
        def _(r):
            at = pl.ds(pl.multiple_of(r * 32, 32), 32)
            to = pl.ds(pl.multiple_of(first + r * 32, 32), 32)
            target[to, :] = slot[at, :].astype(BF16)

    cast(0, featb, 0)
    cast(1, board_b, 0)
    cast(2, board_b, rows)

    @pl.loop(0, CHUNKS)
    def _(k):
        at = pl.ds(pl.multiple_of(k * part, part), part)
        proj = jnp.dot(featb[...], board_b[:, at], preferred_element_type=F32)
        hid[:, at] = jnp.where(mask > 0.5, proj, stage[0, :, at]).astype(BF16)

    cast(3, neigh_b, 0)
    cast(4, neigh_b, rows)
    for i in range(n_stage, len(sources)):
        load(i).start()
    load_cot.start()

    def up_copy(src, k):
        piece = msg.at[src, k]
        index = src * CHUNKS + k
        return remote(
            piece, piece, up_send.at[index], msg_recv.at[index], place.member("z", z + 1)
        )

    def down_copy(src, k):
        piece = msg.at[src, k]
        index = src * CHUNKS + k
        return remote(
            piece, piece, down_send.at[index], msg_recv.at[index], place.member("z", z - 1)
        )

    def message(k):
        at = pl.ds(k * part, part)
        value = jnp.dot(hid[...], neigh_b[:, at], preferred_element_type=F32) + nbias_ref[:, at]
        pre[:, at] = value
        msg[z, k] = gelu(value).astype(BF16)

        @pl.when(z < LINE - 1)
        def _():
            up_copy(z, k).start()

        @pl.when(z > 0)
        def _():
            down_copy(z, k).start()

    def forward(j, k):
        below = z - 1 - j
        above = z + 1 + j

        @pl.when(below >= 0)
        def _():
            up_copy(below, k).wait_recv()

            @pl.when(z < LINE - 1)
            def _():
                up_copy(below, k).start()

        @pl.when(above < LINE)
        def _():
            down_copy(above, k).wait_recv()

            @pl.when(z > 0)
            def _():
                down_copy(above, k).start()

    def tot_copy(src, far, index, device):
        at = (layer - 1) * src + far
        return remote(
            out_tot.at[src, pl.ds(pl.multiple_of(index * cap, cap), cap)],
            in_tot.at[src, pl.ds(pl.multiple_of(low * cap, cap), cap)],
            tot_send.at[at],
            tot_recv.at[at],
            device,
        )

    def finish_spread(src):
        total = acc[...]
        spread[src] = total.astype(BF16)
        spread_t[src] = total.astype(BF16).T
        sums = jnp.sum(total, axis=1, keepdims=True).astype(jnp.int32)
        lane = lax.broadcasted_iota(jnp.int32, (layer_slots, 128), 1)
        digit = jnp.where(
            lane == 0, sums & 255, jnp.where(lane == 1, (sums >> 8) & 255, jnp.where(lane == 2, sums >> 16, 0))
        )
        out_tot[src] = digit.astype(F32).astype(BF16)
        own = pl.ds(pl.multiple_of(low * cap, cap), cap)
        in_tot[src, own] = out_tot[src, own]
        for far, index, device in place.others("l"):
            tot_copy(src, far, index, device).start()

    def source(which):
        flip = z // 2
        inner = z * (1 - 2 * flip) + (LINE - 1) * flip
        index = ORDER[0][which] * (1 - inner) + ORDER[1][which] * inner
        return index * (1 - 2 * flip) + (LINE - 1) * flip

    def build(which, ticks):
        src = source(which)
        acc[...] = jnp.zeros_like(acc)
        if which > 0:
            far = lax.rem(z - src - 1 + LINE, LINE)
            remote(
                keys.at[src], keys.at[src], key_send.at[0], key_recv.at[far], place.member("z", src)
            ).wait_recv()

        @pl.loop(0, steps)
        def _(t):
            second = t // (steps // 2)
            key = keys[src, :, pl.ds(pl.multiple_of(t * turn, turn), turn)]
            start = edges + (t - second * (steps // 2)) * turn
            pair = keys[src, :, pl.ds(pl.multiple_of(start, turn), turn)]
            weight = (lax.shift_right_logical(pair, second * 16) & 65535).astype(F32).astype(F8)
            child = (key & 65535).astype(jnp.int16)
            slot = (lax.shift_right_logical(key, 16) - z * layer_slots).astype(jnp.int16)
            right = jnp.where(
                lax.broadcasted_iota(jnp.int16, (rows, turn), 0) == child, weight, jnp.zeros((), F8)
            )
            block = 256
            for first in range(0, layer_slots, block):
                ids = lax.broadcasted_iota(jnp.int16, (block, turn), 0) + jnp.asarray(
                    first, jnp.int16
                )
                left = jnp.where(ids == slot, jnp.ones((), F8), jnp.zeros((), F8))
                acc[pl.ds(first, block), :] += dot_nt(left, right)
            run_ticks(t, ticks)

        finish_spread(src)

    def slot_copy(src, k, far, index, device):
        at = (src * CHUNKS + k) * (layer - 1) + far
        return remote(
            out_slots.at[src, k, pl.ds(pl.multiple_of(index * cap, cap), cap)],
            in_slots.at[src, k, pl.ds(pl.multiple_of(low * cap, cap), cap)],
            slot_send.at[at],
            slot_recv.at[at],
            device,
        )

    def piece(src, k):
        out_slots[src, k] = jnp.dot(spread[src], msg[src, k], preferred_element_type=F32).astype(BF16)
        for far, index, device in place.others("l"):
            slot_copy(src, k, far, index, device).start()
        own = pl.ds(pl.multiple_of(low * cap, cap), cap)
        in_slots[src, k, own] = out_slots[src, k, own]

    def pick(src, k):
        for far, index, device in place.others("l"):
            slot_copy(src, k, far, index, device).wait_recv()
        num[k] += jnp.dot(picker[src], in_slots[src, k], preferred_element_type=F32)

    def make_picker():
        @pl.loop(0, LINE)
        def _(src):
            at = pl.ds(pl.multiple_of(src * layer_slots, layer_slots), layer_slots)
            ids = lax.broadcasted_iota(jnp.int32, (rows, layer_slots), 0)
            picker[src] = jnp.where(ids == targets_ref[:, at], 1.0, 0.0).astype(BF16)

        num[...] = jnp.zeros_like(num)

    def comb_piece(i):
        for j in range(i, 2 * width // rows, CHUNKS):
            cast(5 + j, comb_b, j * rows)

    def self_part():
        @pl.loop(0, CHUNKS)
        def _(k):
            at = pl.ds(pl.multiple_of(k * part, part), part)
            zpre[:, at] = (
                jnp.dot(hid[...], comb_b[0:width, at], preferred_element_type=F32)
                + cbias_ref[:, at]
            )

    def results():
        store(hid, hid_h)
        store(pre, pre_h)
        store(featb, featb_h)
        store(board_b, board_b_h)
        store(neigh_b, neigh_b_h)
        store(comb_b.at[pl.ds(0, width)], comb1_b_h)
        store(spread_t, st_h)

    def totals():
        digits = jnp.zeros((rows, 128), F32)
        for src in range(LINE):
            for far, index, device in place.others("l"):
                tot_copy(src, far, index, device).wait_recv()
            digits += jnp.dot(picker[src], in_tot[src], preferred_element_type=F32)
        lane = lax.broadcasted_iota(jnp.int32, (rows, 128), 1)
        worth = jnp.where(
            lane == 0, 1.0, jnp.where(lane == 1, 256.0, jnp.where(lane == 2, 65536.0, 0.0))
        )
        den_ref[...] = jnp.broadcast_to(
            1.0 + jnp.sum(digits * worth, axis=1, keepdims=True), (rows, 128)
        )

    def neighbours(k):
        at = pl.ds(k * part, part)
        agg[:, at] = (num[k] / den_ref[:, 0:1]).astype(BF16)
        if k < CHUNKS - 1:

            @pl.loop(0, CHUNKS)
            def _(n):
                to = pl.ds(pl.multiple_of(n * part, part), part)
                zpre[:, to] += jnp.dot(
                    agg[:, at], comb_b[pl.ds(width + k * part, part), to], preferred_element_type=F32
                )

    def step_share(stage):
        if stage in (1, 2):
            share.start(stage, share.finish(stage - 1))
        elif stage == 3:
            boards = share.finish(2)
            scale_ref[...] = 1.0 / (width * (1.0 + boards))

    acts = {
        "P": step_share,
        "m": message,
        "f": forward,
        "p": lambda which, k: piece(source(which), k),
        "i": lambda which, k: pick(source(which), k),
        "G": lambda _: make_picker(),
        "D": comb_piece,
        "X": lambda _: self_part(),
        "R": lambda _: results(),
        "d": lambda _: totals(),
        "a": neighbours,
    }

    def act(step):
        acts[step[0]](*(int(c) for c in step[1:]))

    run_order(FORWARD, steps, build, act)
    neighbours(CHUNKS - 1)
    load_cot.wait()
    den = den_ref[:, 0:1]
    scale = scale_ref[0:1, 0:1]
    last = pl.ds(width - part, part)

    def dense(k, carry):
        square, along = carry
        at = pl.ds(pl.multiple_of(k * part, part), part)
        value = zpre[:, at] + jnp.dot(
            agg[:, last], comb_b[pl.ds(2 * width - part, part), at], preferred_element_type=F32
        )
        zpre[:, at] = value
        out = gelu(value)
        zval[:, at] = out
        square += jnp.sum(out * out, axis=1, keepdims=True)
        along += jnp.sum(out * cot[:, at], axis=1, keepdims=True)
        return square, along

    zero = jnp.zeros((rows, 1), F32)
    square, along = lax.fori_loop(0, CHUNKS, dense, (zero, zero))
    inverse = lax.rsqrt(square + 1e-06)
    along = along * inverse
    push = jnp.where(mask > 0.5, 2.0 * scale, 0.0)
    stats_ref[...] = jnp.concatenate(
        [
            jnp.full((8, 128), jnp.sum(jnp.where(mask > 0.5, square, 0.0))),
            jnp.broadcast_to(scale, (8, 128)),
        ],
        axis=0,
    )

    @pl.loop(0, CHUNKS)
    def _(k):
        at = pl.ds(pl.multiple_of(k * part, part), part)
        out = zval[:, at]
        emb = out * inverse
        grad = inverse * (cot[:, at] - emb * along) + push * out
        dz[:, at] = (grad * gelu_slope(zpre[:, at])).astype(BF16)
        zval[:, at] = emb

    store(zval, embed_h)
    store(dz, dz_h)
    store(agg, agg_h)

    @pl.loop(0, CHUNKS)
    def _(k):
        at = pl.ds(pl.multiple_of(k * part, part), part)
        back = dot_nt(dz[...], comb_b[pl.ds(pl.multiple_of(width + k * part, part), part), :])
        dnum[:, at] = (back / den).astype(BF16)

    store(dnum, dnum_h)

    for far, _, device in place.others("z"):
        key_copy(far, device).wait_send()

    @pl.loop(0, LINE * CHUNKS)
    def _(i):
        src = i // CHUNKS
        k = lax.rem(i, CHUNKS)

        @pl.when(jnp.logical_and(src <= z, z < LINE - 1))
        def _():
            up_copy(src, k).wait_send()

        @pl.when(jnp.logical_and(src >= z, z > 0))
        def _():
            down_copy(src, k).wait_send()

        for far, index, device in place.others("l"):
            slot_copy(src, k, far, index, device).wait_send()

    for src in range(LINE):
        for far, index, device in place.others("l"):
            tot_copy(src, far, index, device).wait_send()
    for copy in stores:
        copy.wait()


def forward_pass(n_nodes, n_grp, feats, mask, edges_of, targets, board, neigh, nbias, comb, cbias, cot):
    rows, width = feats.shape
    edges = edges_of[0].shape[1]
    layer = n_nodes // LINE
    layer_slots = targets.shape[1] // LINE
    part = width // CHUNKS
    dma = pltpu.SemaphoreType.DMA
    n_stage = 5
    big = pl.BlockSpec(memory_space=pl.ANY)
    small = pl.BlockSpec(memory_space=pltpu.VMEM)

    def hbm(shape, dtype):
        return jax.ShapeDtypeStruct(shape, dtype)

    return pl.pallas_call(
        functools.partial(forward_kernel, n_nodes, n_grp),
        out_shape=[
            hbm((rows, width), F32),
            hbm((rows, width), BF16),
            hbm((rows, width), F32),
            hbm((rows, width), BF16),
            hbm((width, width), BF16),
            hbm((width, width), BF16),
            hbm((width, width), BF16),
            hbm((LINE, rows, layer_slots), BF16),
            hbm((rows, width), BF16),
            hbm((rows, width), BF16),
            hbm((rows, width), BF16),
            hbm((16, 128), F32),
        ],
        in_specs=[big] + [small] * 5 + [big, big, small, big, small, big],
        out_specs=[big] * 11 + [small],
        scratch_shapes=[
            pltpu.VMEM((n_stage, rows, width), F32),
            pltpu.VMEM((rows, width), BF16),
            pltpu.VMEM((rows, width), BF16),
            pltpu.VMEM((rows, width), F32),
            pltpu.VMEM((width, width), BF16),
            pltpu.VMEM((width, width), BF16),
            pltpu.VMEM((2 * width, width), BF16),
            pltpu.VMEM((LINE, 1, edges + edges // 2), jnp.int32),
            pltpu.VMEM((LINE, CHUNKS, rows, part), BF16),
            pltpu.VMEM((layer_slots, rows), F32),
            pltpu.VMEM((LINE, layer_slots, rows), BF16),
            pltpu.VMEM((LINE, rows, layer_slots), BF16),
            pltpu.VMEM((LINE, CHUNKS, layer_slots, part), BF16),
            pltpu.VMEM((LINE, CHUNKS, layer_slots, part), BF16),
            pltpu.VMEM((LINE, layer_slots, 128), BF16),
            pltpu.VMEM((LINE, layer_slots, 128), BF16),
            pltpu.VMEM((LINE, rows, layer_slots), BF16),
            pltpu.VMEM((CHUNKS, rows, part), F32),
            pltpu.VMEM((rows, width), F32),
            pltpu.VMEM((rows, width), F32),
            pltpu.VMEM((rows, width), F32),
            pltpu.VMEM((rows, width), BF16),
            pltpu.VMEM((rows, width), BF16),
            pltpu.VMEM((rows, width), BF16),
            pltpu.VMEM((rows, 128), F32),
            pltpu.VMEM((8, 128), F32),
            pltpu.VMEM((layer, 8, 128), F32),
            pltpu.VMEM((LINE, 8, 128), F32),
            pltpu.VMEM((n_grp, 8, 128), F32),
            dma((n_stage + 1,)),
            dma((11,)),
            dma((LINE - 1,)),
            dma((LINE - 1,)),
            dma((LINE * CHUNKS,)),
            dma((LINE * CHUNKS,)),
            dma((LINE * CHUNKS,)),
            dma((LINE * CHUNKS * (layer - 1),)),
            dma((LINE * CHUNKS * (layer - 1),)),
            dma((LINE * (layer - 1),)),
            dma((LINE * (layer - 1),)),
            dma((share_sems(n_nodes, n_grp),)),
            dma((share_sems(n_nodes, n_grp),)),
        ],
        compiler_params=pltpu.CompilerParams(
            vmem_limit_bytes=60 * MIB, collective_id=2, has_side_effects=True
        ),
        name="forward_pass",
    )(feats, mask, *edges_of, targets, board, neigh, nbias, comb, cbias, cot)


def add_into(target, first, count, columns, parts, step=16):
    @pl.loop(0, count // step)
    def _(i):
        at = pl.ds(pl.multiple_of(first + i * step, step), step)
        total = target[at, columns].astype(F32)
        for part in parts:
            total += part[pl.ds(pl.multiple_of(i * step, step), step), :].astype(F32)
        target[at, columns] = total.astype(target.dtype)


def reduce_job(place, order, grad, region, arrive, land, last, send, recv, free, base):
    first, rows, left, columns = region
    half = columns // 2
    core = place.at["c"]
    mine = pl.ds(pl.multiple_of(left + core * half, half), half)
    theirs = pl.ds(pl.multiple_of(left + (1 - core) * half, half), half)
    mate = place.member("c", 1 - core)
    block = pl.ds(first, rows)
    sems = iter(range(base, base + send.shape[0]))

    def lay(src, dst, device):
        sem = next(sems)
        return remote(src, dst, send.at[sem], recv.at[sem], device)

    across = lay(grad.at[block, theirs], arrive, mate)
    down = []
    begin, length, used = first, rows, 0
    for axis in order:
        length //= place.size[axis]
        copies, parts, devices = [], [], []
        for far, index, device in place.others(axis):
            start = pl.multiple_of(begin + index * length, 16)
            slot = land.at[pl.ds(used, length)]
            used += length
            copies.append(lay(grad.at[pl.ds(start, length), mine], slot, device))
            parts.append(slot)
            devices.append(device)
        parent = begin
        begin = pl.multiple_of(begin + place.at[axis] * length, 16)
        down.append((axis, parent, begin, length, copies, parts, devices))
    axis, parent, begin, length, _, _, devices = down[-1]
    here = pl.ds(pl.multiple_of(place.at[axis] * length, 16), length)
    whole = pl.ds(pl.multiple_of(parent, 16), length * place.size[axis])
    end = [lay(last.at[here], last.at[here], device) for device in devices]
    up = []
    for stage in range(len(down) - 1, 0, -1):
        axis, _, start, piece, _, _, devices = down[stage - 1]
        own = grad.at[pl.ds(start, piece), mine]
        up.append((stage, len(devices), [lay(own, own, device) for device in devices]))
    own = grad.at[block, mine]
    back = lay(own, own, mate)
    yield

    def release(at, devices):
        for device in devices:
            pl.semaphore_signal(free.at[base + at], inc=1, device_id=device, device_id_type=MESH)

    across.start()
    yield
    across.wait()
    release(0, [mate])
    add_into(grad, first, rows, mine, [arrive])
    for stage, (_, _, begin, length, copies, parts, devices) in enumerate(down):
        for copy in copies:
            copy.start()
        yield
        for copy in copies:
            copy.wait()
        if stage < len(down) - 1:
            release(stage + 1, devices)
        add_into(grad, begin, length, mine, parts)
    last[here] = grad[pl.ds(begin, length), mine]
    for copy in end:
        copy.start()
    yield
    for copy in end:
        copy.wait()
    grad[whole, mine] = last[pl.ds(0, whole.size)]
    for stage, count, copies in up:
        pl.semaphore_wait(free.at[base + stage], count)
        for copy in copies:
            copy.start()
        yield
        for copy in copies:
            copy.wait()
    pl.semaphore_wait(free.at[base], 1)
    back.start()
    yield
    back.wait()


def job_sems(n_nodes, n_grp):
    return 2 * (1 + (n_nodes // LINE // 2 - 1) + (LINE - 1) + (n_grp - 1))


AHEAD = 2
BEHIND = CHUNKS - AHEAD
JOBS = {
    kind[0] + str(i): kind + str(i) for kind, count in (("comb", 4), ("neigh", 4), ("board", 4)) for i in range(count)
}
BACKWARD = (
    "l0", "A1", "B2", "A0", "G0", "c0", "c1", "L2", "W0", "Y10", "c3", "B3", "f01", "c2", "c0",
    "32", "c3", "c1", "Y11", "f00", "q01", "Y12", "L1", "33", "L3", "c2", "22", "Y13", "f11",
    "Y14", "12", "Z1", "q11", "Y20", "f10", "c0", "q00", "Y21", "23", "c1", "q10", "c2", "Y22",
    "q20", "q21", "13", "Y23", "Y24", "c0", "S0", "Z2", "O2", "c3", "f21", "c1", "f20", "n2", "O3",
    "n3", "c0", "Y30", "n2", "q31", "c1", "Y31", "c2", "n3", "Y32", "c0", "q30", "c1", "Y33", "c3",
    "n3", "n2", "Y34", "c2", "c0", "c1", "Z3", "O1", "n1", "c3", "O0", "n0", "n1", "c2", "n3",
    "E0", "H1", "b2", "c3", "n2", "b3", "n0", "n3", "H0", "b1", "b2", "b3", "n1", "b0", "b1", "n0",
    "n3", "b0", "n1", "P0", "b2", "c0", "F0", "b1", "n0", "n2", "c2", "b3", "n1", "b0", "b1", "c3",
    "b3", "n0", "b0", "n1", "b2", "n2", "c0", "b3", "n3", "b1", "b0", "b3", "n2", "c2", "b2", "n0",
    "b1", "c1", "n1", "b3", "n3", "b0", "P1", "b2", "c3", "c1", "b1", "b0", "b2", "n3", "n2", "n0",
    "b3", "n1", "b0", "b1", "n0", "c2", "n2", "P2", "b2", "n0", "b1", "b2", "b0", "n1", "P3", "c3",
    "b3",
)


def gradient_regions(n_nodes, n_grp, width):
    pieces = n_nodes * n_grp // 2
    x_first, y_first = ("x", "y", "z"), ("y", "x", "z")
    regions = {}
    count = max(1, min(4, 2 * width // (16 * pieces)))
    n_rows = 2 * width // count
    for j in range(count):
        regions[f"comb{j}"] = (j * n_rows, n_rows, 0, width, y_first if j % 2 else x_first)
    if width % (16 * pieces) == 0:
        part = width // CHUNKS
        for k in range(CHUNKS):
            regions[f"neigh{k}"] = (2 * width, width, k * part, part, x_first if k % 2 else y_first)
        count = max(1, min(4, width // (16 * pieces)))
        n_rows = width // count
        for j in range(count):
            order = (x_first, y_first, x_first, ("z", "y", "x"))[j]
            regions[f"board{j}"] = (3 * width + j * n_rows, n_rows, 0, width, order)
    else:
        regions["board0"] = (2 * width, 2 * width, 0, width, x_first)
    return regions


def backward_kernel(
    n_nodes,
    n_grp,
    mask_ref,
    targets_ref,
    stats_ref,
    place_h,
    child_h,
    weight_h,
    hid_h,
    pre_h,
    featb_h,
    board_b_h,
    neigh_b_h,
    comb1_b_h,
    st_h,
    dnum_h,
    dz_h,
    agg_h,
    gfeat_h,
    summed_h,
    small_ref,
    hid,
    pre,
    featb,
    board_b,
    neigh_b,
    comb1_b,
    spread_t,
    dnum,
    dz,
    agg,
    picker_t,
    picker_l,
    lines,
    edge_place,
    edge_child,
    edge_weight,
    acc,
    own_t,
    parents,
    out_slots,
    in_slots,
    chain,
    tmp,
    dpre,
    dh,
    grad,
    arrive,
    land,
    gather,
    share_l,
    share_z,
    share_x,
    small,
    load_sem,
    store_sem,
    slot_send,
    slot_recv,
    up_send,
    down_send,
    chain_recv,
    line_send,
    line_recv,
    parent_up,
    parent_down,
    parent_recv,
    job_send,
    job_recv,
    job_free,
    share_send,
    share_recv,
):
    place = Place(n_nodes, n_grp)
    z, low = place.at["z"], place.at["l"]
    layer = place.size["l"]
    rows, width = hid.shape
    layer_slots = spread_t.shape[2]
    cap = layer_slots // layer
    part = width // CHUNKS

    loads = {}
    for i, (name, src, dst) in enumerate(
        (
            ("dnum", dnum_h, dnum),
            ("hid", hid_h, hid),
            ("agg", agg_h, agg),
            ("dz", dz_h, dz),
            ("spread_t", st_h, spread_t),
            ("comb1_b", comb1_b_h, comb1_b),
            ("pre", pre_h, pre),
            ("neigh_b", neigh_b_h, neigh_b),
            ("featb", featb_h, featb),
            ("board_b", board_b_h, board_b),
            ("place", place_h, edge_place),
            ("child", child_h, edge_child),
            ("weight", weight_h, edge_weight),
        )
    ):
        loads[name] = pltpu.make_async_copy(src, dst, load_sem.at[i])
        loads[name].start()
    def make_pickers():
        @pl.loop(0, LINE)
        def _(src):
            at = pl.ds(pl.multiple_of(src * layer_slots, layer_slots), layer_slots)
            ids = lax.broadcasted_iota(jnp.int32, (rows, layer_slots), 0)
            picker_t[src] = jnp.where(ids == targets_ref[:, at], 1.0, 0.0).astype(BF16).T

    barrier(place, ("l", "z", "x"), make_pickers)
    stores = []

    def store(src, dst):
        copy = pltpu.make_async_copy(src, dst, store_sem.at[len(stores)])
        copy.start()
        stores.append(copy)

    mask = column_of(mask_ref) > 0.5

    def source(which):
        flip = z // 2
        inner = z * (1 - 2 * flip) + (LINE - 1) * flip
        index = ORDER[0][which] * (1 - inner) + ORDER[1][which] * inner
        return index * (1 - 2 * flip) + (LINE - 1) * flip

    def cols(k):
        return pl.ds(pl.multiple_of(k * part, part), part)

    def slot_copy(dst, k, far, index, device):
        at = (dst * CHUNKS + k) * (layer - 1) + far
        return remote(
            out_slots.at[dst, k, pl.ds(pl.multiple_of(index * cap, cap), cap)],
            in_slots.at[dst, k, pl.ds(pl.multiple_of(low * cap, cap), cap)],
            slot_send.at[at],
            slot_recv.at[at],
            device,
        )

    def back(dst, k):
        out_slots[dst, k] = jnp.dot(
            picker_t[dst], dnum[:, cols(k)], preferred_element_type=F32
        ).astype(BF16)
        for far, index, device in place.others("l"):
            slot_copy(dst, k, far, index, device).start()
        own = pl.ds(pl.multiple_of(low * cap, cap), cap)
        in_slots[dst, k, own] = out_slots[dst, k, own]

    def child_sums(dst, k):
        for far, index, device in place.others("l"):
            slot_copy(dst, k, far, index, device).wait_recv()
        tmp[...] = jnp.dot(spread_t[dst], in_slots[dst, k], preferred_element_type=F32)

    def up_copy(dst, k):
        k = k - AHEAD
        at = dst * BEHIND + k
        return remote(
            chain.at[dst, k],
            chain.at[dst, k],
            up_send.at[at],
            chain_recv.at[at],
            place.member("z", z + 1),
        )

    def down_copy(dst, k, last):
        slot = LINE if last else dst
        k = k - AHEAD
        return remote(
            chain.at[dst, k],
            chain.at[slot, k],
            down_send.at[dst * BEHIND + k],
            chain_recv.at[slot * BEHIND + k],
            place.member("z", z - 1),
        )

    def arrived(slot, k):
        k = k - AHEAD
        remote(
            chain.at[slot, k],
            chain.at[slot, k],
            up_send.at[0],
            chain_recv.at[slot * BEHIND + k],
            place.member("z", lax.rem(z + 1, LINE)),
        ).wait_recv()

    def hand_on(dst, k):
        child_sums(dst, k)

        @pl.when(dst > z)
        def _():
            @pl.when(z > 0)
            def _():
                up_copy(dst, k).wait_recv()
                chain[dst, k - AHEAD] = (chain[dst, k - AHEAD].astype(F32) + tmp[...]).astype(BF16)

            @pl.when(z == 0)
            def _():
                chain[dst, k - AHEAD] = tmp[...].astype(BF16)

            up_copy(dst, k).start()

        @pl.when(dst < z)
        def _():
            @pl.when(z < LINE - 1)
            def _():
                down_copy(dst, k, False).wait_recv()
                chain[dst, k - AHEAD] = (chain[dst, k - AHEAD].astype(F32) + tmp[...]).astype(BF16)

            @pl.when(z == LINE - 1)
            def _():
                chain[dst, k - AHEAD] = tmp[...].astype(BF16)

            @pl.when(dst == z - 1)
            def _():
                down_copy(dst, k, True).start()

            @pl.when(dst < z - 1)
            def _():
                down_copy(dst, k, False).start()

    regions = gradient_regions(n_nodes, n_grp, width)
    per_job = job_sems(n_nodes, n_grp)

    def job(name):
        first, n_rows, left, columns, order = regions[name]
        rows_at, cols_at = pl.ds(first, n_rows), pl.ds(left, columns)
        land_at = pl.ds(left // 2, columns // 2)
        yield from reduce_job(
            place,
            order,
            grad,
            (first, n_rows, left, columns),
            arrive.at[rows_at, land_at],
            land.at[rows_at, land_at],
            gather.at[pl.ds(first // 4, n_rows // 4), land_at],
            job_send,
            job_recv,
            job_free,
            list(regions).index(name) * per_job,
        )
        store(grad.at[rows_at, cols_at], summed_h.at[rows_at, cols_at])

    jobs = {name: job(name) for name in regions}
    for lay_out in jobs.values():
        next(lay_out)

    def step_job(name, last=False):
        if name in jobs and (last or name != "board0" or "board3" in regions):
            try:
                next(jobs[name])
            except StopIteration:
                del jobs[name]

    loads["dnum"].wait()

    def back_all(k):
        for which in (3, 2, 1, 0):
            back(source(which), k)

    def comb_grad(left, first):
        @pl.loop(0, CHUNKS)
        def _(k):
            grad[pl.ds(first, width), cols(k)] = dot_tn(left[...], dz[:, cols(k)]).astype(BF16)

    def line_targets():
        lines[z] = targets_ref[:, pl.ds(pl.multiple_of(z * layer_slots, layer_slots), layer_slots)]
        for far, index, device in place.others("z"):
            at = pl.ds(pl.multiple_of(index * layer_slots, layer_slots), layer_slots)
            remote(
                targets_ref.at[:, at], lines.at[z], line_send.at[far], line_recv.at[far], device
            ).start()

    def line_picker(which):
        src = source(which)
        far = lax.rem(z - src - 1 + LINE, LINE)
        remote(
            lines.at[src], lines.at[src], line_send.at[0], line_recv.at[far], place.member("z", src)
        ).wait_recv()
        ids = lax.broadcasted_iota(jnp.int32, (rows, layer_slots), 0)
        picker_l[src] = jnp.where(ids == lines[src], 1.0, 0.0).astype(BF16).T

    def parent_copy(src, k, sems, to):
        piece = parents.at[src, k]
        at = src * AHEAD + k
        return remote(piece, piece, sems.at[at], parent_recv.at[at], place.member("z", to))

    def parent_send(k):
        parents[z, k] = dnum[:, cols(k)]

        @pl.when(z < LINE - 1)
        def _():
            parent_copy(z, k, parent_up, z + 1).start()

        @pl.when(z > 0)
        def _():
            parent_copy(z, k, parent_down, z - 1).start()

    def parent_forward(j, k):
        below = z - 1 - j
        above = z + 1 + j

        @pl.when(below >= 0)
        def _():
            parent_copy(below, k, parent_up, z + 1).wait_recv()

            @pl.when(z < LINE - 1)
            def _():
                parent_copy(below, k, parent_up, z + 1).start()

        @pl.when(above < LINE)
        def _():
            parent_copy(above, k, parent_down, z - 1).wait_recv()

            @pl.when(z > 0)
            def _():
                parent_copy(above, k, parent_down, z - 1).start()

    def parent_slots(which, k):
        src = source(which)
        choose = picker_t[z] if which == 0 else picker_l[src]
        out_slots[src, k] = jnp.dot(choose, parents[src, k], preferred_element_type=F32).astype(
            BF16
        )
        for far, index, device in place.others("l"):
            slot_copy(src, k, far, index, device).start()
        own = pl.ds(pl.multiple_of(low * cap, cap), cap)
        in_slots[src, k, own] = out_slots[src, k, own]

    edges = edge_place.shape[1]
    turn = math.gcd(edges, 5120)
    steps = edges // turn

    def build_own(which, ticks):
        src = source(which)
        if which == 1:
            for name in ("place", "child", "weight"):
                loads[name].wait()
        acc[...] = jnp.zeros_like(acc)

        @pl.loop(0, steps)
        def _(t):
            at = pl.ds(pl.multiple_of(t * turn, turn), turn)
            slot = (edge_place[:, at] - src * layer_slots).astype(jnp.int16)
            child = edge_child[:, at].astype(jnp.int16)
            weight = edge_weight[:, at].astype(F32).astype(F8)
            right = jnp.where(
                lax.broadcasted_iota(jnp.int16, (layer_slots, turn), 0) == slot,
                jnp.ones((), F8),
                jnp.zeros((), F8),
            )
            block = 256
            for first in range(0, rows, block):
                ids = lax.broadcasted_iota(jnp.int16, (block, turn), 0) + jnp.asarray(
                    first, jnp.int16
                )
                left = jnp.where(ids == child, weight, jnp.zeros((), F8))
                acc[pl.ds(first, block), :] += dot_nt(left, right)
            run_ticks(t, ticks)

        own_t[src] = acc[...].astype(BF16)

    def own(k):
        if k < AHEAD:
            for which in range(LINE):
                src = source(which)
                for far, index, device in place.others("l"):
                    slot_copy(src, k, far, index, device).wait_recv()
                weights = spread_t[z] if which == 0 else own_t[src]
                value = jnp.dot(weights, in_slots[src, k], preferred_element_type=F32)
                if which == 0:
                    tmp[...] = value
                else:
                    tmp[...] += value
        else:
            child_sums(z, k)

            @pl.when(z > 0)
            def _():
                arrived(z, k)
                tmp[...] += chain[z, k - AHEAD].astype(F32)

            @pl.when(z < LINE - 1)
            def _():
                arrived(LINE, k)
                tmp[...] += chain[LINE, k - AHEAD].astype(F32)

        down = (tmp[...] * gelu_slope(pre[:, cols(k)])).astype(BF16)
        dpre[:, cols(k)] = down
        small[0:1, cols(k)] = jnp.sum(down.astype(F32), axis=0, keepdims=True)
        dh[...] += dot_nt(down, neigh_b[:, cols(k)])

    def neigh_grad(k):
        grad[pl.ds(2 * width, width), cols(k)] = dot_tn(hid[...], dpre[:, cols(k)]).astype(BF16)

    def comb_grads():
        for name in ("hid", "agg", "dz", "comb1_b"):
            loads[name].wait()
        comb_grad(hid, 0)
        comb_grad(agg, width)

    def self_part():
        small[...] = jnp.zeros_like(small)
        small[1:2, :] = jnp.sum(dz[...].astype(F32), axis=0, keepdims=True)
        small[2:3, :] = jnp.broadcast_to(stats_ref[0:1, 0:1], (1, width))

        @pl.loop(0, CHUNKS)
        def _(k):
            dh[:, cols(k)] = dot_nt(dz[...], comb1_b[cols(k), :])

        for name in ("pre", "neigh_b", "featb", "board_b"):
            loads[name].wait()

    def own_and_grad(k):
        own(k)
        neigh_grad(k)

    def end_of_line():
        last = dh[...].astype(BF16)
        dpre[...] = jnp.where(mask, last, jnp.zeros_like(last))
        pre[...] = last.astype(F32)

    def board_grad(i):
        half = width // 2
        grad[pl.ds(3 * width + i * half, half), :] = dot_tn(
            featb[:, i * half : (i + 1) * half], dpre[...]
        ).astype(BF16)

    def feature_grad():
        @pl.loop(0, CHUNKS)
        def _(k):
            pre[:, cols(k)] = jnp.where(
                mask, dot_nt(dpre[...], board_b[cols(k), :]), pre[:, cols(k)]
            )

        store(pre, gfeat_h)

    share = Share(place, (share_l, share_z, share_x), share_send, share_recv)

    def step_share(stage):
        if stage == 0:
            share.start(0, small[...])
        elif stage < 3:
            share.start(stage, share.finish(stage - 1))
        else:
            row = lax.broadcasted_iota(jnp.int32, small_ref.shape, 0)
            small_ref[...] = share.finish(2) * jnp.where(row == 2, stats_ref[8:9, 0:1], 1.0)

    acts = {
        "l": lambda _: line_targets(),
        "L": line_picker,
        "A": parent_send,
        "f": parent_forward,
        "q": parent_slots,
        "B": back_all,
        "W": lambda _: loads["spread_t"].wait(),
        "G": lambda _: comb_grads(),
        "S": lambda _: self_part(),
        "O": own_and_grad,
        "E": lambda _: end_of_line(),
        "H": board_grad,
        "F": lambda _: feature_grad(),
        "P": step_share,
        "3": lambda k: hand_on(source(3), k),
        "2": lambda k: hand_on(source(2), k),
        "1": lambda k: hand_on(source(1), k),
    }
    def act(name):
        if name in JOBS:
            step_job(JOBS[name])
        else:
            acts[name[0]](*(int(c) for c in name[1:]))

    run_order(BACKWARD, steps, build_own, act)
    while jobs:
        for name in list(jobs):
            step_job(name, last=True)

    for far, index, device in place.others("z"):
        remote(lines.at[z], lines.at[z], line_send.at[far], line_recv.at[far], device).wait_send()

    @pl.loop(0, LINE * CHUNKS)
    def _(i):
        dst = i // CHUNKS
        k = lax.rem(i, CHUNKS)

        @pl.when(k < AHEAD)
        def _():
            @pl.when(jnp.logical_and(dst <= z, z < LINE - 1))
            def _():
                parent_copy(dst, k, parent_up, z + 1).wait_send()

            @pl.when(jnp.logical_and(dst >= z, z > 0))
            def _():
                parent_copy(dst, k, parent_down, z - 1).wait_send()

        @pl.when(k >= AHEAD)
        def _():
            @pl.when(dst > z)
            def _():
                up_copy(dst, k).wait_send()

            @pl.when(dst < z)
            def _():
                down_copy(dst, k, False).wait_send()

        for far, index, device in place.others("l"):
            slot_copy(dst, k, far, index, device).wait_send()

    for copy in stores:
        copy.wait()


def backward_pass(n_nodes, n_grp, mask, targets, stats, edges_of, hid, pre, featb, board_b, neigh_b, comb1_b, st, dnum, dz, agg):
    rows, width = hid.shape
    edges = edges_of[0].shape[1]
    layer = n_nodes // LINE
    layer_slots = st.shape[2]
    part = width // CHUNKS
    n_rows = 4 * width
    count = len(gradient_regions(n_nodes, n_grp, width))
    dma = pltpu.SemaphoreType.DMA
    big = pl.BlockSpec(memory_space=pl.ANY)
    vmem = pl.BlockSpec(memory_space=pltpu.VMEM)
    sems = count * job_sems(n_nodes, n_grp)
    pieces = LINE * CHUNKS
    return pl.pallas_call(
        functools.partial(backward_kernel, n_nodes, n_grp),
        out_shape=[
            jax.ShapeDtypeStruct((rows, width), F32),
            jax.ShapeDtypeStruct((n_rows, width), BF16),
            jax.ShapeDtypeStruct((8, width), F32),
        ],
        in_specs=[vmem, vmem, vmem] + [big] * 13,
        out_specs=[big, big, vmem],
        scratch_shapes=[
            pltpu.VMEM((rows, width), BF16),
            pltpu.VMEM((rows, width), F32),
            pltpu.VMEM((rows, width), BF16),
            pltpu.VMEM((width, width), BF16),
            pltpu.VMEM((width, width), BF16),
            pltpu.VMEM((width, width), BF16),
            pltpu.VMEM((LINE, rows, layer_slots), BF16),
            pltpu.VMEM((rows, width), BF16),
            pltpu.VMEM((rows, width), BF16),
            pltpu.VMEM((rows, width), BF16),
            pltpu.VMEM((LINE, layer_slots, rows), BF16),
            pltpu.VMEM((LINE, layer_slots, rows), BF16),
            pltpu.VMEM((LINE, 1, layer_slots), jnp.int32),
            pltpu.VMEM((1, edges), jnp.int32),
            pltpu.VMEM((1, edges), jnp.int32),
            pltpu.VMEM((1, edges), jnp.int32),
            pltpu.VMEM((rows, layer_slots), F32),
            pltpu.VMEM((LINE, rows, layer_slots), BF16),
            pltpu.VMEM((LINE, AHEAD, rows, part), BF16),
            pltpu.VMEM((LINE, CHUNKS, layer_slots, part), BF16),
            pltpu.VMEM((LINE, CHUNKS, layer_slots, part), BF16),
            pltpu.VMEM((LINE + 1, BEHIND, rows, part), BF16),
            pltpu.VMEM((rows, part), F32),
            pltpu.VMEM((rows, width), BF16),
            pltpu.VMEM((rows, width), F32),
            pltpu.VMEM((n_rows, width), BF16),
            pltpu.VMEM((n_rows, width // 2), BF16),
            pltpu.VMEM((n_rows, width // 2), BF16),
            pltpu.VMEM((n_rows // 4, width // 2), BF16),
            pltpu.VMEM((layer, 8, width), F32),
            pltpu.VMEM((LINE, 8, width), F32),
            pltpu.VMEM((n_grp, 8, width), F32),
            pltpu.VMEM((8, width), F32),
            dma((13,)),
            dma((count + 1,)),
            dma((pieces * (layer - 1),)),
            dma((pieces * (layer - 1),)),
            dma((LINE * BEHIND,)),
            dma((LINE * BEHIND,)),
            dma(((LINE + 1) * BEHIND,)),
            dma((LINE - 1,)),
            dma((LINE - 1,)),
            dma((LINE * AHEAD,)),
            dma((LINE * AHEAD,)),
            dma((LINE * AHEAD,)),
            dma((sems,)),
            dma((sems,)),
            pltpu.SemaphoreType.REGULAR((sems,)),
            dma((share_sems(n_nodes, n_grp),)),
            dma((share_sems(n_nodes, n_grp),)),
        ],
        compiler_params=pltpu.CompilerParams(
            vmem_limit_bytes=63 * MIB, collective_id=3, has_side_effects=True
        ),
        name="backward_pass",
    )(mask, targets, stats, *edges_of, hid, pre, featb, board_b, neigh_b, comb1_b, st, dnum, dz, agg)


def unpack_kernel(
    rows, joined, small_ref, comb, neigh, board, nbias_ref, cbias_ref, penalty_ref, low, wide, load_sem, store_sem
):
    width = joined.shape[1]
    blocks = joined.shape[0] // rows

    def load(i):
        at = pl.ds(i * rows, rows)
        return pltpu.make_async_copy(joined.at[at], low.at[at], load_sem.at[i])

    def store(i):
        first = i * rows
        if first < 2 * width:
            target = comb.at[pl.ds(first, rows)]
        elif first < 3 * width:
            target = neigh.at[pl.ds(first - 2 * width, rows)]
        else:
            target = board.at[pl.ds(first - 3 * width, rows)]
        return pltpu.make_async_copy(wide.at[pl.ds(first, rows)], target, store_sem.at[i])

    for i in range(blocks):
        load(i).start()
    nbias_ref[...] = small_ref[0:1, :]
    cbias_ref[...] = small_ref[1:2, :]
    penalty_ref[...] = small_ref[2:3, 0:1]
    for i in range(blocks):
        load(i).wait()

        @pl.loop(0, rows // 32)
        def _(r, i=i):
            at = pl.ds(pl.multiple_of(i * rows + r * 32, 32), 32)
            wide[at, :] = low[at, :].astype(F32)

        store(i).start()
    for i in range(blocks):
        store(i).wait()


def unpack(joined, small):
    n_rows, width = joined.shape
    rows = math.gcd(width, 256)
    big = pl.BlockSpec(memory_space=pl.ANY)
    vmem = pl.BlockSpec(memory_space=pltpu.VMEM)
    dma = pltpu.SemaphoreType.DMA
    return pl.pallas_call(
        functools.partial(unpack_kernel, rows),
        out_shape=[
            jax.ShapeDtypeStruct((2 * width, width), F32),
            jax.ShapeDtypeStruct((width, width), F32),
            jax.ShapeDtypeStruct((width, width), F32),
            jax.ShapeDtypeStruct((1, width), F32),
            jax.ShapeDtypeStruct((1, width), F32),
            jax.ShapeDtypeStruct((1, 1), F32),
        ],
        in_specs=[big, vmem],
        out_specs=[big] * 3 + [vmem] * 3,
        scratch_shapes=[
            pltpu.VMEM((n_rows, width), BF16),
            pltpu.VMEM((n_rows, width), F32),
            dma((n_rows // rows,)),
            dma((n_rows // rows,)),
        ],
        compiler_params=pltpu.CompilerParams(vmem_limit_bytes=60 * MIB),
        name="unpack",
    )(joined, small)


def on_device(
    n_nodes,
    n_grp,
    features,
    type_mask,
    edge_child,
    edge_slot,
    edge_weight,
    recv_rows,
    board_proj,
    neigh_proj,
    neigh_bias,
    combine_proj,
    combine_bias,
    out_cot,
):
    feats = features[0]
    rows, width = feats.shape
    peers = recv_rows.shape[2]
    cap = recv_rows.shape[3]
    slots = peers * cap
    targets = recv_rows[0, 0].reshape(1, slots)
    mask = type_mask.astype(F32)
    embed, hidden, pre, featb, pbl, qwl, cwl1, spread_t, dnum, dzb, aggb, stats = forward_pass(
        n_nodes,
        n_grp,
        feats,
        mask,
        (edge_slot, edge_child, edge_weight),
        targets,
        board_proj,
        neigh_proj,
        neigh_bias.reshape(1, width),
        combine_proj,
        combine_bias.reshape(1, width),
        out_cot[0],
    )
    grad_feats, summed, small = backward_pass(
        n_nodes,
        n_grp,
        mask,
        targets,
        stats,
        (edge_slot, edge_child, edge_weight),
        hidden,
        pre,
        featb,
        pbl,
        qwl,
        cwl1,
        spread_t,
        dnum,
        dzb,
        aggb,
    )
    grad_comb, grad_neigh, grad_board, grad_nbias, grad_cbias, penalty = unpack(summed, small)
    return (
        embed[None],
        penalty[0, 0],
        grad_feats[None],
        grad_board,
        grad_neigh,
        grad_nbias[0],
        grad_comb,
        grad_cbias[0],
    )


def solution(mesh):
    in_specs = (
        P("grp", "nodes", None),
        P("grp", "nodes"),
        P("grp", "nodes"),
        P("grp", "nodes"),
        P("grp", "nodes"),
        P("grp", "nodes", None, None),
        P(),
        P(),
        P(),
        P(),
        P(),
        P("grp", "nodes", None),
    )
    out_specs = (P("grp", "nodes", None), P(), P("grp", "nodes", None), P(), P(), P(), P(), P())
    return jax.shard_map(
        functools.partial(on_device, mesh.shape["nodes"], mesh.shape["grp"]),
        mesh=mesh,
        in_specs=in_specs,
        out_specs=out_specs,
        check_vma=False,
    )
```

```python
import functools
import math

import jax
import jax.numpy as jnp
from jax import lax
from jax.experimental import pallas as pl
from jax.experimental.pallas import tpu as pltpu
from jax.sharding import PartitionSpec as P

HIGH = lax.Precision.HIGHEST
MESH = pl.DeviceIdType.MESH
BF16 = jnp.bfloat16
F32 = jnp.float32
F8 = jnp.float8_e4m3fn
MIB = 2**20


def gelu_tanh(v):
    return jax.nn.gelu(v, approximate=True)


def dot_nt(left, right):
    return lax.dot_general(
        left, right, (((1,), (1,)), ((), ())), preferred_element_type=F32
    )


def dot_tn(left, right):
    return lax.dot_general(
        left, right, (((0,), (0,)), ((), ())), preferred_element_type=F32
    )


LINE = 4
CHUNKS = 4
FORWARD = (
    "m0", "m1", "m2", "m3", "Y00", "Y01", "Y02", "Y03", "Z0", "f00", "p00", "p01", "p02", "p03",
    "Y10", "P1", "Y11", "f01", "Y12", "f02", "Y13", "Z1", "p10", "p11", "p12", "Y20", "P2", "Y21",
    "f03", "Y22", "Y23", "f10", "Z2", "p13", "p20", "Y30", "Y31", "f11", "Y32", "Y33", "f12", "Z3",
    "p21", "p22", "G0", "P3", "f13", "p23", "D0", "D1", "D2", "D3", "X0", "R0", "i00", "i01",
    "i02", "i03", "f20", "p30", "i10", "i11", "i12", "i13", "f21", "p31", "i20", "i21", "i22",
    "i23", "f22", "p32", "i30", "d0", "a0", "f23", "p33", "i31", "a1", "i32", "a2", "i33",
)
ORDER = ((0, 1, 2, 3), (1, 2, 0, 3))


class Place:
    def __init__(self, n_nodes, n_grp):
        layer = n_nodes // LINE
        node = lax.axis_index("nodes")
        grp = lax.axis_index("grp")
        self.node, self.grp = node, grp
        self.size = {"l": layer, "c": 2, "y": layer // 2, "z": LINE, "x": n_grp}
        low = lax.rem(node, layer)
        self.at = {"l": low, "c": lax.rem(low, 2), "y": low // 2, "z": node // layer, "x": grp}

    def member(self, axis, index):
        layer = self.size["l"]
        low, line, grp = self.at["l"], self.at["z"], self.at["x"]
        if axis == "l":
            low = index
        elif axis == "c":
            low = self.at["y"] * 2 + index
        elif axis == "y":
            low = index * 2 + self.at["c"]
        elif axis == "z":
            line = index
        else:
            grp = index
        return {"nodes": line * layer + low, "grp": grp}

    def others(self, axis):
        size = self.size[axis]
        for far in range(1, size):
            index = lax.rem(self.at[axis] + far, size)
            yield far - 1, index, self.member(axis, index)


def remote(src, dst, send, recv, device):
    return pltpu.make_async_remote_copy(
        src_ref=src, dst_ref=dst, send_sem=send, recv_sem=recv, device_id=device, device_id_type=MESH
    )


def barrier(place, axes, meanwhile=None):
    sem = pltpu.get_barrier_semaphore()
    count = 0
    for axis in axes:
        for _, _, device in place.others(axis):
            pl.semaphore_signal(sem, inc=1, device_id=device, device_id_type=MESH)
            count += 1
    if meanwhile is not None:
        meanwhile()
    pl.semaphore_wait(sem, count)


def column_of(row_ref):
    row = row_ref[...].astype(F32)
    return jnp.broadcast_to(row, (128, row.shape[1])).T[:, 0:1]


def gelu(v):
    t = jnp.tanh(0.7978845608028654 * (v + 0.044715 * (v * v * v)))
    return v * (0.5 * (1.0 + t))


def gelu_slope(v):
    square = v * v
    t = jnp.tanh(0.7978845608028654 * (v + 0.044715 * (v * square)))
    bend = 0.7978845608028654 * (1.0 + 0.134145 * square)
    return 0.5 * (1.0 + t) + 0.5 * v * (1.0 - t * t) * bend


class Share:
    def __init__(self, place, bufs, send, recv):
        self.place, self.send, self.recv = place, send, recv
        self.stages, base = [], 0
        for axis, buf in zip(("l", "z", "x"), bufs):
            self.stages.append((axis, buf, base))
            base += place.size[axis] - 1

    def start(self, stage, value):
        axis, buf, base = self.stages[stage]
        me = self.place.at[axis]
        buf[me] = value
        for far, _, device in self.place.others(axis):
            remote(
                buf.at[me], buf.at[me], self.send.at[base + far], self.recv.at[base + far], device
            ).start()

    def finish(self, stage):
        axis, buf, base = self.stages[stage]
        me = self.place.at[axis]
        for far, _, device in self.place.others(axis):
            remote(
                buf.at[me], buf.at[me], self.send.at[base + far], self.recv.at[base + far], device
            ).wait()
        total = buf[0]
        for i in range(1, self.place.size[axis]):
            total += buf[i]
        return total


def run_ticks(t, ticks):
    for at, acts in enumerate(ticks):
        if acts:

            @pl.when(t == at)
            def _(acts=acts):
                for act in acts:
                    act()


def run_order(order, steps, build, act):
    ticks = None
    for name in order:
        if name[0] == "Y":
            if ticks is None:
                ticks = [[] for _ in range(steps)]
                marks = sum(other[:2] == name[:2] for other in order)
            now = (int(name[2]) + 1) * steps // marks - 1
        elif name[0] == "Z":
            build(int(name[1]), ticks)
            ticks = None
        elif ticks is not None:
            ticks[max(now, 0)].append(functools.partial(act, name))
        else:
            act(name)


def share_sems(n_nodes, n_grp):
    return (n_nodes // LINE - 1) + (LINE - 1) + max(1, n_grp - 1)


def forward_kernel(
    n_nodes,
    n_grp,
    feats_h,
    mask_ref,
    place_ref,
    child_ref,
    weight_ref,
    targets_ref,
    board_h,
    neigh_h,
    nbias_ref,
    comb_h,
    cbias_ref,
    cot_h,
    embed_h,
    hid_h,
    pre_h,
    featb_h,
    board_b_h,
    neigh_b_h,
    comb1_b_h,
    st_h,
    dnum_h,
    dz_h,
    agg_h,
    stats_ref,
    stage,
    featb,
    hid,
    pre,
    board_b,
    neigh_b,
    comb_b,
    keys,
    msg,
    acc,
    spread,
    spread_t,
    out_slots,
    in_slots,
    out_tot,
    in_tot,
    picker,
    num,
    zval,
    zpre,
    cot,
    agg,
    dz,
    dnum,
    den_ref,
    scale_ref,
    count_l,
    count_z,
    count_x,
    load_sem,
    store_sem,
    key_send,
    key_recv,
    up_send,
    down_send,
    msg_recv,
    slot_send,
    slot_recv,
    tot_send,
    tot_recv,
    count_send,
    count_recv,
):
    place = Place(n_nodes, n_grp)
    z, low = place.at["z"], place.at["l"]
    layer = place.size["l"]
    rows, width = featb.shape
    edges = place_ref.shape[1]
    half = edges // 2
    layer_slots = spread.shape[1]
    cap = layer_slots // layer
    part = width // CHUNKS
    turn = math.gcd(half, 2560)
    steps = edges // turn

    sources = [feats_h.at[:]]
    for whole in (board_h, neigh_h, comb_h):
        for first in range(0, whole.shape[0], rows):
            sources.append(whole.at[pl.ds(first, rows)])
    n_stage = stage.shape[0]

    def load(i):
        return pltpu.make_async_copy(sources[i], stage.at[i % n_stage], load_sem.at[i % n_stage])

    for i in range(n_stage):
        load(i).start()
    load_cot = pltpu.make_async_copy(cot_h, cot, load_sem.at[n_stage])
    stores = []

    def store(src, dst):
        copy = pltpu.make_async_copy(src, dst, store_sem.at[len(stores)])
        copy.start()
        stores.append(copy)

    barrier(place, ("l", "z", "x"))
    keys[z, :, pl.ds(0, edges)] = place_ref[...] * 65536 + child_ref[...]
    keys[z, :, pl.ds(edges, half)] = (
        weight_ref[:, pl.ds(half, half)] * 65536 + weight_ref[:, pl.ds(0, half)]
    )

    def key_copy(far, device):
        return remote(keys.at[z], keys.at[z], key_send.at[far], key_recv.at[far], device)

    for far, _, device in place.others("z"):
        key_copy(far, device).start()
    share = Share(place, (count_l, count_z, count_x), count_send, count_recv)
    mask = column_of(mask_ref)
    share.start(0, jnp.full((8, 128), jnp.sum(mask)))

    def cast(i, target, first):
        load(i).wait()
        slot = stage.at[i % n_stage]

        @pl.loop(0, rows // 32)
        def _(r):
            at = pl.ds(pl.multiple_of(r * 32, 32), 32)
            to = pl.ds(pl.multiple_of(first + r * 32, 32), 32)
            target[to, :] = slot[at, :].astype(BF16)

    cast(0, featb, 0)
    cast(1, board_b, 0)
    cast(2, board_b, rows)

    @pl.loop(0, CHUNKS)
    def _(k):
        at = pl.ds(pl.multiple_of(k * part, part), part)
        proj = jnp.dot(featb[...], board_b[:, at], preferred_element_type=F32)
        hid[:, at] = jnp.where(mask > 0.5, proj, stage[0, :, at]).astype(BF16)

    cast(3, neigh_b, 0)
    cast(4, neigh_b, rows)
    for i in range(n_stage, len(sources)):
        load(i).start()
    load_cot.start()

    def up_copy(src, k):
        piece = msg.at[src, k]
        index = src * CHUNKS + k
        return remote(
            piece, piece, up_send.at[index], msg_recv.at[index], place.member("z", z + 1)
        )

    def down_copy(src, k):
        piece = msg.at[src, k]
        index = src * CHUNKS + k
        return remote(
            piece, piece, down_send.at[index], msg_recv.at[index], place.member("z", z - 1)
        )

    def message(k):
        at = pl.ds(k * part, part)
        value = jnp.dot(hid[...], neigh_b[:, at], preferred_element_type=F32) + nbias_ref[:, at]
        pre[:, at] = value
        msg[z, k] = gelu(value).astype(BF16)

        @pl.when(z < LINE - 1)
        def _():
            up_copy(z, k).start()

        @pl.when(z > 0)
        def _():
            down_copy(z, k).start()

    def forward(j, k):
        below = z - 1 - j
        above = z + 1 + j

        @pl.when(below >= 0)
        def _():
            up_copy(below, k).wait_recv()

            @pl.when(z < LINE - 1)
            def _():
                up_copy(below, k).start()

        @pl.when(above < LINE)
        def _():
            down_copy(above, k).wait_recv()

            @pl.when(z > 0)
            def _():
                down_copy(above, k).start()

    def tot_copy(src, far, index, device):
        at = (layer - 1) * src + far
        return remote(
            out_tot.at[src, pl.ds(pl.multiple_of(index * cap, cap), cap)],
            in_tot.at[src, pl.ds(pl.multiple_of(low * cap, cap), cap)],
            tot_send.at[at],
            tot_recv.at[at],
            device,
        )

    def finish_spread(src):
        total = acc[...]
        spread[src] = total.astype(BF16)
        spread_t[src] = total.astype(BF16).T
        sums = jnp.sum(total, axis=1, keepdims=True).astype(jnp.int32)
        lane = lax.broadcasted_iota(jnp.int32, (layer_slots, 128), 1)
        digit = jnp.where(
            lane == 0, sums & 255, jnp.where(lane == 1, (sums >> 8) & 255, jnp.where(lane == 2, sums >> 16, 0))
        )
        out_tot[src] = digit.astype(F32).astype(BF16)
        own = pl.ds(pl.multiple_of(low * cap, cap), cap)
        in_tot[src, own] = out_tot[src, own]
        for far, index, device in place.others("l"):
            tot_copy(src, far, index, device).start()

    def source(which):
        flip = z // 2
        inner = z * (1 - 2 * flip) + (LINE - 1) * flip
        index = ORDER[0][which] * (1 - inner) + ORDER[1][which] * inner
        return index * (1 - 2 * flip) + (LINE - 1) * flip

    def build(which, ticks):
        src = source(which)
        acc[...] = jnp.zeros_like(acc)
        if which > 0:
            far = lax.rem(z - src - 1 + LINE, LINE)
            remote(
                keys.at[src], keys.at[src], key_send.at[0], key_recv.at[far], place.member("z", src)
            ).wait_recv()

        @pl.loop(0, steps)
        def _(t):
            second = t // (steps // 2)
            key = keys[src, :, pl.ds(pl.multiple_of(t * turn, turn), turn)]
            start = edges + (t - second * (steps // 2)) * turn
            pair = keys[src, :, pl.ds(pl.multiple_of(start, turn), turn)]
            weight = (lax.shift_right_logical(pair, second * 16) & 65535).astype(F32).astype(F8)
            child = (key & 65535).astype(jnp.int16)
            slot = (lax.shift_right_logical(key, 16) - z * layer_slots).astype(jnp.int16)
            right = jnp.where(
                lax.broadcasted_iota(jnp.int16, (rows, turn), 0) == child, weight, jnp.zeros((), F8)
            )
            block = 256
            for first in range(0, layer_slots, block):
                ids = lax.broadcasted_iota(jnp.int16, (block, turn), 0) + jnp.asarray(
                    first, jnp.int16
                )
                left = jnp.where(ids == slot, jnp.ones((), F8), jnp.zeros((), F8))
                acc[pl.ds(first, block), :] += dot_nt(left, right)
            run_ticks(t, ticks)

        finish_spread(src)

    def slot_copy(src, k, far, index, device):
        at = (src * CHUNKS + k) * (layer - 1) + far
        return remote(
            out_slots.at[src, k, pl.ds(pl.multiple_of(index * cap, cap), cap)],
            in_slots.at[src, k, pl.ds(pl.multiple_of(low * cap, cap), cap)],
            slot_send.at[at],
            slot_recv.at[at],
            device,
        )

    def piece(src, k):
        out_slots[src, k] = jnp.dot(spread[src], msg[src, k], preferred_element_type=F32).astype(BF16)
        for far, index, device in place.others("l"):
            slot_copy(src, k, far, index, device).start()
        own = pl.ds(pl.multiple_of(low * cap, cap), cap)
        in_slots[src, k, own] = out_slots[src, k, own]

    def pick(src, k):
        for far, index, device in place.others("l"):
            slot_copy(src, k, far, index, device).wait_recv()
        num[k] += jnp.dot(picker[src], in_slots[src, k], preferred_element_type=F32)

    def make_picker():
        @pl.loop(0, LINE)
        def _(src):
            at = pl.ds(pl.multiple_of(src * layer_slots, layer_slots), layer_slots)
            ids = lax.broadcasted_iota(jnp.int32, (rows, layer_slots), 0)
            picker[src] = jnp.where(ids == targets_ref[:, at], 1.0, 0.0).astype(BF16)

        num[...] = jnp.zeros_like(num)

    def comb_piece(i):
        for j in range(i, 2 * width // rows, CHUNKS):
            cast(5 + j, comb_b, j * rows)

    def self_part():
        @pl.loop(0, CHUNKS)
        def _(k):
            at = pl.ds(pl.multiple_of(k * part, part), part)
            zpre[:, at] = (
                jnp.dot(hid[...], comb_b[0:width, at], preferred_element_type=F32)
                + cbias_ref[:, at]
            )

    def results():
        store(hid, hid_h)
        store(pre, pre_h)
        store(featb, featb_h)
        store(board_b, board_b_h)
        store(neigh_b, neigh_b_h)
        store(comb_b.at[pl.ds(0, width)], comb1_b_h)
        store(spread_t, st_h)

    def totals():
        digits = jnp.zeros((rows, 128), F32)
        for src in range(LINE):
            for far, index, device in place.others("l"):
                tot_copy(src, far, index, device).wait_recv()
            digits += jnp.dot(picker[src], in_tot[src], preferred_element_type=F32)
        lane = lax.broadcasted_iota(jnp.int32, (rows, 128), 1)
        worth = jnp.where(
            lane == 0, 1.0, jnp.where(lane == 1, 256.0, jnp.where(lane == 2, 65536.0, 0.0))
        )
        den_ref[...] = jnp.broadcast_to(
            1.0 + jnp.sum(digits * worth, axis=1, keepdims=True), (rows, 128)
        )

    def neighbours(k):
        at = pl.ds(k * part, part)
        agg[:, at] = (num[k] / den_ref[:, 0:1]).astype(BF16)
        if k < CHUNKS - 1:

            @pl.loop(0, CHUNKS)
            def _(n):
                to = pl.ds(pl.multiple_of(n * part, part), part)
                zpre[:, to] += jnp.dot(
                    agg[:, at], comb_b[pl.ds(width + k * part, part), to], preferred_element_type=F32
                )

    def step_share(stage):
        if stage in (1, 2):
            share.start(stage, share.finish(stage - 1))
        elif stage == 3:
            boards = share.finish(2)
            scale_ref[...] = 1.0 / (width * (1.0 + boards))

    acts = {
        "P": step_share,
        "m": message,
        "f": forward,
        "p": lambda which, k: piece(source(which), k),
        "i": lambda which, k: pick(source(which), k),
        "G": lambda _: make_picker(),
        "D": comb_piece,
        "X": lambda _: self_part(),
        "R": lambda _: results(),
        "d": lambda _: totals(),
        "a": neighbours,
    }

    def act(step):
        acts[step[0]](*(int(c) for c in step[1:]))

    run_order(FORWARD, steps, build, act)
    neighbours(CHUNKS - 1)
    load_cot.wait()
    den = den_ref[:, 0:1]
    scale = scale_ref[0:1, 0:1]
    last = pl.ds(width - part, part)

    def dense(k, carry):
        square, along = carry
        at = pl.ds(pl.multiple_of(k * part, part), part)
        value = zpre[:, at] + jnp.dot(
            agg[:, last], comb_b[pl.ds(2 * width - part, part), at], preferred_element_type=F32
        )
        zpre[:, at] = value
        out = gelu(value)
        zval[:, at] = out
        square += jnp.sum(out * out, axis=1, keepdims=True)
        along += jnp.sum(out * cot[:, at], axis=1, keepdims=True)
        return square, along

    zero = jnp.zeros((rows, 1), F32)
    square, along = lax.fori_loop(0, CHUNKS, dense, (zero, zero))
    inverse = lax.rsqrt(square + 1e-06)
    along = along * inverse
    push = jnp.where(mask > 0.5, 2.0 * scale, 0.0)
    stats_ref[...] = jnp.concatenate(
        [
            jnp.full((8, 128), jnp.sum(jnp.where(mask > 0.5, square, 0.0))),
            jnp.broadcast_to(scale, (8, 128)),
        ],
        axis=0,
    )

    @pl.loop(0, CHUNKS)
    def _(k):
        at = pl.ds(pl.multiple_of(k * part, part), part)
        out = zval[:, at]
        emb = out * inverse
        grad = inverse * (cot[:, at] - emb * along) + push * out
        dz[:, at] = (grad * gelu_slope(zpre[:, at])).astype(BF16)
        zval[:, at] = emb

    store(zval, embed_h)
    store(dz, dz_h)
    store(agg, agg_h)

    @pl.loop(0, CHUNKS)
    def _(k):
        at = pl.ds(pl.multiple_of(k * part, part), part)
        back = dot_nt(dz[...], comb_b[pl.ds(pl.multiple_of(width + k * part, part), part), :])
        dnum[:, at] = (back / den).astype(BF16)

    store(dnum, dnum_h)

    for far, _, device in place.others("z"):
        key_copy(far, device).wait_send()

    @pl.loop(0, LINE * CHUNKS)
    def _(i):
        src = i // CHUNKS
        k = lax.rem(i, CHUNKS)

        @pl.when(jnp.logical_and(src <= z, z < LINE - 1))
        def _():
            up_copy(src, k).wait_send()

        @pl.when(jnp.logical_and(src >= z, z > 0))
        def _():
            down_copy(src, k).wait_send()

        for far, index, device in place.others("l"):
            slot_copy(src, k, far, index, device).wait_send()

    for src in range(LINE):
        for far, index, device in place.others("l"):
            tot_copy(src, far, index, device).wait_send()
    for copy in stores:
        copy.wait()


def forward_pass(n_nodes, n_grp, feats, mask, edges_of, targets, board, neigh, nbias, comb, cbias, cot):
    rows, width = feats.shape
    edges = edges_of[0].shape[1]
    layer = n_nodes // LINE
    layer_slots = targets.shape[1] // LINE
    part = width // CHUNKS
    dma = pltpu.SemaphoreType.DMA
    n_stage = 5
    big = pl.BlockSpec(memory_space=pl.ANY)
    small = pl.BlockSpec(memory_space=pltpu.VMEM)

    def hbm(shape, dtype):
        return jax.ShapeDtypeStruct(shape, dtype)

    return pl.pallas_call(
        functools.partial(forward_kernel, n_nodes, n_grp),
        out_shape=[
            hbm((rows, width), F32),
            hbm((rows, width), BF16),
            hbm((rows, width), F32),
            hbm((rows, width), BF16),
            hbm((width, width), BF16),
            hbm((width, width), BF16),
            hbm((width, width), BF16),
            hbm((LINE, rows, layer_slots), BF16),
            hbm((rows, width), BF16),
            hbm((rows, width), BF16),
            hbm((rows, width), BF16),
            hbm((16, 128), F32),
        ],
        in_specs=[big] + [small] * 5 + [big, big, small, big, small, big],
        out_specs=[big] * 11 + [small],
        scratch_shapes=[
            pltpu.VMEM((n_stage, rows, width), F32),
            pltpu.VMEM((rows, width), BF16),
            pltpu.VMEM((rows, width), BF16),
            pltpu.VMEM((rows, width), F32),
            pltpu.VMEM((width, width), BF16),
            pltpu.VMEM((width, width), BF16),
            pltpu.VMEM((2 * width, width), BF16),
            pltpu.VMEM((LINE, 1, edges + edges // 2), jnp.int32),
            pltpu.VMEM((LINE, CHUNKS, rows, part), BF16),
            pltpu.VMEM((layer_slots, rows), F32),
            pltpu.VMEM((LINE, layer_slots, rows), BF16),
            pltpu.VMEM((LINE, rows, layer_slots), BF16),
            pltpu.VMEM((LINE, CHUNKS, layer_slots, part), BF16),
            pltpu.VMEM((LINE, CHUNKS, layer_slots, part), BF16),
            pltpu.VMEM((LINE, layer_slots, 128), BF16),
            pltpu.VMEM((LINE, layer_slots, 128), BF16),
            pltpu.VMEM((LINE, rows, layer_slots), BF16),
            pltpu.VMEM((CHUNKS, rows, part), F32),
            pltpu.VMEM((rows, width), F32),
            pltpu.VMEM((rows, width), F32),
            pltpu.VMEM((rows, width), F32),
            pltpu.VMEM((rows, width), BF16),
            pltpu.VMEM((rows, width), BF16),
            pltpu.VMEM((rows, width), BF16),
            pltpu.VMEM((rows, 128), F32),
            pltpu.VMEM((8, 128), F32),
            pltpu.VMEM((layer, 8, 128), F32),
            pltpu.VMEM((LINE, 8, 128), F32),
            pltpu.VMEM((n_grp, 8, 128), F32),
            dma((n_stage + 1,)),
            dma((11,)),
            dma((LINE - 1,)),
            dma((LINE - 1,)),
            dma((LINE * CHUNKS,)),
            dma((LINE * CHUNKS,)),
            dma((LINE * CHUNKS,)),
            dma((LINE * CHUNKS * (layer - 1),)),
            dma((LINE * CHUNKS * (layer - 1),)),
            dma((LINE * (layer - 1),)),
            dma((LINE * (layer - 1),)),
            dma((share_sems(n_nodes, n_grp),)),
            dma((share_sems(n_nodes, n_grp),)),
        ],
        compiler_params=pltpu.CompilerParams(
            vmem_limit_bytes=60 * MIB, collective_id=2, has_side_effects=True
        ),
        name="forward_pass",
    )(feats, mask, *edges_of, targets, board, neigh, nbias, comb, cbias, cot)


def add_into(target, first, count, columns, parts, step=16):
    @pl.loop(0, count // step)
    def _(i):
        at = pl.ds(pl.multiple_of(first + i * step, step), step)
        total = target[at, columns].astype(F32)
        for part in parts:
            total += part[pl.ds(pl.multiple_of(i * step, step), step), :].astype(F32)
        target[at, columns] = total.astype(target.dtype)


def reduce_job(place, order, grad, region, arrive, land, last, send, recv, free, base):
    first, rows, left, columns = region
    half = columns // 2
    core = place.at["c"]
    mine = pl.ds(pl.multiple_of(left + core * half, half), half)
    theirs = pl.ds(pl.multiple_of(left + (1 - core) * half, half), half)
    mate = place.member("c", 1 - core)
    block = pl.ds(first, rows)
    sems = iter(range(base, base + send.shape[0]))

    def lay(src, dst, device):
        sem = next(sems)
        return remote(src, dst, send.at[sem], recv.at[sem], device)

    across = lay(grad.at[block, theirs], arrive, mate)
    down = []
    begin, length, used = first, rows, 0
    for axis in order:
        length //= place.size[axis]
        copies, parts, devices = [], [], []
        for far, index, device in place.others(axis):
            start = pl.multiple_of(begin + index * length, 16)
            slot = land.at[pl.ds(used, length)]
            used += length
            copies.append(lay(grad.at[pl.ds(start, length), mine], slot, device))
            parts.append(slot)
            devices.append(device)
        parent = begin
        begin = pl.multiple_of(begin + place.at[axis] * length, 16)
        down.append((axis, parent, begin, length, copies, parts, devices))
    axis, parent, begin, length, _, _, devices = down[-1]
    here = pl.ds(pl.multiple_of(place.at[axis] * length, 16), length)
    whole = pl.ds(pl.multiple_of(parent, 16), length * place.size[axis])
    end = [lay(last.at[here], last.at[here], device) for device in devices]
    up = []
    for stage in range(len(down) - 1, 0, -1):
        axis, _, start, piece, _, _, devices = down[stage - 1]
        own = grad.at[pl.ds(start, piece), mine]
        up.append((stage, len(devices), [lay(own, own, device) for device in devices]))
    own = grad.at[block, mine]
    back = lay(own, own, mate)
    yield

    def release(at, devices):
        for device in devices:
            pl.semaphore_signal(free.at[base + at], inc=1, device_id=device, device_id_type=MESH)

    across.start()
    yield
    across.wait()
    release(0, [mate])
    add_into(grad, first, rows, mine, [arrive])
    for stage, (_, _, begin, length, copies, parts, devices) in enumerate(down):
        for copy in copies:
            copy.start()
        yield
        for copy in copies:
            copy.wait()
        if stage < len(down) - 1:
            release(stage + 1, devices)
        add_into(grad, begin, length, mine, parts)
    last[here] = grad[pl.ds(begin, length), mine]
    for copy in end:
        copy.start()
    yield
    for copy in end:
        copy.wait()
    grad[whole, mine] = last[pl.ds(0, whole.size)]
    for stage, count, copies in up:
        pl.semaphore_wait(free.at[base + stage], count)
        for copy in copies:
            copy.start()
        yield
        for copy in copies:
            copy.wait()
    pl.semaphore_wait(free.at[base], 1)
    back.start()
    yield
    back.wait()


def job_sems(n_nodes, n_grp):
    return 2 * (1 + (n_nodes // LINE // 2 - 1) + (LINE - 1) + (n_grp - 1))


AHEAD = 2
BEHIND = CHUNKS - AHEAD
JOBS = {
    kind[0] + str(i): kind + str(i) for kind, count in (("comb", 4), ("neigh", 4), ("board", 4)) for i in range(count)
}
BACKWARD = (
    "l0", "A1", "B2", "A0", "G0", "c0", "c1", "L2", "W0", "Y10", "c3", "B3", "f01", "c2", "c0",
    "32", "c3", "c1", "Y11", "f00", "q01", "Y12", "L1", "33", "L3", "c2", "22", "Y13", "f11",
    "Y14", "12", "Z1", "q11", "Y20", "f10", "c0", "q00", "Y21", "23", "c1", "q10", "c2", "Y22",
    "q20", "q21", "13", "Y23", "Y24", "c0", "S0", "Z2", "O2", "c3", "f21", "c1", "f20", "n2", "O3",
    "n3", "c0", "Y30", "n2", "q31", "c1", "Y31", "c2", "n3", "Y32", "c0", "q30", "c1", "Y33", "c3",
    "n3", "n2", "Y34", "c2", "c0", "c1", "Z3", "O1", "n1", "c3", "O0", "n0", "n1", "c2", "n3",
    "E0", "H1", "b2", "c3", "n2", "b3", "n0", "n3", "H0", "b1", "b2", "b3", "n1", "b0", "b1", "n0",
    "n3", "b0", "n1", "P0", "b2", "c0", "F0", "b1", "n0", "n2", "c2", "b3", "n1", "b0", "b1", "c3",
    "b3", "n0", "b0", "n1", "b2", "n2", "c0", "b3", "n3", "b1", "b0", "b3", "n2", "c2", "b2", "n0",
    "b1", "c1", "n1", "b3", "n3", "b0", "P1", "b2", "c3", "c1", "b1", "b0", "b2", "n3", "n2", "n0",
    "b3", "n1", "b0", "b1", "n0", "c2", "n2", "P2", "b2", "n0", "b1", "b2", "b0", "n1", "P3", "c3",
    "b3",
)


def gradient_regions(n_nodes, n_grp, width):
    pieces = n_nodes * n_grp // 2
    x_first, y_first = ("x", "y", "z"), ("y", "x", "z")
    regions = {}
    count = max(1, min(4, 2 * width // (16 * pieces)))
    n_rows = 2 * width // count
    for j in range(count):
        regions[f"comb{j}"] = (j * n_rows, n_rows, 0, width, y_first if j % 2 else x_first)
    if width % (16 * pieces) == 0:
        part = width // CHUNKS
        for k in range(CHUNKS):
            regions[f"neigh{k}"] = (2 * width, width, k * part, part, x_first if k % 2 else y_first)
        count = max(1, min(4, width // (16 * pieces)))
        n_rows = width // count
        for j in range(count):
            order = (x_first, y_first, x_first, ("z", "y", "x"))[j]
            regions[f"board{j}"] = (3 * width + j * n_rows, n_rows, 0, width, order)
    else:
        regions["board0"] = (2 * width, 2 * width, 0, width, x_first)
    return regions


def backward_kernel(
    n_nodes,
    n_grp,
    mask_ref,
    targets_ref,
    stats_ref,
    place_h,
    child_h,
    weight_h,
    hid_h,
    pre_h,
    featb_h,
    board_b_h,
    neigh_b_h,
    comb1_b_h,
    st_h,
    dnum_h,
    dz_h,
    agg_h,
    gfeat_h,
    summed_h,
    small_ref,
    hid,
    pre,
    featb,
    board_b,
    neigh_b,
    comb1_b,
    spread_t,
    dnum,
    dz,
    agg,
    picker_t,
    picker_l,
    lines,
    edge_place,
    edge_child,
    edge_weight,
    acc,
    own_t,
    parents,
    out_slots,
    in_slots,
    chain,
    tmp,
    dpre,
    dh,
    grad,
    arrive,
    land,
    gather,
    share_l,
    share_z,
    share_x,
    small,
    load_sem,
    store_sem,
    slot_send,
    slot_recv,
    up_send,
    down_send,
    chain_recv,
    line_send,
    line_recv,
    parent_up,
    parent_down,
    parent_recv,
    job_send,
    job_recv,
    job_free,
    share_send,
    share_recv,
):
    place = Place(n_nodes, n_grp)
    z, low = place.at["z"], place.at["l"]
    layer = place.size["l"]
    rows, width = hid.shape
    layer_slots = spread_t.shape[2]
    cap = layer_slots // layer
    part = width // CHUNKS

    loads = {}
    for i, (name, src, dst) in enumerate(
        (
            ("dnum", dnum_h, dnum),
            ("hid", hid_h, hid),
            ("agg", agg_h, agg),
            ("dz", dz_h, dz),
            ("spread_t", st_h, spread_t),
            ("comb1_b", comb1_b_h, comb1_b),
            ("pre", pre_h, pre),
            ("neigh_b", neigh_b_h, neigh_b),
            ("featb", featb_h, featb),
            ("board_b", board_b_h, board_b),
            ("place", place_h, edge_place),
            ("child", child_h, edge_child),
            ("weight", weight_h, edge_weight),
        )
    ):
        loads[name] = pltpu.make_async_copy(src, dst, load_sem.at[i])
        loads[name].start()
    def make_pickers():
        @pl.loop(0, LINE)
        def _(src):
            at = pl.ds(pl.multiple_of(src * layer_slots, layer_slots), layer_slots)
            ids = lax.broadcasted_iota(jnp.int32, (rows, layer_slots), 0)
            picker_t[src] = jnp.where(ids == targets_ref[:, at], 1.0, 0.0).astype(BF16).T

    barrier(place, ("l", "z", "x"), make_pickers)
    stores = []

    def store(src, dst):
        copy = pltpu.make_async_copy(src, dst, store_sem.at[len(stores)])
        copy.start()
        stores.append(copy)

    mask = column_of(mask_ref) > 0.5

    def source(which):
        flip = z // 2
        inner = z * (1 - 2 * flip) + (LINE - 1) * flip
        index = ORDER[0][which] * (1 - inner) + ORDER[1][which] * inner
        return index * (1 - 2 * flip) + (LINE - 1) * flip

    def cols(k):
        return pl.ds(pl.multiple_of(k * part, part), part)

    def slot_copy(dst, k, far, index, device):
        at = (dst * CHUNKS + k) * (layer - 1) + far
        return remote(
            out_slots.at[dst, k, pl.ds(pl.multiple_of(index * cap, cap), cap)],
            in_slots.at[dst, k, pl.ds(pl.multiple_of(low * cap, cap), cap)],
            slot_send.at[at],
            slot_recv.at[at],
            device,
        )

    def back(dst, k):
        out_slots[dst, k] = jnp.dot(
            picker_t[dst], dnum[:, cols(k)], preferred_element_type=F32
        ).astype(BF16)
        for far, index, device in place.others("l"):
            slot_copy(dst, k, far, index, device).start()
        own = pl.ds(pl.multiple_of(low * cap, cap), cap)
        in_slots[dst, k, own] = out_slots[dst, k, own]

    def child_sums(dst, k):
        for far, index, device in place.others("l"):
            slot_copy(dst, k, far, index, device).wait_recv()
        tmp[...] = jnp.dot(spread_t[dst], in_slots[dst, k], preferred_element_type=F32)

    def up_copy(dst, k):
        k = k - AHEAD
        at = dst * BEHIND + k
        return remote(
            chain.at[dst, k],
            chain.at[dst, k],
            up_send.at[at],
            chain_recv.at[at],
            place.member("z", z + 1),
        )

    def down_copy(dst, k, last):
        slot = LINE if last else dst
        k = k - AHEAD
        return remote(
            chain.at[dst, k],
            chain.at[slot, k],
            down_send.at[dst * BEHIND + k],
            chain_recv.at[slot * BEHIND + k],
            place.member("z", z - 1),
        )

    def arrived(slot, k):
        k = k - AHEAD
        remote(
            chain.at[slot, k],
            chain.at[slot, k],
            up_send.at[0],
            chain_recv.at[slot * BEHIND + k],
            place.member("z", lax.rem(z + 1, LINE)),
        ).wait_recv()

    def hand_on(dst, k):
        child_sums(dst, k)

        @pl.when(dst > z)
        def _():
            @pl.when(z > 0)
            def _():
                up_copy(dst, k).wait_recv()
                chain[dst, k - AHEAD] = (chain[dst, k - AHEAD].astype(F32) + tmp[...]).astype(BF16)

            @pl.when(z == 0)
            def _():
                chain[dst, k - AHEAD] = tmp[...].astype(BF16)

            up_copy(dst, k).start()

        @pl.when(dst < z)
        def _():
            @pl.when(z < LINE - 1)
            def _():
                down_copy(dst, k, False).wait_recv()
                chain[dst, k - AHEAD] = (chain[dst, k - AHEAD].astype(F32) + tmp[...]).astype(BF16)

            @pl.when(z == LINE - 1)
            def _():
                chain[dst, k - AHEAD] = tmp[...].astype(BF16)

            @pl.when(dst == z - 1)
            def _():
                down_copy(dst, k, True).start()

            @pl.when(dst < z - 1)
            def _():
                down_copy(dst, k, False).start()

    regions = gradient_regions(n_nodes, n_grp, width)
    per_job = job_sems(n_nodes, n_grp)

    def job(name):
        first, n_rows, left, columns, order = regions[name]
        rows_at, cols_at = pl.ds(first, n_rows), pl.ds(left, columns)
        land_at = pl.ds(left // 2, columns // 2)
        yield from reduce_job(
            place,
            order,
            grad,
            (first, n_rows, left, columns),
            arrive.at[rows_at, land_at],
            land.at[rows_at, land_at],
            gather.at[pl.ds(first // 4, n_rows // 4), land_at],
            job_send,
            job_recv,
            job_free,
            list(regions).index(name) * per_job,
        )
        store(grad.at[rows_at, cols_at], summed_h.at[rows_at, cols_at])

    jobs = {name: job(name) for name in regions}
    for lay_out in jobs.values():
        next(lay_out)

    def step_job(name, last=False):
        if name in jobs and (last or name != "board0" or "board3" in regions):
            try:
                next(jobs[name])
            except StopIteration:
                del jobs[name]

    loads["dnum"].wait()

    def back_all(k):
        for which in (3, 2, 1, 0):
            back(source(which), k)

    def comb_grad(left, first):
        @pl.loop(0, CHUNKS)
        def _(k):
            grad[pl.ds(first, width), cols(k)] = dot_tn(left[...], dz[:, cols(k)]).astype(BF16)

    def line_targets():
        lines[z] = targets_ref[:, pl.ds(pl.multiple_of(z * layer_slots, layer_slots), layer_slots)]
        for far, index, device in place.others("z"):
            at = pl.ds(pl.multiple_of(index * layer_slots, layer_slots), layer_slots)
            remote(
                targets_ref.at[:, at], lines.at[z], line_send.at[far], line_recv.at[far], device
            ).start()

    def line_picker(which):
        src = source(which)
        far = lax.rem(z - src - 1 + LINE, LINE)
        remote(
            lines.at[src], lines.at[src], line_send.at[0], line_recv.at[far], place.member("z", src)
        ).wait_recv()
        ids = lax.broadcasted_iota(jnp.int32, (rows, layer_slots), 0)
        picker_l[src] = jnp.where(ids == lines[src], 1.0, 0.0).astype(BF16).T

    def parent_copy(src, k, sems, to):
        piece = parents.at[src, k]
        at = src * AHEAD + k
        return remote(piece, piece, sems.at[at], parent_recv.at[at], place.member("z", to))

    def parent_send(k):
        parents[z, k] = dnum[:, cols(k)]

        @pl.when(z < LINE - 1)
        def _():
            parent_copy(z, k, parent_up, z + 1).start()

        @pl.when(z > 0)
        def _():
            parent_copy(z, k, parent_down, z - 1).start()

    def parent_forward(j, k):
        below = z - 1 - j
        above = z + 1 + j

        @pl.when(below >= 0)
        def _():
            parent_copy(below, k, parent_up, z + 1).wait_recv()

            @pl.when(z < LINE - 1)
            def _():
                parent_copy(below, k, parent_up, z + 1).start()

        @pl.when(above < LINE)
        def _():
            parent_copy(above, k, parent_down, z - 1).wait_recv()

            @pl.when(z > 0)
            def _():
                parent_copy(above, k, parent_down, z - 1).start()

    def parent_slots(which, k):
        src = source(which)
        choose = picker_t[z] if which == 0 else picker_l[src]
        out_slots[src, k] = jnp.dot(choose, parents[src, k], preferred_element_type=F32).astype(
            BF16
        )
        for far, index, device in place.others("l"):
            slot_copy(src, k, far, index, device).start()
        own = pl.ds(pl.multiple_of(low * cap, cap), cap)
        in_slots[src, k, own] = out_slots[src, k, own]

    edges = edge_place.shape[1]
    turn = math.gcd(edges, 2560)
    steps = edges // turn

    def build_own(which, ticks):
        src = source(which)
        if which == 1:
            for name in ("place", "child", "weight"):
                loads[name].wait()
        acc[...] = jnp.zeros_like(acc)

        @pl.loop(0, steps)
        def _(t):
            at = pl.ds(pl.multiple_of(t * turn, turn), turn)
            slot = (edge_place[:, at] - src * layer_slots).astype(jnp.int16)
            child = edge_child[:, at].astype(jnp.int16)
            weight = edge_weight[:, at].astype(F32).astype(F8)
            right = jnp.where(
                lax.broadcasted_iota(jnp.int16, (layer_slots, turn), 0) == slot,
                jnp.ones((), F8),
                jnp.zeros((), F8),
            )
            block = 256
            for first in range(0, rows, block):
                ids = lax.broadcasted_iota(jnp.int16, (block, turn), 0) + jnp.asarray(
                    first, jnp.int16
                )
                left = jnp.where(ids == child, weight, jnp.zeros((), F8))
                acc[pl.ds(first, block), :] += dot_nt(left, right)
            run_ticks(t, ticks)

        own_t[src] = acc[...].astype(BF16)

    def own(k):
        if k < AHEAD:
            for which in range(LINE):
                src = source(which)
                for far, index, device in place.others("l"):
                    slot_copy(src, k, far, index, device).wait_recv()
                weights = spread_t[z] if which == 0 else own_t[src]
                value = jnp.dot(weights, in_slots[src, k], preferred_element_type=F32)
                if which == 0:
                    tmp[...] = value
                else:
                    tmp[...] += value
        else:
            child_sums(z, k)

            @pl.when(z > 0)
            def _():
                arrived(z, k)
                tmp[...] += chain[z, k - AHEAD].astype(F32)

            @pl.when(z < LINE - 1)
            def _():
                arrived(LINE, k)
                tmp[...] += chain[LINE, k - AHEAD].astype(F32)

        down = (tmp[...] * gelu_slope(pre[:, cols(k)])).astype(BF16)
        dpre[:, cols(k)] = down
        small[0:1, cols(k)] = jnp.sum(down.astype(F32), axis=0, keepdims=True)
        dh[...] += dot_nt(down, neigh_b[:, cols(k)])

    def neigh_grad(k):
        grad[pl.ds(2 * width, width), cols(k)] = dot_tn(hid[...], dpre[:, cols(k)]).astype(BF16)

    def comb_grads():
        for name in ("hid", "agg", "dz", "comb1_b"):
            loads[name].wait()
        comb_grad(hid, 0)
        comb_grad(agg, width)

    def self_part():
        small[...] = jnp.zeros_like(small)
        small[1:2, :] = jnp.sum(dz[...].astype(F32), axis=0, keepdims=True)
        small[2:3, :] = jnp.broadcast_to(stats_ref[0:1, 0:1], (1, width))

        @pl.loop(0, CHUNKS)
        def _(k):
            dh[:, cols(k)] = dot_nt(dz[...], comb1_b[cols(k), :])

        for name in ("pre", "neigh_b", "featb", "board_b"):
            loads[name].wait()

    def own_and_grad(k):
        own(k)
        neigh_grad(k)

    def end_of_line():
        last = dh[...].astype(BF16)
        dpre[...] = jnp.where(mask, last, jnp.zeros_like(last))
        pre[...] = last.astype(F32)

    def board_grad(i):
        half = width // 2
        grad[pl.ds(3 * width + i * half, half), :] = dot_tn(
            featb[:, i * half : (i + 1) * half], dpre[...]
        ).astype(BF16)

    def feature_grad():
        @pl.loop(0, CHUNKS)
        def _(k):
            pre[:, cols(k)] = jnp.where(
                mask, dot_nt(dpre[...], board_b[cols(k), :]), pre[:, cols(k)]
            )

        store(pre, gfeat_h)

    share = Share(place, (share_l, share_z, share_x), share_send, share_recv)

    def step_share(stage):
        if stage == 0:
            share.start(0, small[...])
        elif stage < 3:
            share.start(stage, share.finish(stage - 1))
        else:
            row = lax.broadcasted_iota(jnp.int32, small_ref.shape, 0)
            small_ref[...] = share.finish(2) * jnp.where(row == 2, stats_ref[8:9, 0:1], 1.0)

    acts = {
        "l": lambda _: line_targets(),
        "L": line_picker,
        "A": parent_send,
        "f": parent_forward,
        "q": parent_slots,
        "B": back_all,
        "W": lambda _: loads["spread_t"].wait(),
        "G": lambda _: comb_grads(),
        "S": lambda _: self_part(),
        "O": own_and_grad,
        "E": lambda _: end_of_line(),
        "H": board_grad,
        "F": lambda _: feature_grad(),
        "P": step_share,
        "3": lambda k: hand_on(source(3), k),
        "2": lambda k: hand_on(source(2), k),
        "1": lambda k: hand_on(source(1), k),
    }
    def act(name):
        if name in JOBS:
            step_job(JOBS[name])
        else:
            acts[name[0]](*(int(c) for c in name[1:]))

    run_order(BACKWARD, steps, build_own, act)
    while jobs:
        for name in list(jobs):
            step_job(name, last=True)

    for far, index, device in place.others("z"):
        remote(lines.at[z], lines.at[z], line_send.at[far], line_recv.at[far], device).wait_send()

    @pl.loop(0, LINE * CHUNKS)
    def _(i):
        dst = i // CHUNKS
        k = lax.rem(i, CHUNKS)

        @pl.when(k < AHEAD)
        def _():
            @pl.when(jnp.logical_and(dst <= z, z < LINE - 1))
            def _():
                parent_copy(dst, k, parent_up, z + 1).wait_send()

            @pl.when(jnp.logical_and(dst >= z, z > 0))
            def _():
                parent_copy(dst, k, parent_down, z - 1).wait_send()

        @pl.when(k >= AHEAD)
        def _():
            @pl.when(dst > z)
            def _():
                up_copy(dst, k).wait_send()

            @pl.when(dst < z)
            def _():
                down_copy(dst, k, False).wait_send()

        for far, index, device in place.others("l"):
            slot_copy(dst, k, far, index, device).wait_send()

    for copy in stores:
        copy.wait()


def backward_pass(n_nodes, n_grp, mask, targets, stats, edges_of, hid, pre, featb, board_b, neigh_b, comb1_b, st, dnum, dz, agg):
    rows, width = hid.shape
    edges = edges_of[0].shape[1]
    layer = n_nodes // LINE
    layer_slots = st.shape[2]
    part = width // CHUNKS
    n_rows = 4 * width
    count = len(gradient_regions(n_nodes, n_grp, width))
    dma = pltpu.SemaphoreType.DMA
    big = pl.BlockSpec(memory_space=pl.ANY)
    vmem = pl.BlockSpec(memory_space=pltpu.VMEM)
    sems = count * job_sems(n_nodes, n_grp)
    pieces = LINE * CHUNKS
    return pl.pallas_call(
        functools.partial(backward_kernel, n_nodes, n_grp),
        out_shape=[
            jax.ShapeDtypeStruct((rows, width), F32),
            jax.ShapeDtypeStruct((n_rows, width), BF16),
            jax.ShapeDtypeStruct((8, width), F32),
        ],
        in_specs=[vmem, vmem, vmem] + [big] * 13,
        out_specs=[big, big, vmem],
        scratch_shapes=[
            pltpu.VMEM((rows, width), BF16),
            pltpu.VMEM((rows, width), F32),
            pltpu.VMEM((rows, width), BF16),
            pltpu.VMEM((width, width), BF16),
            pltpu.VMEM((width, width), BF16),
            pltpu.VMEM((width, width), BF16),
            pltpu.VMEM((LINE, rows, layer_slots), BF16),
            pltpu.VMEM((rows, width), BF16),
            pltpu.VMEM((rows, width), BF16),
            pltpu.VMEM((rows, width), BF16),
            pltpu.VMEM((LINE, layer_slots, rows), BF16),
            pltpu.VMEM((LINE, layer_slots, rows), BF16),
            pltpu.VMEM((LINE, 1, layer_slots), jnp.int32),
            pltpu.VMEM((1, edges), jnp.int32),
            pltpu.VMEM((1, edges), jnp.int32),
            pltpu.VMEM((1, edges), jnp.int32),
            pltpu.VMEM((rows, layer_slots), F32),
            pltpu.VMEM((LINE, rows, layer_slots), BF16),
            pltpu.VMEM((LINE, AHEAD, rows, part), BF16),
            pltpu.VMEM((LINE, CHUNKS, layer_slots, part), BF16),
            pltpu.VMEM((LINE, CHUNKS, layer_slots, part), BF16),
            pltpu.VMEM((LINE + 1, BEHIND, rows, part), BF16),
            pltpu.VMEM((rows, part), F32),
            pltpu.VMEM((rows, width), BF16),
            pltpu.VMEM((rows, width), F32),
            pltpu.VMEM((n_rows, width), BF16),
            pltpu.VMEM((n_rows, width // 2), BF16),
            pltpu.VMEM((n_rows, width // 2), BF16),
            pltpu.VMEM((n_rows // 4, width // 2), BF16),
            pltpu.VMEM((layer, 8, width), F32),
            pltpu.VMEM((LINE, 8, width), F32),
            pltpu.VMEM((n_grp, 8, width), F32),
            pltpu.VMEM((8, width), F32),
            dma((13,)),
            dma((count + 1,)),
            dma((pieces * (layer - 1),)),
            dma((pieces * (layer - 1),)),
            dma((LINE * BEHIND,)),
            dma((LINE * BEHIND,)),
            dma(((LINE + 1) * BEHIND,)),
            dma((LINE - 1,)),
            dma((LINE - 1,)),
            dma((LINE * AHEAD,)),
            dma((LINE * AHEAD,)),
            dma((LINE * AHEAD,)),
            dma((sems,)),
            dma((sems,)),
            pltpu.SemaphoreType.REGULAR((sems,)),
            dma((share_sems(n_nodes, n_grp),)),
            dma((share_sems(n_nodes, n_grp),)),
        ],
        compiler_params=pltpu.CompilerParams(
            vmem_limit_bytes=63 * MIB, collective_id=3, has_side_effects=True
        ),
        name="backward_pass",
    )(mask, targets, stats, *edges_of, hid, pre, featb, board_b, neigh_b, comb1_b, st, dnum, dz, agg)


def unpack_kernel(
    rows, joined, small_ref, comb, neigh, board, nbias_ref, cbias_ref, penalty_ref, low, wide, load_sem, store_sem
):
    width = joined.shape[1]
    blocks = joined.shape[0] // rows

    def load(i):
        at = pl.ds(i * rows, rows)
        return pltpu.make_async_copy(joined.at[at], low.at[at], load_sem.at[i])

    def store(i):
        first = i * rows
        if first < 2 * width:
            target = comb.at[pl.ds(first, rows)]
        elif first < 3 * width:
            target = neigh.at[pl.ds(first - 2 * width, rows)]
        else:
            target = board.at[pl.ds(first - 3 * width, rows)]
        return pltpu.make_async_copy(wide.at[pl.ds(first, rows)], target, store_sem.at[i])

    for i in range(blocks):
        load(i).start()
    nbias_ref[...] = small_ref[0:1, :]
    cbias_ref[...] = small_ref[1:2, :]
    penalty_ref[...] = small_ref[2:3, 0:1]
    for i in range(blocks):
        load(i).wait()

        @pl.loop(0, rows // 32)
        def _(r, i=i):
            at = pl.ds(pl.multiple_of(i * rows + r * 32, 32), 32)
            wide[at, :] = low[at, :].astype(F32)

        store(i).start()
    for i in range(blocks):
        store(i).wait()


def unpack(joined, small):
    n_rows, width = joined.shape
    rows = math.gcd(width, 256)
    big = pl.BlockSpec(memory_space=pl.ANY)
    vmem = pl.BlockSpec(memory_space=pltpu.VMEM)
    dma = pltpu.SemaphoreType.DMA
    return pl.pallas_call(
        functools.partial(unpack_kernel, rows),
        out_shape=[
            jax.ShapeDtypeStruct((2 * width, width), F32),
            jax.ShapeDtypeStruct((width, width), F32),
            jax.ShapeDtypeStruct((width, width), F32),
            jax.ShapeDtypeStruct((1, width), F32),
            jax.ShapeDtypeStruct((1, width), F32),
            jax.ShapeDtypeStruct((1, 1), F32),
        ],
        in_specs=[big, vmem],
        out_specs=[big] * 3 + [vmem] * 3,
        scratch_shapes=[
            pltpu.VMEM((n_rows, width), BF16),
            pltpu.VMEM((n_rows, width), F32),
            dma((n_rows // rows,)),
            dma((n_rows // rows,)),
        ],
        compiler_params=pltpu.CompilerParams(vmem_limit_bytes=60 * MIB),
        name="unpack",
    )(joined, small)


def on_device(
    n_nodes,
    n_grp,
    features,
    type_mask,
    edge_child,
    edge_slot,
    edge_weight,
    recv_rows,
    board_proj,
    neigh_proj,
    neigh_bias,
    combine_proj,
    combine_bias,
    out_cot,
):
    feats = features[0]
    rows, width = feats.shape
    peers = recv_rows.shape[2]
    cap = recv_rows.shape[3]
    slots = peers * cap
    targets = recv_rows[0, 0].reshape(1, slots)
    embed, hidden, pre, featb, pbl, qwl, cwl1, spread_t, dnum, dzb, aggb, stats = forward_pass(
        n_nodes,
        n_grp,
        feats,
        type_mask,
        (edge_slot, edge_child, edge_weight),
        targets,
        board_proj,
        neigh_proj,
        neigh_bias.reshape(1, width),
        combine_proj,
        combine_bias.reshape(1, width),
        out_cot[0],
    )
    grad_feats, summed, small = backward_pass(
        n_nodes,
        n_grp,
        type_mask,
        targets,
        stats,
        (edge_slot, edge_child, edge_weight),
        hidden,
        pre,
        featb,
        pbl,
        qwl,
        cwl1,
        spread_t,
        dnum,
        dzb,
        aggb,
    )
    grad_comb, grad_neigh, grad_board, grad_nbias, grad_cbias, penalty = unpack(summed, small)
    return (
        embed[None],
        penalty[0, 0],
        grad_feats[None],
        grad_board,
        grad_neigh,
        grad_nbias[0],
        grad_comb,
        grad_cbias[0],
    )


def solution(mesh):
    in_specs = (
        P("grp", "nodes", None),
        P("grp", "nodes"),
        P("grp", "nodes"),
        P("grp", "nodes"),
        P("grp", "nodes"),
        P("grp", "nodes", None, None),
        P(),
        P(),
        P(),
        P(),
        P(),
        P("grp", "nodes", None),
    )
    out_specs = (P("grp", "nodes", None), P(), P("grp", "nodes", None), P(), P(), P(), P(), P())
    return jax.shard_map(
        functools.partial(on_device, mesh.shape["nodes"], mesh.shape["grp"]),
        mesh=mesh,
        in_specs=in_specs,
        out_specs=out_specs,
        check_vma=False,
    )
```

```python
import functools
import math

import jax
import jax.numpy as jnp
from jax import lax
from jax.experimental import pallas as pl
from jax.experimental.pallas import tpu as pltpu
from jax.sharding import PartitionSpec as P

HIGH = lax.Precision.HIGHEST
MESH = pl.DeviceIdType.MESH
BF16 = jnp.bfloat16
F32 = jnp.float32
F8 = jnp.float8_e4m3fn
MIB = 2**20


def gelu_tanh(v):
    return jax.nn.gelu(v, approximate=True)


def dot_nt(left, right):
    return lax.dot_general(
        left, right, (((1,), (1,)), ((), ())), preferred_element_type=F32
    )


def dot_tn(left, right):
    return lax.dot_general(
        left, right, (((0,), (0,)), ((), ())), preferred_element_type=F32
    )


LINE = 4
CHUNKS = 4
FAR = 2
FORWARD = (
    "m0", "m1", "m2", "m3", "Y00", "Y01", "Y02", "Y03", "Z0", "p03", "p02", "Y40", "Y41", "Y42",
    "Y43", "g0", "p01", "G0", "f00", "Z4", "Y10", "u3", "Y11", "D0", "p00", "f01", "u2", "Y12",
    "Y13", "f02", "Z1", "p11", "p12", "Y20", "Y21", "v2", "Y22", "p10", "Y23", "f03", "Z2", "p13",
    "f10", "Y30", "D1", "p20", "v3", "f11", "p21", "Y31", "P1", "x2", "Y32", "f12", "p22", "Y33",
    "f20", "Z3", "p30", "D2", "i20", "f21", "R0", "i02", "p32", "i11", "x3", "d0", "f13", "i10",
    "p33", "p31", "i22", "i01", "X0", "D3", "i03", "p23", "i32", "i12", "i21", "w2", "P2", "i33",
    "a2", "i31", "i30", "i00", "P3", "a0", "a1", "i13", "w3", "i23",
)
ORDER = ((0, 1, 2, 3), (1, 2, 0, 3))


class Place:
    def __init__(self, n_nodes, n_grp):
        layer = n_nodes // LINE
        node = lax.axis_index("nodes")
        grp = lax.axis_index("grp")
        self.node, self.grp = node, grp
        self.size = {"l": layer, "c": 2, "y": layer // 2, "z": LINE, "x": n_grp}
        low = lax.rem(node, layer)
        self.at = {"l": low, "c": lax.rem(low, 2), "y": low // 2, "z": node // layer, "x": grp}

    def member(self, axis, index):
        layer = self.size["l"]
        low, line, grp = self.at["l"], self.at["z"], self.at["x"]
        if axis == "l":
            low = index
        elif axis == "c":
            low = self.at["y"] * 2 + index
        elif axis == "y":
            low = index * 2 + self.at["c"]
        elif axis == "z":
            line = index
        else:
            grp = index
        return {"nodes": line * layer + low, "grp": grp}

    def others(self, axis):
        size = self.size[axis]
        for far in range(1, size):
            index = lax.rem(self.at[axis] + far, size)
            yield far - 1, index, self.member(axis, index)


def remote(src, dst, send, recv, device):
    return pltpu.make_async_remote_copy(
        src_ref=src, dst_ref=dst, send_sem=send, recv_sem=recv, device_id=device, device_id_type=MESH
    )


def barrier(place, axes, meanwhile=None):
    sem = pltpu.get_barrier_semaphore()
    count = 0
    for axis in axes:
        for _, _, device in place.others(axis):
            pl.semaphore_signal(sem, inc=1, device_id=device, device_id_type=MESH)
            count += 1
    if meanwhile is not None:
        meanwhile()
    pl.semaphore_wait(sem, count)


def column_of(row_ref):
    row = row_ref[...].astype(F32)
    return jnp.broadcast_to(row, (128, row.shape[1])).T[:, 0:1]


def gelu(v):
    t = jnp.tanh(0.7978845608028654 * (v + 0.044715 * (v * v * v)))
    return v * (0.5 * (1.0 + t))


def gelu_slope(v):
    square = v * v
    t = jnp.tanh(0.7978845608028654 * (v + 0.044715 * (v * square)))
    bend = 0.7978845608028654 * (1.0 + 0.134145 * square)
    return 0.5 * (1.0 + t) + 0.5 * v * (1.0 - t * t) * bend


class Share:
    def __init__(self, place, bufs, send, recv):
        self.place, self.send, self.recv = place, send, recv
        self.stages, base = [], 0
        for axis, buf in zip(("l", "z", "x"), bufs):
            self.stages.append((axis, buf, base))
            base += place.size[axis] - 1

    def start(self, stage, value):
        axis, buf, base = self.stages[stage]
        me = self.place.at[axis]
        buf[me] = value
        for far, _, device in self.place.others(axis):
            remote(
                buf.at[me], buf.at[me], self.send.at[base + far], self.recv.at[base + far], device
            ).start()

    def finish(self, stage):
        axis, buf, base = self.stages[stage]
        me = self.place.at[axis]
        for far, _, device in self.place.others(axis):
            remote(
                buf.at[me], buf.at[me], self.send.at[base + far], self.recv.at[base + far], device
            ).wait()
        total = buf[0]
        for i in range(1, self.place.size[axis]):
            total += buf[i]
        return total


def run_ticks(t, ticks):
    for at, acts in enumerate(ticks):
        if acts:

            @pl.when(t == at)
            def _(acts=acts):
                for act in acts:
                    act()


def run_order(order, steps, build, act):
    ticks = None
    for name in order:
        if name[0] == "Y":
            if ticks is None:
                ticks = [[] for _ in range(steps)]
                marks = sum(other[:2] == name[:2] for other in order)
            now = (int(name[2]) + 1) * steps // marks - 1
        elif name[0] == "Z":
            build(int(name[1]), ticks)
            ticks = None
        elif ticks is not None:
            ticks[max(now, 0)].append(functools.partial(act, name))
        else:
            act(name)


def share_sems(n_nodes, n_grp):
    return (n_nodes // LINE - 1) + (LINE - 1) + max(1, n_grp - 1)


def forward_kernel(
    n_nodes,
    n_grp,
    feats_h,
    mask_ref,
    place_ref,
    child_ref,
    weight_ref,
    targets_ref,
    board_h,
    neigh_h,
    nbias_ref,
    comb_h,
    cbias_ref,
    cot_h,
    embed_h,
    hid_h,
    pre_h,
    featb_h,
    board_b_h,
    neigh_b_h,
    comb1_b_h,
    st_h,
    dnum_h,
    dz_h,
    agg_h,
    stats_ref,
    stage,
    featb,
    hid,
    pre,
    board_b,
    neigh_b,
    comb_b,
    keys,
    msg,
    acc,
    spread,
    spread_t,
    out_slots,
    in_slots,
    out_tot,
    in_tot,
    picker,
    num,
    zval,
    zpre,
    cot,
    agg,
    dz,
    dnum,
    lines,
    far_spread,
    far_picker,
    far_out,
    far_in,
    far_sum,
    end_sum,
    den_ref,
    scale_ref,
    count_l,
    count_z,
    count_x,
    load_sem,
    store_sem,
    key_send,
    key_recv,
    up_send,
    down_send,
    msg_recv,
    slot_send,
    slot_recv,
    tot_send,
    tot_recv,
    count_send,
    count_recv,
    line_send,
    line_recv,
    far_send,
    far_recv,
    sum_send,
    sum_recv,
    end_recv,
):
    place = Place(n_nodes, n_grp)
    z, low = place.at["z"], place.at["l"]
    layer = place.size["l"]
    rows, width = featb.shape
    edges = place_ref.shape[1]
    half = edges // 2
    layer_slots = spread.shape[1]
    cap = layer_slots // layer
    part = width // CHUNKS
    turn = math.gcd(half, 6400)
    steps = edges // turn

    sources = [feats_h.at[:]]
    for whole in (board_h, neigh_h, comb_h):
        for first in range(0, whole.shape[0], rows):
            sources.append(whole.at[pl.ds(first, rows)])
    n_stage = stage.shape[0]

    def load(i):
        return pltpu.make_async_copy(sources[i], stage.at[i % n_stage], load_sem.at[i % n_stage])

    for i in range(n_stage):
        load(i).start()
    load_cot = pltpu.make_async_copy(cot_h, cot, load_sem.at[n_stage])
    stores = []

    def store(src, dst):
        copy = pltpu.make_async_copy(src, dst, store_sem.at[len(stores)])
        copy.start()
        stores.append(copy)

    barrier(place, ("l", "z", "x"))
    keys[z, :, pl.ds(0, edges)] = place_ref[...] * 65536 + child_ref[...]
    keys[z, :, pl.ds(edges, half)] = (
        weight_ref[:, pl.ds(half, half)] * 65536 + weight_ref[:, pl.ds(0, half)]
    )

    def key_copy(far, device):
        return remote(keys.at[z], keys.at[z], key_send.at[far], key_recv.at[far], device)

    for far, _, device in place.others("z"):
        key_copy(far, device).start()
    inner = jnp.logical_and(z > 0, z < LINE - 1)
    outer = jnp.logical_or(z == 0, z == LINE - 1)
    half_at = z // 2
    far_end = (LINE - 1) * (1 - half_at)

    def line_copy(far, index, device):
        at = pl.ds(pl.multiple_of(index * layer_slots, layer_slots), layer_slots)
        return remote(
            targets_ref.at[:, at], lines.at[z], line_send.at[far], line_recv.at[far], device
        )

    @pl.when(outer)
    def _():
        for far, index, device in place.others("z"):
            line_copy(far, index, device).start()

    share = Share(place, (count_l, count_z, count_x), count_send, count_recv)
    mask = column_of(mask_ref)
    share.start(0, jnp.full((8, 128), jnp.sum(mask)))

    def cast(i, target, first):
        load(i).wait()
        slot = stage.at[i % n_stage]

        @pl.loop(0, rows // 32)
        def _(r):
            at = pl.ds(pl.multiple_of(r * 32, 32), 32)
            to = pl.ds(pl.multiple_of(first + r * 32, 32), 32)
            target[to, :] = slot[at, :].astype(BF16)

    cast(0, featb, 0)
    cast(1, board_b, 0)
    cast(2, board_b, rows)

    @pl.loop(0, CHUNKS)
    def _(k):
        at = pl.ds(pl.multiple_of(k * part, part), part)
        proj = jnp.dot(featb[...], board_b[:, at], preferred_element_type=F32)
        hid[:, at] = jnp.where(mask > 0.5, proj, stage[0, :, at]).astype(BF16)

    cast(3, neigh_b, 0)
    cast(4, neigh_b, rows)
    for i in range(n_stage, len(sources)):
        load(i).start()
    load_cot.start()

    def up_copy(src, k):
        piece = msg.at[src, k]
        index = src * CHUNKS + k
        return remote(
            piece, piece, up_send.at[index], msg_recv.at[index], place.member("z", z + 1)
        )

    def down_copy(src, k):
        piece = msg.at[src, k]
        index = src * CHUNKS + k
        return remote(
            piece, piece, down_send.at[index], msg_recv.at[index], place.member("z", z - 1)
        )

    def message(k):
        at = pl.ds(k * part, part)
        value = jnp.dot(hid[...], neigh_b[:, at], preferred_element_type=F32) + nbias_ref[:, at]
        pre[:, at] = value
        msg[z, k] = gelu(value).astype(BF16)

        @pl.when(z < LINE - 1)
        def _():
            up_copy(z, k).start()

        @pl.when(z > 0)
        def _():
            down_copy(z, k).start()

    def passes_up(k):
        return z < LINE - (1 if k < FAR else 2)

    def passes_down(k):
        return z > (0 if k < FAR else 1)

    def forward(j, k):
        below = z - 1 - j
        above = z + 1 + j

        comes = True if k < FAR or j == 0 else inner

        @pl.when(jnp.logical_and(below >= 0, comes))
        def _():
            up_copy(below, k).wait_recv()

            @pl.when(passes_up(k))
            def _():
                up_copy(below, k).start()

        @pl.when(jnp.logical_and(above < LINE, comes))
        def _():
            down_copy(above, k).wait_recv()

            @pl.when(passes_down(k))
            def _():
                down_copy(above, k).start()

    def tot_copy(src, far, index, device):
        at = (layer - 1) * src + far
        return remote(
            out_tot.at[src, pl.ds(pl.multiple_of(index * cap, cap), cap)],
            in_tot.at[src, pl.ds(pl.multiple_of(low * cap, cap), cap)],
            tot_send.at[at],
            tot_recv.at[at],
            device,
        )

    def finish_spread(src):
        total = acc[...]
        spread[src] = total.astype(BF16)
        spread_t[src] = total.astype(BF16).T
        sums = jnp.sum(total, axis=1, keepdims=True).astype(jnp.int32)
        lane = lax.broadcasted_iota(jnp.int32, (layer_slots, 128), 1)
        digit = jnp.where(
            lane == 0, sums & 255, jnp.where(lane == 1, (sums >> 8) & 255, jnp.where(lane == 2, sums >> 16, 0))
        )
        out_tot[src] = digit.astype(F32).astype(BF16)
        own = pl.ds(pl.multiple_of(low * cap, cap), cap)
        in_tot[src, own] = out_tot[src, own]
        for far, index, device in place.others("l"):
            tot_copy(src, far, index, device).start()

    def source(which):
        flip = z // 2
        depth = z * (1 - 2 * flip) + (LINE - 1) * flip
        index = ORDER[0][which] * (1 - depth) + ORDER[1][which] * depth
        return index * (1 - 2 * flip) + (LINE - 1) * flip

    def build(which, ticks):
        src, target = (source(which), z) if which < LINE else (z, far_end)
        acc[...] = jnp.zeros_like(acc)
        if 0 < which < LINE:
            far = lax.rem(z - src - 1 + LINE, LINE)
            remote(
                keys.at[src], keys.at[src], key_send.at[0], key_recv.at[far], place.member("z", src)
            ).wait_recv()

        @pl.loop(0, steps)
        def _(t):
            second = t // (steps // 2)
            key = keys[src, :, pl.ds(pl.multiple_of(t * turn, turn), turn)]
            start = edges + (t - second * (steps // 2)) * turn
            pair = keys[src, :, pl.ds(pl.multiple_of(start, turn), turn)]
            weight = (lax.shift_right_logical(pair, second * 16) & 65535).astype(F32).astype(F8)
            child = (key & 65535).astype(jnp.int16)
            slot = (lax.shift_right_logical(key, 16) - target * layer_slots).astype(jnp.int16)
            right = jnp.where(
                lax.broadcasted_iota(jnp.int16, (rows, turn), 0) == child, weight, jnp.zeros((), F8)
            )
            block = 256
            for first in range(0, layer_slots, block):
                ids = lax.broadcasted_iota(jnp.int16, (block, turn), 0) + jnp.asarray(
                    first, jnp.int16
                )
                left = jnp.where(ids == slot, jnp.ones((), F8), jnp.zeros((), F8))
                acc[pl.ds(first, block), :] += dot_nt(left, right)
            run_ticks(t, ticks)

        if which < LINE:
            finish_spread(src)
        else:
            far_spread[...] = acc[...].astype(BF16)

    def slot_copy(src, k, far, index, device):
        at = (src * CHUNKS + k) * (layer - 1) + far
        return remote(
            out_slots.at[src, k, pl.ds(pl.multiple_of(index * cap, cap), cap)],
            in_slots.at[src, k, pl.ds(pl.multiple_of(low * cap, cap), cap)],
            slot_send.at[at],
            slot_recv.at[at],
            device,
        )

    def piece(src, k):
        out_slots[src, k] = jnp.dot(spread[src], msg[src, k], preferred_element_type=F32).astype(BF16)
        for far, index, device in place.others("l"):
            slot_copy(src, k, far, index, device).start()
        own = pl.ds(pl.multiple_of(low * cap, cap), cap)
        in_slots[src, k, own] = out_slots[src, k, own]

    def pick(src, k):
        for far, index, device in place.others("l"):
            slot_copy(src, k, far, index, device).wait_recv()
        num[k] += jnp.dot(picker[src], in_slots[src, k], preferred_element_type=F32)

    def unless_far(which, k, act):
        if which < 2 or k < FAR:
            act(source(which), k)
        else:

            @pl.when(inner)
            def _():
                act(source(which), k)

    def far_copy(k, far, index, device):
        at = k * (layer - 1) + far
        return remote(
            far_out.at[k, pl.ds(pl.multiple_of(index * cap, cap), cap)],
            far_in.at[k, pl.ds(pl.multiple_of(low * cap, cap), cap)],
            far_send.at[at],
            far_recv.at[at],
            device,
        )

    onward = 1 - 2 * half_at

    def sum_copy(i):
        return remote(
            far_sum.at[i], far_sum.at[i], sum_send.at[i], sum_recv.at[i], place.member("z", z + onward)
        )

    def end_copy(i):
        return remote(
            far_sum.at[i],
            end_sum.at[i],
            sum_send.at[i],
            end_recv.at[i],
            place.member("z", z + 2 * onward),
        )

    def far_slots(k):
        i = k - FAR
        far_out[i] = jnp.dot(far_spread[...], msg[z, k], preferred_element_type=F32).astype(BF16)
        for far, index, device in place.others("l"):
            far_copy(i, far, index, device).start()
        own = pl.ds(pl.multiple_of(low * cap, cap), cap)
        far_in[i, own] = far_out[i, own]

    def make_far_picker():
        far = lax.rem(z - far_end - 1 + LINE, LINE)
        remote(
            lines.at[far_end],
            lines.at[far_end],
            line_send.at[0],
            line_recv.at[far],
            place.member("z", far_end),
        ).wait_recv()
        ids = lax.broadcasted_iota(jnp.int32, (rows, layer_slots), 0)
        far_picker[...] = jnp.where(ids == lines[far_end], 1.0, 0.0).astype(BF16)

        @pl.when(inner)
        def _():
            near = (LINE - 1) - far_end
            back = lax.rem(z - near - 1 + LINE, LINE)
            remote(
                lines.at[near],
                lines.at[near],
                line_send.at[0],
                line_recv.at[back],
                place.member("z", near),
            ).wait_recv()

    def far_parents(i):
        for far, index, device in place.others("l"):
            far_copy(i, far, index, device).wait_recv()
        return jnp.dot(far_picker[...], far_in[i], preferred_element_type=F32)

    def first_sum(k):
        @pl.when(outer)
        def _():
            far_sum[k - FAR] = far_parents(k - FAR).astype(BF16)
            sum_copy(k - FAR).start()

    def second_sum(k):
        @pl.when(inner)
        def _():
            i = k - FAR
            value = far_parents(i)
            sum_copy(i).wait_recv()
            far_sum[i] = (far_sum[i].astype(F32) + value).astype(BF16)
            end_copy(i).start()

    def add_far(k):
        @pl.when(outer)
        def _():
            end_copy(k - FAR).wait_recv()
            num[k] += end_sum[k - FAR].astype(F32)

    def make_picker():
        @pl.loop(0, LINE)
        def _(src):
            at = pl.ds(pl.multiple_of(src * layer_slots, layer_slots), layer_slots)
            ids = lax.broadcasted_iota(jnp.int32, (rows, layer_slots), 0)
            picker[src] = jnp.where(ids == targets_ref[:, at], 1.0, 0.0).astype(BF16)

        num[...] = jnp.zeros_like(num)

    def comb_piece(i):
        for j in range(i, 2 * width // rows, CHUNKS):
            cast(5 + j, comb_b, j * rows)

    def self_part():
        @pl.loop(0, CHUNKS)
        def _(k):
            at = pl.ds(pl.multiple_of(k * part, part), part)
            zpre[:, at] = (
                jnp.dot(hid[...], comb_b[0:width, at], preferred_element_type=F32)
                + cbias_ref[:, at]
            )

    def results():
        store(hid, hid_h)
        store(pre, pre_h)
        store(featb, featb_h)
        store(board_b, board_b_h)
        store(neigh_b, neigh_b_h)
        store(comb_b.at[pl.ds(0, width)], comb1_b_h)
        store(spread_t, st_h)

    def totals():
        digits = jnp.zeros((rows, 128), F32)
        for src in range(LINE):
            for far, index, device in place.others("l"):
                tot_copy(src, far, index, device).wait_recv()
            digits += jnp.dot(picker[src], in_tot[src], preferred_element_type=F32)
        lane = lax.broadcasted_iota(jnp.int32, (rows, 128), 1)
        worth = jnp.where(
            lane == 0, 1.0, jnp.where(lane == 1, 256.0, jnp.where(lane == 2, 65536.0, 0.0))
        )
        den_ref[...] = jnp.broadcast_to(
            1.0 + jnp.sum(digits * worth, axis=1, keepdims=True), (rows, 128)
        )

    def neighbours(k):
        at = pl.ds(k * part, part)
        agg[:, at] = (num[k] / den_ref[:, 0:1]).astype(BF16)
        if k < CHUNKS - 1:

            @pl.loop(0, CHUNKS)
            def _(n):
                to = pl.ds(pl.multiple_of(n * part, part), part)
                zpre[:, to] += jnp.dot(
                    agg[:, at], comb_b[pl.ds(width + k * part, part), to], preferred_element_type=F32
                )

    def step_share(stage):
        if stage in (1, 2):
            share.start(stage, share.finish(stage - 1))
        elif stage == 3:
            boards = share.finish(2)
            scale_ref[...] = 1.0 / (width * (1.0 + boards))

    acts = {
        "P": step_share,
        "m": message,
        "f": forward,
        "p": lambda which, k: unless_far(which, k, piece),
        "i": lambda which, k: unless_far(which, k, pick),
        "u": far_slots,
        "g": lambda _: make_far_picker(),
        "v": first_sum,
        "x": second_sum,
        "w": add_far,
        "G": lambda _: make_picker(),
        "D": comb_piece,
        "X": lambda _: self_part(),
        "R": lambda _: results(),
        "d": lambda _: totals(),
        "a": neighbours,
    }

    def act(step):
        acts[step[0]](*(int(c) for c in step[1:]))

    run_order(FORWARD, steps, build, act)
    neighbours(CHUNKS - 1)
    load_cot.wait()
    den = den_ref[:, 0:1]
    scale = scale_ref[0:1, 0:1]
    last = pl.ds(width - part, part)

    def dense(k, carry):
        square, along = carry
        at = pl.ds(pl.multiple_of(k * part, part), part)
        value = zpre[:, at] + jnp.dot(
            agg[:, last], comb_b[pl.ds(2 * width - part, part), at], preferred_element_type=F32
        )
        zpre[:, at] = value
        out = gelu(value)
        zval[:, at] = out
        square += jnp.sum(out * out, axis=1, keepdims=True)
        along += jnp.sum(out * cot[:, at], axis=1, keepdims=True)
        return square, along

    zero = jnp.zeros((rows, 1), F32)
    square, along = lax.fori_loop(0, CHUNKS, dense, (zero, zero))
    inverse = lax.rsqrt(square + 1e-06)
    along = along * inverse
    push = jnp.where(mask > 0.5, 2.0 * scale, 0.0)
    stats_ref[...] = jnp.concatenate(
        [
            jnp.full((8, 128), jnp.sum(jnp.where(mask > 0.5, square, 0.0))),
            jnp.broadcast_to(scale, (8, 128)),
        ],
        axis=0,
    )

    @pl.loop(0, CHUNKS)
    def _(k):
        at = pl.ds(pl.multiple_of(k * part, part), part)
        out = zval[:, at]
        emb = out * inverse
        grad = inverse * (cot[:, at] - emb * along) + push * out
        dz[:, at] = (grad * gelu_slope(zpre[:, at])).astype(BF16)
        zval[:, at] = emb

    store(zval, embed_h)
    store(dz, dz_h)
    store(agg, agg_h)

    @pl.loop(0, CHUNKS)
    def _(k):
        at = pl.ds(pl.multiple_of(k * part, part), part)
        back = dot_nt(dz[...], comb_b[pl.ds(pl.multiple_of(width + k * part, part), part), :])
        dnum[:, at] = (back / den).astype(BF16)

    store(dnum, dnum_h)

    for far, _, device in place.others("z"):
        key_copy(far, device).wait_send()

    @pl.loop(0, LINE * CHUNKS)
    def _(i):
        src = i // CHUNKS
        k = lax.rem(i, CHUNKS)

        early = k < FAR

        @pl.when(
            jnp.logical_or(
                jnp.logical_and(src == z, z < LINE - 1),
                jnp.logical_and(
                    src < z, jnp.logical_or(jnp.logical_and(early, z < LINE - 1), z < LINE - 2)
                ),
            )
        )
        def _():
            up_copy(src, k).wait_send()

        @pl.when(
            jnp.logical_or(
                jnp.logical_and(src == z, z > 0),
                jnp.logical_and(src > z, jnp.logical_or(jnp.logical_and(early, z > 0), z > 1)),
            )
        )
        def _():
            down_copy(src, k).wait_send()

        near = jnp.logical_and(src - z < 2, z - src < 2)

        @pl.when(jnp.logical_or(jnp.logical_or(early, inner), near))
        def _():
            for far, index, device in place.others("l"):
                slot_copy(src, k, far, index, device).wait_send()

    for i in range(CHUNKS - FAR):
        sum_copy(i).wait_send()
        for far, index, device in place.others("l"):
            far_copy(i, far, index, device).wait_send()

    @pl.when(outer)
    def _():
        for far, index, device in place.others("z"):
            line_copy(far, index, device).wait_send()

    for src in range(LINE):
        for far, index, device in place.others("l"):
            tot_copy(src, far, index, device).wait_send()
    for copy in stores:
        copy.wait()


def forward_pass(n_nodes, n_grp, feats, mask, edges_of, targets, board, neigh, nbias, comb, cbias, cot):
    rows, width = feats.shape
    edges = edges_of[0].shape[1]
    layer = n_nodes // LINE
    layer_slots = targets.shape[1] // LINE
    part = width // CHUNKS
    dma = pltpu.SemaphoreType.DMA
    n_stage = 5
    big = pl.BlockSpec(memory_space=pl.ANY)
    small = pl.BlockSpec(memory_space=pltpu.VMEM)

    def hbm(shape, dtype):
        return jax.ShapeDtypeStruct(shape, dtype)

    return pl.pallas_call(
        functools.partial(forward_kernel, n_nodes, n_grp),
        out_shape=[
            hbm((rows, width), F32),
            hbm((rows, width), BF16),
            hbm((rows, width), F32),
            hbm((rows, width), BF16),
            hbm((width, width), BF16),
            hbm((width, width), BF16),
            hbm((width, width), BF16),
            hbm((LINE, rows, layer_slots), BF16),
            hbm((rows, width), BF16),
            hbm((rows, width), BF16),
            hbm((rows, width), BF16),
            hbm((16, 128), F32),
        ],
        in_specs=[big] + [small] * 5 + [big, big, small, big, small, big],
        out_specs=[big] * 11 + [small],
        scratch_shapes=[
            pltpu.VMEM((n_stage, rows, width), F32),
            pltpu.VMEM((rows, width), BF16),
            pltpu.VMEM((rows, width), BF16),
            pltpu.VMEM((rows, width), F32),
            pltpu.VMEM((width, width), BF16),
            pltpu.VMEM((width, width), BF16),
            pltpu.VMEM((2 * width, width), BF16),
            pltpu.VMEM((LINE, 1, edges + edges // 2), jnp.int32),
            pltpu.VMEM((LINE, CHUNKS, rows, part), BF16),
            pltpu.VMEM((layer_slots, rows), F32),
            pltpu.VMEM((LINE, layer_slots, rows), BF16),
            pltpu.VMEM((LINE, rows, layer_slots), BF16),
            pltpu.VMEM((LINE, CHUNKS, layer_slots, part), BF16),
            pltpu.VMEM((LINE, CHUNKS, layer_slots, part), BF16),
            pltpu.VMEM((LINE, layer_slots, 128), BF16),
            pltpu.VMEM((LINE, layer_slots, 128), BF16),
            pltpu.VMEM((LINE, rows, layer_slots), BF16),
            pltpu.VMEM((CHUNKS, rows, part), F32),
            pltpu.VMEM((rows, width), F32),
            pltpu.VMEM((rows, width), F32),
            pltpu.VMEM((rows, width), F32),
            pltpu.VMEM((rows, width), BF16),
            pltpu.VMEM((rows, width), BF16),
            pltpu.VMEM((rows, width), BF16),
            pltpu.VMEM((LINE, 1, layer_slots), jnp.int32),
            pltpu.VMEM((layer_slots, rows), BF16),
            pltpu.VMEM((rows, layer_slots), BF16),
            pltpu.VMEM((CHUNKS - FAR, layer_slots, part), BF16),
            pltpu.VMEM((CHUNKS - FAR, layer_slots, part), BF16),
            pltpu.VMEM((CHUNKS - FAR, rows, part), BF16),
            pltpu.VMEM((CHUNKS - FAR, rows, part), BF16),
            pltpu.VMEM((rows, 128), F32),
            pltpu.VMEM((8, 128), F32),
            pltpu.VMEM((layer, 8, 128), F32),
            pltpu.VMEM((LINE, 8, 128), F32),
            pltpu.VMEM((n_grp, 8, 128), F32),
            dma((n_stage + 1,)),
            dma((11,)),
            dma((LINE - 1,)),
            dma((LINE - 1,)),
            dma((LINE * CHUNKS,)),
            dma((LINE * CHUNKS,)),
            dma((LINE * CHUNKS,)),
            dma((LINE * CHUNKS * (layer - 1),)),
            dma((LINE * CHUNKS * (layer - 1),)),
            dma((LINE * (layer - 1),)),
            dma((LINE * (layer - 1),)),
            dma((share_sems(n_nodes, n_grp),)),
            dma((share_sems(n_nodes, n_grp),)),
            dma((LINE - 1,)),
            dma((LINE - 1,)),
            dma(((CHUNKS - FAR) * (layer - 1),)),
            dma(((CHUNKS - FAR) * (layer - 1),)),
            dma((CHUNKS - FAR,)),
            dma((CHUNKS - FAR,)),
            dma((CHUNKS - FAR,)),
        ],
        compiler_params=pltpu.CompilerParams(
            vmem_limit_bytes=63 * MIB, collective_id=2, has_side_effects=True
        ),
        name="forward_pass",
    )(feats, mask, *edges_of, targets, board, neigh, nbias, comb, cbias, cot)


def add_into(target, first, count, columns, parts, step=16):
    @pl.loop(0, count // step)
    def _(i):
        at = pl.ds(pl.multiple_of(first + i * step, step), step)
        total = target[at, columns].astype(F32)
        for part in parts:
            total += part[pl.ds(pl.multiple_of(i * step, step), step), :].astype(F32)
        target[at, columns] = total.astype(target.dtype)


def reduce_job(place, order, grad, region, arrive, land, last, send, recv, free, base):
    first, rows, left, columns = region
    half = columns // 2
    core = place.at["c"]
    mine = pl.ds(pl.multiple_of(left + core * half, half), half)
    theirs = pl.ds(pl.multiple_of(left + (1 - core) * half, half), half)
    mate = place.member("c", 1 - core)
    block = pl.ds(first, rows)
    sems = iter(range(base, base + send.shape[0]))

    def lay(src, dst, device):
        sem = next(sems)
        return remote(src, dst, send.at[sem], recv.at[sem], device)

    across = lay(grad.at[block, theirs], arrive, mate)
    down = []
    begin, length, used = first, rows, 0
    for axis in order:
        length //= place.size[axis]
        copies, parts, devices = [], [], []
        for far, index, device in place.others(axis):
            start = pl.multiple_of(begin + index * length, 16)
            slot = land.at[pl.ds(used, length)]
            used += length
            copies.append(lay(grad.at[pl.ds(start, length), mine], slot, device))
            parts.append(slot)
            devices.append(device)
        parent = begin
        begin = pl.multiple_of(begin + place.at[axis] * length, 16)
        down.append((axis, parent, begin, length, copies, parts, devices))
    axis, parent, begin, length, _, _, devices = down[-1]
    here = pl.ds(pl.multiple_of(place.at[axis] * length, 16), length)
    whole = pl.ds(pl.multiple_of(parent, 16), length * place.size[axis])
    end = [lay(last.at[here], last.at[here], device) for device in devices]
    up = []
    for stage in range(len(down) - 1, 0, -1):
        axis, _, start, piece, _, _, devices = down[stage - 1]
        own = grad.at[pl.ds(start, piece), mine]
        up.append((stage, len(devices), [lay(own, own, device) for device in devices]))
    own = grad.at[block, mine]
    back = lay(own, own, mate)
    yield

    def release(at, devices):
        for device in devices:
            pl.semaphore_signal(free.at[base + at], inc=1, device_id=device, device_id_type=MESH)

    across.start()
    yield
    across.wait()
    release(0, [mate])
    add_into(grad, first, rows, mine, [arrive])
    for stage, (_, _, begin, length, copies, parts, devices) in enumerate(down):
        for copy in copies:
            copy.start()
        yield
        for copy in copies:
            copy.wait()
        if stage < len(down) - 1:
            release(stage + 1, devices)
        add_into(grad, begin, length, mine, parts)
    last[here] = grad[pl.ds(begin, length), mine]
    for copy in end:
        copy.start()
    yield
    for copy in end:
        copy.wait()
    grad[whole, mine] = last[pl.ds(0, whole.size)]
    for stage, count, copies in up:
        pl.semaphore_wait(free.at[base + stage], count)
        for copy in copies:
            copy.start()
        yield
        for copy in copies:
            copy.wait()
    pl.semaphore_wait(free.at[base], 1)
    back.start()
    yield
    back.wait()


def job_sems(n_nodes, n_grp):
    return 2 * (1 + (n_nodes // LINE // 2 - 1) + (LINE - 1) + (n_grp - 1))


AHEAD = 2
BEHIND = CHUNKS - AHEAD
JOBS = {
    kind[0] + str(i): kind + str(i) for kind, count in (("comb", 4), ("neigh", 4), ("board", 4)) for i in range(count)
}
BACKWARD = (
    "l0", "A1", "B2", "A0", "G0", "c0", "c1", "L2", "W0", "Y10", "c3", "B3", "f01", "c2", "c0",
    "32", "c3", "c1", "Y11", "f00", "q01", "Y12", "L1", "33", "L3", "c2", "22", "Y13", "f11",
    "Y14", "12", "Z1", "q11", "Y20", "f10", "c0", "q00", "Y21", "23", "c1", "q10", "c2", "Y22",
    "q20", "q21", "13", "Y23", "Y24", "c0", "S0", "Z2", "O2", "c3", "f21", "c1", "f20", "n2", "O3",
    "n3", "c0", "Y30", "n2", "q31", "c1", "Y31", "c2", "n3", "Y32", "c0", "q30", "c1", "Y33", "c3",
    "n3", "n2", "Y34", "c2", "c0", "c1", "Z3", "O1", "n1", "c3", "O0", "n0", "n1", "c2", "n3",
    "E0", "H1", "b2", "c3", "n2", "b3", "n0", "n3", "H0", "b1", "b2", "b3", "n1", "b0", "b1", "n0",
    "n3", "b0", "n1", "P0", "b2", "c0", "F0", "b1", "n0", "n2", "c2", "b3", "n1", "b0", "b1", "c3",
    "b3", "n0", "b0", "n1", "b2", "n2", "c0", "b3", "n3", "b1", "b0", "b3", "n2", "c2", "b2", "n0",
    "b1", "c1", "n1", "b3", "n3", "b0", "P1", "b2", "c3", "c1", "b1", "b0", "b2", "n3", "n2", "n0",
    "b3", "n1", "b0", "b1", "n0", "c2", "n2", "P2", "b2", "n0", "b1", "b2", "b0", "n1", "P3", "c3",
    "b3",
)


def gradient_regions(n_nodes, n_grp, width):
    pieces = n_nodes * n_grp // 2
    x_first, y_first = ("x", "y", "z"), ("y", "x", "z")
    regions = {}
    count = max(1, min(4, 2 * width // (16 * pieces)))
    n_rows = 2 * width // count
    for j in range(count):
        regions[f"comb{j}"] = (j * n_rows, n_rows, 0, width, y_first if j % 2 else x_first)
    if width % (16 * pieces) == 0:
        part = width // CHUNKS
        for k in range(CHUNKS):
            regions[f"neigh{k}"] = (2 * width, width, k * part, part, x_first if k % 2 else y_first)
        count = max(1, min(4, width // (16 * pieces)))
        n_rows = width // count
        for j in range(count):
            order = (x_first, y_first, x_first, ("z", "y", "x"))[j]
            regions[f"board{j}"] = (3 * width + j * n_rows, n_rows, 0, width, order)
    else:
        regions["board0"] = (2 * width, 2 * width, 0, width, x_first)
    return regions


def backward_kernel(
    n_nodes,
    n_grp,
    mask_ref,
    targets_ref,
    stats_ref,
    place_h,
    child_h,
    weight_h,
    hid_h,
    pre_h,
    featb_h,
    board_b_h,
    neigh_b_h,
    comb1_b_h,
    st_h,
    dnum_h,
    dz_h,
    agg_h,
    gfeat_h,
    summed_h,
    small_ref,
    hid,
    pre,
    featb,
    board_b,
    neigh_b,
    comb1_b,
    spread_t,
    dnum,
    dz,
    agg,
    picker_t,
    picker_l,
    lines,
    edge_place,
    edge_child,
    edge_weight,
    acc,
    own_t,
    parents,
    out_slots,
    in_slots,
    chain,
    tmp,
    dpre,
    dh,
    grad,
    arrive,
    land,
    gather,
    share_l,
    share_z,
    share_x,
    small,
    load_sem,
    store_sem,
    slot_send,
    slot_recv,
    up_send,
    down_send,
    chain_recv,
    line_send,
    line_recv,
    parent_up,
    parent_down,
    parent_recv,
    job_send,
    job_recv,
    job_free,
    share_send,
    share_recv,
):
    place = Place(n_nodes, n_grp)
    z, low = place.at["z"], place.at["l"]
    layer = place.size["l"]
    rows, width = hid.shape
    layer_slots = spread_t.shape[2]
    cap = layer_slots // layer
    part = width // CHUNKS

    loads = {}
    for i, (name, src, dst) in enumerate(
        (
            ("dnum", dnum_h, dnum),
            ("hid", hid_h, hid),
            ("agg", agg_h, agg),
            ("dz", dz_h, dz),
            ("spread_t", st_h, spread_t),
            ("comb1_b", comb1_b_h, comb1_b),
            ("pre", pre_h, pre),
            ("neigh_b", neigh_b_h, neigh_b),
            ("featb", featb_h, featb),
            ("board_b", board_b_h, board_b),
            ("place", place_h, edge_place),
            ("child", child_h, edge_child),
            ("weight", weight_h, edge_weight),
        )
    ):
        loads[name] = pltpu.make_async_copy(src, dst, load_sem.at[i])
        loads[name].start()
    def make_pickers():
        @pl.loop(0, LINE)
        def _(src):
            at = pl.ds(pl.multiple_of(src * layer_slots, layer_slots), layer_slots)
            ids = lax.broadcasted_iota(jnp.int32, (rows, layer_slots), 0)
            picker_t[src] = jnp.where(ids == targets_ref[:, at], 1.0, 0.0).astype(BF16).T

    barrier(place, ("l", "z", "x"), make_pickers)
    stores = []

    def store(src, dst):
        copy = pltpu.make_async_copy(src, dst, store_sem.at[len(stores)])
        copy.start()
        stores.append(copy)

    mask = column_of(mask_ref) > 0.5

    def source(which):
        flip = z // 2
        inner = z * (1 - 2 * flip) + (LINE - 1) * flip
        index = ORDER[0][which] * (1 - inner) + ORDER[1][which] * inner
        return index * (1 - 2 * flip) + (LINE - 1) * flip

    def cols(k):
        return pl.ds(pl.multiple_of(k * part, part), part)

    def slot_copy(dst, k, far, index, device):
        at = (dst * CHUNKS + k) * (layer - 1) + far
        return remote(
            out_slots.at[dst, k, pl.ds(pl.multiple_of(index * cap, cap), cap)],
            in_slots.at[dst, k, pl.ds(pl.multiple_of(low * cap, cap), cap)],
            slot_send.at[at],
            slot_recv.at[at],
            device,
        )

    def back(dst, k):
        out_slots[dst, k] = jnp.dot(
            picker_t[dst], dnum[:, cols(k)], preferred_element_type=F32
        ).astype(BF16)
        for far, index, device in place.others("l"):
            slot_copy(dst, k, far, index, device).start()
        own = pl.ds(pl.multiple_of(low * cap, cap), cap)
        in_slots[dst, k, own] = out_slots[dst, k, own]

    def child_sums(dst, k):
        for far, index, device in place.others("l"):
            slot_copy(dst, k, far, index, device).wait_recv()
        tmp[...] = jnp.dot(spread_t[dst], in_slots[dst, k], preferred_element_type=F32)

    def up_copy(dst, k):
        k = k - AHEAD
        at = dst * BEHIND + k
        return remote(
            chain.at[dst, k],
            chain.at[dst, k],
            up_send.at[at],
            chain_recv.at[at],
            place.member("z", z + 1),
        )

    def down_copy(dst, k, last):
        slot = LINE if last else dst
        k = k - AHEAD
        return remote(
            chain.at[dst, k],
            chain.at[slot, k],
            down_send.at[dst * BEHIND + k],
            chain_recv.at[slot * BEHIND + k],
            place.member("z", z - 1),
        )

    def arrived(slot, k):
        k = k - AHEAD
        remote(
            chain.at[slot, k],
            chain.at[slot, k],
            up_send.at[0],
            chain_recv.at[slot * BEHIND + k],
            place.member("z", lax.rem(z + 1, LINE)),
        ).wait_recv()

    def hand_on(dst, k):
        child_sums(dst, k)

        @pl.when(dst > z)
        def _():
            @pl.when(z > 0)
            def _():
                up_copy(dst, k).wait_recv()
                chain[dst, k - AHEAD] = (chain[dst, k - AHEAD].astype(F32) + tmp[...]).astype(BF16)

            @pl.when(z == 0)
            def _():
                chain[dst, k - AHEAD] = tmp[...].astype(BF16)

            up_copy(dst, k).start()

        @pl.when(dst < z)
        def _():
            @pl.when(z < LINE - 1)
            def _():
                down_copy(dst, k, False).wait_recv()
                chain[dst, k - AHEAD] = (chain[dst, k - AHEAD].astype(F32) + tmp[...]).astype(BF16)

            @pl.when(z == LINE - 1)
            def _():
                chain[dst, k - AHEAD] = tmp[...].astype(BF16)

            @pl.when(dst == z - 1)
            def _():
                down_copy(dst, k, True).start()

            @pl.when(dst < z - 1)
            def _():
                down_copy(dst, k, False).start()

    regions = gradient_regions(n_nodes, n_grp, width)
    per_job = job_sems(n_nodes, n_grp)

    def job(name):
        first, n_rows, left, columns, order = regions[name]
        rows_at, cols_at = pl.ds(first, n_rows), pl.ds(left, columns)
        land_at = pl.ds(left // 2, columns // 2)
        yield from reduce_job(
            place,
            order,
            grad,
            (first, n_rows, left, columns),
            arrive.at[rows_at, land_at],
            land.at[rows_at, land_at],
            gather.at[pl.ds(first // 4, n_rows // 4), land_at],
            job_send,
            job_recv,
            job_free,
            list(regions).index(name) * per_job,
        )
        store(grad.at[rows_at, cols_at], summed_h.at[rows_at, cols_at])

    jobs = {name: job(name) for name in regions}
    for lay_out in jobs.values():
        next(lay_out)

    def step_job(name, last=False):
        if name in jobs and (last or name != "board0" or "board3" in regions):
            try:
                next(jobs[name])
            except StopIteration:
                del jobs[name]

    loads["dnum"].wait()

    def back_all(k):
        for which in (3, 2, 1, 0):
            back(source(which), k)

    def comb_grad(left, first):
        @pl.loop(0, CHUNKS)
        def _(k):
            grad[pl.ds(first, width), cols(k)] = dot_tn(left[...], dz[:, cols(k)]).astype(BF16)

    def line_targets():
        lines[z] = targets_ref[:, pl.ds(pl.multiple_of(z * layer_slots, layer_slots), layer_slots)]
        for far, index, device in place.others("z"):
            at = pl.ds(pl.multiple_of(index * layer_slots, layer_slots), layer_slots)
            remote(
                targets_ref.at[:, at], lines.at[z], line_send.at[far], line_recv.at[far], device
            ).start()

    def line_picker(which):
        src = source(which)
        far = lax.rem(z - src - 1 + LINE, LINE)
        remote(
            lines.at[src], lines.at[src], line_send.at[0], line_recv.at[far], place.member("z", src)
        ).wait_recv()
        ids = lax.broadcasted_iota(jnp.int32, (rows, layer_slots), 0)
        picker_l[src] = jnp.where(ids == lines[src], 1.0, 0.0).astype(BF16).T

    def parent_copy(src, k, sems, to):
        piece = parents.at[src, k]
        at = src * AHEAD + k
        return remote(piece, piece, sems.at[at], parent_recv.at[at], place.member("z", to))

    def parent_send(k):
        parents[z, k] = dnum[:, cols(k)]

        @pl.when(z < LINE - 1)
        def _():
            parent_copy(z, k, parent_up, z + 1).start()

        @pl.when(z > 0)
        def _():
            parent_copy(z, k, parent_down, z - 1).start()

    def parent_forward(j, k):
        below = z - 1 - j
        above = z + 1 + j

        @pl.when(below >= 0)
        def _():
            parent_copy(below, k, parent_up, z + 1).wait_recv()

            @pl.when(z < LINE - 1)
            def _():
                parent_copy(below, k, parent_up, z + 1).start()

        @pl.when(above < LINE)
        def _():
            parent_copy(above, k, parent_down, z - 1).wait_recv()

            @pl.when(z > 0)
            def _():
                parent_copy(above, k, parent_down, z - 1).start()

    def parent_slots(which, k):
        src = source(which)
        choose = picker_t[z] if which == 0 else picker_l[src]
        out_slots[src, k] = jnp.dot(choose, parents[src, k], preferred_element_type=F32).astype(
            BF16
        )
        for far, index, device in place.others("l"):
            slot_copy(src, k, far, index, device).start()
        own = pl.ds(pl.multiple_of(low * cap, cap), cap)
        in_slots[src, k, own] = out_slots[src, k, own]

    edges = edge_place.shape[1]
    turn = math.gcd(edges, 2560)
    steps = edges // turn

    def build_own(which, ticks):
        src = source(which)
        if which == 1:
            for name in ("place", "child", "weight"):
                loads[name].wait()
        acc[...] = jnp.zeros_like(acc)

        @pl.loop(0, steps)
        def _(t):
            at = pl.ds(pl.multiple_of(t * turn, turn), turn)
            slot = (edge_place[:, at] - src * layer_slots).astype(jnp.int16)
            child = edge_child[:, at].astype(jnp.int16)
            weight = edge_weight[:, at].astype(F32).astype(F8)
            right = jnp.where(
                lax.broadcasted_iota(jnp.int16, (layer_slots, turn), 0) == slot,
                jnp.ones((), F8),
                jnp.zeros((), F8),
            )
            block = 256
            for first in range(0, rows, block):
                ids = lax.broadcasted_iota(jnp.int16, (block, turn), 0) + jnp.asarray(
                    first, jnp.int16
                )
                left = jnp.where(ids == child, weight, jnp.zeros((), F8))
                acc[pl.ds(first, block), :] += dot_nt(left, right)
            run_ticks(t, ticks)

        own_t[src] = acc[...].astype(BF16)

    def own(k):
        if k < AHEAD:
            for which in range(LINE):
                src = source(which)
                for far, index, device in place.others("l"):
                    slot_copy(src, k, far, index, device).wait_recv()
                weights = spread_t[z] if which == 0 else own_t[src]
                value = jnp.dot(weights, in_slots[src, k], preferred_element_type=F32)
                if which == 0:
                    tmp[...] = value
                else:
                    tmp[...] += value
        else:
            child_sums(z, k)

            @pl.when(z > 0)
            def _():
                arrived(z, k)
                tmp[...] += chain[z, k - AHEAD].astype(F32)

            @pl.when(z < LINE - 1)
            def _():
                arrived(LINE, k)
                tmp[...] += chain[LINE, k - AHEAD].astype(F32)

        down = (tmp[...] * gelu_slope(pre[:, cols(k)])).astype(BF16)
        dpre[:, cols(k)] = down
        small[0:1, cols(k)] = jnp.sum(down.astype(F32), axis=0, keepdims=True)
        dh[...] += dot_nt(down, neigh_b[:, cols(k)])

    def neigh_grad(k):
        grad[pl.ds(2 * width, width), cols(k)] = dot_tn(hid[...], dpre[:, cols(k)]).astype(BF16)

    def comb_grads():
        for name in ("hid", "agg", "dz", "comb1_b"):
            loads[name].wait()
        comb_grad(hid, 0)
        comb_grad(agg, width)

    def self_part():
        small[...] = jnp.zeros_like(small)
        small[1:2, :] = jnp.sum(dz[...].astype(F32), axis=0, keepdims=True)
        small[2:3, :] = jnp.broadcast_to(stats_ref[0:1, 0:1], (1, width))

        @pl.loop(0, CHUNKS)
        def _(k):
            dh[:, cols(k)] = dot_nt(dz[...], comb1_b[cols(k), :])

        for name in ("pre", "neigh_b", "featb", "board_b"):
            loads[name].wait()

    def own_and_grad(k):
        own(k)
        neigh_grad(k)

    def end_of_line():
        last = dh[...].astype(BF16)
        dpre[...] = jnp.where(mask, last, jnp.zeros_like(last))
        pre[...] = last.astype(F32)

    def board_grad(i):
        half = width // 2
        grad[pl.ds(3 * width + i * half, half), :] = dot_tn(
            featb[:, i * half : (i + 1) * half], dpre[...]
        ).astype(BF16)

    def feature_grad():
        @pl.loop(0, CHUNKS)
        def _(k):
            pre[:, cols(k)] = jnp.where(
                mask, dot_nt(dpre[...], board_b[cols(k), :]), pre[:, cols(k)]
            )

        store(pre, gfeat_h)

    share = Share(place, (share_l, share_z, share_x), share_send, share_recv)

    def step_share(stage):
        if stage == 0:
            share.start(0, small[...])
        elif stage < 3:
            share.start(stage, share.finish(stage - 1))
        else:
            row = lax.broadcasted_iota(jnp.int32, small_ref.shape, 0)
            small_ref[...] = share.finish(2) * jnp.where(row == 2, stats_ref[8:9, 0:1], 1.0)

    acts = {
        "l": lambda _: line_targets(),
        "L": line_picker,
        "A": parent_send,
        "f": parent_forward,
        "q": parent_slots,
        "B": back_all,
        "W": lambda _: loads["spread_t"].wait(),
        "G": lambda _: comb_grads(),
        "S": lambda _: self_part(),
        "O": own_and_grad,
        "E": lambda _: end_of_line(),
        "H": board_grad,
        "F": lambda _: feature_grad(),
        "P": step_share,
        "3": lambda k: hand_on(source(3), k),
        "2": lambda k: hand_on(source(2), k),
        "1": lambda k: hand_on(source(1), k),
    }
    def act(name):
        if name in JOBS:
            step_job(JOBS[name])
        else:
            acts[name[0]](*(int(c) for c in name[1:]))

    run_order(BACKWARD, steps, build_own, act)
    while jobs:
        for name in list(jobs):
            step_job(name, last=True)

    for far, index, device in place.others("z"):
        remote(lines.at[z], lines.at[z], line_send.at[far], line_recv.at[far], device).wait_send()

    @pl.loop(0, LINE * CHUNKS)
    def _(i):
        dst = i // CHUNKS
        k = lax.rem(i, CHUNKS)

        @pl.when(k < AHEAD)
        def _():
            @pl.when(jnp.logical_and(dst <= z, z < LINE - 1))
            def _():
                parent_copy(dst, k, parent_up, z + 1).wait_send()

            @pl.when(jnp.logical_and(dst >= z, z > 0))
            def _():
                parent_copy(dst, k, parent_down, z - 1).wait_send()

        @pl.when(k >= AHEAD)
        def _():
            @pl.when(dst > z)
            def _():
                up_copy(dst, k).wait_send()

            @pl.when(dst < z)
            def _():
                down_copy(dst, k, False).wait_send()

        for far, index, device in place.others("l"):
            slot_copy(dst, k, far, index, device).wait_send()

    for copy in stores:
        copy.wait()


def backward_pass(n_nodes, n_grp, mask, targets, stats, edges_of, hid, pre, featb, board_b, neigh_b, comb1_b, st, dnum, dz, agg):
    rows, width = hid.shape
    edges = edges_of[0].shape[1]
    layer = n_nodes // LINE
    layer_slots = st.shape[2]
    part = width // CHUNKS
    n_rows = 4 * width
    count = len(gradient_regions(n_nodes, n_grp, width))
    dma = pltpu.SemaphoreType.DMA
    big = pl.BlockSpec(memory_space=pl.ANY)
    vmem = pl.BlockSpec(memory_space=pltpu.VMEM)
    sems = count * job_sems(n_nodes, n_grp)
    pieces = LINE * CHUNKS
    return pl.pallas_call(
        functools.partial(backward_kernel, n_nodes, n_grp),
        out_shape=[
            jax.ShapeDtypeStruct((rows, width), F32),
            jax.ShapeDtypeStruct((n_rows, width), BF16),
            jax.ShapeDtypeStruct((8, width), F32),
        ],
        in_specs=[vmem, vmem, vmem] + [big] * 13,
        out_specs=[big, big, vmem],
        scratch_shapes=[
            pltpu.VMEM((rows, width), BF16),
            pltpu.VMEM((rows, width), F32),
            pltpu.VMEM((rows, width), BF16),
            pltpu.VMEM((width, width), BF16),
            pltpu.VMEM((width, width), BF16),
            pltpu.VMEM((width, width), BF16),
            pltpu.VMEM((LINE, rows, layer_slots), BF16),
            pltpu.VMEM((rows, width), BF16),
            pltpu.VMEM((rows, width), BF16),
            pltpu.VMEM((rows, width), BF16),
            pltpu.VMEM((LINE, layer_slots, rows), BF16),
            pltpu.VMEM((LINE, layer_slots, rows), BF16),
            pltpu.VMEM((LINE, 1, layer_slots), jnp.int32),
            pltpu.VMEM((1, edges), jnp.int32),
            pltpu.VMEM((1, edges), jnp.int32),
            pltpu.VMEM((1, edges), jnp.int32),
            pltpu.VMEM((rows, layer_slots), F32),
            pltpu.VMEM((LINE, rows, layer_slots), BF16),
            pltpu.VMEM((LINE, AHEAD, rows, part), BF16),
            pltpu.VMEM((LINE, CHUNKS, layer_slots, part), BF16),
            pltpu.VMEM((LINE, CHUNKS, layer_slots, part), BF16),
            pltpu.VMEM((LINE + 1, BEHIND, rows, part), BF16),
            pltpu.VMEM((rows, part), F32),
            pltpu.VMEM((rows, width), BF16),
            pltpu.VMEM((rows, width), F32),
            pltpu.VMEM((n_rows, width), BF16),
            pltpu.VMEM((n_rows, width // 2), BF16),
            pltpu.VMEM((n_rows, width // 2), BF16),
            pltpu.VMEM((n_rows // 4, width // 2), BF16),
            pltpu.VMEM((layer, 8, width), F32),
            pltpu.VMEM((LINE, 8, width), F32),
            pltpu.VMEM((n_grp, 8, width), F32),
            pltpu.VMEM((8, width), F32),
            dma((13,)),
            dma((count + 1,)),
            dma((pieces * (layer - 1),)),
            dma((pieces * (layer - 1),)),
            dma((LINE * BEHIND,)),
            dma((LINE * BEHIND,)),
            dma(((LINE + 1) * BEHIND,)),
            dma((LINE - 1,)),
            dma((LINE - 1,)),
            dma((LINE * AHEAD,)),
            dma((LINE * AHEAD,)),
            dma((LINE * AHEAD,)),
            dma((sems,)),
            dma((sems,)),
            pltpu.SemaphoreType.REGULAR((sems,)),
            dma((share_sems(n_nodes, n_grp),)),
            dma((share_sems(n_nodes, n_grp),)),
        ],
        compiler_params=pltpu.CompilerParams(
            vmem_limit_bytes=63 * MIB, collective_id=3, has_side_effects=True
        ),
        name="backward_pass",
    )(mask, targets, stats, *edges_of, hid, pre, featb, board_b, neigh_b, comb1_b, st, dnum, dz, agg)


def unpack_kernel(
    rows, joined, small_ref, comb, neigh, board, nbias_ref, cbias_ref, penalty_ref, low, wide, load_sem, store_sem
):
    width = joined.shape[1]
    blocks = joined.shape[0] // rows

    def load(i):
        at = pl.ds(i * rows, rows)
        return pltpu.make_async_copy(joined.at[at], low.at[at], load_sem.at[i])

    def store(i):
        first = i * rows
        if first < 2 * width:
            target = comb.at[pl.ds(first, rows)]
        elif first < 3 * width:
            target = neigh.at[pl.ds(first - 2 * width, rows)]
        else:
            target = board.at[pl.ds(first - 3 * width, rows)]
        return pltpu.make_async_copy(wide.at[pl.ds(first, rows)], target, store_sem.at[i])

    for i in range(blocks):
        load(i).start()
    nbias_ref[...] = small_ref[0:1, :]
    cbias_ref[...] = small_ref[1:2, :]
    penalty_ref[...] = small_ref[2:3, 0:1]
    for i in range(blocks):
        load(i).wait()

        @pl.loop(0, rows // 32)
        def _(r, i=i):
            at = pl.ds(pl.multiple_of(i * rows + r * 32, 32), 32)
            wide[at, :] = low[at, :].astype(F32)

        store(i).start()
    for i in range(blocks):
        store(i).wait()


def unpack(joined, small):
    n_rows, width = joined.shape
    rows = math.gcd(width, 256)
    big = pl.BlockSpec(memory_space=pl.ANY)
    vmem = pl.BlockSpec(memory_space=pltpu.VMEM)
    dma = pltpu.SemaphoreType.DMA
    return pl.pallas_call(
        functools.partial(unpack_kernel, rows),
        out_shape=[
            jax.ShapeDtypeStruct((2 * width, width), F32),
            jax.ShapeDtypeStruct((width, width), F32),
            jax.ShapeDtypeStruct((width, width), F32),
            jax.ShapeDtypeStruct((1, width), F32),
            jax.ShapeDtypeStruct((1, width), F32),
            jax.ShapeDtypeStruct((1, 1), F32),
        ],
        in_specs=[big, vmem],
        out_specs=[big] * 3 + [vmem] * 3,
        scratch_shapes=[
            pltpu.VMEM((n_rows, width), BF16),
            pltpu.VMEM((n_rows, width), F32),
            dma((n_rows // rows,)),
            dma((n_rows // rows,)),
        ],
        compiler_params=pltpu.CompilerParams(vmem_limit_bytes=60 * MIB),
        name="unpack",
    )(joined, small)


def on_device(
    n_nodes,
    n_grp,
    features,
    type_mask,
    edge_child,
    edge_slot,
    edge_weight,
    recv_rows,
    board_proj,
    neigh_proj,
    neigh_bias,
    combine_proj,
    combine_bias,
    out_cot,
):
    feats = features[0]
    rows, width = feats.shape
    peers = recv_rows.shape[2]
    cap = recv_rows.shape[3]
    slots = peers * cap
    targets = recv_rows[0, 0].reshape(1, slots)
    embed, hidden, pre, featb, pbl, qwl, cwl1, spread_t, dnum, dzb, aggb, stats = forward_pass(
        n_nodes,
        n_grp,
        feats,
        type_mask,
        (edge_slot, edge_child, edge_weight),
        targets,
        board_proj,
        neigh_proj,
        neigh_bias.reshape(1, width),
        combine_proj,
        combine_bias.reshape(1, width),
        out_cot[0],
    )
    grad_feats, summed, small = backward_pass(
        n_nodes,
        n_grp,
        type_mask,
        targets,
        stats,
        (edge_slot, edge_child, edge_weight),
        hidden,
        pre,
        featb,
        pbl,
        qwl,
        cwl1,
        spread_t,
        dnum,
        dzb,
        aggb,
    )
    grad_comb, grad_neigh, grad_board, grad_nbias, grad_cbias, penalty = unpack(summed, small)
    return (
        embed[None],
        penalty[0, 0],
        grad_feats[None],
        grad_board,
        grad_neigh,
        grad_nbias[0],
        grad_comb,
        grad_cbias[0],
    )


def solution(mesh):
    in_specs = (
        P("grp", "nodes", None),
        P("grp", "nodes"),
        P("grp", "nodes"),
        P("grp", "nodes"),
        P("grp", "nodes"),
        P("grp", "nodes", None, None),
        P(),
        P(),
        P(),
        P(),
        P(),
        P("grp", "nodes", None),
    )
    out_specs = (P("grp", "nodes", None), P(), P("grp", "nodes", None), P(), P(), P(), P(), P())
    return jax.shard_map(
        functools.partial(on_device, mesh.shape["nodes"], mesh.shape["grp"]),
        mesh=mesh,
        in_specs=in_specs,
        out_specs=out_specs,
        check_vma=False,
    )
```

```python
import functools
import math

import jax
import jax.numpy as jnp
from jax import lax
from jax.experimental import pallas as pl
from jax.experimental.pallas import tpu as pltpu
from jax.sharding import PartitionSpec as P

HIGH = lax.Precision.HIGHEST
MESH = pl.DeviceIdType.MESH
BF16 = jnp.bfloat16
F32 = jnp.float32
F8 = jnp.float8_e4m3fn
MIB = 2**20


def gelu_tanh(v):
    return jax.nn.gelu(v, approximate=True)


def dot_nt(left, right):
    return lax.dot_general(
        left, right, (((1,), (1,)), ((), ())), preferred_element_type=F32
    )


def dot_tn(left, right):
    return lax.dot_general(
        left, right, (((0,), (0,)), ((), ())), preferred_element_type=F32
    )


LINE = 4
CHUNKS = 4
FAR = 2
FORWARD_ACTS = "mYZfpiGDXRdaPugvxw"
FORWARD = (
    10, 11, 12, 13, 1100, 1101, 1102, 1103, 2010, 1140, 4102, 1141, 6010, 4100, 1142, 1143, 2014, 1110, 4101,
    3100, 13012, 13013, 1111, 1112, 3101, 1113, 3102, 2011, 4112, 14010, 1120, 4103, 4110, 1121, 1122, 3103,
    7010, 12011, 4113, 4111, 3110, 15012, 1123, 2012, 4120, 1130, 1131, 3111, 4121, 1132, 3112, 4122, 15013,
    1133, 7011, 2013, 16012, 3120, 3121, 4132, 4131, 5113, 4130, 3113, 5120, 5100, 12012, 10010, 16013, 8010,
    5101, 5132, 9010, 4133, 4123, 5131, 5122, 7012, 5111, 5112, 5102, 7013, 5121, 5110, 5130, 11011, 5103,
    17012, 11010, 11012, 5133, 17013, 5123, 12013,
)
ORDER = ((0, 1, 2, 3), (1, 2, 0, 3))


class Place:
    def __init__(self, n_nodes, n_grp):
        layer = n_nodes // LINE
        node = lax.axis_index("nodes")
        grp = lax.axis_index("grp")
        self.node, self.grp = node, grp
        self.size = {"l": layer, "c": 2, "y": layer // 2, "z": LINE, "x": n_grp}
        low = lax.rem(node, layer)
        self.at = {"l": low, "c": lax.rem(low, 2), "y": low // 2, "z": node // layer, "x": grp}

    def member(self, axis, index):
        layer = self.size["l"]
        low, line, grp = self.at["l"], self.at["z"], self.at["x"]
        if axis == "l":
            low = index
        elif axis == "c":
            low = self.at["y"] * 2 + index
        elif axis == "y":
            low = index * 2 + self.at["c"]
        elif axis == "z":
            line = index
        else:
            grp = index
        return {"nodes": line * layer + low, "grp": grp}

    def others(self, axis):
        size = self.size[axis]
        for far in range(1, size):
            index = lax.rem(self.at[axis] + far, size)
            yield far - 1, index, self.member(axis, index)


def remote(src, dst, send, recv, device):
    return pltpu.make_async_remote_copy(
        src_ref=src, dst_ref=dst, send_sem=send, recv_sem=recv, device_id=device, device_id_type=MESH
    )


def barrier(place, axes, meanwhile=None):
    sem = pltpu.get_barrier_semaphore()
    count = 0
    for axis in axes:
        for _, _, device in place.others(axis):
            pl.semaphore_signal(sem, inc=1, device_id=device, device_id_type=MESH)
            count += 1
    if meanwhile is not None:
        meanwhile()
    pl.semaphore_wait(sem, count)


def column_of(row_ref):
    row = row_ref[...].astype(F32)
    return jnp.broadcast_to(row, (128, row.shape[1])).T[:, 0:1]


def gelu(v):
    t = jnp.tanh(0.7978845608028654 * (v + 0.044715 * (v * v * v)))
    return v * (0.5 * (1.0 + t))


def gelu_slope(v):
    square = v * v
    t = jnp.tanh(0.7978845608028654 * (v + 0.044715 * (v * square)))
    bend = 0.7978845608028654 * (1.0 + 0.134145 * square)
    return 0.5 * (1.0 + t) + 0.5 * v * (1.0 - t * t) * bend


class Share:
    def __init__(self, place, bufs, send, recv):
        self.place, self.send, self.recv = place, send, recv
        self.stages, base = [], 0
        for axis, buf in zip(("l", "z", "x"), bufs):
            self.stages.append((axis, buf, base))
            base += place.size[axis] - 1

    def start(self, stage, value):
        axis, buf, base = self.stages[stage]
        me = self.place.at[axis]
        buf[me] = value
        for far, _, device in self.place.others(axis):
            remote(
                buf.at[me], buf.at[me], self.send.at[base + far], self.recv.at[base + far], device
            ).start()

    def finish(self, stage):
        axis, buf, base = self.stages[stage]
        me = self.place.at[axis]
        for far, _, device in self.place.others(axis):
            remote(
                buf.at[me], buf.at[me], self.send.at[base + far], self.recv.at[base + far], device
            ).wait()
        total = buf[0]
        for i in range(1, self.place.size[axis]):
            total += buf[i]
        return total


def run_ticks(t, ticks):
    for at, acts in enumerate(ticks):
        if acts:

            @pl.when(t == at)
            def _(acts=acts):
                for act in acts:
                    act()


def run_order(order, letters, steps, build, act):
    ticks = None
    names = [letters[number // 1000] + str(number % 1000)[1:] for number in order]
    for name in names:
        if name[0] == "Y":
            if ticks is None:
                ticks = [[] for _ in range(steps)]
                marks = sum(other[:2] == name[:2] for other in names)
            now = (int(name[2]) + 1) * steps // marks - 1
        elif name[0] == "Z":
            build(int(name[1]), ticks)
            ticks = None
        elif ticks is not None:
            ticks[max(now, 0)].append(functools.partial(act, name))
        else:
            act(name)


def share_sems(n_nodes, n_grp):
    return (n_nodes // LINE - 1) + (LINE - 1) + max(1, n_grp - 1)


def forward_kernel(
    n_nodes,
    n_grp,
    feats_h,
    mask_ref,
    place_ref,
    child_ref,
    weight_ref,
    targets_ref,
    board_h,
    neigh_h,
    nbias_ref,
    comb_h,
    cbias_ref,
    cot_h,
    embed_h,
    hid_h,
    pre_h,
    featb_h,
    board_b_h,
    neigh_b_h,
    comb1_b_h,
    st_h,
    far_h,
    dnum_h,
    dz_h,
    agg_h,
    stats_ref,
    stage,
    featb,
    hid,
    pre,
    board_b,
    neigh_b,
    comb_b,
    keys,
    msg,
    acc,
    spread,
    spread_t,
    out_slots,
    in_slots,
    out_tot,
    in_tot,
    picker,
    num,
    zval,
    zpre,
    cot,
    agg,
    dz,
    dnum,
    lines,
    far_spread,
    far_turned,
    far_picker,
    far_out,
    far_in,
    far_sum,
    end_sum,
    den_ref,
    scale_ref,
    count_l,
    count_z,
    count_x,
    load_sem,
    store_sem,
    key_send,
    key_recv,
    up_send,
    down_send,
    msg_recv,
    slot_send,
    slot_recv,
    tot_send,
    tot_recv,
    count_send,
    count_recv,
    line_send,
    line_recv,
    far_send,
    far_recv,
    sum_send,
    sum_recv,
    end_recv,
):
    place = Place(n_nodes, n_grp)
    z, low = place.at["z"], place.at["l"]
    layer = place.size["l"]
    rows, width = featb.shape
    edges = place_ref.shape[1]
    half = edges // 2
    layer_slots = spread.shape[1]
    cap = layer_slots // layer
    part = width // CHUNKS
    turn = math.gcd(half, 6400)
    steps = edges // turn

    sources = [feats_h.at[:]]
    for whole in (board_h, neigh_h, comb_h):
        for first in range(0, whole.shape[0], rows):
            sources.append(whole.at[pl.ds(first, rows)])
    n_stage = stage.shape[0]

    def load(i):
        return pltpu.make_async_copy(sources[i], stage.at[i % n_stage], load_sem.at[i % n_stage])

    for i in range(n_stage):
        load(i).start()
    load_cot = pltpu.make_async_copy(cot_h, cot, load_sem.at[n_stage])
    stores = []

    def store(src, dst):
        copy = pltpu.make_async_copy(src, dst, store_sem.at[len(stores)])
        copy.start()
        stores.append(copy)

    barrier(place, ("l", "z", "x"))
    keys[z, :, pl.ds(0, edges)] = place_ref[...] * 65536 + child_ref[...]
    keys[z, :, pl.ds(edges, half)] = (
        weight_ref[:, pl.ds(half, half)] * 65536 + weight_ref[:, pl.ds(0, half)]
    )

    def key_copy(far, device):
        return remote(keys.at[z], keys.at[z], key_send.at[far], key_recv.at[far], device)

    for far, _, device in place.others("z"):
        key_copy(far, device).start()
    inner = jnp.logical_and(z > 0, z < LINE - 1)
    outer = jnp.logical_or(z == 0, z == LINE - 1)
    half_at = z // 2
    far_end = (LINE - 1) * (1 - half_at)

    def line_copy(far, index, device):
        at = pl.ds(pl.multiple_of(index * layer_slots, layer_slots), layer_slots)
        return remote(
            targets_ref.at[:, at], lines.at[z], line_send.at[far], line_recv.at[far], device
        )

    @pl.when(outer)
    def _():
        for far, index, device in place.others("z"):
            line_copy(far, index, device).start()

    share = Share(place, (count_l, count_z, count_x), count_send, count_recv)
    mask = column_of(mask_ref)
    share.start(0, jnp.full((8, 128), jnp.sum(mask)))

    def cast(i, target, first):
        load(i).wait()
        slot = stage.at[i % n_stage]

        @pl.loop(0, rows // 32)
        def _(r):
            at = pl.ds(pl.multiple_of(r * 32, 32), 32)
            to = pl.ds(pl.multiple_of(first + r * 32, 32), 32)
            target[to, :] = slot[at, :].astype(BF16)

    cast(0, featb, 0)
    cast(1, board_b, 0)
    cast(2, board_b, rows)

    @pl.loop(0, CHUNKS)
    def _(k):
        at = pl.ds(pl.multiple_of(k * part, part), part)
        proj = jnp.dot(featb[...], board_b[:, at], preferred_element_type=F32)
        hid[:, at] = jnp.where(mask > 0.5, proj, stage[0, :, at]).astype(BF16)

    cast(3, neigh_b, 0)
    cast(4, neigh_b, rows)
    for i in range(n_stage, len(sources)):
        load(i).start()
    load_cot.start()

    def up_copy(src, k):
        piece = msg.at[src, k]
        index = src * CHUNKS + k
        return remote(
            piece, piece, up_send.at[index], msg_recv.at[index], place.member("z", z + 1)
        )

    def down_copy(src, k):
        piece = msg.at[src, k]
        index = src * CHUNKS + k
        return remote(
            piece, piece, down_send.at[index], msg_recv.at[index], place.member("z", z - 1)
        )

    def message(k):
        at = pl.ds(k * part, part)
        value = jnp.dot(hid[...], neigh_b[:, at], preferred_element_type=F32) + nbias_ref[:, at]
        pre[:, at] = value
        msg[z, k] = gelu(value).astype(BF16)

        @pl.when(z < LINE - 1)
        def _():
            up_copy(z, k).start()

        @pl.when(z > 0)
        def _():
            down_copy(z, k).start()

    def passes_up(k):
        return z < LINE - (1 if k < FAR else 2)

    def passes_down(k):
        return z > (0 if k < FAR else 1)

    def forward(j, k):
        below = z - 1 - j
        above = z + 1 + j

        comes = True if k < FAR or j == 0 else inner

        @pl.when(jnp.logical_and(below >= 0, comes))
        def _():
            up_copy(below, k).wait_recv()

            @pl.when(passes_up(k))
            def _():
                up_copy(below, k).start()

        @pl.when(jnp.logical_and(above < LINE, comes))
        def _():
            down_copy(above, k).wait_recv()

            @pl.when(passes_down(k))
            def _():
                down_copy(above, k).start()

    def tot_copy(src, far, index, device):
        at = (layer - 1) * src + far
        return remote(
            out_tot.at[src, pl.ds(pl.multiple_of(index * cap, cap), cap)],
            in_tot.at[src, pl.ds(pl.multiple_of(low * cap, cap), cap)],
            tot_send.at[at],
            tot_recv.at[at],
            device,
        )

    def finish_spread(src):
        total = acc[...]
        spread[src] = total.astype(BF16)
        spread_t[src] = total.astype(BF16).T
        sums = jnp.sum(total, axis=1, keepdims=True).astype(jnp.int32)
        lane = lax.broadcasted_iota(jnp.int32, (layer_slots, 128), 1)
        digit = jnp.where(
            lane == 0, sums & 255, jnp.where(lane == 1, (sums >> 8) & 255, jnp.where(lane == 2, sums >> 16, 0))
        )
        out_tot[src] = digit.astype(F32).astype(BF16)
        own = pl.ds(pl.multiple_of(low * cap, cap), cap)
        in_tot[src, own] = out_tot[src, own]
        for far, index, device in place.others("l"):
            tot_copy(src, far, index, device).start()

    def source(which):
        flip = z // 2
        depth = z * (1 - 2 * flip) + (LINE - 1) * flip
        index = ORDER[0][which] * (1 - depth) + ORDER[1][which] * depth
        return index * (1 - 2 * flip) + (LINE - 1) * flip

    def build(which, ticks):
        src, target = (source(which), z) if which < LINE else (z, far_end)
        acc[...] = jnp.zeros_like(acc)
        if 0 < which < LINE:
            far = lax.rem(z - src - 1 + LINE, LINE)
            remote(
                keys.at[src], keys.at[src], key_send.at[0], key_recv.at[far], place.member("z", src)
            ).wait_recv()

        @pl.loop(0, steps)
        def _(t):
            second = t // (steps // 2)
            key = keys[src, :, pl.ds(pl.multiple_of(t * turn, turn), turn)]
            start = edges + (t - second * (steps // 2)) * turn
            pair = keys[src, :, pl.ds(pl.multiple_of(start, turn), turn)]
            weight = (lax.shift_right_logical(pair, second * 16) & 65535).astype(F32).astype(F8)
            child = (key & 65535).astype(jnp.int16)
            slot = (lax.shift_right_logical(key, 16) - target * layer_slots).astype(jnp.int16)
            right = jnp.where(
                lax.broadcasted_iota(jnp.int16, (rows, turn), 0) == child, weight, jnp.zeros((), F8)
            )
            block = 256
            for first in range(0, layer_slots, block):
                ids = lax.broadcasted_iota(jnp.int16, (block, turn), 0) + jnp.asarray(
                    first, jnp.int16
                )
                left = jnp.where(ids == slot, jnp.ones((), F8), jnp.zeros((), F8))
                acc[pl.ds(first, block), :] += dot_nt(left, right)
            run_ticks(t, ticks)

        if which < LINE:
            finish_spread(src)
        else:
            far_spread[...] = acc[...].astype(BF16)
            far_turned[...] = acc[...].astype(BF16).T

    def slot_copy(src, k, far, index, device):
        at = (src * CHUNKS + k) * (layer - 1) + far
        return remote(
            out_slots.at[src, k, pl.ds(pl.multiple_of(index * cap, cap), cap)],
            in_slots.at[src, k, pl.ds(pl.multiple_of(low * cap, cap), cap)],
            slot_send.at[at],
            slot_recv.at[at],
            device,
        )

    def piece(src, k):
        out_slots[src, k] = jnp.dot(spread[src], msg[src, k], preferred_element_type=F32).astype(BF16)
        for far, index, device in place.others("l"):
            slot_copy(src, k, far, index, device).start()
        own = pl.ds(pl.multiple_of(low * cap, cap), cap)
        in_slots[src, k, own] = out_slots[src, k, own]

    def pick(src, k):
        for far, index, device in place.others("l"):
            slot_copy(src, k, far, index, device).wait_recv()
        num[k] += jnp.dot(picker[src], in_slots[src, k], preferred_element_type=F32)

    def unless_far(which, k, act):
        if which < 2 or k < FAR:
            act(source(which), k)
        else:

            @pl.when(inner)
            def _():
                act(source(which), k)

    def far_copy(k, far, index, device):
        at = k * (layer - 1) + far
        return remote(
            far_out.at[k, pl.ds(pl.multiple_of(index * cap, cap), cap)],
            far_in.at[k, pl.ds(pl.multiple_of(low * cap, cap), cap)],
            far_send.at[at],
            far_recv.at[at],
            device,
        )

    onward = 1 - 2 * half_at

    def sum_copy(i):
        return remote(
            far_sum.at[i], far_sum.at[i], sum_send.at[i], sum_recv.at[i], place.member("z", z + onward)
        )

    def end_copy(i):
        return remote(
            far_sum.at[i],
            end_sum.at[i],
            sum_send.at[i],
            end_recv.at[i],
            place.member("z", z + 2 * onward),
        )

    def far_slots(k):
        i = k - FAR
        far_out[i] = jnp.dot(far_spread[...], msg[z, k], preferred_element_type=F32).astype(BF16)
        for far, index, device in place.others("l"):
            far_copy(i, far, index, device).start()
        own = pl.ds(pl.multiple_of(low * cap, cap), cap)
        far_in[i, own] = far_out[i, own]

    def make_far_picker():
        far = lax.rem(z - far_end - 1 + LINE, LINE)
        remote(
            lines.at[far_end],
            lines.at[far_end],
            line_send.at[0],
            line_recv.at[far],
            place.member("z", far_end),
        ).wait_recv()
        ids = lax.broadcasted_iota(jnp.int32, (rows, layer_slots), 0)
        far_picker[...] = jnp.where(ids == lines[far_end], 1.0, 0.0).astype(BF16)

        @pl.when(inner)
        def _():
            near = (LINE - 1) - far_end
            back = lax.rem(z - near - 1 + LINE, LINE)
            remote(
                lines.at[near],
                lines.at[near],
                line_send.at[0],
                line_recv.at[back],
                place.member("z", near),
            ).wait_recv()

    def far_parents(i):
        for far, index, device in place.others("l"):
            far_copy(i, far, index, device).wait_recv()
        return jnp.dot(far_picker[...], far_in[i], preferred_element_type=F32)

    def first_sum(k):
        @pl.when(outer)
        def _():
            far_sum[k - FAR] = far_parents(k - FAR).astype(BF16)
            sum_copy(k - FAR).start()

    def second_sum(k):
        @pl.when(inner)
        def _():
            i = k - FAR
            value = far_parents(i)
            sum_copy(i).wait_recv()
            far_sum[i] = (far_sum[i].astype(F32) + value).astype(BF16)
            end_copy(i).start()

    def add_far(k):
        @pl.when(outer)
        def _():
            end_copy(k - FAR).wait_recv()
            num[k] += end_sum[k - FAR].astype(F32)

    def make_picker():
        @pl.loop(0, LINE)
        def _(src):
            at = pl.ds(pl.multiple_of(src * layer_slots, layer_slots), layer_slots)
            ids = lax.broadcasted_iota(jnp.int32, (rows, layer_slots), 0)
            picker[src] = jnp.where(ids == targets_ref[:, at], 1.0, 0.0).astype(BF16)

        num[...] = jnp.zeros_like(num)

    def comb_piece(i):
        for j in range(i, 2 * width // rows, CHUNKS):
            cast(5 + j, comb_b, j * rows)

    def self_part():
        @pl.loop(0, CHUNKS)
        def _(k):
            at = pl.ds(pl.multiple_of(k * part, part), part)
            zpre[:, at] = (
                jnp.dot(hid[...], comb_b[0:width, at], preferred_element_type=F32)
                + cbias_ref[:, at]
            )

    def results():
        store(hid, hid_h)
        store(pre, pre_h)
        store(featb, featb_h)
        store(board_b, board_b_h)
        store(neigh_b, neigh_b_h)
        store(comb_b.at[pl.ds(0, width)], comb1_b_h)
        store(spread_t, st_h)
        store(far_turned, far_h)

    def totals():
        digits = jnp.zeros((rows, 128), F32)
        for src in range(LINE):
            for far, index, device in place.others("l"):
                tot_copy(src, far, index, device).wait_recv()
            digits += jnp.dot(picker[src], in_tot[src], preferred_element_type=F32)
        lane = lax.broadcasted_iota(jnp.int32, (rows, 128), 1)
        worth = jnp.where(
            lane == 0, 1.0, jnp.where(lane == 1, 256.0, jnp.where(lane == 2, 65536.0, 0.0))
        )
        den_ref[...] = jnp.broadcast_to(
            1.0 + jnp.sum(digits * worth, axis=1, keepdims=True), (rows, 128)
        )

    def neighbours(k):
        at = pl.ds(k * part, part)
        agg[:, at] = (num[k] / den_ref[:, 0:1]).astype(BF16)
        if k < CHUNKS - 1:

            @pl.loop(0, CHUNKS)
            def _(n):
                to = pl.ds(pl.multiple_of(n * part, part), part)
                zpre[:, to] += jnp.dot(
                    agg[:, at], comb_b[pl.ds(width + k * part, part), to], preferred_element_type=F32
                )

    def step_share(stage):
        if stage in (1, 2):
            share.start(stage, share.finish(stage - 1))
        elif stage == 3:
            boards = share.finish(2)
            scale_ref[...] = 1.0 / (width * (1.0 + boards))

    acts = {
        "P": step_share,
        "m": message,
        "f": forward,
        "p": lambda which, k: unless_far(which, k, piece),
        "i": lambda which, k: unless_far(which, k, pick),
        "u": far_slots,
        "g": lambda _: make_far_picker(),
        "v": first_sum,
        "x": second_sum,
        "w": add_far,
        "G": lambda _: make_picker(),
        "D": comb_piece,
        "X": lambda _: self_part(),
        "R": lambda _: results(),
        "d": lambda _: totals(),
        "a": neighbours,
    }

    def act(step):
        acts[step[0]](*(int(c) for c in step[1:]))

    run_order(FORWARD, FORWARD_ACTS, steps, build, act)
    neighbours(CHUNKS - 1)
    load_cot.wait()
    den = den_ref[:, 0:1]
    scale = scale_ref[0:1, 0:1]
    last = pl.ds(width - part, part)

    def dense(k, carry):
        square, along = carry
        at = pl.ds(pl.multiple_of(k * part, part), part)
        value = zpre[:, at] + jnp.dot(
            agg[:, last], comb_b[pl.ds(2 * width - part, part), at], preferred_element_type=F32
        )
        zpre[:, at] = value
        out = gelu(value)
        zval[:, at] = out
        square += jnp.sum(out * out, axis=1, keepdims=True)
        along += jnp.sum(out * cot[:, at], axis=1, keepdims=True)
        return square, along

    zero = jnp.zeros((rows, 1), F32)
    square, along = lax.fori_loop(0, CHUNKS, dense, (zero, zero))
    inverse = lax.rsqrt(square + 1e-06)
    along = along * inverse
    push = jnp.where(mask > 0.5, 2.0 * scale, 0.0)
    stats_ref[...] = jnp.concatenate(
        [
            jnp.full((8, 128), jnp.sum(jnp.where(mask > 0.5, square, 0.0))),
            jnp.broadcast_to(scale, (8, 128)),
        ],
        axis=0,
    )

    @pl.loop(0, CHUNKS)
    def _(k):
        at = pl.ds(pl.multiple_of(k * part, part), part)
        out = zval[:, at]
        emb = out * inverse
        grad = inverse * (cot[:, at] - emb * along) + push * out
        dz[:, at] = (grad * gelu_slope(zpre[:, at])).astype(BF16)
        zval[:, at] = emb

    store(zval, embed_h)
    store(dz, dz_h)
    store(agg, agg_h)

    @pl.loop(0, CHUNKS)
    def _(k):
        at = pl.ds(pl.multiple_of(k * part, part), part)
        back = dot_nt(dz[...], comb_b[pl.ds(pl.multiple_of(width + k * part, part), part), :])
        dnum[:, at] = (back / den).astype(BF16)

    store(dnum, dnum_h)

    for far, _, device in place.others("z"):
        key_copy(far, device).wait_send()

    @pl.loop(0, LINE * CHUNKS)
    def _(i):
        src = i // CHUNKS
        k = lax.rem(i, CHUNKS)

        early = k < FAR

        @pl.when(
            jnp.logical_or(
                jnp.logical_and(src == z, z < LINE - 1),
                jnp.logical_and(
                    src < z, jnp.logical_or(jnp.logical_and(early, z < LINE - 1), z < LINE - 2)
                ),
            )
        )
        def _():
            up_copy(src, k).wait_send()

        @pl.when(
            jnp.logical_or(
                jnp.logical_and(src == z, z > 0),
                jnp.logical_and(src > z, jnp.logical_or(jnp.logical_and(early, z > 0), z > 1)),
            )
        )
        def _():
            down_copy(src, k).wait_send()

        near = jnp.logical_and(src - z < 2, z - src < 2)

        @pl.when(jnp.logical_or(jnp.logical_or(early, inner), near))
        def _():
            for far, index, device in place.others("l"):
                slot_copy(src, k, far, index, device).wait_send()

    for i in range(CHUNKS - FAR):
        sum_copy(i).wait_send()
        for far, index, device in place.others("l"):
            far_copy(i, far, index, device).wait_send()

    @pl.when(outer)
    def _():
        for far, index, device in place.others("z"):
            line_copy(far, index, device).wait_send()

    for src in range(LINE):
        for far, index, device in place.others("l"):
            tot_copy(src, far, index, device).wait_send()
    for copy in stores:
        copy.wait()


def forward_pass(n_nodes, n_grp, feats, mask, edges_of, targets, board, neigh, nbias, comb, cbias, cot):
    rows, width = feats.shape
    edges = edges_of[0].shape[1]
    layer = n_nodes // LINE
    layer_slots = targets.shape[1] // LINE
    part = width // CHUNKS
    dma = pltpu.SemaphoreType.DMA
    n_stage = 5
    big = pl.BlockSpec(memory_space=pl.ANY)
    small = pl.BlockSpec(memory_space=pltpu.VMEM)

    def hbm(shape, dtype):
        return jax.ShapeDtypeStruct(shape, dtype)

    return pl.pallas_call(
        functools.partial(forward_kernel, n_nodes, n_grp),
        out_shape=[
            hbm((rows, width), F32),
            hbm((rows, width), BF16),
            hbm((rows, width), F32),
            hbm((rows, width), BF16),
            hbm((width, width), BF16),
            hbm((width, width), BF16),
            hbm((width, width), BF16),
            hbm((LINE, rows, layer_slots), BF16),
            hbm((rows, layer_slots), BF16),
            hbm((rows, width), BF16),
            hbm((rows, width), BF16),
            hbm((rows, width), BF16),
            hbm((16, 128), F32),
        ],
        in_specs=[big] + [small] * 5 + [big, big, small, big, small, big],
        out_specs=[big] * 12 + [small],
        scratch_shapes=[
            pltpu.VMEM((n_stage, rows, width), F32),
            pltpu.VMEM((rows, width), BF16),
            pltpu.VMEM((rows, width), BF16),
            pltpu.VMEM((rows, width), F32),
            pltpu.VMEM((width, width), BF16),
            pltpu.VMEM((width, width), BF16),
            pltpu.VMEM((2 * width, width), BF16),
            pltpu.VMEM((LINE, 1, edges + edges // 2), jnp.int32),
            pltpu.VMEM((LINE, CHUNKS, rows, part), BF16),
            pltpu.VMEM((layer_slots, rows), F32),
            pltpu.VMEM((LINE, layer_slots, rows), BF16),
            pltpu.VMEM((LINE, rows, layer_slots), BF16),
            pltpu.VMEM((LINE, CHUNKS, layer_slots, part), BF16),
            pltpu.VMEM((LINE, CHUNKS, layer_slots, part), BF16),
            pltpu.VMEM((LINE, layer_slots, 128), BF16),
            pltpu.VMEM((LINE, layer_slots, 128), BF16),
            pltpu.VMEM((LINE, rows, layer_slots), BF16),
            pltpu.VMEM((CHUNKS, rows, part), F32),
            pltpu.VMEM((rows, width), F32),
            pltpu.VMEM((rows, width), F32),
            pltpu.VMEM((rows, width), F32),
            pltpu.VMEM((rows, width), BF16),
            pltpu.VMEM((rows, width), BF16),
            pltpu.VMEM((rows, width), BF16),
            pltpu.VMEM((LINE, 1, layer_slots), jnp.int32),
            pltpu.VMEM((layer_slots, rows), BF16),
            pltpu.VMEM((rows, layer_slots), BF16),
            pltpu.VMEM((rows, layer_slots), BF16),
            pltpu.VMEM((CHUNKS - FAR, layer_slots, part), BF16),
            pltpu.VMEM((CHUNKS - FAR, layer_slots, part), BF16),
            pltpu.VMEM((CHUNKS - FAR, rows, part), BF16),
            pltpu.VMEM((CHUNKS - FAR, rows, part), BF16),
            pltpu.VMEM((rows, 128), F32),
            pltpu.VMEM((8, 128), F32),
            pltpu.VMEM((layer, 8, 128), F32),
            pltpu.VMEM((LINE, 8, 128), F32),
            pltpu.VMEM((n_grp, 8, 128), F32),
            dma((n_stage + 1,)),
            dma((12,)),
            dma((LINE - 1,)),
            dma((LINE - 1,)),
            dma((LINE * CHUNKS,)),
            dma((LINE * CHUNKS,)),
            dma((LINE * CHUNKS,)),
            dma((LINE * CHUNKS * (layer - 1),)),
            dma((LINE * CHUNKS * (layer - 1),)),
            dma((LINE * (layer - 1),)),
            dma((LINE * (layer - 1),)),
            dma((share_sems(n_nodes, n_grp),)),
            dma((share_sems(n_nodes, n_grp),)),
            dma((LINE - 1,)),
            dma((LINE - 1,)),
            dma(((CHUNKS - FAR) * (layer - 1),)),
            dma(((CHUNKS - FAR) * (layer - 1),)),
            dma((CHUNKS - FAR,)),
            dma((CHUNKS - FAR,)),
            dma((CHUNKS - FAR,)),
        ],
        compiler_params=pltpu.CompilerParams(
            vmem_limit_bytes=63 * MIB, collective_id=2, has_side_effects=True
        ),
        name="forward_pass",
    )(feats, mask, *edges_of, targets, board, neigh, nbias, comb, cbias, cot)


def add_into(target, first, count, columns, parts, step=16):
    @pl.loop(0, count // step)
    def _(i):
        at = pl.ds(pl.multiple_of(first + i * step, step), step)
        total = target[at, columns].astype(F32)
        for part in parts:
            total += part[pl.ds(pl.multiple_of(i * step, step), step), :].astype(F32)
        target[at, columns] = total.astype(target.dtype)


def reduce_job(place, order, grad, region, arrive, land, last, send, recv, free, base):
    first, rows, left, columns = region
    half = columns // 2
    core = place.at["c"]
    mine = pl.ds(pl.multiple_of(left + core * half, half), half)
    theirs = pl.ds(pl.multiple_of(left + (1 - core) * half, half), half)
    mate = place.member("c", 1 - core)
    block = pl.ds(first, rows)
    sems = iter(range(base, base + send.shape[0]))

    def lay(src, dst, device):
        sem = next(sems)
        return remote(src, dst, send.at[sem], recv.at[sem], device)

    across = lay(grad.at[block, theirs], arrive, mate)
    down = []
    begin, length, used = first, rows, 0
    for axis in order:
        length //= place.size[axis]
        copies, parts, devices = [], [], []
        for far, index, device in place.others(axis):
            start = pl.multiple_of(begin + index * length, 16)
            slot = land.at[pl.ds(used, length)]
            used += length
            copies.append(lay(grad.at[pl.ds(start, length), mine], slot, device))
            parts.append(slot)
            devices.append(device)
        parent = begin
        begin = pl.multiple_of(begin + place.at[axis] * length, 16)
        down.append((axis, parent, begin, length, copies, parts, devices))
    axis, parent, begin, length, _, _, devices = down[-1]
    here = pl.ds(pl.multiple_of(place.at[axis] * length, 16), length)
    whole = pl.ds(pl.multiple_of(parent, 16), length * place.size[axis])
    end = [lay(last.at[here], last.at[here], device) for device in devices]
    up = []
    for stage in range(len(down) - 1, 0, -1):
        axis, _, start, piece, _, _, devices = down[stage - 1]
        own = grad.at[pl.ds(start, piece), mine]
        up.append((stage, len(devices), [lay(own, own, device) for device in devices]))
    own = grad.at[block, mine]
    back = lay(own, own, mate)
    yield

    def release(at, devices):
        for device in devices:
            pl.semaphore_signal(free.at[base + at], inc=1, device_id=device, device_id_type=MESH)

    across.start()
    yield
    across.wait()
    release(0, [mate])
    add_into(grad, first, rows, mine, [arrive])
    for stage, (_, _, begin, length, copies, parts, devices) in enumerate(down):
        for copy in copies:
            copy.start()
        yield
        for copy in copies:
            copy.wait()
        if stage < len(down) - 1:
            release(stage + 1, devices)
        add_into(grad, begin, length, mine, parts)
    last[here] = grad[pl.ds(begin, length), mine]
    for copy in end:
        copy.start()
    yield
    for copy in end:
        copy.wait()
    grad[whole, mine] = last[pl.ds(0, whole.size)]
    for stage, count, copies in up:
        pl.semaphore_wait(free.at[base + stage], count)
        for copy in copies:
            copy.start()
        yield
        for copy in copies:
            copy.wait()
    pl.semaphore_wait(free.at[base], 1)
    back.start()
    yield
    back.wait()


def job_sems(n_nodes, n_grp):
    return 2 * (1 + (n_nodes // LINE // 2 - 1) + (LINE - 1) + (n_grp - 1))


AHEAD = 2
BEHIND = CHUNKS - AHEAD
BACKWARD_ACTS = "lLAfqYZBW321OGSEHFPcnb"
BACKWARD = (
    10, 2011, 7012, 13010, 2010, 8010, 5110, 19011, 5111, 19013, 19012, 19010, 4101, 7013, 3101, 5112, 1011,
    3100, 9012, 19010, 4111, 19013, 5113, 1013, 3111, 19011, 9013, 4100, 5114, 3110, 6011, 19010, 19012,
    10012, 14010, 1012, 10013, 11012, 5120, 5121, 11013, 19011, 4121, 19013, 3121, 5122, 12012, 4131, 19010,
    3120, 4130, 19011, 5123, 4120, 5124, 4110, 19010, 6012, 12013, 19011, 19012, 20012, 20013, 12011, 20013,
    19010, 20012, 19013, 20011, 19011, 12010, 19012, 20013, 20011, 20010, 15010, 19013, 16011, 21012, 21013,
    19010, 20010, 19012, 16010, 20012, 20011, 21013, 21010, 21011, 21012, 19011, 20011, 20010, 21011, 21010,
    20013, 21013, 19013, 19011, 19012, 20010, 20011, 21012, 20013, 21013, 21011, 20010, 21010, 19012, 20011,
    20012, 21012, 20013, 21013, 21010, 21011, 19013, 21012, 20013, 20010, 21010, 20011, 21011, 21013, 21012,
    18010, 20012, 21010, 20010, 21013, 19010, 21011, 19012, 20012, 20011, 21012, 20013, 18011, 19013, 21011,
    20012, 19011, 21010, 21013, 19012, 21012, 19010, 20010, 21011, 18012, 21010, 19013, 20011, 20012, 17010,
    20013, 21010, 21012, 21011, 21013, 18013, 20010, 20012,
)


def gradient_regions(n_nodes, n_grp, width):
    pieces = n_nodes * n_grp // 2
    x_first, y_first = ("x", "y", "z"), ("y", "x", "z")
    regions = {}
    count = max(1, min(4, 2 * width // (16 * pieces)))
    n_rows = 2 * width // count
    for j in range(count):
        regions[f"comb{j}"] = (j * n_rows, n_rows, 0, width, y_first if j % 2 else x_first)
    if width % (16 * pieces) == 0:
        part = width // CHUNKS
        for k in range(CHUNKS):
            regions[f"neigh{k}"] = (2 * width, width, k * part, part, x_first if k % 2 else y_first)
        count = max(1, min(4, width // (16 * pieces)))
        n_rows = width // count
        for j in range(count):
            order = (x_first, y_first, x_first, ("z", "y", "x"))[j]
            regions[f"board{j}"] = (3 * width + j * n_rows, n_rows, 0, width, order)
    else:
        regions["board0"] = (2 * width, 2 * width, 0, width, x_first)
    return regions


def backward_kernel(
    n_nodes,
    n_grp,
    mask_ref,
    targets_ref,
    stats_ref,
    place_h,
    child_h,
    weight_h,
    hid_h,
    pre_h,
    featb_h,
    board_b_h,
    neigh_b_h,
    comb1_b_h,
    st_h,
    far_h,
    dnum_h,
    dz_h,
    agg_h,
    gfeat_h,
    comb_h,
    neigh_h,
    board_h,
    small_ref,
    hid,
    pre,
    featb,
    board_b,
    neigh_b,
    comb1_b,
    spread_t,
    dnum,
    dz,
    agg,
    picker_t,
    picker_l,
    lines,
    edge_place,
    edge_child,
    edge_weight,
    acc,
    own_t,
    parents,
    out_slots,
    in_slots,
    chain,
    tmp,
    dpre,
    dh,
    grad,
    arrive,
    land,
    gather,
    share_l,
    share_z,
    share_x,
    small,
    load_sem,
    store_sem,
    slot_send,
    slot_recv,
    up_send,
    down_send,
    chain_recv,
    line_send,
    line_recv,
    parent_up,
    parent_down,
    parent_recv,
    job_send,
    job_recv,
    job_free,
    share_send,
    share_recv,
):
    place = Place(n_nodes, n_grp)
    z, low = place.at["z"], place.at["l"]
    layer = place.size["l"]
    rows, width = hid.shape
    layer_slots = spread_t.shape[2]
    cap = layer_slots // layer
    part = width // CHUNKS

    loads = {}
    for i, (name, src, dst) in enumerate(
        (
            ("dnum", dnum_h, dnum),
            ("hid", hid_h, hid),
            ("agg", agg_h, agg),
            ("dz", dz_h, dz),
            ("spread_t", st_h, spread_t),
            ("comb1_b", comb1_b_h, comb1_b),
            ("pre", pre_h, pre),
            ("neigh_b", neigh_b_h, neigh_b),
            ("featb", featb_h, featb),
            ("board_b", board_b_h, board_b),
            ("place", place_h, edge_place),
            ("child", child_h, edge_child),
            ("weight", weight_h, edge_weight),
            ("far", far_h, own_t.at[(LINE - 1) * (1 - place.at["z"] // 2)]),
        )
    ):
        loads[name] = pltpu.make_async_copy(src, dst, load_sem.at[i])
        loads[name].start()
    def make_pickers():
        @pl.loop(0, LINE)
        def _(src):
            at = pl.ds(pl.multiple_of(src * layer_slots, layer_slots), layer_slots)
            ids = lax.broadcasted_iota(jnp.int32, (rows, layer_slots), 0)
            picker_t[src] = jnp.where(ids == targets_ref[:, at], 1.0, 0.0).astype(BF16).T

    barrier(place, ("l", "z", "x"), make_pickers)
    stores = []

    def store(src, dst):
        copy = pltpu.make_async_copy(src, dst, store_sem.at[len(stores)])
        copy.start()
        stores.append(copy)

    mask = column_of(mask_ref) > 0.5

    def source(which):
        flip = z // 2
        inner = z * (1 - 2 * flip) + (LINE - 1) * flip
        index = ORDER[0][which] * (1 - inner) + ORDER[1][which] * inner
        return index * (1 - 2 * flip) + (LINE - 1) * flip

    def cols(k):
        return pl.ds(pl.multiple_of(k * part, part), part)

    def slot_copy(dst, k, far, index, device):
        at = (dst * CHUNKS + k) * (layer - 1) + far
        return remote(
            out_slots.at[dst, k, pl.ds(pl.multiple_of(index * cap, cap), cap)],
            in_slots.at[dst, k, pl.ds(pl.multiple_of(low * cap, cap), cap)],
            slot_send.at[at],
            slot_recv.at[at],
            device,
        )

    def back(dst, k):
        out_slots[dst, k] = jnp.dot(
            picker_t[dst], dnum[:, cols(k)], preferred_element_type=F32
        ).astype(BF16)
        for far, index, device in place.others("l"):
            slot_copy(dst, k, far, index, device).start()
        own = pl.ds(pl.multiple_of(low * cap, cap), cap)
        in_slots[dst, k, own] = out_slots[dst, k, own]

    def child_sums(dst, k):
        for far, index, device in place.others("l"):
            slot_copy(dst, k, far, index, device).wait_recv()
        tmp[...] = jnp.dot(spread_t[dst], in_slots[dst, k], preferred_element_type=F32)

    def up_copy(dst, k):
        k = k - AHEAD
        at = dst * BEHIND + k
        return remote(
            chain.at[dst, k],
            chain.at[dst, k],
            up_send.at[at],
            chain_recv.at[at],
            place.member("z", z + 1),
        )

    def down_copy(dst, k, last):
        slot = LINE if last else dst
        k = k - AHEAD
        return remote(
            chain.at[dst, k],
            chain.at[slot, k],
            down_send.at[dst * BEHIND + k],
            chain_recv.at[slot * BEHIND + k],
            place.member("z", z - 1),
        )

    def arrived(slot, k):
        k = k - AHEAD
        remote(
            chain.at[slot, k],
            chain.at[slot, k],
            up_send.at[0],
            chain_recv.at[slot * BEHIND + k],
            place.member("z", lax.rem(z + 1, LINE)),
        ).wait_recv()

    def hand_on(dst, k):
        child_sums(dst, k)

        @pl.when(dst > z)
        def _():
            @pl.when(z > 0)
            def _():
                up_copy(dst, k).wait_recv()
                chain[dst, k - AHEAD] = (chain[dst, k - AHEAD].astype(F32) + tmp[...]).astype(BF16)

            @pl.when(z == 0)
            def _():
                chain[dst, k - AHEAD] = tmp[...].astype(BF16)

            up_copy(dst, k).start()

        @pl.when(dst < z)
        def _():
            @pl.when(z < LINE - 1)
            def _():
                down_copy(dst, k, False).wait_recv()
                chain[dst, k - AHEAD] = (chain[dst, k - AHEAD].astype(F32) + tmp[...]).astype(BF16)

            @pl.when(z == LINE - 1)
            def _():
                chain[dst, k - AHEAD] = tmp[...].astype(BF16)

            @pl.when(dst == z - 1)
            def _():
                down_copy(dst, k, True).start()

            @pl.when(dst < z - 1)
            def _():
                down_copy(dst, k, False).start()

    regions = gradient_regions(n_nodes, n_grp, width)
    per_job = job_sems(n_nodes, n_grp)

    def job(name):
        first, n_rows, left, columns, order = regions[name]
        rows_at, cols_at = pl.ds(first, n_rows), pl.ds(left, columns)
        land_at = pl.ds(left // 2, columns // 2)
        yield from reduce_job(
            place,
            order,
            grad,
            (first, n_rows, left, columns),
            arrive.at[rows_at, land_at],
            land.at[rows_at, land_at],
            gather.at[pl.ds(first // 4, n_rows // 4), land_at],
            job_send,
            job_recv,
            job_free,
            list(regions).index(name) * per_job,
        )
        for target, low_row, count in ((comb_h, 0, 2), (neigh_h, 2, 1), (board_h, 3, 1)):
            start = max(first, low_row * width)
            stop = min(first + n_rows, (low_row + count) * width)
            if start < stop:
                store(
                    grad.at[pl.ds(start, stop - start), cols_at],
                    target.at[pl.ds(start - low_row * width, stop - start), cols_at],
                )

    jobs = {name: job(name) for name in regions}
    for lay_out in jobs.values():
        next(lay_out)

    def step_job(name, last=False):
        if name in jobs and (last or name != "board0" or "board3" in regions):
            try:
                next(jobs[name])
            except StopIteration:
                del jobs[name]

    loads["dnum"].wait()

    def back_all(k):
        for which in (3, 2, 1, 0):
            back(source(which), k)

    def comb_grad(left, first):
        @pl.loop(0, CHUNKS)
        def _(k):
            grad[pl.ds(first, width), cols(k)] = dot_tn(left[...], dz[:, cols(k)]).astype(BF16)

    def line_targets():
        lines[z] = targets_ref[:, pl.ds(pl.multiple_of(z * layer_slots, layer_slots), layer_slots)]
        for far, index, device in place.others("z"):
            at = pl.ds(pl.multiple_of(index * layer_slots, layer_slots), layer_slots)
            remote(
                targets_ref.at[:, at], lines.at[z], line_send.at[far], line_recv.at[far], device
            ).start()

    def line_picker(which):
        src = source(which)
        far = lax.rem(z - src - 1 + LINE, LINE)
        remote(
            lines.at[src], lines.at[src], line_send.at[0], line_recv.at[far], place.member("z", src)
        ).wait_recv()
        ids = lax.broadcasted_iota(jnp.int32, (rows, layer_slots), 0)
        picker_l[src] = jnp.where(ids == lines[src], 1.0, 0.0).astype(BF16).T

    def parent_copy(src, k, sems, to):
        piece = parents.at[src, k]
        at = src * AHEAD + k
        return remote(piece, piece, sems.at[at], parent_recv.at[at], place.member("z", to))

    def parent_send(k):
        parents[z, k] = dnum[:, cols(k)]

        @pl.when(z < LINE - 1)
        def _():
            parent_copy(z, k, parent_up, z + 1).start()

        @pl.when(z > 0)
        def _():
            parent_copy(z, k, parent_down, z - 1).start()

    def parent_forward(j, k):
        below = z - 1 - j
        above = z + 1 + j

        @pl.when(below >= 0)
        def _():
            parent_copy(below, k, parent_up, z + 1).wait_recv()

            @pl.when(z < LINE - 1)
            def _():
                parent_copy(below, k, parent_up, z + 1).start()

        @pl.when(above < LINE)
        def _():
            parent_copy(above, k, parent_down, z - 1).wait_recv()

            @pl.when(z > 0)
            def _():
                parent_copy(above, k, parent_down, z - 1).start()

    def parent_slots(which, k):
        src = source(which)
        choose = picker_t[z] if which == 0 else picker_l[src]
        out_slots[src, k] = jnp.dot(choose, parents[src, k], preferred_element_type=F32).astype(
            BF16
        )
        for far, index, device in place.others("l"):
            slot_copy(src, k, far, index, device).start()
        own = pl.ds(pl.multiple_of(low * cap, cap), cap)
        in_slots[src, k, own] = out_slots[src, k, own]

    edges = edge_place.shape[1]
    turn = math.gcd(edges, 2560)
    steps = edges // turn

    def build_own(which, ticks):
        src = source(which)
        if which == 1:
            for name in ("place", "child", "weight", "far"):
                loads[name].wait()
        acc[...] = jnp.zeros_like(acc)

        @pl.loop(0, steps)
        def _(t):
            at = pl.ds(pl.multiple_of(t * turn, turn), turn)
            slot = (edge_place[:, at] - src * layer_slots).astype(jnp.int16)
            child = edge_child[:, at].astype(jnp.int16)
            weight = edge_weight[:, at].astype(F32).astype(F8)
            right = jnp.where(
                lax.broadcasted_iota(jnp.int16, (layer_slots, turn), 0) == slot,
                jnp.ones((), F8),
                jnp.zeros((), F8),
            )
            block = 256
            for first in range(0, rows, block):
                ids = lax.broadcasted_iota(jnp.int16, (block, turn), 0) + jnp.asarray(
                    first, jnp.int16
                )
                left = jnp.where(ids == child, weight, jnp.zeros((), F8))
                acc[pl.ds(first, block), :] += dot_nt(left, right)
            run_ticks(t, ticks)

        own_t[src] = acc[...].astype(BF16)

    def own(k):
        if k < AHEAD:
            for which in range(LINE):
                src = source(which)
                for far, index, device in place.others("l"):
                    slot_copy(src, k, far, index, device).wait_recv()
                weights = spread_t[z] if which == 0 else own_t[src]
                value = jnp.dot(weights, in_slots[src, k], preferred_element_type=F32)
                if which == 0:
                    tmp[...] = value
                else:
                    tmp[...] += value
        else:
            child_sums(z, k)

            @pl.when(z > 0)
            def _():
                arrived(z, k)
                tmp[...] += chain[z, k - AHEAD].astype(F32)

            @pl.when(z < LINE - 1)
            def _():
                arrived(LINE, k)
                tmp[...] += chain[LINE, k - AHEAD].astype(F32)

        down = (tmp[...] * gelu_slope(pre[:, cols(k)])).astype(BF16)
        dpre[:, cols(k)] = down
        small[0:1, cols(k)] = jnp.sum(down.astype(F32), axis=0, keepdims=True)
        dh[...] += dot_nt(down, neigh_b[:, cols(k)])

    def neigh_grad(k):
        grad[pl.ds(2 * width, width), cols(k)] = dot_tn(hid[...], dpre[:, cols(k)]).astype(BF16)

    def comb_grads():
        for name in ("hid", "agg", "dz", "comb1_b"):
            loads[name].wait()
        comb_grad(hid, 0)
        comb_grad(agg, width)

    def self_part():
        small[...] = jnp.zeros_like(small)
        small[1:2, :] = jnp.sum(dz[...].astype(F32), axis=0, keepdims=True)
        small[2:3, :] = jnp.broadcast_to(stats_ref[0:1, 0:1], (1, width))

        @pl.loop(0, CHUNKS)
        def _(k):
            dh[:, cols(k)] = dot_nt(dz[...], comb1_b[cols(k), :])

        for name in ("pre", "neigh_b", "featb", "board_b"):
            loads[name].wait()

    def own_and_grad(k):
        own(k)
        neigh_grad(k)

    def end_of_line():
        last = dh[...].astype(BF16)
        dpre[...] = jnp.where(mask, last, jnp.zeros_like(last))
        pre[...] = last.astype(F32)

    def board_grad(i):
        half = width // 2
        grad[pl.ds(3 * width + i * half, half), :] = dot_tn(
            featb[:, i * half : (i + 1) * half], dpre[...]
        ).astype(BF16)

    def feature_grad():
        @pl.loop(0, CHUNKS)
        def _(k):
            pre[:, cols(k)] = jnp.where(
                mask, dot_nt(dpre[...], board_b[cols(k), :]), pre[:, cols(k)]
            )

        store(pre, gfeat_h)

    share = Share(place, (share_l, share_z, share_x), share_send, share_recv)

    def step_share(stage):
        if stage == 0:
            share.start(0, small[...])
        elif stage < 3:
            share.start(stage, share.finish(stage - 1))
        else:
            row = lax.broadcasted_iota(jnp.int32, small_ref.shape, 0)
            small_ref[...] = share.finish(2) * jnp.where(row == 2, stats_ref[8:9, 0:1], 1.0)

    acts = {
        "l": lambda _: line_targets(),
        "L": line_picker,
        "A": parent_send,
        "f": parent_forward,
        "q": parent_slots,
        "B": back_all,
        "W": lambda _: loads["spread_t"].wait(),
        "G": lambda _: comb_grads(),
        "S": lambda _: self_part(),
        "O": own_and_grad,
        "E": lambda _: end_of_line(),
        "H": board_grad,
        "F": lambda _: feature_grad(),
        "P": step_share,
        "c": lambda j: step_job(f"comb{j}"),
        "n": lambda j: step_job(f"neigh{j}"),
        "b": lambda j: step_job(f"board{j}"),
        "3": lambda k: hand_on(source(3), k),
        "2": lambda k: hand_on(source(2), k),
        "1": lambda k: hand_on(source(1), k),
    }
    def act(name):
        acts[name[0]](*(int(c) for c in name[1:]))

    run_order(BACKWARD, BACKWARD_ACTS, steps, build_own, act)
    while jobs:
        for name in list(jobs):
            step_job(name, last=True)

    for far, index, device in place.others("z"):
        remote(lines.at[z], lines.at[z], line_send.at[far], line_recv.at[far], device).wait_send()

    @pl.loop(0, LINE * CHUNKS)
    def _(i):
        dst = i // CHUNKS
        k = lax.rem(i, CHUNKS)

        @pl.when(k < AHEAD)
        def _():
            @pl.when(jnp.logical_and(dst <= z, z < LINE - 1))
            def _():
                parent_copy(dst, k, parent_up, z + 1).wait_send()

            @pl.when(jnp.logical_and(dst >= z, z > 0))
            def _():
                parent_copy(dst, k, parent_down, z - 1).wait_send()

        @pl.when(k >= AHEAD)
        def _():
            @pl.when(dst > z)
            def _():
                up_copy(dst, k).wait_send()

            @pl.when(dst < z)
            def _():
                down_copy(dst, k, False).wait_send()

        for far, index, device in place.others("l"):
            slot_copy(dst, k, far, index, device).wait_send()

    for copy in stores:
        copy.wait()


def backward_pass(n_nodes, n_grp, mask, targets, stats, edges_of, hid, pre, featb, board_b, neigh_b, comb1_b, st, far, dnum, dz, agg):
    rows, width = hid.shape
    edges = edges_of[0].shape[1]
    layer = n_nodes // LINE
    layer_slots = st.shape[2]
    part = width // CHUNKS
    n_rows = 4 * width
    count = len(gradient_regions(n_nodes, n_grp, width))
    dma = pltpu.SemaphoreType.DMA
    big = pl.BlockSpec(memory_space=pl.ANY)
    vmem = pl.BlockSpec(memory_space=pltpu.VMEM)
    sems = count * job_sems(n_nodes, n_grp)
    pieces = LINE * CHUNKS
    return pl.pallas_call(
        functools.partial(backward_kernel, n_nodes, n_grp),
        out_shape=[
            jax.ShapeDtypeStruct((rows, width), F32),
            jax.ShapeDtypeStruct((2 * width, width), BF16),
            jax.ShapeDtypeStruct((width, width), BF16),
            jax.ShapeDtypeStruct((width, width), BF16),
            jax.ShapeDtypeStruct((8, width), F32),
        ],
        in_specs=[vmem, vmem, vmem] + [big] * 14,
        out_specs=[big] * 4 + [vmem],
        scratch_shapes=[
            pltpu.VMEM((rows, width), BF16),
            pltpu.VMEM((rows, width), F32),
            pltpu.VMEM((rows, width), BF16),
            pltpu.VMEM((width, width), BF16),
            pltpu.VMEM((width, width), BF16),
            pltpu.VMEM((width, width), BF16),
            pltpu.VMEM((LINE, rows, layer_slots), BF16),
            pltpu.VMEM((rows, width), BF16),
            pltpu.VMEM((rows, width), BF16),
            pltpu.VMEM((rows, width), BF16),
            pltpu.VMEM((LINE, layer_slots, rows), BF16),
            pltpu.VMEM((LINE, layer_slots, rows), BF16),
            pltpu.VMEM((LINE, 1, layer_slots), jnp.int32),
            pltpu.VMEM((1, edges), jnp.int32),
            pltpu.VMEM((1, edges), jnp.int32),
            pltpu.VMEM((1, edges), jnp.int32),
            pltpu.VMEM((rows, layer_slots), F32),
            pltpu.VMEM((LINE, rows, layer_slots), BF16),
            pltpu.VMEM((LINE, AHEAD, rows, part), BF16),
            pltpu.VMEM((LINE, CHUNKS, layer_slots, part), BF16),
            pltpu.VMEM((LINE, CHUNKS, layer_slots, part), BF16),
            pltpu.VMEM((LINE + 1, BEHIND, rows, part), BF16),
            pltpu.VMEM((rows, part), F32),
            pltpu.VMEM((rows, width), BF16),
            pltpu.VMEM((rows, width), F32),
            pltpu.VMEM((n_rows, width), BF16),
            pltpu.VMEM((n_rows, width // 2), BF16),
            pltpu.VMEM((n_rows, width // 2), BF16),
            pltpu.VMEM((n_rows // 4, width // 2), BF16),
            pltpu.VMEM((layer, 8, width), F32),
            pltpu.VMEM((LINE, 8, width), F32),
            pltpu.VMEM((n_grp, 8, width), F32),
            pltpu.VMEM((8, width), F32),
            dma((14,)),
            dma((count + 2,)),
            dma((pieces * (layer - 1),)),
            dma((pieces * (layer - 1),)),
            dma((LINE * BEHIND,)),
            dma((LINE * BEHIND,)),
            dma(((LINE + 1) * BEHIND,)),
            dma((LINE - 1,)),
            dma((LINE - 1,)),
            dma((LINE * AHEAD,)),
            dma((LINE * AHEAD,)),
            dma((LINE * AHEAD,)),
            dma((sems,)),
            dma((sems,)),
            pltpu.SemaphoreType.REGULAR((sems,)),
            dma((share_sems(n_nodes, n_grp),)),
            dma((share_sems(n_nodes, n_grp),)),
        ],
        compiler_params=pltpu.CompilerParams(
            vmem_limit_bytes=63 * MIB, collective_id=3, has_side_effects=True
        ),
        name="backward_pass",
    )(mask, targets, stats, *edges_of, hid, pre, featb, board_b, neigh_b, comb1_b, st, far, dnum, dz, agg)


def on_device(
    n_nodes,
    n_grp,
    features,
    type_mask,
    edge_child,
    edge_slot,
    edge_weight,
    recv_rows,
    board_proj,
    neigh_proj,
    neigh_bias,
    combine_proj,
    combine_bias,
    out_cot,
):
    feats = features[0]
    rows, width = feats.shape
    peers = recv_rows.shape[2]
    cap = recv_rows.shape[3]
    slots = peers * cap
    targets = recv_rows[0, 0].reshape(1, slots)
    embed, hidden, pre, featb, pbl, qwl, cwl1, spread_t, far, dnum, dzb, aggb, stats = forward_pass(
        n_nodes,
        n_grp,
        feats,
        type_mask,
        (edge_slot, edge_child, edge_weight),
        targets,
        board_proj,
        neigh_proj,
        neigh_bias.reshape(1, width),
        combine_proj,
        combine_bias.reshape(1, width),
        out_cot[0],
    )
    grad_feats, grad_comb, grad_neigh, grad_board, small = backward_pass(
        n_nodes,
        n_grp,
        type_mask,
        targets,
        stats,
        (edge_slot, edge_child, edge_weight),
        hidden,
        pre,
        featb,
        pbl,
        qwl,
        cwl1,
        spread_t,
        far,
        dnum,
        dzb,
        aggb,
    )
    return (
        embed[None],
        small[2, 0],
        grad_feats[None],
        grad_board.astype(F32),
        grad_neigh.astype(F32),
        small[0],
        grad_comb.astype(F32),
        small[1],
    )


def solution(mesh):
    in_specs = (
        P("grp", "nodes", None),
        P("grp", "nodes"),
        P("grp", "nodes"),
        P("grp", "nodes"),
        P("grp", "nodes"),
        P("grp", "nodes", None, None),
        P(),
        P(),
        P(),
        P(),
        P(),
        P("grp", "nodes", None),
    )
    out_specs = (P("grp", "nodes", None), P(), P("grp", "nodes", None), P(), P(), P(), P(), P())
    return jax.shard_map(
        functools.partial(on_device, mesh.shape["nodes"], mesh.shape["grp"]),
        mesh=mesh,
        in_specs=in_specs,
        out_specs=out_specs,
        check_vma=False,
    )
```

```python
import functools
import math

import jax
import jax.numpy as jnp
from jax import lax
from jax.experimental import pallas as pl
from jax.experimental.pallas import tpu as pltpu
from jax.sharding import PartitionSpec as P

HIGH = lax.Precision.HIGHEST
MESH = pl.DeviceIdType.MESH
BF16 = jnp.bfloat16
F32 = jnp.float32
F8 = jnp.float8_e4m3fn
MIB = 2**20


def gelu_tanh(v):
    return jax.nn.gelu(v, approximate=True)


def dot_nt(left, right):
    return lax.dot_general(
        left, right, (((1,), (1,)), ((), ())), preferred_element_type=F32
    )


def dot_tn(left, right):
    return lax.dot_general(
        left, right, (((0,), (0,)), ((), ())), preferred_element_type=F32
    )


LINE = 4
CHUNKS = 4
FAR = 2
FORWARD_ACTS = "mYZfpiGDXRdaPugvxw"
FORWARD = (
    10, 11, 12, 13, 1100, 1101, 1102, 1103, 2010, 1140, 4102, 1141, 6010, 4100, 1142, 1143, 2014, 1110, 4101,
    3100, 13012, 13013, 1111, 1112, 3101, 1113, 3102, 2011, 4112, 14010, 1120, 4103, 4110, 1121, 1122, 3103,
    7010, 12011, 4113, 4111, 3110, 15012, 1123, 2012, 4120, 1130, 1131, 3111, 4121, 1132, 3112, 4122, 15013,
    1133, 7011, 2013, 16012, 3120, 3121, 4132, 4131, 5113, 4130, 3113, 5120, 5100, 12012, 10010, 16013, 8010,
    5101, 5132, 9010, 4133, 4123, 5131, 5122, 7012, 5111, 5112, 5102, 7013, 5121, 5110, 5130, 11011, 5103,
    17012, 11010, 11012, 5133, 17013, 5123, 12013,
)
ORDER = ((0, 1, 2, 3), (1, 2, 0, 3))


class Place:
    def __init__(self, n_nodes, n_grp):
        layer = n_nodes // LINE
        node = lax.axis_index("nodes")
        grp = lax.axis_index("grp")
        self.node, self.grp = node, grp
        self.size = {"l": layer, "c": 2, "y": layer // 2, "z": LINE, "x": n_grp}
        low = lax.rem(node, layer)
        self.at = {"l": low, "c": lax.rem(low, 2), "y": low // 2, "z": node // layer, "x": grp}

    def member(self, axis, index):
        layer = self.size["l"]
        low, line, grp = self.at["l"], self.at["z"], self.at["x"]
        if axis == "l":
            low = index
        elif axis == "c":
            low = self.at["y"] * 2 + index
        elif axis == "y":
            low = index * 2 + self.at["c"]
        elif axis == "z":
            line = index
        else:
            grp = index
        return {"nodes": line * layer + low, "grp": grp}

    def others(self, axis):
        size = self.size[axis]
        for far in range(1, size):
            index = lax.rem(self.at[axis] + far, size)
            yield far - 1, index, self.member(axis, index)


def remote(src, dst, send, recv, device):
    return pltpu.make_async_remote_copy(
        src_ref=src, dst_ref=dst, send_sem=send, recv_sem=recv, device_id=device, device_id_type=MESH
    )


def barrier(place, axes, meanwhile=None):
    sem = pltpu.get_barrier_semaphore()
    count = 0
    for axis in axes:
        for _, _, device in place.others(axis):
            pl.semaphore_signal(sem, inc=1, device_id=device, device_id_type=MESH)
            count += 1
    if meanwhile is not None:
        meanwhile()
    pl.semaphore_wait(sem, count)


def column_of(row_ref):
    row = row_ref[...].astype(F32)
    return jnp.broadcast_to(row, (128, row.shape[1])).T[:, 0:1]


def gelu(v):
    t = jnp.tanh(0.7978845608028654 * (v + 0.044715 * (v * v * v)))
    return v * (0.5 * (1.0 + t))


def gelu_slope(v):
    square = v * v
    t = jnp.tanh(0.7978845608028654 * (v + 0.044715 * (v * square)))
    bend = 0.7978845608028654 * (1.0 + 0.134145 * square)
    return 0.5 * (1.0 + t) + 0.5 * v * (1.0 - t * t) * bend


class Share:
    def __init__(self, place, bufs, send, recv):
        self.place, self.send, self.recv = place, send, recv
        self.stages, base = [], 0
        for axis, buf in zip(("l", "z", "x"), bufs):
            self.stages.append((axis, buf, base))
            base += place.size[axis] - 1

    def start(self, stage, value):
        axis, buf, base = self.stages[stage]
        me = self.place.at[axis]
        buf[me] = value
        for far, _, device in self.place.others(axis):
            remote(
                buf.at[me], buf.at[me], self.send.at[base + far], self.recv.at[base + far], device
            ).start()

    def finish(self, stage):
        axis, buf, base = self.stages[stage]
        me = self.place.at[axis]
        for far, _, device in self.place.others(axis):
            remote(
                buf.at[me], buf.at[me], self.send.at[base + far], self.recv.at[base + far], device
            ).wait()
        total = buf[0]
        for i in range(1, self.place.size[axis]):
            total += buf[i]
        return total


def run_ticks(t, ticks):
    for at, acts in enumerate(ticks):
        if acts:

            @pl.when(t == at)
            def _(acts=acts):
                for act in acts:
                    act()


def run_order(order, letters, steps, build, act):
    ticks = None
    names = [letters[number // 1000] + str(number % 1000)[1:] for number in order]
    for name in names:
        if name[0] == "Y":
            if ticks is None:
                ticks = [[] for _ in range(steps)]
                marks = sum(other[:2] == name[:2] for other in names)
            now = (int(name[2]) + 1) * steps // marks - 1
        elif name[0] == "Z":
            build(int(name[1]), ticks)
            ticks = None
        elif ticks is not None:
            ticks[max(now, 0)].append(functools.partial(act, name))
        else:
            act(name)


def share_sems(n_nodes, n_grp):
    return (n_nodes // LINE - 1) + (LINE - 1) + max(1, n_grp - 1)


def forward_kernel(
    n_nodes,
    n_grp,
    feats_h,
    mask_ref,
    place_ref,
    child_ref,
    weight_ref,
    targets_ref,
    board_h,
    neigh_h,
    nbias_ref,
    comb_h,
    cbias_ref,
    cot_h,
    embed_h,
    hid_h,
    pre_h,
    featb_h,
    board_b_h,
    neigh_b_h,
    comb1_b_h,
    st_h,
    dnum_h,
    dz_h,
    agg_h,
    stats_ref,
    stage,
    featb,
    hid,
    pre,
    board_b,
    neigh_b,
    comb_b,
    keys,
    msg,
    acc,
    spread,
    spread_t,
    out_slots,
    in_slots,
    out_tot,
    in_tot,
    picker,
    num,
    zval,
    zpre,
    cot,
    agg,
    dz,
    dnum,
    lines,
    far_spread,
    far_picker,
    far_out,
    far_in,
    far_sum,
    end_sum,
    den_ref,
    scale_ref,
    count_l,
    count_z,
    count_x,
    load_sem,
    store_sem,
    key_send,
    key_recv,
    up_send,
    down_send,
    msg_recv,
    slot_send,
    slot_recv,
    tot_send,
    tot_recv,
    count_send,
    count_recv,
    line_send,
    line_recv,
    far_send,
    far_recv,
    sum_send,
    sum_recv,
    end_recv,
):
    place = Place(n_nodes, n_grp)
    z, low = place.at["z"], place.at["l"]
    layer = place.size["l"]
    rows, width = featb.shape
    edges = place_ref.shape[1]
    half = edges // 2
    layer_slots = spread.shape[1]
    cap = layer_slots // layer
    part = width // CHUNKS
    turn = math.gcd(half, 6400)
    steps = edges // turn

    sources = [feats_h.at[:]]
    for whole in (board_h, neigh_h, comb_h):
        for first in range(0, whole.shape[0], rows):
            sources.append(whole.at[pl.ds(first, rows)])
    n_stage = stage.shape[0]

    def load(i):
        return pltpu.make_async_copy(sources[i], stage.at[i % n_stage], load_sem.at[i % n_stage])

    for i in range(n_stage):
        load(i).start()
    load_cot = pltpu.make_async_copy(cot_h, cot, load_sem.at[n_stage])
    stores = []

    def store(src, dst):
        copy = pltpu.make_async_copy(src, dst, store_sem.at[len(stores)])
        copy.start()
        stores.append(copy)

    barrier(place, ("l", "z", "x"))
    keys[z, :, pl.ds(0, edges)] = place_ref[...] * 65536 + child_ref[...]
    keys[z, :, pl.ds(edges, half)] = (
        weight_ref[:, pl.ds(half, half)] * 65536 + weight_ref[:, pl.ds(0, half)]
    )

    def key_copy(far, device):
        return remote(keys.at[z], keys.at[z], key_send.at[far], key_recv.at[far], device)

    for far, _, device in place.others("z"):
        key_copy(far, device).start()
    inner = jnp.logical_and(z > 0, z < LINE - 1)
    outer = jnp.logical_or(z == 0, z == LINE - 1)
    half_at = z // 2
    far_end = (LINE - 1) * (1 - half_at)

    def line_copy(far, index, device):
        at = pl.ds(pl.multiple_of(index * layer_slots, layer_slots), layer_slots)
        return remote(
            targets_ref.at[:, at], lines.at[z], line_send.at[far], line_recv.at[far], device
        )

    @pl.when(outer)
    def _():
        for far, index, device in place.others("z"):
            line_copy(far, index, device).start()

    share = Share(place, (count_l, count_z, count_x), count_send, count_recv)
    mask = column_of(mask_ref)
    share.start(0, jnp.full((8, 128), jnp.sum(mask)))

    def cast(i, target, first):
        load(i).wait()
        slot = stage.at[i % n_stage]

        @pl.loop(0, rows // 32)
        def _(r):
            at = pl.ds(pl.multiple_of(r * 32, 32), 32)
            to = pl.ds(pl.multiple_of(first + r * 32, 32), 32)
            target[to, :] = slot[at, :].astype(BF16)

    cast(0, featb, 0)
    cast(1, board_b, 0)
    cast(2, board_b, rows)

    @pl.loop(0, CHUNKS)
    def _(k):
        at = pl.ds(pl.multiple_of(k * part, part), part)
        proj = jnp.dot(featb[...], board_b[:, at], preferred_element_type=F32)
        hid[:, at] = jnp.where(mask > 0.5, proj, stage[0, :, at]).astype(BF16)

    cast(3, neigh_b, 0)
    cast(4, neigh_b, rows)
    for i in range(n_stage, len(sources)):
        load(i).start()
    load_cot.start()

    def up_copy(src, k):
        piece = msg.at[src, k]
        index = src * CHUNKS + k
        return remote(
            piece, piece, up_send.at[index], msg_recv.at[index], place.member("z", z + 1)
        )

    def down_copy(src, k):
        piece = msg.at[src, k]
        index = src * CHUNKS + k
        return remote(
            piece, piece, down_send.at[index], msg_recv.at[index], place.member("z", z - 1)
        )

    def message(k):
        at = pl.ds(k * part, part)
        value = jnp.dot(hid[...], neigh_b[:, at], preferred_element_type=F32) + nbias_ref[:, at]
        pre[:, at] = value
        msg[z, k] = gelu(value).astype(BF16)

        @pl.when(z < LINE - 1)
        def _():
            up_copy(z, k).start()

        @pl.when(z > 0)
        def _():
            down_copy(z, k).start()

    def passes_up(k):
        return z < LINE - (1 if k < FAR else 2)

    def passes_down(k):
        return z > (0 if k < FAR else 1)

    def forward(j, k):
        below = z - 1 - j
        above = z + 1 + j

        comes = True if k < FAR or j == 0 else inner

        @pl.when(jnp.logical_and(below >= 0, comes))
        def _():
            up_copy(below, k).wait_recv()

            @pl.when(passes_up(k))
            def _():
                up_copy(below, k).start()

        @pl.when(jnp.logical_and(above < LINE, comes))
        def _():
            down_copy(above, k).wait_recv()

            @pl.when(passes_down(k))
            def _():
                down_copy(above, k).start()

    def tot_copy(src, far, index, device):
        at = (layer - 1) * src + far
        return remote(
            out_tot.at[src, pl.ds(pl.multiple_of(index * cap, cap), cap)],
            in_tot.at[src, pl.ds(pl.multiple_of(low * cap, cap), cap)],
            tot_send.at[at],
            tot_recv.at[at],
            device,
        )

    def finish_spread(src):
        total = acc[...]
        spread[src] = total.astype(BF16)
        spread_t[src] = total.astype(BF16).T
        sums = jnp.sum(total, axis=1, keepdims=True).astype(jnp.int32)
        lane = lax.broadcasted_iota(jnp.int32, (layer_slots, 128), 1)
        digit = jnp.where(
            lane == 0, sums & 255, jnp.where(lane == 1, (sums >> 8) & 255, jnp.where(lane == 2, sums >> 16, 0))
        )
        out_tot[src] = digit.astype(F32).astype(BF16)
        own = pl.ds(pl.multiple_of(low * cap, cap), cap)
        in_tot[src, own] = out_tot[src, own]
        for far, index, device in place.others("l"):
            tot_copy(src, far, index, device).start()

    def source(which):
        flip = z // 2
        depth = z * (1 - 2 * flip) + (LINE - 1) * flip
        index = ORDER[0][which] * (1 - depth) + ORDER[1][which] * depth
        return index * (1 - 2 * flip) + (LINE - 1) * flip

    def build(which, ticks):
        src, target = (source(which), z) if which < LINE else (z, far_end)
        acc[...] = jnp.zeros_like(acc)
        if 0 < which < LINE:
            far = lax.rem(z - src - 1 + LINE, LINE)
            remote(
                keys.at[src], keys.at[src], key_send.at[0], key_recv.at[far], place.member("z", src)
            ).wait_recv()

        @pl.loop(0, steps)
        def _(t):
            second = t // (steps // 2)
            key = keys[src, :, pl.ds(pl.multiple_of(t * turn, turn), turn)]
            start = edges + (t - second * (steps // 2)) * turn
            pair = keys[src, :, pl.ds(pl.multiple_of(start, turn), turn)]
            weight = (lax.shift_right_logical(pair, second * 16) & 65535).astype(F32).astype(F8)
            child = (key & 65535).astype(jnp.int16)
            slot = (lax.shift_right_logical(key, 16) - target * layer_slots).astype(jnp.int16)
            right = jnp.where(
                lax.broadcasted_iota(jnp.int16, (rows, turn), 0) == child, weight, jnp.zeros((), F8)
            )
            block = 256
            for first in range(0, layer_slots, block):
                ids = lax.broadcasted_iota(jnp.int16, (block, turn), 0) + jnp.asarray(
                    first, jnp.int16
                )
                left = jnp.where(ids == slot, jnp.ones((), F8), jnp.zeros((), F8))
                acc[pl.ds(first, block), :] += dot_nt(left, right)
            run_ticks(t, ticks)

        if which < LINE:
            finish_spread(src)
        else:
            far_spread[...] = acc[...].astype(BF16)

    def slot_copy(src, k, far, index, device):
        at = (src * CHUNKS + k) * (layer - 1) + far
        return remote(
            out_slots.at[src, k, pl.ds(pl.multiple_of(index * cap, cap), cap)],
            in_slots.at[src, k, pl.ds(pl.multiple_of(low * cap, cap), cap)],
            slot_send.at[at],
            slot_recv.at[at],
            device,
        )

    def piece(src, k):
        out_slots[src, k] = jnp.dot(spread[src], msg[src, k], preferred_element_type=F32).astype(BF16)
        for far, index, device in place.others("l"):
            slot_copy(src, k, far, index, device).start()
        own = pl.ds(pl.multiple_of(low * cap, cap), cap)
        in_slots[src, k, own] = out_slots[src, k, own]

    def pick(src, k):
        for far, index, device in place.others("l"):
            slot_copy(src, k, far, index, device).wait_recv()
        num[k] += jnp.dot(picker[src], in_slots[src, k], preferred_element_type=F32)

    def unless_far(which, k, act):
        if which < 2 or k < FAR:
            act(source(which), k)
        else:

            @pl.when(inner)
            def _():
                act(source(which), k)

    def far_copy(k, far, index, device):
        at = k * (layer - 1) + far
        return remote(
            far_out.at[k, pl.ds(pl.multiple_of(index * cap, cap), cap)],
            far_in.at[k, pl.ds(pl.multiple_of(low * cap, cap), cap)],
            far_send.at[at],
            far_recv.at[at],
            device,
        )

    onward = 1 - 2 * half_at

    def sum_copy(i):
        return remote(
            far_sum.at[i], far_sum.at[i], sum_send.at[i], sum_recv.at[i], place.member("z", z + onward)
        )

    def end_copy(i):
        return remote(
            far_sum.at[i],
            end_sum.at[i],
            sum_send.at[i],
            end_recv.at[i],
            place.member("z", z + 2 * onward),
        )

    def far_slots(k):
        i = k - FAR
        far_out[i] = jnp.dot(far_spread[...], msg[z, k], preferred_element_type=F32).astype(BF16)
        for far, index, device in place.others("l"):
            far_copy(i, far, index, device).start()
        own = pl.ds(pl.multiple_of(low * cap, cap), cap)
        far_in[i, own] = far_out[i, own]

    def make_far_picker():
        far = lax.rem(z - far_end - 1 + LINE, LINE)
        remote(
            lines.at[far_end],
            lines.at[far_end],
            line_send.at[0],
            line_recv.at[far],
            place.member("z", far_end),
        ).wait_recv()
        ids = lax.broadcasted_iota(jnp.int32, (rows, layer_slots), 0)
        far_picker[...] = jnp.where(ids == lines[far_end], 1.0, 0.0).astype(BF16)

        @pl.when(inner)
        def _():
            near = (LINE - 1) - far_end
            back = lax.rem(z - near - 1 + LINE, LINE)
            remote(
                lines.at[near],
                lines.at[near],
                line_send.at[0],
                line_recv.at[back],
                place.member("z", near),
            ).wait_recv()

    def far_parents(i):
        for far, index, device in place.others("l"):
            far_copy(i, far, index, device).wait_recv()
        return jnp.dot(far_picker[...], far_in[i], preferred_element_type=F32)

    def first_sum(k):
        @pl.when(outer)
        def _():
            far_sum[k - FAR] = far_parents(k - FAR).astype(BF16)
            sum_copy(k - FAR).start()

    def second_sum(k):
        @pl.when(inner)
        def _():
            i = k - FAR
            value = far_parents(i)
            sum_copy(i).wait_recv()
            far_sum[i] = (far_sum[i].astype(F32) + value).astype(BF16)
            end_copy(i).start()

    def add_far(k):
        @pl.when(outer)
        def _():
            end_copy(k - FAR).wait_recv()
            num[k] += end_sum[k - FAR].astype(F32)

    def make_picker():
        @pl.loop(0, LINE)
        def _(src):
            at = pl.ds(pl.multiple_of(src * layer_slots, layer_slots), layer_slots)
            ids = lax.broadcasted_iota(jnp.int32, (rows, layer_slots), 0)
            picker[src] = jnp.where(ids == targets_ref[:, at], 1.0, 0.0).astype(BF16)

        num[...] = jnp.zeros_like(num)

    def comb_piece(i):
        for j in range(i, 2 * width // rows, CHUNKS):
            cast(5 + j, comb_b, j * rows)

    def self_part():
        @pl.loop(0, CHUNKS)
        def _(k):
            at = pl.ds(pl.multiple_of(k * part, part), part)
            zpre[:, at] = (
                jnp.dot(hid[...], comb_b[0:width, at], preferred_element_type=F32)
                + cbias_ref[:, at]
            )

    def results():
        store(hid, hid_h)
        store(pre, pre_h)
        store(featb, featb_h)
        store(board_b, board_b_h)
        store(neigh_b, neigh_b_h)
        store(comb_b.at[pl.ds(0, width)], comb1_b_h)
        store(spread_t, st_h)

    def totals():
        digits = jnp.zeros((rows, 128), F32)
        for src in range(LINE):
            for far, index, device in place.others("l"):
                tot_copy(src, far, index, device).wait_recv()
            digits += jnp.dot(picker[src], in_tot[src], preferred_element_type=F32)
        lane = lax.broadcasted_iota(jnp.int32, (rows, 128), 1)
        worth = jnp.where(
            lane == 0, 1.0, jnp.where(lane == 1, 256.0, jnp.where(lane == 2, 65536.0, 0.0))
        )
        den_ref[...] = jnp.broadcast_to(
            1.0 + jnp.sum(digits * worth, axis=1, keepdims=True), (rows, 128)
        )

    def neighbours(k):
        at = pl.ds(k * part, part)
        agg[:, at] = (num[k] / den_ref[:, 0:1]).astype(BF16)
        if k < CHUNKS - 1:

            @pl.loop(0, CHUNKS)
            def _(n):
                to = pl.ds(pl.multiple_of(n * part, part), part)
                zpre[:, to] += jnp.dot(
                    agg[:, at], comb_b[pl.ds(width + k * part, part), to], preferred_element_type=F32
                )

    def step_share(stage):
        if stage in (1, 2):
            share.start(stage, share.finish(stage - 1))
        elif stage == 3:
            boards = share.finish(2)
            scale_ref[...] = 1.0 / (width * (1.0 + boards))

    acts = {
        "P": step_share,
        "m": message,
        "f": forward,
        "p": lambda which, k: unless_far(which, k, piece),
        "i": lambda which, k: unless_far(which, k, pick),
        "u": far_slots,
        "g": lambda _: make_far_picker(),
        "v": first_sum,
        "x": second_sum,
        "w": add_far,
        "G": lambda _: make_picker(),
        "D": comb_piece,
        "X": lambda _: self_part(),
        "R": lambda _: results(),
        "d": lambda _: totals(),
        "a": neighbours,
    }

    def act(step):
        acts[step[0]](*(int(c) for c in step[1:]))

    run_order(FORWARD, FORWARD_ACTS, steps, build, act)
    neighbours(CHUNKS - 1)
    load_cot.wait()
    den = den_ref[:, 0:1]
    scale = scale_ref[0:1, 0:1]
    last = pl.ds(width - part, part)

    def dense(k, carry):
        square, along = carry
        at = pl.ds(pl.multiple_of(k * part, part), part)
        value = zpre[:, at] + jnp.dot(
            agg[:, last], comb_b[pl.ds(2 * width - part, part), at], preferred_element_type=F32
        )
        zpre[:, at] = value
        out = gelu(value)
        zval[:, at] = out
        square += jnp.sum(out * out, axis=1, keepdims=True)
        along += jnp.sum(out * cot[:, at], axis=1, keepdims=True)
        return square, along

    zero = jnp.zeros((rows, 1), F32)
    square, along = lax.fori_loop(0, CHUNKS, dense, (zero, zero))
    inverse = lax.rsqrt(square + 1e-06)
    along = along * inverse
    push = jnp.where(mask > 0.5, 2.0 * scale, 0.0)
    stats_ref[...] = jnp.concatenate(
        [
            jnp.full((8, 128), jnp.sum(jnp.where(mask > 0.5, square, 0.0))),
            jnp.broadcast_to(scale, (8, 128)),
        ],
        axis=0,
    )

    @pl.loop(0, CHUNKS)
    def _(k):
        at = pl.ds(pl.multiple_of(k * part, part), part)
        out = zval[:, at]
        emb = out * inverse
        grad = inverse * (cot[:, at] - emb * along) + push * out
        dz[:, at] = (grad * gelu_slope(zpre[:, at])).astype(BF16)
        zval[:, at] = emb

    store(zval, embed_h)
    store(dz, dz_h)
    store(agg, agg_h)

    @pl.loop(0, CHUNKS)
    def _(k):
        at = pl.ds(pl.multiple_of(k * part, part), part)
        back = dot_nt(dz[...], comb_b[pl.ds(pl.multiple_of(width + k * part, part), part), :])
        dnum[:, at] = (back / den).astype(BF16)

    store(dnum, dnum_h)

    for far, _, device in place.others("z"):
        key_copy(far, device).wait_send()

    @pl.loop(0, LINE * CHUNKS)
    def _(i):
        src = i // CHUNKS
        k = lax.rem(i, CHUNKS)

        early = k < FAR

        @pl.when(
            jnp.logical_or(
                jnp.logical_and(src == z, z < LINE - 1),
                jnp.logical_and(
                    src < z, jnp.logical_or(jnp.logical_and(early, z < LINE - 1), z < LINE - 2)
                ),
            )
        )
        def _():
            up_copy(src, k).wait_send()

        @pl.when(
            jnp.logical_or(
                jnp.logical_and(src == z, z > 0),
                jnp.logical_and(src > z, jnp.logical_or(jnp.logical_and(early, z > 0), z > 1)),
            )
        )
        def _():
            down_copy(src, k).wait_send()

        near = jnp.logical_and(src - z < 2, z - src < 2)

        @pl.when(jnp.logical_or(jnp.logical_or(early, inner), near))
        def _():
            for far, index, device in place.others("l"):
                slot_copy(src, k, far, index, device).wait_send()

    for i in range(CHUNKS - FAR):
        sum_copy(i).wait_send()
        for far, index, device in place.others("l"):
            far_copy(i, far, index, device).wait_send()

    @pl.when(outer)
    def _():
        for far, index, device in place.others("z"):
            line_copy(far, index, device).wait_send()

    for src in range(LINE):
        for far, index, device in place.others("l"):
            tot_copy(src, far, index, device).wait_send()
    for copy in stores:
        copy.wait()


def forward_pass(n_nodes, n_grp, feats, mask, edges_of, targets, board, neigh, nbias, comb, cbias, cot):
    rows, width = feats.shape
    edges = edges_of[0].shape[1]
    layer = n_nodes // LINE
    layer_slots = targets.shape[1] // LINE
    part = width // CHUNKS
    dma = pltpu.SemaphoreType.DMA
    n_stage = 5
    big = pl.BlockSpec(memory_space=pl.ANY)
    small = pl.BlockSpec(memory_space=pltpu.VMEM)

    def hbm(shape, dtype):
        return jax.ShapeDtypeStruct(shape, dtype)

    return pl.pallas_call(
        functools.partial(forward_kernel, n_nodes, n_grp),
        out_shape=[
            hbm((rows, width), F32),
            hbm((rows, width), BF16),
            hbm((rows, width), F32),
            hbm((rows, width), BF16),
            hbm((width, width), BF16),
            hbm((width, width), BF16),
            hbm((width, width), BF16),
            hbm((LINE, rows, layer_slots), BF16),
            hbm((rows, width), BF16),
            hbm((rows, width), BF16),
            hbm((rows, width), BF16),
            hbm((16, 128), F32),
        ],
        in_specs=[big] + [small] * 5 + [big, big, small, big, small, big],
        out_specs=[big] * 11 + [small],
        scratch_shapes=[
            pltpu.VMEM((n_stage, rows, width), F32),
            pltpu.VMEM((rows, width), BF16),
            pltpu.VMEM((rows, width), BF16),
            pltpu.VMEM((rows, width), F32),
            pltpu.VMEM((width, width), BF16),
            pltpu.VMEM((width, width), BF16),
            pltpu.VMEM((2 * width, width), BF16),
            pltpu.VMEM((LINE, 1, edges + edges // 2), jnp.int32),
            pltpu.VMEM((LINE, CHUNKS, rows, part), BF16),
            pltpu.VMEM((layer_slots, rows), F32),
            pltpu.VMEM((LINE, layer_slots, rows), BF16),
            pltpu.VMEM((LINE, rows, layer_slots), BF16),
            pltpu.VMEM((LINE, CHUNKS, layer_slots, part), BF16),
            pltpu.VMEM((LINE, CHUNKS, layer_slots, part), BF16),
            pltpu.VMEM((LINE, layer_slots, 128), BF16),
            pltpu.VMEM((LINE, layer_slots, 128), BF16),
            pltpu.VMEM((LINE, rows, layer_slots), BF16),
            pltpu.VMEM((CHUNKS, rows, part), F32),
            pltpu.VMEM((rows, width), F32),
            pltpu.VMEM((rows, width), F32),
            pltpu.VMEM((rows, width), F32),
            pltpu.VMEM((rows, width), BF16),
            pltpu.VMEM((rows, width), BF16),
            pltpu.VMEM((rows, width), BF16),
            pltpu.VMEM((LINE, 1, layer_slots), jnp.int32),
            pltpu.VMEM((layer_slots, rows), BF16),
            pltpu.VMEM((rows, layer_slots), BF16),
            pltpu.VMEM((CHUNKS - FAR, layer_slots, part), BF16),
            pltpu.VMEM((CHUNKS - FAR, layer_slots, part), BF16),
            pltpu.VMEM((CHUNKS - FAR, rows, part), BF16),
            pltpu.VMEM((CHUNKS - FAR, rows, part), BF16),
            pltpu.VMEM((rows, 128), F32),
            pltpu.VMEM((8, 128), F32),
            pltpu.VMEM((layer, 8, 128), F32),
            pltpu.VMEM((LINE, 8, 128), F32),
            pltpu.VMEM((n_grp, 8, 128), F32),
            dma((n_stage + 1,)),
            dma((11,)),
            dma((LINE - 1,)),
            dma((LINE - 1,)),
            dma((LINE * CHUNKS,)),
            dma((LINE * CHUNKS,)),
            dma((LINE * CHUNKS,)),
            dma((LINE * CHUNKS * (layer - 1),)),
            dma((LINE * CHUNKS * (layer - 1),)),
            dma((LINE * (layer - 1),)),
            dma((LINE * (layer - 1),)),
            dma((share_sems(n_nodes, n_grp),)),
            dma((share_sems(n_nodes, n_grp),)),
            dma((LINE - 1,)),
            dma((LINE - 1,)),
            dma(((CHUNKS - FAR) * (layer - 1),)),
            dma(((CHUNKS - FAR) * (layer - 1),)),
            dma((CHUNKS - FAR,)),
            dma((CHUNKS - FAR,)),
            dma((CHUNKS - FAR,)),
        ],
        compiler_params=pltpu.CompilerParams(
            vmem_limit_bytes=63 * MIB, collective_id=2, has_side_effects=True
        ),
        name="forward_pass",
    )(feats, mask, *edges_of, targets, board, neigh, nbias, comb, cbias, cot)


def add_into(target, first, count, columns, parts, step=16):
    @pl.loop(0, count // step)
    def _(i):
        at = pl.ds(pl.multiple_of(first + i * step, step), step)
        total = target[at, columns].astype(F32)
        for part in parts:
            total += part[pl.ds(pl.multiple_of(i * step, step), step), :].astype(F32)
        target[at, columns] = total.astype(target.dtype)


def reduce_job(place, order, grad, region, arrive, land, last, send, recv, free, base):
    first, rows, left, columns = region
    half = columns // 2
    core = place.at["c"]
    mine = pl.ds(pl.multiple_of(left + core * half, half), half)
    theirs = pl.ds(pl.multiple_of(left + (1 - core) * half, half), half)
    mate = place.member("c", 1 - core)
    block = pl.ds(first, rows)
    sems = iter(range(base, base + send.shape[0]))

    def lay(src, dst, device):
        sem = next(sems)
        return remote(src, dst, send.at[sem], recv.at[sem], device)

    across = lay(grad.at[block, theirs], arrive, mate)
    down = []
    begin, length, used = first, rows, 0
    for axis in order:
        length //= place.size[axis]
        copies, parts, devices = [], [], []
        for far, index, device in place.others(axis):
            start = pl.multiple_of(begin + index * length, 16)
            slot = land.at[pl.ds(used, length)]
            used += length
            copies.append(lay(grad.at[pl.ds(start, length), mine], slot, device))
            parts.append(slot)
            devices.append(device)
        parent = begin
        begin = pl.multiple_of(begin + place.at[axis] * length, 16)
        down.append((axis, parent, begin, length, copies, parts, devices))
    axis, parent, begin, length, _, _, devices = down[-1]
    here = pl.ds(pl.multiple_of(place.at[axis] * length, 16), length)
    whole = pl.ds(pl.multiple_of(parent, 16), length * place.size[axis])
    end = [lay(last.at[here], last.at[here], device) for device in devices]
    up = []
    for stage in range(len(down) - 1, 0, -1):
        axis, _, start, piece, _, _, devices = down[stage - 1]
        own = grad.at[pl.ds(start, piece), mine]
        up.append((stage, len(devices), [lay(own, own, device) for device in devices]))
    own = grad.at[block, mine]
    back = lay(own, own, mate)
    yield

    def release(at, devices):
        for device in devices:
            pl.semaphore_signal(free.at[base + at], inc=1, device_id=device, device_id_type=MESH)

    across.start()
    yield
    across.wait()
    release(0, [mate])
    add_into(grad, first, rows, mine, [arrive])
    for stage, (_, _, begin, length, copies, parts, devices) in enumerate(down):
        for copy in copies:
            copy.start()
        yield
        for copy in copies:
            copy.wait()
        if stage < len(down) - 1:
            release(stage + 1, devices)
        add_into(grad, begin, length, mine, parts)
    last[here] = grad[pl.ds(begin, length), mine]
    for copy in end:
        copy.start()
    yield
    for copy in end:
        copy.wait()
    grad[whole, mine] = last[pl.ds(0, whole.size)]
    for stage, count, copies in up:
        pl.semaphore_wait(free.at[base + stage], count)
        for copy in copies:
            copy.start()
        yield
        for copy in copies:
            copy.wait()
    pl.semaphore_wait(free.at[base], 1)
    back.start()
    yield
    back.wait()


def job_sems(n_nodes, n_grp):
    return 2 * (1 + (n_nodes // LINE // 2 - 1) + (LINE - 1) + (n_grp - 1))


AHEAD = 2
BEHIND = CHUNKS - AHEAD
BACKWARD_ACTS = "lLAfqYZBW321OGSEHFPcnb"
BACKWARD = (
    10, 2011, 7012, 2010, 13010, 19010, 19011, 1012, 8010, 5110, 19013, 7013, 3101, 19012, 19010, 9012,
    19013, 19011, 5111, 3100, 4101, 5112, 1011, 9013, 1013, 19012, 10012, 5113, 3111, 5114, 11012, 6011,
    4111, 5120, 3110, 19010, 4100, 5121, 10013, 19011, 4110, 19012, 5122, 4120, 4121, 11013, 5123, 5124,
    19010, 14010, 6012, 12012, 19013, 3121, 19011, 3120, 20012, 12013, 20013, 19010, 5130, 20012, 4131,
    19011, 5131, 19012, 20013, 5132, 19010, 4130, 19011, 5133, 19013, 20013, 20012, 5134, 19012, 19010,
    19011, 6013, 12011, 20011, 19013, 12010, 20010, 20011, 19012, 20013, 15010, 16011, 21012, 19013, 20012,
    21013, 20010, 20013, 16010, 21011, 21012, 21013, 20011, 21010, 21011, 20010, 20013, 21010, 20011, 18010,
    21012, 19010, 17010, 21011, 20010, 20012, 19012, 21013, 20011, 21010, 21011, 19013, 21013, 20010, 21010,
    20011, 21012, 20012, 19010, 21013, 20013, 21011, 21010, 21013, 20012, 19012, 21012, 20010, 21011, 19011,
    20011, 21013, 20013, 21010, 18011, 21012, 19013, 19011, 21011, 21010, 21012, 20013, 20012, 20010, 21013,
    20011, 21010, 21011, 20010, 19012, 20012, 18012, 21012, 20010, 21011, 21012, 21010, 20011, 18013, 19013,
    21013,
)


def gradient_regions(n_nodes, n_grp, width):
    pieces = n_nodes * n_grp // 2
    x_first, y_first = ("x", "y", "z"), ("y", "x", "z")
    regions = {}
    count = max(1, min(4, 2 * width // (16 * pieces)))
    n_rows = 2 * width // count
    for j in range(count):
        regions[f"comb{j}"] = (j * n_rows, n_rows, 0, width, y_first if j % 2 else x_first)
    if width % (16 * pieces) == 0:
        part = width // CHUNKS
        for k in range(CHUNKS):
            regions[f"neigh{k}"] = (2 * width, width, k * part, part, x_first if k % 2 else y_first)
        count = max(1, min(4, width // (16 * pieces)))
        n_rows = width // count
        for j in range(count):
            order = (x_first, y_first, x_first, ("z", "y", "x"))[j]
            regions[f"board{j}"] = (3 * width + j * n_rows, n_rows, 0, width, order)
    else:
        regions["board0"] = (2 * width, 2 * width, 0, width, x_first)
    return regions


def backward_kernel(
    n_nodes,
    n_grp,
    mask_ref,
    targets_ref,
    stats_ref,
    place_h,
    child_h,
    weight_h,
    hid_h,
    pre_h,
    featb_h,
    board_b_h,
    neigh_b_h,
    comb1_b_h,
    st_h,
    dnum_h,
    dz_h,
    agg_h,
    gfeat_h,
    summed_h,
    small_ref,
    hid,
    pre,
    featb,
    board_b,
    neigh_b,
    comb1_b,
    spread_t,
    dnum,
    dz,
    agg,
    picker_t,
    picker_l,
    lines,
    edge_place,
    edge_child,
    edge_weight,
    acc,
    own_t,
    parents,
    out_slots,
    in_slots,
    chain,
    tmp,
    dpre,
    dh,
    grad,
    arrive,
    land,
    gather,
    share_l,
    share_z,
    share_x,
    small,
    load_sem,
    store_sem,
    slot_send,
    slot_recv,
    up_send,
    down_send,
    chain_recv,
    line_send,
    line_recv,
    parent_up,
    parent_down,
    parent_recv,
    job_send,
    job_recv,
    job_free,
    share_send,
    share_recv,
):
    place = Place(n_nodes, n_grp)
    z, low = place.at["z"], place.at["l"]
    layer = place.size["l"]
    rows, width = hid.shape
    layer_slots = spread_t.shape[2]
    cap = layer_slots // layer
    part = width // CHUNKS

    loads = {}
    for i, (name, src, dst) in enumerate(
        (
            ("dnum", dnum_h, dnum),
            ("hid", hid_h, hid),
            ("agg", agg_h, agg),
            ("dz", dz_h, dz),
            ("spread_t", st_h, spread_t),
            ("comb1_b", comb1_b_h, comb1_b),
            ("pre", pre_h, pre),
            ("neigh_b", neigh_b_h, neigh_b),
            ("featb", featb_h, featb),
            ("board_b", board_b_h, board_b),
            ("place", place_h, edge_place),
            ("child", child_h, edge_child),
            ("weight", weight_h, edge_weight),
        )
    ):
        loads[name] = pltpu.make_async_copy(src, dst, load_sem.at[i])
        loads[name].start()
    def make_pickers():
        @pl.loop(0, LINE)
        def _(src):
            at = pl.ds(pl.multiple_of(src * layer_slots, layer_slots), layer_slots)
            ids = lax.broadcasted_iota(jnp.int32, (rows, layer_slots), 0)
            picker_t[src] = jnp.where(ids == targets_ref[:, at], 1.0, 0.0).astype(BF16).T

    barrier(place, ("l", "z", "x"), make_pickers)
    stores = []

    def store(src, dst):
        copy = pltpu.make_async_copy(src, dst, store_sem.at[len(stores)])
        copy.start()
        stores.append(copy)

    mask = column_of(mask_ref) > 0.5

    def source(which):
        flip = z // 2
        inner = z * (1 - 2 * flip) + (LINE - 1) * flip
        index = ORDER[0][which] * (1 - inner) + ORDER[1][which] * inner
        return index * (1 - 2 * flip) + (LINE - 1) * flip

    def cols(k):
        return pl.ds(pl.multiple_of(k * part, part), part)

    def slot_copy(dst, k, far, index, device):
        at = (dst * CHUNKS + k) * (layer - 1) + far
        return remote(
            out_slots.at[dst, k, pl.ds(pl.multiple_of(index * cap, cap), cap)],
            in_slots.at[dst, k, pl.ds(pl.multiple_of(low * cap, cap), cap)],
            slot_send.at[at],
            slot_recv.at[at],
            device,
        )

    def back(dst, k):
        out_slots[dst, k] = jnp.dot(
            picker_t[dst], dnum[:, cols(k)], preferred_element_type=F32
        ).astype(BF16)
        for far, index, device in place.others("l"):
            slot_copy(dst, k, far, index, device).start()
        own = pl.ds(pl.multiple_of(low * cap, cap), cap)
        in_slots[dst, k, own] = out_slots[dst, k, own]

    def child_sums(dst, k):
        for far, index, device in place.others("l"):
            slot_copy(dst, k, far, index, device).wait_recv()
        tmp[...] = jnp.dot(spread_t[dst], in_slots[dst, k], preferred_element_type=F32)

    def up_copy(dst, k):
        k = k - AHEAD
        at = dst * BEHIND + k
        return remote(
            chain.at[dst, k],
            chain.at[dst, k],
            up_send.at[at],
            chain_recv.at[at],
            place.member("z", z + 1),
        )

    def down_copy(dst, k, last):
        slot = LINE if last else dst
        k = k - AHEAD
        return remote(
            chain.at[dst, k],
            chain.at[slot, k],
            down_send.at[dst * BEHIND + k],
            chain_recv.at[slot * BEHIND + k],
            place.member("z", z - 1),
        )

    def arrived(slot, k):
        k = k - AHEAD
        remote(
            chain.at[slot, k],
            chain.at[slot, k],
            up_send.at[0],
            chain_recv.at[slot * BEHIND + k],
            place.member("z", lax.rem(z + 1, LINE)),
        ).wait_recv()

    def hand_on(dst, k):
        child_sums(dst, k)

        @pl.when(dst > z)
        def _():
            @pl.when(z > 0)
            def _():
                up_copy(dst, k).wait_recv()
                chain[dst, k - AHEAD] = (chain[dst, k - AHEAD].astype(F32) + tmp[...]).astype(BF16)

            @pl.when(z == 0)
            def _():
                chain[dst, k - AHEAD] = tmp[...].astype(BF16)

            up_copy(dst, k).start()

        @pl.when(dst < z)
        def _():
            @pl.when(z < LINE - 1)
            def _():
                down_copy(dst, k, False).wait_recv()
                chain[dst, k - AHEAD] = (chain[dst, k - AHEAD].astype(F32) + tmp[...]).astype(BF16)

            @pl.when(z == LINE - 1)
            def _():
                chain[dst, k - AHEAD] = tmp[...].astype(BF16)

            @pl.when(dst == z - 1)
            def _():
                down_copy(dst, k, True).start()

            @pl.when(dst < z - 1)
            def _():
                down_copy(dst, k, False).start()

    regions = gradient_regions(n_nodes, n_grp, width)
    per_job = job_sems(n_nodes, n_grp)

    def job(name):
        first, n_rows, left, columns, order = regions[name]
        rows_at, cols_at = pl.ds(first, n_rows), pl.ds(left, columns)
        land_at = pl.ds(left // 2, columns // 2)
        yield from reduce_job(
            place,
            order,
            grad,
            (first, n_rows, left, columns),
            arrive.at[rows_at, land_at],
            land.at[rows_at, land_at],
            gather.at[pl.ds(first // 4, n_rows // 4), land_at],
            job_send,
            job_recv,
            job_free,
            list(regions).index(name) * per_job,
        )
        store(grad.at[rows_at, cols_at], summed_h.at[rows_at, cols_at])

    jobs = {name: job(name) for name in regions}
    for lay_out in jobs.values():
        next(lay_out)

    def step_job(name, last=False):
        if name in jobs and (last or name != "board0" or "board3" in regions):
            try:
                next(jobs[name])
            except StopIteration:
                del jobs[name]

    loads["dnum"].wait()

    def back_all(k):
        for which in (3, 2, 1, 0):
            back(source(which), k)

    def comb_grad(left, first):
        @pl.loop(0, CHUNKS)
        def _(k):
            grad[pl.ds(first, width), cols(k)] = dot_tn(left[...], dz[:, cols(k)]).astype(BF16)

    def line_targets():
        lines[z] = targets_ref[:, pl.ds(pl.multiple_of(z * layer_slots, layer_slots), layer_slots)]
        for far, index, device in place.others("z"):
            at = pl.ds(pl.multiple_of(index * layer_slots, layer_slots), layer_slots)
            remote(
                targets_ref.at[:, at], lines.at[z], line_send.at[far], line_recv.at[far], device
            ).start()

    def line_picker(which):
        src = source(which)
        far = lax.rem(z - src - 1 + LINE, LINE)
        remote(
            lines.at[src], lines.at[src], line_send.at[0], line_recv.at[far], place.member("z", src)
        ).wait_recv()
        ids = lax.broadcasted_iota(jnp.int32, (rows, layer_slots), 0)
        picker_l[src] = jnp.where(ids == lines[src], 1.0, 0.0).astype(BF16).T

    def parent_copy(src, k, sems, to):
        piece = parents.at[src, k]
        at = src * AHEAD + k
        return remote(piece, piece, sems.at[at], parent_recv.at[at], place.member("z", to))

    def parent_send(k):
        parents[z, k] = dnum[:, cols(k)]

        @pl.when(z < LINE - 1)
        def _():
            parent_copy(z, k, parent_up, z + 1).start()

        @pl.when(z > 0)
        def _():
            parent_copy(z, k, parent_down, z - 1).start()

    def parent_forward(j, k):
        below = z - 1 - j
        above = z + 1 + j

        @pl.when(below >= 0)
        def _():
            parent_copy(below, k, parent_up, z + 1).wait_recv()

            @pl.when(z < LINE - 1)
            def _():
                parent_copy(below, k, parent_up, z + 1).start()

        @pl.when(above < LINE)
        def _():
            parent_copy(above, k, parent_down, z - 1).wait_recv()

            @pl.when(z > 0)
            def _():
                parent_copy(above, k, parent_down, z - 1).start()

    def parent_slots(which, k):
        src = source(which)
        choose = picker_t[z] if which == 0 else picker_l[src]
        out_slots[src, k] = jnp.dot(choose, parents[src, k], preferred_element_type=F32).astype(
            BF16
        )
        for far, index, device in place.others("l"):
            slot_copy(src, k, far, index, device).start()
        own = pl.ds(pl.multiple_of(low * cap, cap), cap)
        in_slots[src, k, own] = out_slots[src, k, own]

    edges = edge_place.shape[1]
    turn = math.gcd(edges, 2560)
    steps = edges // turn

    def build_own(which, ticks):
        src = source(which)
        if which == 1:
            for name in ("place", "child", "weight"):
                loads[name].wait()
        acc[...] = jnp.zeros_like(acc)

        @pl.loop(0, steps)
        def _(t):
            at = pl.ds(pl.multiple_of(t * turn, turn), turn)
            slot = (edge_place[:, at] - src * layer_slots).astype(jnp.int16)
            child = edge_child[:, at].astype(jnp.int16)
            weight = edge_weight[:, at].astype(F32).astype(F8)
            right = jnp.where(
                lax.broadcasted_iota(jnp.int16, (layer_slots, turn), 0) == slot,
                jnp.ones((), F8),
                jnp.zeros((), F8),
            )
            block = 256
            for first in range(0, rows, block):
                ids = lax.broadcasted_iota(jnp.int16, (block, turn), 0) + jnp.asarray(
                    first, jnp.int16
                )
                left = jnp.where(ids == child, weight, jnp.zeros((), F8))
                acc[pl.ds(first, block), :] += dot_nt(left, right)
            run_ticks(t, ticks)

        own_t[src] = acc[...].astype(BF16)

    def own(k):
        if k < AHEAD:
            for which in range(LINE):
                src = source(which)
                for far, index, device in place.others("l"):
                    slot_copy(src, k, far, index, device).wait_recv()
                weights = spread_t[z] if which == 0 else own_t[src]
                value = jnp.dot(weights, in_slots[src, k], preferred_element_type=F32)
                if which == 0:
                    tmp[...] = value
                else:
                    tmp[...] += value
        else:
            child_sums(z, k)

            @pl.when(z > 0)
            def _():
                arrived(z, k)
                tmp[...] += chain[z, k - AHEAD].astype(F32)

            @pl.when(z < LINE - 1)
            def _():
                arrived(LINE, k)
                tmp[...] += chain[LINE, k - AHEAD].astype(F32)

        down = (tmp[...] * gelu_slope(pre[:, cols(k)])).astype(BF16)
        dpre[:, cols(k)] = down
        small[0:1, cols(k)] = jnp.sum(down.astype(F32), axis=0, keepdims=True)
        dh[...] += dot_nt(down, neigh_b[:, cols(k)])

    def neigh_grad(k):
        grad[pl.ds(2 * width, width), cols(k)] = dot_tn(hid[...], dpre[:, cols(k)]).astype(BF16)

    def comb_grads():
        for name in ("hid", "agg", "dz", "comb1_b"):
            loads[name].wait()
        comb_grad(hid, 0)
        comb_grad(agg, width)

    def self_part():
        small[...] = jnp.zeros_like(small)
        small[1:2, :] = jnp.sum(dz[...].astype(F32), axis=0, keepdims=True)
        small[2:3, :] = jnp.broadcast_to(stats_ref[0:1, 0:1], (1, width))

        @pl.loop(0, CHUNKS)
        def _(k):
            dh[:, cols(k)] = dot_nt(dz[...], comb1_b[cols(k), :])

        for name in ("pre", "neigh_b", "featb", "board_b"):
            loads[name].wait()

    def own_and_grad(k):
        own(k)
        neigh_grad(k)

    def end_of_line():
        last = dh[...].astype(BF16)
        dpre[...] = jnp.where(mask, last, jnp.zeros_like(last))
        pre[...] = last.astype(F32)

    def board_grad(i):
        half = width // 2
        grad[pl.ds(3 * width + i * half, half), :] = dot_tn(
            featb[:, i * half : (i + 1) * half], dpre[...]
        ).astype(BF16)

    def feature_grad():
        @pl.loop(0, CHUNKS)
        def _(k):
            pre[:, cols(k)] = jnp.where(
                mask, dot_nt(dpre[...], board_b[cols(k), :]), pre[:, cols(k)]
            )

        store(pre, gfeat_h)

    share = Share(place, (share_l, share_z, share_x), share_send, share_recv)

    def step_share(stage):
        if stage == 0:
            share.start(0, small[...])
        elif stage < 3:
            share.start(stage, share.finish(stage - 1))
        else:
            row = lax.broadcasted_iota(jnp.int32, small_ref.shape, 0)
            small_ref[...] = share.finish(2) * jnp.where(row == 2, stats_ref[8:9, 0:1], 1.0)

    acts = {
        "l": lambda _: line_targets(),
        "L": line_picker,
        "A": parent_send,
        "f": parent_forward,
        "q": parent_slots,
        "B": back_all,
        "W": lambda _: loads["spread_t"].wait(),
        "G": lambda _: comb_grads(),
        "S": lambda _: self_part(),
        "O": own_and_grad,
        "E": lambda _: end_of_line(),
        "H": board_grad,
        "F": lambda _: feature_grad(),
        "P": step_share,
        "c": lambda j: step_job(f"comb{j}"),
        "n": lambda j: step_job(f"neigh{j}"),
        "b": lambda j: step_job(f"board{j}"),
        "3": lambda k: hand_on(source(3), k),
        "2": lambda k: hand_on(source(2), k),
        "1": lambda k: hand_on(source(1), k),
    }
    def act(name):
        acts[name[0]](*(int(c) for c in name[1:]))

    run_order(BACKWARD, BACKWARD_ACTS, steps, build_own, act)
    while jobs:
        for name in list(jobs):
            step_job(name, last=True)

    for far, index, device in place.others("z"):
        remote(lines.at[z], lines.at[z], line_send.at[far], line_recv.at[far], device).wait_send()

    @pl.loop(0, LINE * CHUNKS)
    def _(i):
        dst = i // CHUNKS
        k = lax.rem(i, CHUNKS)

        @pl.when(k < AHEAD)
        def _():
            @pl.when(jnp.logical_and(dst <= z, z < LINE - 1))
            def _():
                parent_copy(dst, k, parent_up, z + 1).wait_send()

            @pl.when(jnp.logical_and(dst >= z, z > 0))
            def _():
                parent_copy(dst, k, parent_down, z - 1).wait_send()

        @pl.when(k >= AHEAD)
        def _():
            @pl.when(dst > z)
            def _():
                up_copy(dst, k).wait_send()

            @pl.when(dst < z)
            def _():
                down_copy(dst, k, False).wait_send()

        for far, index, device in place.others("l"):
            slot_copy(dst, k, far, index, device).wait_send()

    for copy in stores:
        copy.wait()


def backward_pass(n_nodes, n_grp, mask, targets, stats, edges_of, hid, pre, featb, board_b, neigh_b, comb1_b, st, dnum, dz, agg):
    rows, width = hid.shape
    edges = edges_of[0].shape[1]
    layer = n_nodes // LINE
    layer_slots = st.shape[2]
    part = width // CHUNKS
    n_rows = 4 * width
    count = len(gradient_regions(n_nodes, n_grp, width))
    dma = pltpu.SemaphoreType.DMA
    big = pl.BlockSpec(memory_space=pl.ANY)
    vmem = pl.BlockSpec(memory_space=pltpu.VMEM)
    sems = count * job_sems(n_nodes, n_grp)
    pieces = LINE * CHUNKS
    return pl.pallas_call(
        functools.partial(backward_kernel, n_nodes, n_grp),
        out_shape=[
            jax.ShapeDtypeStruct((rows, width), F32),
            jax.ShapeDtypeStruct((n_rows, width), BF16),
            jax.ShapeDtypeStruct((8, width), F32),
        ],
        in_specs=[vmem, vmem, vmem] + [big] * 13,
        out_specs=[big, big, vmem],
        scratch_shapes=[
            pltpu.VMEM((rows, width), BF16),
            pltpu.VMEM((rows, width), F32),
            pltpu.VMEM((rows, width), BF16),
            pltpu.VMEM((width, width), BF16),
            pltpu.VMEM((width, width), BF16),
            pltpu.VMEM((width, width), BF16),
            pltpu.VMEM((LINE, rows, layer_slots), BF16),
            pltpu.VMEM((rows, width), BF16),
            pltpu.VMEM((rows, width), BF16),
            pltpu.VMEM((rows, width), BF16),
            pltpu.VMEM((LINE, layer_slots, rows), BF16),
            pltpu.VMEM((LINE, layer_slots, rows), BF16),
            pltpu.VMEM((LINE, 1, layer_slots), jnp.int32),
            pltpu.VMEM((1, edges), jnp.int32),
            pltpu.VMEM((1, edges), jnp.int32),
            pltpu.VMEM((1, edges), jnp.int32),
            pltpu.VMEM((rows, layer_slots), F32),
            pltpu.VMEM((LINE, rows, layer_slots), BF16),
            pltpu.VMEM((LINE, AHEAD, rows, part), BF16),
            pltpu.VMEM((LINE, CHUNKS, layer_slots, part), BF16),
            pltpu.VMEM((LINE, CHUNKS, layer_slots, part), BF16),
            pltpu.VMEM((LINE + 1, BEHIND, rows, part), BF16),
            pltpu.VMEM((rows, part), F32),
            pltpu.VMEM((rows, width), BF16),
            pltpu.VMEM((rows, width), F32),
            pltpu.VMEM((n_rows, width), BF16),
            pltpu.VMEM((n_rows, width // 2), BF16),
            pltpu.VMEM((n_rows, width // 2), BF16),
            pltpu.VMEM((n_rows // 4, width // 2), BF16),
            pltpu.VMEM((layer, 8, width), F32),
            pltpu.VMEM((LINE, 8, width), F32),
            pltpu.VMEM((n_grp, 8, width), F32),
            pltpu.VMEM((8, width), F32),
            dma((13,)),
            dma((count + 1,)),
            dma((pieces * (layer - 1),)),
            dma((pieces * (layer - 1),)),
            dma((LINE * BEHIND,)),
            dma((LINE * BEHIND,)),
            dma(((LINE + 1) * BEHIND,)),
            dma((LINE - 1,)),
            dma((LINE - 1,)),
            dma((LINE * AHEAD,)),
            dma((LINE * AHEAD,)),
            dma((LINE * AHEAD,)),
            dma((sems,)),
            dma((sems,)),
            pltpu.SemaphoreType.REGULAR((sems,)),
            dma((share_sems(n_nodes, n_grp),)),
            dma((share_sems(n_nodes, n_grp),)),
        ],
        compiler_params=pltpu.CompilerParams(
            vmem_limit_bytes=63 * MIB, collective_id=3, has_side_effects=True
        ),
        name="backward_pass",
    )(mask, targets, stats, *edges_of, hid, pre, featb, board_b, neigh_b, comb1_b, st, dnum, dz, agg)


def unpack_kernel(
    rows, joined, small_ref, comb, neigh, board, nbias_ref, cbias_ref, penalty_ref, low, wide, load_sem, store_sem
):
    width = joined.shape[1]
    blocks = joined.shape[0] // rows

    def load(i):
        at = pl.ds(i * rows, rows)
        return pltpu.make_async_copy(joined.at[at], low.at[at], load_sem.at[i])

    def store(i):
        first = i * rows
        if first < 2 * width:
            target = comb.at[pl.ds(first, rows)]
        elif first < 3 * width:
            target = neigh.at[pl.ds(first - 2 * width, rows)]
        else:
            target = board.at[pl.ds(first - 3 * width, rows)]
        return pltpu.make_async_copy(wide.at[pl.ds(first, rows)], target, store_sem.at[i])

    for i in range(blocks):
        load(i).start()
    nbias_ref[...] = small_ref[0:1, :]
    cbias_ref[...] = small_ref[1:2, :]
    penalty_ref[...] = small_ref[2:3, 0:1]
    for i in range(blocks):
        load(i).wait()

        @pl.loop(0, rows // 32)
        def _(r, i=i):
            at = pl.ds(pl.multiple_of(i * rows + r * 32, 32), 32)
            wide[at, :] = low[at, :].astype(F32)

        store(i).start()
    for i in range(blocks):
        store(i).wait()


def unpack(joined, small):
    n_rows, width = joined.shape
    rows = math.gcd(width, 256)
    big = pl.BlockSpec(memory_space=pl.ANY)
    vmem = pl.BlockSpec(memory_space=pltpu.VMEM)
    dma = pltpu.SemaphoreType.DMA
    return pl.pallas_call(
        functools.partial(unpack_kernel, rows),
        out_shape=[
            jax.ShapeDtypeStruct((2 * width, width), F32),
            jax.ShapeDtypeStruct((width, width), F32),
            jax.ShapeDtypeStruct((width, width), F32),
            jax.ShapeDtypeStruct((1, width), F32),
            jax.ShapeDtypeStruct((1, width), F32),
            jax.ShapeDtypeStruct((1, 1), F32),
        ],
        in_specs=[big, vmem],
        out_specs=[big] * 3 + [vmem] * 3,
        scratch_shapes=[
            pltpu.VMEM((n_rows, width), BF16),
            pltpu.VMEM((n_rows, width), F32),
            dma((n_rows // rows,)),
            dma((n_rows // rows,)),
        ],
        compiler_params=pltpu.CompilerParams(vmem_limit_bytes=60 * MIB),
        name="unpack",
    )(joined, small)


def on_device(
    n_nodes,
    n_grp,
    features,
    type_mask,
    edge_child,
    edge_slot,
    edge_weight,
    recv_rows,
    board_proj,
    neigh_proj,
    neigh_bias,
    combine_proj,
    combine_bias,
    out_cot,
):
    feats = features[0]
    rows, width = feats.shape
    peers = recv_rows.shape[2]
    cap = recv_rows.shape[3]
    slots = peers * cap
    targets = recv_rows[0, 0].reshape(1, slots)
    embed, hidden, pre, featb, pbl, qwl, cwl1, spread_t, dnum, dzb, aggb, stats = forward_pass(
        n_nodes,
        n_grp,
        feats,
        type_mask,
        (edge_slot, edge_child, edge_weight),
        targets,
        board_proj,
        neigh_proj,
        neigh_bias.reshape(1, width),
        combine_proj,
        combine_bias.reshape(1, width),
        out_cot[0],
    )
    grad_feats, summed, small = backward_pass(
        n_nodes,
        n_grp,
        type_mask,
        targets,
        stats,
        (edge_slot, edge_child, edge_weight),
        hidden,
        pre,
        featb,
        pbl,
        qwl,
        cwl1,
        spread_t,
        dnum,
        dzb,
        aggb,
    )
    grad_comb, grad_neigh, grad_board, grad_nbias, grad_cbias, penalty = unpack(summed, small)
    return (
        embed[None],
        penalty[0, 0],
        grad_feats[None],
        grad_board,
        grad_neigh,
        grad_nbias[0],
        grad_comb,
        grad_cbias[0],
    )


def solution(mesh):
    in_specs = (
        P("grp", "nodes", None),
        P("grp", "nodes"),
        P("grp", "nodes"),
        P("grp", "nodes"),
        P("grp", "nodes"),
        P("grp", "nodes", None, None),
        P(),
        P(),
        P(),
        P(),
        P(),
        P("grp", "nodes", None),
    )
    out_specs = (P("grp", "nodes", None), P(), P("grp", "nodes", None), P(), P(), P(), P(), P())
    return jax.shard_map(
        functools.partial(on_device, mesh.shape["nodes"], mesh.shape["grp"]),
        mesh=mesh,
        in_specs=in_specs,
        out_specs=out_specs,
        check_vma=False,
    )
```

```python
import functools
import math

import jax
import jax.numpy as jnp
from jax import lax
from jax.experimental import pallas as pl
from jax.experimental.pallas import tpu as pltpu
from jax.sharding import PartitionSpec as P

HIGH = lax.Precision.HIGHEST
MESH = pl.DeviceIdType.MESH
BF16 = jnp.bfloat16
F32 = jnp.float32
F8 = jnp.float8_e4m3fn
MIB = 2**20


def gelu_tanh(v):
    return jax.nn.gelu(v, approximate=True)


def dot_nt(left, right):
    return lax.dot_general(
        left, right, (((1,), (1,)), ((), ())), preferred_element_type=F32
    )


def dot_tn(left, right):
    return lax.dot_general(
        left, right, (((0,), (0,)), ((), ())), preferred_element_type=F32
    )


LINE = 4
CHUNKS = 4
FAR = 2
FORWARD_ACTS = "mYZfpiGDXRdaPugvxw"
FORWARD = (
    10, 11, 12, 13, 1100, 1101, 1102, 1103, 2010, 1140, 4102, 1141, 6010, 4100, 1142, 1143, 2014, 1110, 4101,
    3100, 13012, 13013, 1111, 1112, 3101, 1113, 3102, 2011, 4112, 14010, 1120, 4103, 4110, 1121, 1122, 3103,
    7010, 12011, 4113, 4111, 3110, 15012, 1123, 2012, 4120, 1130, 1131, 3111, 4121, 1132, 3112, 4122, 15013,
    1133, 7011, 2013, 16012, 3120, 3121, 4132, 4131, 5113, 4130, 3113, 5120, 5100, 12012, 10010, 16013, 8010,
    5101, 5132, 9010, 4133, 4123, 5131, 5122, 7012, 5111, 5112, 5102, 7013, 5121, 5110, 5130, 11011, 5103,
    17012, 11010, 11012, 5133, 17013, 5123, 12013,
)
ORDER = ((0, 1, 2, 3), (1, 2, 0, 3))


class Place:
    def __init__(self, n_nodes, n_grp):
        layer = n_nodes // LINE
        node = lax.axis_index("nodes")
        grp = lax.axis_index("grp")
        self.node, self.grp = node, grp
        self.size = {"l": layer, "c": 2, "y": layer // 2, "z": LINE, "x": n_grp}
        low = lax.rem(node, layer)
        self.at = {"l": low, "c": lax.rem(low, 2), "y": low // 2, "z": node // layer, "x": grp}

    def member(self, axis, index):
        layer = self.size["l"]
        low, line, grp = self.at["l"], self.at["z"], self.at["x"]
        if axis == "l":
            low = index
        elif axis == "c":
            low = self.at["y"] * 2 + index
        elif axis == "y":
            low = index * 2 + self.at["c"]
        elif axis == "z":
            line = index
        else:
            grp = index
        return {"nodes": line * layer + low, "grp": grp}

    def others(self, axis):
        size = self.size[axis]
        for far in range(1, size):
            index = lax.rem(self.at[axis] + far, size)
            yield far - 1, index, self.member(axis, index)


def remote(src, dst, send, recv, device):
    return pltpu.make_async_remote_copy(
        src_ref=src, dst_ref=dst, send_sem=send, recv_sem=recv, device_id=device, device_id_type=MESH
    )


def barrier(place, axes, meanwhile=None):
    sem = pltpu.get_barrier_semaphore()
    count = 0
    for axis in axes:
        for _, _, device in place.others(axis):
            pl.semaphore_signal(sem, inc=1, device_id=device, device_id_type=MESH)
            count += 1
    if meanwhile is not None:
        meanwhile()
    pl.semaphore_wait(sem, count)


def column_of(row_ref):
    row = row_ref[...].astype(F32)
    return jnp.broadcast_to(row, (128, row.shape[1])).T[:, 0:1]


def gelu(v):
    t = jnp.tanh(0.7978845608028654 * (v + 0.044715 * (v * v * v)))
    return v * (0.5 * (1.0 + t))


def gelu_and_slope(v):
    square = v * v
    t = jnp.tanh(0.7978845608028654 * (v + 0.044715 * (v * square)))
    bend = 0.7978845608028654 * (1.0 + 0.134145 * square)
    share = 0.5 * (1.0 + t)
    return v * share, share + 0.5 * v * (1.0 - t * t) * bend


def gelu_slope(v):
    square = v * v
    t = jnp.tanh(0.7978845608028654 * (v + 0.044715 * (v * square)))
    bend = 0.7978845608028654 * (1.0 + 0.134145 * square)
    return 0.5 * (1.0 + t) + 0.5 * v * (1.0 - t * t) * bend


class Share:
    def __init__(self, place, bufs, send, recv):
        self.place, self.send, self.recv = place, send, recv
        self.stages, base = [], 0
        for axis, buf in zip(("l", "z", "x"), bufs):
            self.stages.append((axis, buf, base))
            base += place.size[axis] - 1

    def start(self, stage, value):
        axis, buf, base = self.stages[stage]
        me = self.place.at[axis]
        buf[me] = value
        for far, _, device in self.place.others(axis):
            remote(
                buf.at[me], buf.at[me], self.send.at[base + far], self.recv.at[base + far], device
            ).start()

    def finish(self, stage):
        axis, buf, base = self.stages[stage]
        me = self.place.at[axis]
        for far, _, device in self.place.others(axis):
            remote(
                buf.at[me], buf.at[me], self.send.at[base + far], self.recv.at[base + far], device
            ).wait()
        total = buf[0]
        for i in range(1, self.place.size[axis]):
            total += buf[i]
        return total


def run_ticks(t, ticks):
    for at, acts in enumerate(ticks):
        if acts:

            @pl.when(t == at)
            def _(acts=acts):
                for act in acts:
                    act()


def run_order(order, letters, steps, build, act):
    ticks = None
    names = [letters[number // 1000] + str(number % 1000)[1:] for number in order]
    for name in names:
        if name[0] == "Y":
            if ticks is None:
                ticks = [[] for _ in range(steps)]
                marks = sum(other[:2] == name[:2] for other in names)
            now = (int(name[2]) + 1) * steps // marks - 1
        elif name[0] == "Z":
            build(int(name[1]), ticks)
            ticks = None
        elif ticks is not None:
            ticks[max(now, 0)].append(functools.partial(act, name))
        else:
            act(name)


def share_sems(n_nodes, n_grp):
    return (n_nodes // LINE - 1) + (LINE - 1) + max(1, n_grp - 1)


def forward_kernel(
    n_nodes,
    n_grp,
    feats_h,
    mask_ref,
    place_ref,
    child_ref,
    weight_ref,
    targets_ref,
    board_h,
    neigh_h,
    nbias_ref,
    comb_h,
    cbias_ref,
    cot_h,
    embed_h,
    hid_h,
    pre_h,
    featb_h,
    board_b_h,
    neigh_b_h,
    comb1_b_h,
    st_h,
    dnum_h,
    dz_h,
    agg_h,
    stats_ref,
    stage,
    featb,
    hid,
    pre,
    board_b,
    neigh_b,
    comb_b,
    keys,
    msg,
    acc,
    spread,
    spread_t,
    out_slots,
    in_slots,
    out_tot,
    in_tot,
    picker,
    num,
    zval,
    zpre,
    cot,
    agg,
    dz,
    dnum,
    lines,
    far_spread,
    far_picker,
    far_out,
    far_in,
    far_sum,
    end_sum,
    den_ref,
    scale_ref,
    count_l,
    count_z,
    count_x,
    load_sem,
    store_sem,
    key_send,
    key_recv,
    up_send,
    down_send,
    msg_recv,
    slot_send,
    slot_recv,
    tot_send,
    tot_recv,
    count_send,
    count_recv,
    line_send,
    line_recv,
    far_send,
    far_recv,
    sum_send,
    sum_recv,
    end_recv,
):
    place = Place(n_nodes, n_grp)
    z, low = place.at["z"], place.at["l"]
    layer = place.size["l"]
    rows, width = featb.shape
    edges = place_ref.shape[1]
    half = edges // 2
    layer_slots = spread.shape[1]
    cap = layer_slots // layer
    part = width // CHUNKS
    turn = math.gcd(half, 6400)
    steps = edges // turn

    sources = [feats_h.at[:]]
    for whole in (board_h, neigh_h, comb_h):
        for first in range(0, whole.shape[0], rows):
            sources.append(whole.at[pl.ds(first, rows)])
    n_stage = stage.shape[0]

    def load(i):
        return pltpu.make_async_copy(sources[i], stage.at[i % n_stage], load_sem.at[i % n_stage])

    for i in range(n_stage):
        load(i).start()
    load_cot = pltpu.make_async_copy(cot_h, cot, load_sem.at[n_stage])
    stores = []

    def store(src, dst):
        copy = pltpu.make_async_copy(src, dst, store_sem.at[len(stores)])
        copy.start()
        stores.append(copy)

    barrier(place, ("l", "z", "x"))
    keys[z, :, pl.ds(0, edges)] = place_ref[...] * 65536 + child_ref[...]
    keys[z, :, pl.ds(edges, half)] = (
        weight_ref[:, pl.ds(half, half)] * 65536 + weight_ref[:, pl.ds(0, half)]
    )

    def key_copy(far, device):
        return remote(keys.at[z], keys.at[z], key_send.at[far], key_recv.at[far], device)

    for far, _, device in place.others("z"):
        key_copy(far, device).start()
    inner = jnp.logical_and(z > 0, z < LINE - 1)
    outer = jnp.logical_or(z == 0, z == LINE - 1)
    half_at = z // 2
    far_end = (LINE - 1) * (1 - half_at)

    def line_copy(far, index, device):
        at = pl.ds(pl.multiple_of(index * layer_slots, layer_slots), layer_slots)
        return remote(
            targets_ref.at[:, at], lines.at[z], line_send.at[far], line_recv.at[far], device
        )

    @pl.when(outer)
    def _():
        for far, index, device in place.others("z"):
            line_copy(far, index, device).start()

    share = Share(place, (count_l, count_z, count_x), count_send, count_recv)
    mask = column_of(mask_ref)
    share.start(0, jnp.full((8, 128), jnp.sum(mask)))

    def cast(i, target, first):
        load(i).wait()
        slot = stage.at[i % n_stage]

        @pl.loop(0, rows // 32)
        def _(r):
            at = pl.ds(pl.multiple_of(r * 32, 32), 32)
            to = pl.ds(pl.multiple_of(first + r * 32, 32), 32)
            target[to, :] = slot[at, :].astype(BF16)

    cast(0, featb, 0)
    cast(1, board_b, 0)
    cast(2, board_b, rows)

    @pl.loop(0, CHUNKS)
    def _(k):
        at = pl.ds(pl.multiple_of(k * part, part), part)
        proj = jnp.dot(featb[...], board_b[:, at], preferred_element_type=F32)
        hid[:, at] = jnp.where(mask > 0.5, proj, stage[0, :, at]).astype(BF16)

    cast(3, neigh_b, 0)
    cast(4, neigh_b, rows)
    for i in range(n_stage, len(sources)):
        load(i).start()
    load_cot.start()

    def up_copy(src, k):
        piece = msg.at[src, k]
        index = src * CHUNKS + k
        return remote(
            piece, piece, up_send.at[index], msg_recv.at[index], place.member("z", z + 1)
        )

    def down_copy(src, k):
        piece = msg.at[src, k]
        index = src * CHUNKS + k
        return remote(
            piece, piece, down_send.at[index], msg_recv.at[index], place.member("z", z - 1)
        )

    def message(k):
        at = pl.ds(k * part, part)
        value = jnp.dot(hid[...], neigh_b[:, at], preferred_element_type=F32) + nbias_ref[:, at]
        pre[:, at] = value
        msg[z, k] = gelu(value).astype(BF16)

        @pl.when(z < LINE - 1)
        def _():
            up_copy(z, k).start()

        @pl.when(z > 0)
        def _():
            down_copy(z, k).start()

    def passes_up(k):
        return z < LINE - (1 if k < FAR else 2)

    def passes_down(k):
        return z > (0 if k < FAR else 1)

    def forward(j, k):
        below = z - 1 - j
        above = z + 1 + j

        comes = True if k < FAR or j == 0 else inner

        @pl.when(jnp.logical_and(below >= 0, comes))
        def _():
            up_copy(below, k).wait_recv()

            @pl.when(passes_up(k))
            def _():
                up_copy(below, k).start()

        @pl.when(jnp.logical_and(above < LINE, comes))
        def _():
            down_copy(above, k).wait_recv()

            @pl.when(passes_down(k))
            def _():
                down_copy(above, k).start()

    def tot_copy(src, far, index, device):
        at = (layer - 1) * src + far
        return remote(
            out_tot.at[src, pl.ds(pl.multiple_of(index * cap, cap), cap)],
            in_tot.at[src, pl.ds(pl.multiple_of(low * cap, cap), cap)],
            tot_send.at[at],
            tot_recv.at[at],
            device,
        )

    def finish_spread(src):
        total = acc[...]
        spread[src] = total.astype(BF16)
        spread_t[src] = total.astype(BF16).T
        sums = jnp.sum(total, axis=1, keepdims=True).astype(jnp.int32)
        lane = lax.broadcasted_iota(jnp.int32, (layer_slots, 128), 1)
        digit = jnp.where(
            lane == 0, sums & 255, jnp.where(lane == 1, (sums >> 8) & 255, jnp.where(lane == 2, sums >> 16, 0))
        )
        out_tot[src] = digit.astype(F32).astype(BF16)
        own = pl.ds(pl.multiple_of(low * cap, cap), cap)
        in_tot[src, own] = out_tot[src, own]
        for far, index, device in place.others("l"):
            tot_copy(src, far, index, device).start()

    def source(which):
        flip = z // 2
        depth = z * (1 - 2 * flip) + (LINE - 1) * flip
        index = ORDER[0][which] * (1 - depth) + ORDER[1][which] * depth
        return index * (1 - 2 * flip) + (LINE - 1) * flip

    def build(which, ticks):
        src, target = (source(which), z) if which < LINE else (z, far_end)
        acc[...] = jnp.zeros_like(acc)
        if 0 < which < LINE:
            far = lax.rem(z - src - 1 + LINE, LINE)
            remote(
                keys.at[src], keys.at[src], key_send.at[0], key_recv.at[far], place.member("z", src)
            ).wait_recv()

        @pl.loop(0, steps)
        def _(t):
            second = t // (steps // 2)
            key = keys[src, :, pl.ds(pl.multiple_of(t * turn, turn), turn)]
            start = edges + (t - second * (steps // 2)) * turn
            pair = keys[src, :, pl.ds(pl.multiple_of(start, turn), turn)]
            weight = (lax.shift_right_logical(pair, second * 16) & 65535).astype(F32).astype(F8)
            child = (key & 65535).astype(jnp.int16)
            slot = (lax.shift_right_logical(key, 16) - target * layer_slots).astype(jnp.int16)
            right = jnp.where(
                lax.broadcasted_iota(jnp.int16, (rows, turn), 0) == child, weight, jnp.zeros((), F8)
            )
            block = 256
            for first in range(0, layer_slots, block):
                ids = lax.broadcasted_iota(jnp.int16, (block, turn), 0) + jnp.asarray(
                    first, jnp.int16
                )
                left = jnp.where(ids == slot, jnp.ones((), F8), jnp.zeros((), F8))
                acc[pl.ds(first, block), :] += dot_nt(left, right)
            run_ticks(t, ticks)

        if which < LINE:
            finish_spread(src)
        else:
            far_spread[...] = acc[...].astype(BF16)

    def slot_copy(src, k, far, index, device):
        at = (src * CHUNKS + k) * (layer - 1) + far
        return remote(
            out_slots.at[src, k, pl.ds(pl.multiple_of(index * cap, cap), cap)],
            in_slots.at[src, k, pl.ds(pl.multiple_of(low * cap, cap), cap)],
            slot_send.at[at],
            slot_recv.at[at],
            device,
        )

    def piece(src, k):
        out_slots[src, k] = jnp.dot(spread[src], msg[src, k], preferred_element_type=F32).astype(BF16)
        for far, index, device in place.others("l"):
            slot_copy(src, k, far, index, device).start()
        own = pl.ds(pl.multiple_of(low * cap, cap), cap)
        in_slots[src, k, own] = out_slots[src, k, own]

    def pick(src, k):
        for far, index, device in place.others("l"):
            slot_copy(src, k, far, index, device).wait_recv()
        num[k] += jnp.dot(picker[src], in_slots[src, k], preferred_element_type=F32)

    def unless_far(which, k, act):
        if which < 2 or k < FAR:
            act(source(which), k)
        else:

            @pl.when(inner)
            def _():
                act(source(which), k)

    def far_copy(k, far, index, device):
        at = k * (layer - 1) + far
        return remote(
            far_out.at[k, pl.ds(pl.multiple_of(index * cap, cap), cap)],
            far_in.at[k, pl.ds(pl.multiple_of(low * cap, cap), cap)],
            far_send.at[at],
            far_recv.at[at],
            device,
        )

    onward = 1 - 2 * half_at

    def sum_copy(i):
        return remote(
            far_sum.at[i], far_sum.at[i], sum_send.at[i], sum_recv.at[i], place.member("z", z + onward)
        )

    def end_copy(i):
        return remote(
            far_sum.at[i],
            end_sum.at[i],
            sum_send.at[i],
            end_recv.at[i],
            place.member("z", z + 2 * onward),
        )

    def far_slots(k):
        i = k - FAR
        far_out[i] = jnp.dot(far_spread[...], msg[z, k], preferred_element_type=F32).astype(BF16)
        for far, index, device in place.others("l"):
            far_copy(i, far, index, device).start()
        own = pl.ds(pl.multiple_of(low * cap, cap), cap)
        far_in[i, own] = far_out[i, own]

    def make_far_picker():
        far = lax.rem(z - far_end - 1 + LINE, LINE)
        remote(
            lines.at[far_end],
            lines.at[far_end],
            line_send.at[0],
            line_recv.at[far],
            place.member("z", far_end),
        ).wait_recv()
        ids = lax.broadcasted_iota(jnp.int32, (rows, layer_slots), 0)
        far_picker[...] = jnp.where(ids == lines[far_end], 1.0, 0.0).astype(BF16)

        @pl.when(inner)
        def _():
            near = (LINE - 1) - far_end
            back = lax.rem(z - near - 1 + LINE, LINE)
            remote(
                lines.at[near],
                lines.at[near],
                line_send.at[0],
                line_recv.at[back],
                place.member("z", near),
            ).wait_recv()

    def far_parents(i):
        for far, index, device in place.others("l"):
            far_copy(i, far, index, device).wait_recv()
        return jnp.dot(far_picker[...], far_in[i], preferred_element_type=F32)

    def first_sum(k):
        @pl.when(outer)
        def _():
            far_sum[k - FAR] = far_parents(k - FAR).astype(BF16)
            sum_copy(k - FAR).start()

    def second_sum(k):
        @pl.when(inner)
        def _():
            i = k - FAR
            value = far_parents(i)
            sum_copy(i).wait_recv()
            far_sum[i] = (far_sum[i].astype(F32) + value).astype(BF16)
            end_copy(i).start()

    def add_far(k):
        @pl.when(outer)
        def _():
            end_copy(k - FAR).wait_recv()
            num[k] += end_sum[k - FAR].astype(F32)

    def make_picker():
        @pl.loop(0, LINE)
        def _(src):
            at = pl.ds(pl.multiple_of(src * layer_slots, layer_slots), layer_slots)
            ids = lax.broadcasted_iota(jnp.int32, (rows, layer_slots), 0)
            picker[src] = jnp.where(ids == targets_ref[:, at], 1.0, 0.0).astype(BF16)

        num[...] = jnp.zeros_like(num)

    def comb_piece(i):
        for j in range(i, 2 * width // rows, CHUNKS):
            cast(5 + j, comb_b, j * rows)

    def self_part():
        @pl.loop(0, CHUNKS)
        def _(k):
            at = pl.ds(pl.multiple_of(k * part, part), part)
            zpre[:, at] = (
                jnp.dot(hid[...], comb_b[0:width, at], preferred_element_type=F32)
                + cbias_ref[:, at]
            )

    def results():
        store(hid, hid_h)
        store(pre, pre_h)
        store(featb, featb_h)
        store(board_b, board_b_h)
        store(neigh_b, neigh_b_h)
        store(comb_b.at[pl.ds(0, width)], comb1_b_h)
        store(spread_t, st_h)

    def totals():
        digits = jnp.zeros((rows, 128), F32)
        for src in range(LINE):
            for far, index, device in place.others("l"):
                tot_copy(src, far, index, device).wait_recv()
            digits += jnp.dot(picker[src], in_tot[src], preferred_element_type=F32)
        lane = lax.broadcasted_iota(jnp.int32, (rows, 128), 1)
        worth = jnp.where(
            lane == 0, 1.0, jnp.where(lane == 1, 256.0, jnp.where(lane == 2, 65536.0, 0.0))
        )
        den_ref[...] = jnp.broadcast_to(
            1.0 + jnp.sum(digits * worth, axis=1, keepdims=True), (rows, 128)
        )

    def neighbours(k):
        at = pl.ds(k * part, part)
        agg[:, at] = (num[k] / den_ref[:, 0:1]).astype(BF16)
        if k < CHUNKS - 1:

            @pl.loop(0, CHUNKS)
            def _(n):
                to = pl.ds(pl.multiple_of(n * part, part), part)
                zpre[:, to] += jnp.dot(
                    agg[:, at], comb_b[pl.ds(width + k * part, part), to], preferred_element_type=F32
                )

    def step_share(stage):
        if stage in (1, 2):
            share.start(stage, share.finish(stage - 1))
        elif stage == 3:
            boards = share.finish(2)
            scale_ref[...] = 1.0 / (width * (1.0 + boards))

    acts = {
        "P": step_share,
        "m": message,
        "f": forward,
        "p": lambda which, k: unless_far(which, k, piece),
        "i": lambda which, k: unless_far(which, k, pick),
        "u": far_slots,
        "g": lambda _: make_far_picker(),
        "v": first_sum,
        "x": second_sum,
        "w": add_far,
        "G": lambda _: make_picker(),
        "D": comb_piece,
        "X": lambda _: self_part(),
        "R": lambda _: results(),
        "d": lambda _: totals(),
        "a": neighbours,
    }

    def act(step):
        acts[step[0]](*(int(c) for c in step[1:]))

    run_order(FORWARD, FORWARD_ACTS, steps, build, act)
    neighbours(CHUNKS - 1)
    load_cot.wait()
    den = den_ref[:, 0:1]
    scale = scale_ref[0:1, 0:1]
    last = pl.ds(width - part, part)

    def dense(k, carry):
        square, along = carry
        at = pl.ds(pl.multiple_of(k * part, part), part)
        value = zpre[:, at] + jnp.dot(
            agg[:, last], comb_b[pl.ds(2 * width - part, part), at], preferred_element_type=F32
        )
        out, slope = gelu_and_slope(value)
        zpre[:, at] = slope
        zval[:, at] = out
        square += jnp.sum(out * out, axis=1, keepdims=True)
        along += jnp.sum(out * cot[:, at], axis=1, keepdims=True)
        return square, along

    zero = jnp.zeros((rows, 1), F32)
    square, along = lax.fori_loop(0, CHUNKS, dense, (zero, zero))
    inverse = lax.rsqrt(square + 1e-06)
    along = along * inverse
    push = jnp.where(mask > 0.5, 2.0 * scale, 0.0)
    stats_ref[...] = jnp.concatenate(
        [
            jnp.full((8, 128), jnp.sum(jnp.where(mask > 0.5, square, 0.0))),
            jnp.broadcast_to(scale, (8, 128)),
        ],
        axis=0,
    )

    @pl.loop(0, CHUNKS)
    def _(k):
        at = pl.ds(pl.multiple_of(k * part, part), part)
        out = zval[:, at]
        emb = out * inverse
        grad = inverse * (cot[:, at] - emb * along) + push * out
        dz[:, at] = (grad * zpre[:, at]).astype(BF16)
        zval[:, at] = emb

    store(zval, embed_h)
    store(dz, dz_h)
    store(agg, agg_h)

    @pl.loop(0, CHUNKS)
    def _(k):
        at = pl.ds(pl.multiple_of(k * part, part), part)
        back = dot_nt(dz[...], comb_b[pl.ds(pl.multiple_of(width + k * part, part), part), :])
        dnum[:, at] = (back / den).astype(BF16)

    store(dnum, dnum_h)

    for far, _, device in place.others("z"):
        key_copy(far, device).wait_send()

    @pl.loop(0, LINE * CHUNKS)
    def _(i):
        src = i // CHUNKS
        k = lax.rem(i, CHUNKS)

        early = k < FAR

        @pl.when(
            jnp.logical_or(
                jnp.logical_and(src == z, z < LINE - 1),
                jnp.logical_and(
                    src < z, jnp.logical_or(jnp.logical_and(early, z < LINE - 1), z < LINE - 2)
                ),
            )
        )
        def _():
            up_copy(src, k).wait_send()

        @pl.when(
            jnp.logical_or(
                jnp.logical_and(src == z, z > 0),
                jnp.logical_and(src > z, jnp.logical_or(jnp.logical_and(early, z > 0), z > 1)),
            )
        )
        def _():
            down_copy(src, k).wait_send()

        near = jnp.logical_and(src - z < 2, z - src < 2)

        @pl.when(jnp.logical_or(jnp.logical_or(early, inner), near))
        def _():
            for far, index, device in place.others("l"):
                slot_copy(src, k, far, index, device).wait_send()

    for i in range(CHUNKS - FAR):
        sum_copy(i).wait_send()
        for far, index, device in place.others("l"):
            far_copy(i, far, index, device).wait_send()

    @pl.when(outer)
    def _():
        for far, index, device in place.others("z"):
            line_copy(far, index, device).wait_send()

    for src in range(LINE):
        for far, index, device in place.others("l"):
            tot_copy(src, far, index, device).wait_send()
    for copy in stores:
        copy.wait()


def forward_pass(n_nodes, n_grp, feats, mask, edges_of, targets, board, neigh, nbias, comb, cbias, cot):
    rows, width = feats.shape
    edges = edges_of[0].shape[1]
    layer = n_nodes // LINE
    layer_slots = targets.shape[1] // LINE
    part = width // CHUNKS
    dma = pltpu.SemaphoreType.DMA
    n_stage = 5
    big = pl.BlockSpec(memory_space=pl.ANY)
    small = pl.BlockSpec(memory_space=pltpu.VMEM)

    def hbm(shape, dtype):
        return jax.ShapeDtypeStruct(shape, dtype)

    return pl.pallas_call(
        functools.partial(forward_kernel, n_nodes, n_grp),
        out_shape=[
            hbm((rows, width), F32),
            hbm((rows, width), BF16),
            hbm((rows, width), F32),
            hbm((rows, width), BF16),
            hbm((width, width), BF16),
            hbm((width, width), BF16),
            hbm((width, width), BF16),
            hbm((LINE, rows, layer_slots), BF16),
            hbm((rows, width), BF16),
            hbm((rows, width), BF16),
            hbm((rows, width), BF16),
            hbm((16, 128), F32),
        ],
        in_specs=[big] + [small] * 5 + [big, big, small, big, small, big],
        out_specs=[big] * 11 + [small],
        scratch_shapes=[
            pltpu.VMEM((n_stage, rows, width), F32),
            pltpu.VMEM((rows, width), BF16),
            pltpu.VMEM((rows, width), BF16),
            pltpu.VMEM((rows, width), F32),
            pltpu.VMEM((width, width), BF16),
            pltpu.VMEM((width, width), BF16),
            pltpu.VMEM((2 * width, width), BF16),
            pltpu.VMEM((LINE, 1, edges + edges // 2), jnp.int32),
            pltpu.VMEM((LINE, CHUNKS, rows, part), BF16),
            pltpu.VMEM((layer_slots, rows), F32),
            pltpu.VMEM((LINE, layer_slots, rows), BF16),
            pltpu.VMEM((LINE, rows, layer_slots), BF16),
            pltpu.VMEM((LINE, CHUNKS, layer_slots, part), BF16),
            pltpu.VMEM((LINE, CHUNKS, layer_slots, part), BF16),
            pltpu.VMEM((LINE, layer_slots, 128), BF16),
            pltpu.VMEM((LINE, layer_slots, 128), BF16),
            pltpu.VMEM((LINE, rows, layer_slots), BF16),
            pltpu.VMEM((CHUNKS, rows, part), F32),
            pltpu.VMEM((rows, width), F32),
            pltpu.VMEM((rows, width), F32),
            pltpu.VMEM((rows, width), F32),
            pltpu.VMEM((rows, width), BF16),
            pltpu.VMEM((rows, width), BF16),
            pltpu.VMEM((rows, width), BF16),
            pltpu.VMEM((LINE, 1, layer_slots), jnp.int32),
            pltpu.VMEM((layer_slots, rows), BF16),
            pltpu.VMEM((rows, layer_slots), BF16),
            pltpu.VMEM((CHUNKS - FAR, layer_slots, part), BF16),
            pltpu.VMEM((CHUNKS - FAR, layer_slots, part), BF16),
            pltpu.VMEM((CHUNKS - FAR, rows, part), BF16),
            pltpu.VMEM((CHUNKS - FAR, rows, part), BF16),
            pltpu.VMEM((rows, 128), F32),
            pltpu.VMEM((8, 128), F32),
            pltpu.VMEM((layer, 8, 128), F32),
            pltpu.VMEM((LINE, 8, 128), F32),
            pltpu.VMEM((n_grp, 8, 128), F32),
            dma((n_stage + 1,)),
            dma((11,)),
            dma((LINE - 1,)),
            dma((LINE - 1,)),
            dma((LINE * CHUNKS,)),
            dma((LINE * CHUNKS,)),
            dma((LINE * CHUNKS,)),
            dma((LINE * CHUNKS * (layer - 1),)),
            dma((LINE * CHUNKS * (layer - 1),)),
            dma((LINE * (layer - 1),)),
            dma((LINE * (layer - 1),)),
            dma((share_sems(n_nodes, n_grp),)),
            dma((share_sems(n_nodes, n_grp),)),
            dma((LINE - 1,)),
            dma((LINE - 1,)),
            dma(((CHUNKS - FAR) * (layer - 1),)),
            dma(((CHUNKS - FAR) * (layer - 1),)),
            dma((CHUNKS - FAR,)),
            dma((CHUNKS - FAR,)),
            dma((CHUNKS - FAR,)),
        ],
        compiler_params=pltpu.CompilerParams(
            vmem_limit_bytes=63 * MIB, collective_id=2, has_side_effects=True
        ),
        name="forward_pass",
    )(feats, mask, *edges_of, targets, board, neigh, nbias, comb, cbias, cot)


def add_into(target, first, count, columns, parts, step=16):
    @pl.loop(0, count // step)
    def _(i):
        at = pl.ds(pl.multiple_of(first + i * step, step), step)
        total = target[at, columns].astype(F32)
        for part in parts:
            total += part[pl.ds(pl.multiple_of(i * step, step), step), :].astype(F32)
        target[at, columns] = total.astype(target.dtype)


def reduce_job(place, order, grad, region, arrive, land, last, send, recv, free, base):
    first, rows, left, columns = region
    half = columns // 2
    core = place.at["c"]
    mine = pl.ds(pl.multiple_of(left + core * half, half), half)
    theirs = pl.ds(pl.multiple_of(left + (1 - core) * half, half), half)
    mate = place.member("c", 1 - core)
    block = pl.ds(first, rows)
    sems = iter(range(base, base + send.shape[0]))

    def lay(src, dst, device):
        sem = next(sems)
        return remote(src, dst, send.at[sem], recv.at[sem], device)

    across = lay(grad.at[block, theirs], arrive, mate)
    down = []
    begin, length, used = first, rows, 0
    for axis in order:
        length //= place.size[axis]
        copies, parts, devices = [], [], []
        for far, index, device in place.others(axis):
            start = pl.multiple_of(begin + index * length, 16)
            slot = land.at[pl.ds(used, length)]
            used += length
            copies.append(lay(grad.at[pl.ds(start, length), mine], slot, device))
            parts.append(slot)
            devices.append(device)
        parent = begin
        begin = pl.multiple_of(begin + place.at[axis] * length, 16)
        down.append((axis, parent, begin, length, copies, parts, devices))
    axis, parent, begin, length, _, _, devices = down[-1]
    here = pl.ds(pl.multiple_of(place.at[axis] * length, 16), length)
    whole = pl.ds(pl.multiple_of(parent, 16), length * place.size[axis])
    end = [lay(last.at[here], last.at[here], device) for device in devices]
    up = []
    for stage in range(len(down) - 1, 0, -1):
        axis, _, start, piece, _, _, devices = down[stage - 1]
        own = grad.at[pl.ds(start, piece), mine]
        up.append((stage, len(devices), [lay(own, own, device) for device in devices]))
    own = grad.at[block, mine]
    back = lay(own, own, mate)
    yield

    def release(at, devices):
        for device in devices:
            pl.semaphore_signal(free.at[base + at], inc=1, device_id=device, device_id_type=MESH)

    across.start()
    yield
    across.wait()
    release(0, [mate])
    add_into(grad, first, rows, mine, [arrive])
    for stage, (_, _, begin, length, copies, parts, devices) in enumerate(down):
        for copy in copies:
            copy.start()
        yield
        for copy in copies:
            copy.wait()
        if stage < len(down) - 1:
            release(stage + 1, devices)
        add_into(grad, begin, length, mine, parts)
    last[here] = grad[pl.ds(begin, length), mine]
    for copy in end:
        copy.start()
    yield
    for copy in end:
        copy.wait()
    grad[whole, mine] = last[pl.ds(0, whole.size)]
    for stage, count, copies in up:
        pl.semaphore_wait(free.at[base + stage], count)
        for copy in copies:
            copy.start()
        yield
        for copy in copies:
            copy.wait()
    pl.semaphore_wait(free.at[base], 1)
    back.start()
    yield
    back.wait()


def job_sems(n_nodes, n_grp):
    return 2 * (1 + (n_nodes // LINE // 2 - 1) + (LINE - 1) + (n_grp - 1))


AHEAD = 2
BEHIND = CHUNKS - AHEAD
BACKWARD_ACTS = "lLAfqYZBW321OGSEHFPcnb"
BACKWARD = (
    10, 2011, 7012, 2010, 13010, 19010, 19011, 1012, 8010, 5110, 19013, 7013, 3101, 19012, 19010, 9012,
    19013, 19011, 5111, 3100, 4101, 5112, 1011, 9013, 1013, 19012, 10012, 5113, 3111, 5114, 11012, 6011,
    4111, 5120, 3110, 19010, 4100, 5121, 10013, 19011, 4110, 19012, 5122, 4120, 4121, 11013, 5123, 5124,
    19010, 14010, 6012, 12012, 19013, 3121, 19011, 3120, 20012, 12013, 20013, 19010, 5130, 20012, 4131,
    19011, 5131, 19012, 20013, 5132, 19010, 4130, 19011, 5133, 19013, 20013, 20012, 5134, 19012, 19010,
    19011, 6013, 12011, 20011, 19013, 12010, 20010, 20011, 19012, 20013, 15010, 16011, 21012, 19013, 20012,
    21013, 20010, 20013, 16010, 21011, 21012, 21013, 20011, 21010, 21011, 20010, 20013, 21010, 20011, 18010,
    21012, 19010, 17010, 21011, 20010, 20012, 19012, 21013, 20011, 21010, 21011, 19013, 21013, 20010, 21010,
    20011, 21012, 20012, 19010, 21013, 20013, 21011, 21010, 21013, 20012, 19012, 21012, 20010, 21011, 19011,
    20011, 21013, 20013, 21010, 18011, 21012, 19013, 19011, 21011, 21010, 21012, 20013, 20012, 20010, 21013,
    20011, 21010, 21011, 20010, 19012, 20012, 18012, 21012, 20010, 21011, 21012, 21010, 20011, 18013, 19013,
    21013,
)


def gradient_regions(n_nodes, n_grp, width):
    pieces = n_nodes * n_grp // 2
    x_first, y_first = ("x", "y", "z"), ("y", "x", "z")
    regions = {}
    count = max(1, min(4, 2 * width // (16 * pieces)))
    n_rows = 2 * width // count
    for j in range(count):
        regions[f"comb{j}"] = (j * n_rows, n_rows, 0, width, y_first if j % 2 else x_first)
    if width % (16 * pieces) == 0:
        part = width // CHUNKS
        for k in range(CHUNKS):
            regions[f"neigh{k}"] = (2 * width, width, k * part, part, x_first if k % 2 else y_first)
        count = max(1, min(4, width // (16 * pieces)))
        n_rows = width // count
        for j in range(count):
            order = (x_first, y_first, x_first, ("z", "y", "x"))[j]
            regions[f"board{j}"] = (3 * width + j * n_rows, n_rows, 0, width, order)
    else:
        regions["board0"] = (2 * width, 2 * width, 0, width, x_first)
    return regions


def backward_kernel(
    n_nodes,
    n_grp,
    mask_ref,
    targets_ref,
    stats_ref,
    place_h,
    child_h,
    weight_h,
    hid_h,
    pre_h,
    featb_h,
    board_b_h,
    neigh_b_h,
    comb1_b_h,
    st_h,
    dnum_h,
    dz_h,
    agg_h,
    gfeat_h,
    summed_h,
    small_ref,
    hid,
    pre,
    featb,
    board_b,
    neigh_b,
    comb1_b,
    spread_t,
    dnum,
    dz,
    agg,
    picker_t,
    picker_l,
    lines,
    edge_place,
    edge_child,
    edge_weight,
    acc,
    own_t,
    parents,
    out_slots,
    in_slots,
    chain,
    tmp,
    dpre,
    dh,
    grad,
    arrive,
    land,
    gather,
    share_l,
    share_z,
    share_x,
    small,
    load_sem,
    store_sem,
    slot_send,
    slot_recv,
    up_send,
    down_send,
    chain_recv,
    line_send,
    line_recv,
    parent_up,
    parent_down,
    parent_recv,
    job_send,
    job_recv,
    job_free,
    share_send,
    share_recv,
):
    place = Place(n_nodes, n_grp)
    z, low = place.at["z"], place.at["l"]
    layer = place.size["l"]
    rows, width = hid.shape
    layer_slots = spread_t.shape[2]
    cap = layer_slots // layer
    part = width // CHUNKS

    loads = {}
    for i, (name, src, dst) in enumerate(
        (
            ("dnum", dnum_h, dnum),
            ("hid", hid_h, hid),
            ("agg", agg_h, agg),
            ("dz", dz_h, dz),
            ("spread_t", st_h, spread_t),
            ("comb1_b", comb1_b_h, comb1_b),
            ("pre", pre_h, pre),
            ("neigh_b", neigh_b_h, neigh_b),
            ("featb", featb_h, featb),
            ("board_b", board_b_h, board_b),
            ("place", place_h, edge_place),
            ("child", child_h, edge_child),
            ("weight", weight_h, edge_weight),
        )
    ):
        loads[name] = pltpu.make_async_copy(src, dst, load_sem.at[i])
        loads[name].start()
    def make_pickers():
        @pl.loop(0, LINE)
        def _(src):
            at = pl.ds(pl.multiple_of(src * layer_slots, layer_slots), layer_slots)
            ids = lax.broadcasted_iota(jnp.int32, (rows, layer_slots), 0)
            picker_t[src] = jnp.where(ids == targets_ref[:, at], 1.0, 0.0).astype(BF16).T

    barrier(place, ("l", "z", "x"), make_pickers)
    stores = []

    def store(src, dst):
        copy = pltpu.make_async_copy(src, dst, store_sem.at[len(stores)])
        copy.start()
        stores.append(copy)

    mask = column_of(mask_ref) > 0.5

    def source(which):
        flip = z // 2
        inner = z * (1 - 2 * flip) + (LINE - 1) * flip
        index = ORDER[0][which] * (1 - inner) + ORDER[1][which] * inner
        return index * (1 - 2 * flip) + (LINE - 1) * flip

    def cols(k):
        return pl.ds(pl.multiple_of(k * part, part), part)

    def slot_copy(dst, k, far, index, device):
        at = (dst * CHUNKS + k) * (layer - 1) + far
        return remote(
            out_slots.at[dst, k, pl.ds(pl.multiple_of(index * cap, cap), cap)],
            in_slots.at[dst, k, pl.ds(pl.multiple_of(low * cap, cap), cap)],
            slot_send.at[at],
            slot_recv.at[at],
            device,
        )

    def back(dst, k):
        out_slots[dst, k] = jnp.dot(
            picker_t[dst], dnum[:, cols(k)], preferred_element_type=F32
        ).astype(BF16)
        for far, index, device in place.others("l"):
            slot_copy(dst, k, far, index, device).start()
        own = pl.ds(pl.multiple_of(low * cap, cap), cap)
        in_slots[dst, k, own] = out_slots[dst, k, own]

    def child_sums(dst, k):
        for far, index, device in place.others("l"):
            slot_copy(dst, k, far, index, device).wait_recv()
        tmp[...] = jnp.dot(spread_t[dst], in_slots[dst, k], preferred_element_type=F32)

    def up_copy(dst, k):
        k = k - AHEAD
        at = dst * BEHIND + k
        return remote(
            chain.at[dst, k],
            chain.at[dst, k],
            up_send.at[at],
            chain_recv.at[at],
            place.member("z", z + 1),
        )

    def down_copy(dst, k, last):
        slot = LINE if last else dst
        k = k - AHEAD
        return remote(
            chain.at[dst, k],
            chain.at[slot, k],
            down_send.at[dst * BEHIND + k],
            chain_recv.at[slot * BEHIND + k],
            place.member("z", z - 1),
        )

    def arrived(slot, k):
        k = k - AHEAD
        remote(
            chain.at[slot, k],
            chain.at[slot, k],
            up_send.at[0],
            chain_recv.at[slot * BEHIND + k],
            place.member("z", lax.rem(z + 1, LINE)),
        ).wait_recv()

    def hand_on(dst, k):
        child_sums(dst, k)

        @pl.when(dst > z)
        def _():
            @pl.when(z > 0)
            def _():
                up_copy(dst, k).wait_recv()
                chain[dst, k - AHEAD] = (chain[dst, k - AHEAD].astype(F32) + tmp[...]).astype(BF16)

            @pl.when(z == 0)
            def _():
                chain[dst, k - AHEAD] = tmp[...].astype(BF16)

            up_copy(dst, k).start()

        @pl.when(dst < z)
        def _():
            @pl.when(z < LINE - 1)
            def _():
                down_copy(dst, k, False).wait_recv()
                chain[dst, k - AHEAD] = (chain[dst, k - AHEAD].astype(F32) + tmp[...]).astype(BF16)

            @pl.when(z == LINE - 1)
            def _():
                chain[dst, k - AHEAD] = tmp[...].astype(BF16)

            @pl.when(dst == z - 1)
            def _():
                down_copy(dst, k, True).start()

            @pl.when(dst < z - 1)
            def _():
                down_copy(dst, k, False).start()

    regions = gradient_regions(n_nodes, n_grp, width)
    per_job = job_sems(n_nodes, n_grp)

    def job(name):
        first, n_rows, left, columns, order = regions[name]
        rows_at, cols_at = pl.ds(first, n_rows), pl.ds(left, columns)
        land_at = pl.ds(left // 2, columns // 2)
        yield from reduce_job(
            place,
            order,
            grad,
            (first, n_rows, left, columns),
            arrive.at[rows_at, land_at],
            land.at[rows_at, land_at],
            gather.at[pl.ds(first // 4, n_rows // 4), land_at],
            job_send,
            job_recv,
            job_free,
            list(regions).index(name) * per_job,
        )
        store(grad.at[rows_at, cols_at], summed_h.at[rows_at, cols_at])

    jobs = {name: job(name) for name in regions}
    for lay_out in jobs.values():
        next(lay_out)

    def step_job(name, last=False):
        if name in jobs and (last or name != "board0" or "board3" in regions):
            try:
                next(jobs[name])
            except StopIteration:
                del jobs[name]

    loads["dnum"].wait()

    def back_all(k):
        for which in (3, 2, 1, 0):
            back(source(which), k)

    def comb_grad(left, first):
        @pl.loop(0, CHUNKS)
        def _(k):
            grad[pl.ds(first, width), cols(k)] = dot_tn(left[...], dz[:, cols(k)]).astype(BF16)

    def line_targets():
        lines[z] = targets_ref[:, pl.ds(pl.multiple_of(z * layer_slots, layer_slots), layer_slots)]
        for far, index, device in place.others("z"):
            at = pl.ds(pl.multiple_of(index * layer_slots, layer_slots), layer_slots)
            remote(
                targets_ref.at[:, at], lines.at[z], line_send.at[far], line_recv.at[far], device
            ).start()

    def line_picker(which):
        src = source(which)
        far = lax.rem(z - src - 1 + LINE, LINE)
        remote(
            lines.at[src], lines.at[src], line_send.at[0], line_recv.at[far], place.member("z", src)
        ).wait_recv()
        ids = lax.broadcasted_iota(jnp.int32, (rows, layer_slots), 0)
        picker_l[src] = jnp.where(ids == lines[src], 1.0, 0.0).astype(BF16).T

    def parent_copy(src, k, sems, to):
        piece = parents.at[src, k]
        at = src * AHEAD + k
        return remote(piece, piece, sems.at[at], parent_recv.at[at], place.member("z", to))

    def parent_send(k):
        parents[z, k] = dnum[:, cols(k)]

        @pl.when(z < LINE - 1)
        def _():
            parent_copy(z, k, parent_up, z + 1).start()

        @pl.when(z > 0)
        def _():
            parent_copy(z, k, parent_down, z - 1).start()

    def parent_forward(j, k):
        below = z - 1 - j
        above = z + 1 + j

        @pl.when(below >= 0)
        def _():
            parent_copy(below, k, parent_up, z + 1).wait_recv()

            @pl.when(z < LINE - 1)
            def _():
                parent_copy(below, k, parent_up, z + 1).start()

        @pl.when(above < LINE)
        def _():
            parent_copy(above, k, parent_down, z - 1).wait_recv()

            @pl.when(z > 0)
            def _():
                parent_copy(above, k, parent_down, z - 1).start()

    def parent_slots(which, k):
        src = source(which)
        choose = picker_t[z] if which == 0 else picker_l[src]
        out_slots[src, k] = jnp.dot(choose, parents[src, k], preferred_element_type=F32).astype(
            BF16
        )
        for far, index, device in place.others("l"):
            slot_copy(src, k, far, index, device).start()
        own = pl.ds(pl.multiple_of(low * cap, cap), cap)
        in_slots[src, k, own] = out_slots[src, k, own]

    edges = edge_place.shape[1]
    turn = math.gcd(edges, 2560)
    steps = edges // turn

    def build_own(which, ticks):
        src = source(which)
        if which == 1:
            for name in ("place", "child", "weight"):
                loads[name].wait()
        acc[...] = jnp.zeros_like(acc)

        @pl.loop(0, steps)
        def _(t):
            at = pl.ds(pl.multiple_of(t * turn, turn), turn)
            slot = (edge_place[:, at] - src * layer_slots).astype(jnp.int16)
            child = edge_child[:, at].astype(jnp.int16)
            weight = edge_weight[:, at].astype(F32).astype(F8)
            right = jnp.where(
                lax.broadcasted_iota(jnp.int16, (layer_slots, turn), 0) == slot,
                jnp.ones((), F8),
                jnp.zeros((), F8),
            )
            block = 256
            for first in range(0, rows, block):
                ids = lax.broadcasted_iota(jnp.int16, (block, turn), 0) + jnp.asarray(
                    first, jnp.int16
                )
                left = jnp.where(ids == child, weight, jnp.zeros((), F8))
                acc[pl.ds(first, block), :] += dot_nt(left, right)
            run_ticks(t, ticks)

        own_t[src] = acc[...].astype(BF16)

    def own(k):
        if k < AHEAD:
            for which in range(LINE):
                src = source(which)
                for far, index, device in place.others("l"):
                    slot_copy(src, k, far, index, device).wait_recv()
                weights = spread_t[z] if which == 0 else own_t[src]
                value = jnp.dot(weights, in_slots[src, k], preferred_element_type=F32)
                if which == 0:
                    tmp[...] = value
                else:
                    tmp[...] += value
        else:
            child_sums(z, k)

            @pl.when(z > 0)
            def _():
                arrived(z, k)
                tmp[...] += chain[z, k - AHEAD].astype(F32)

            @pl.when(z < LINE - 1)
            def _():
                arrived(LINE, k)
                tmp[...] += chain[LINE, k - AHEAD].astype(F32)

        down = (tmp[...] * gelu_slope(pre[:, cols(k)])).astype(BF16)
        dpre[:, cols(k)] = down
        small[0:1, cols(k)] = jnp.sum(down.astype(F32), axis=0, keepdims=True)
        dh[...] += dot_nt(down, neigh_b[:, cols(k)])

    def neigh_grad(k):
        grad[pl.ds(2 * width, width), cols(k)] = dot_tn(hid[...], dpre[:, cols(k)]).astype(BF16)

    def comb_grads():
        for name in ("hid", "agg", "dz", "comb1_b"):
            loads[name].wait()
        comb_grad(hid, 0)
        comb_grad(agg, width)

    def self_part():
        small[...] = jnp.zeros_like(small)
        small[1:2, :] = jnp.sum(dz[...].astype(F32), axis=0, keepdims=True)
        small[2:3, :] = jnp.broadcast_to(stats_ref[0:1, 0:1], (1, width))

        @pl.loop(0, CHUNKS)
        def _(k):
            dh[:, cols(k)] = dot_nt(dz[...], comb1_b[cols(k), :])

        for name in ("pre", "neigh_b", "featb", "board_b"):
            loads[name].wait()

    def own_and_grad(k):
        own(k)
        neigh_grad(k)

    def end_of_line():
        last = dh[...].astype(BF16)
        dpre[...] = jnp.where(mask, last, jnp.zeros_like(last))
        pre[...] = last.astype(F32)

    def board_grad(i):
        half = width // 2
        grad[pl.ds(3 * width + i * half, half), :] = dot_tn(
            featb[:, i * half : (i + 1) * half], dpre[...]
        ).astype(BF16)

    def feature_grad():
        @pl.loop(0, CHUNKS)
        def _(k):
            pre[:, cols(k)] = jnp.where(
                mask, dot_nt(dpre[...], board_b[cols(k), :]), pre[:, cols(k)]
            )

        store(pre, gfeat_h)

    share = Share(place, (share_l, share_z, share_x), share_send, share_recv)

    def step_share(stage):
        if stage == 0:
            share.start(0, small[...])
        elif stage < 3:
            share.start(stage, share.finish(stage - 1))
        else:
            row = lax.broadcasted_iota(jnp.int32, small_ref.shape, 0)
            small_ref[...] = share.finish(2) * jnp.where(row == 2, stats_ref[8:9, 0:1], 1.0)

    acts = {
        "l": lambda _: line_targets(),
        "L": line_picker,
        "A": parent_send,
        "f": parent_forward,
        "q": parent_slots,
        "B": back_all,
        "W": lambda _: loads["spread_t"].wait(),
        "G": lambda _: comb_grads(),
        "S": lambda _: self_part(),
        "O": own_and_grad,
        "E": lambda _: end_of_line(),
        "H": board_grad,
        "F": lambda _: feature_grad(),
        "P": step_share,
        "c": lambda j: step_job(f"comb{j}"),
        "n": lambda j: step_job(f"neigh{j}"),
        "b": lambda j: step_job(f"board{j}"),
        "3": lambda k: hand_on(source(3), k),
        "2": lambda k: hand_on(source(2), k),
        "1": lambda k: hand_on(source(1), k),
    }
    def act(name):
        acts[name[0]](*(int(c) for c in name[1:]))

    run_order(BACKWARD, BACKWARD_ACTS, steps, build_own, act)
    while jobs:
        for name in list(jobs):
            step_job(name, last=True)

    for far, index, device in place.others("z"):
        remote(lines.at[z], lines.at[z], line_send.at[far], line_recv.at[far], device).wait_send()

    @pl.loop(0, LINE * CHUNKS)
    def _(i):
        dst = i // CHUNKS
        k = lax.rem(i, CHUNKS)

        @pl.when(k < AHEAD)
        def _():
            @pl.when(jnp.logical_and(dst <= z, z < LINE - 1))
            def _():
                parent_copy(dst, k, parent_up, z + 1).wait_send()

            @pl.when(jnp.logical_and(dst >= z, z > 0))
            def _():
                parent_copy(dst, k, parent_down, z - 1).wait_send()

        @pl.when(k >= AHEAD)
        def _():
            @pl.when(dst > z)
            def _():
                up_copy(dst, k).wait_send()

            @pl.when(dst < z)
            def _():
                down_copy(dst, k, False).wait_send()

        for far, index, device in place.others("l"):
            slot_copy(dst, k, far, index, device).wait_send()

    for copy in stores:
        copy.wait()


def backward_pass(n_nodes, n_grp, mask, targets, stats, edges_of, hid, pre, featb, board_b, neigh_b, comb1_b, st, dnum, dz, agg):
    rows, width = hid.shape
    edges = edges_of[0].shape[1]
    layer = n_nodes // LINE
    layer_slots = st.shape[2]
    part = width // CHUNKS
    n_rows = 4 * width
    count = len(gradient_regions(n_nodes, n_grp, width))
    dma = pltpu.SemaphoreType.DMA
    big = pl.BlockSpec(memory_space=pl.ANY)
    vmem = pl.BlockSpec(memory_space=pltpu.VMEM)
    sems = count * job_sems(n_nodes, n_grp)
    pieces = LINE * CHUNKS
    return pl.pallas_call(
        functools.partial(backward_kernel, n_nodes, n_grp),
        out_shape=[
            jax.ShapeDtypeStruct((rows, width), F32),
            jax.ShapeDtypeStruct((n_rows, width), BF16),
            jax.ShapeDtypeStruct((8, width), F32),
        ],
        in_specs=[vmem, vmem, vmem] + [big] * 13,
        out_specs=[big, big, vmem],
        scratch_shapes=[
            pltpu.VMEM((rows, width), BF16),
            pltpu.VMEM((rows, width), F32),
            pltpu.VMEM((rows, width), BF16),
            pltpu.VMEM((width, width), BF16),
            pltpu.VMEM((width, width), BF16),
            pltpu.VMEM((width, width), BF16),
            pltpu.VMEM((LINE, rows, layer_slots), BF16),
            pltpu.VMEM((rows, width), BF16),
            pltpu.VMEM((rows, width), BF16),
            pltpu.VMEM((rows, width), BF16),
            pltpu.VMEM((LINE, layer_slots, rows), BF16),
            pltpu.VMEM((LINE, layer_slots, rows), BF16),
            pltpu.VMEM((LINE, 1, layer_slots), jnp.int32),
            pltpu.VMEM((1, edges), jnp.int32),
            pltpu.VMEM((1, edges), jnp.int32),
            pltpu.VMEM((1, edges), jnp.int32),
            pltpu.VMEM((rows, layer_slots), F32),
            pltpu.VMEM((LINE, rows, layer_slots), BF16),
            pltpu.VMEM((LINE, AHEAD, rows, part), BF16),
            pltpu.VMEM((LINE, CHUNKS, layer_slots, part), BF16),
            pltpu.VMEM((LINE, CHUNKS, layer_slots, part), BF16),
            pltpu.VMEM((LINE + 1, BEHIND, rows, part), BF16),
            pltpu.VMEM((rows, part), F32),
            pltpu.VMEM((rows, width), BF16),
            pltpu.VMEM((rows, width), F32),
            pltpu.VMEM((n_rows, width), BF16),
            pltpu.VMEM((n_rows, width // 2), BF16),
            pltpu.VMEM((n_rows, width // 2), BF16),
            pltpu.VMEM((n_rows // 4, width // 2), BF16),
            pltpu.VMEM((layer, 8, width), F32),
            pltpu.VMEM((LINE, 8, width), F32),
            pltpu.VMEM((n_grp, 8, width), F32),
            pltpu.VMEM((8, width), F32),
            dma((13,)),
            dma((count + 1,)),
            dma((pieces * (layer - 1),)),
            dma((pieces * (layer - 1),)),
            dma((LINE * BEHIND,)),
            dma((LINE * BEHIND,)),
            dma(((LINE + 1) * BEHIND,)),
            dma((LINE - 1,)),
            dma((LINE - 1,)),
            dma((LINE * AHEAD,)),
            dma((LINE * AHEAD,)),
            dma((LINE * AHEAD,)),
            dma((sems,)),
            dma((sems,)),
            pltpu.SemaphoreType.REGULAR((sems,)),
            dma((share_sems(n_nodes, n_grp),)),
            dma((share_sems(n_nodes, n_grp),)),
        ],
        compiler_params=pltpu.CompilerParams(
            vmem_limit_bytes=63 * MIB, collective_id=3, has_side_effects=True
        ),
        name="backward_pass",
    )(mask, targets, stats, *edges_of, hid, pre, featb, board_b, neigh_b, comb1_b, st, dnum, dz, agg)


def unpack_kernel(
    rows,
    joined,
    small_ref,
    embed_in,
    gfeat_in,
    comb,
    neigh,
    board,
    nbias_ref,
    cbias_ref,
    penalty_ref,
    embed,
    gfeat,
    low,
    wide,
    held,
    load_sem,
    store_sem,
):
    width = joined.shape[1]
    blocks = joined.shape[0] // rows

    def load(i):
        at = pl.ds(i * rows, rows)
        return pltpu.make_async_copy(joined.at[at], low.at[at], load_sem.at[i])

    def store(i):
        first = i * rows
        if first < 2 * width:
            target = comb.at[pl.ds(first, rows)]
        elif first < 3 * width:
            target = neigh.at[pl.ds(first - 2 * width, rows)]
        else:
            target = board.at[pl.ds(first - 3 * width, rows)]
        return pltpu.make_async_copy(wide.at[pl.ds(first, rows)], target, store_sem.at[i])

    through = (embed_in, embed), (gfeat_in, gfeat)

    def load_whole(j):
        return pltpu.make_async_copy(through[j][0], held.at[j], load_sem.at[blocks + j])

    def store_whole(j):
        return pltpu.make_async_copy(held.at[j], through[j][1], store_sem.at[blocks + j])

    for i in range(blocks):
        if i % 4 == 2 and i // 4 < 2:
            load_whole(i // 4).start()
        load(i).start()
    nbias_ref[...] = small_ref[0:1, :]
    cbias_ref[...] = small_ref[1:2, :]
    penalty_ref[...] = small_ref[2:3, 0:1]
    for i in range(blocks):
        load(i).wait()

        @pl.loop(0, rows // 32)
        def _(r, i=i):
            at = pl.ds(pl.multiple_of(i * rows + r * 32, 32), 32)
            wide[at, :] = low[at, :].astype(F32)

        store(i).start()
        if i % 4 == 3 and i // 4 < 2:
            load_whole(i // 4).wait()
            store_whole(i // 4).start()
    for i in range(blocks):
        store(i).wait()
    for j in range(2):
        store_whole(j).wait()


def unpack(joined, small, embed, gfeat):
    n_rows, width = joined.shape
    rows = math.gcd(width, 256)
    big = pl.BlockSpec(memory_space=pl.ANY)
    vmem = pl.BlockSpec(memory_space=pltpu.VMEM)
    dma = pltpu.SemaphoreType.DMA
    return pl.pallas_call(
        functools.partial(unpack_kernel, rows),
        out_shape=[
            jax.ShapeDtypeStruct((2 * width, width), F32),
            jax.ShapeDtypeStruct((width, width), F32),
            jax.ShapeDtypeStruct((width, width), F32),
            jax.ShapeDtypeStruct((1, width), F32),
            jax.ShapeDtypeStruct((1, width), F32),
            jax.ShapeDtypeStruct((1, 1), F32),
            jax.ShapeDtypeStruct(embed.shape, F32),
            jax.ShapeDtypeStruct(gfeat.shape, F32),
        ],
        in_specs=[big, vmem, big, big],
        out_specs=[big] * 3 + [vmem] * 3 + [big] * 2,
        scratch_shapes=[
            pltpu.VMEM((n_rows, width), BF16),
            pltpu.VMEM((n_rows, width), F32),
            pltpu.VMEM((2, *embed.shape), F32),
            dma((n_rows // rows + 2,)),
            dma((n_rows // rows + 2,)),
        ],
        compiler_params=pltpu.CompilerParams(vmem_limit_bytes=60 * MIB),
        name="unpack",
    )(joined, small, embed, gfeat)


def on_device(
    n_nodes,
    n_grp,
    features,
    type_mask,
    edge_child,
    edge_slot,
    edge_weight,
    recv_rows,
    board_proj,
    neigh_proj,
    neigh_bias,
    combine_proj,
    combine_bias,
    out_cot,
):
    feats = features[0]
    rows, width = feats.shape
    peers = recv_rows.shape[2]
    cap = recv_rows.shape[3]
    slots = peers * cap
    targets = recv_rows[0, 0].reshape(1, slots)
    embed, hidden, pre, featb, pbl, qwl, cwl1, spread_t, dnum, dzb, aggb, stats = forward_pass(
        n_nodes,
        n_grp,
        feats,
        type_mask,
        (edge_slot, edge_child, edge_weight),
        targets,
        board_proj,
        neigh_proj,
        neigh_bias.reshape(1, width),
        combine_proj,
        combine_bias.reshape(1, width),
        out_cot[0],
    )
    grad_feats, summed, small = backward_pass(
        n_nodes,
        n_grp,
        type_mask,
        targets,
        stats,
        (edge_slot, edge_child, edge_weight),
        hidden,
        pre,
        featb,
        pbl,
        qwl,
        cwl1,
        spread_t,
        dnum,
        dzb,
        aggb,
    )
    grad_comb, grad_neigh, grad_board, grad_nbias, grad_cbias, penalty, embed, grad_feats = unpack(
        summed, small, embed, grad_feats
    )
    return (
        embed[None],
        penalty[0, 0],
        grad_feats[None],
        grad_board,
        grad_neigh,
        grad_nbias[0],
        grad_comb,
        grad_cbias[0],
    )


def solution(mesh):
    in_specs = (
        P("grp", "nodes", None),
        P("grp", "nodes"),
        P("grp", "nodes"),
        P("grp", "nodes"),
        P("grp", "nodes"),
        P("grp", "nodes", None, None),
        P(),
        P(),
        P(),
        P(),
        P(),
        P("grp", "nodes", None),
    )
    out_specs = (P("grp", "nodes", None), P(), P("grp", "nodes", None), P(), P(), P(), P(), P())
    return jax.shard_map(
        functools.partial(on_device, mesh.shape["nodes"], mesh.shape["grp"]),
        mesh=mesh,
        in_specs=in_specs,
        out_specs=out_specs,
        check_vma=False,
    )
```

```python
import functools
import math

import jax
import jax.numpy as jnp
from jax import lax
from jax.experimental import pallas as pl
from jax.experimental.pallas import tpu as pltpu
from jax.sharding import PartitionSpec as P

HIGH = lax.Precision.HIGHEST
MESH = pl.DeviceIdType.MESH
BF16 = jnp.bfloat16
F32 = jnp.float32
F8 = jnp.float8_e4m3fn
MIB = 2**20


def gelu_tanh(v):
    return jax.nn.gelu(v, approximate=True)


def dot_nt(left, right):
    return lax.dot_general(
        left, right, (((1,), (1,)), ((), ())), preferred_element_type=F32
    )


def dot_tn(left, right):
    return lax.dot_general(
        left, right, (((0,), (0,)), ((), ())), preferred_element_type=F32
    )


LINE = 4
CHUNKS = 4
FAR = 2
FORWARD_ACTS = "mYZfpiGDXRdaPugvxw"
FORWARD = (
    10, 11, 12, 13, 1100, 1101, 1102, 1103, 2010, 1140, 4102, 1141, 6010, 4100, 1142, 1143, 2014, 1110, 4101,
    3100, 13012, 13013, 1111, 1112, 3101, 1113, 3102, 2011, 4112, 14010, 1120, 4103, 4110, 1121, 1122, 3103,
    7010, 12011, 4113, 4111, 3110, 15012, 1123, 2012, 4120, 1130, 1131, 3111, 4121, 1132, 3112, 4122, 15013,
    1133, 7011, 2013, 16012, 3120, 3121, 4132, 4131, 5113, 4130, 3113, 5120, 5100, 12012, 10010, 16013, 8010,
    5101, 5132, 9010, 4133, 4123, 5131, 5122, 7012, 5111, 5112, 5102, 7013, 5121, 5110, 5130, 11011, 5103,
    17012, 11010, 11012, 5133, 17013, 5123, 12013,
)
ORDER = ((0, 1, 2, 3), (1, 2, 0, 3))


class Place:
    def __init__(self, n_nodes, n_grp):
        layer = n_nodes // LINE
        node = lax.axis_index("nodes")
        grp = lax.axis_index("grp")
        self.node, self.grp = node, grp
        self.size = {"l": layer, "c": 2, "y": layer // 2, "z": LINE, "x": n_grp}
        low = lax.rem(node, layer)
        self.at = {"l": low, "c": lax.rem(low, 2), "y": low // 2, "z": node // layer, "x": grp}

    def member(self, axis, index):
        layer = self.size["l"]
        low, line, grp = self.at["l"], self.at["z"], self.at["x"]
        if axis == "l":
            low = index
        elif axis == "c":
            low = self.at["y"] * 2 + index
        elif axis == "y":
            low = index * 2 + self.at["c"]
        elif axis == "z":
            line = index
        else:
            grp = index
        return {"nodes": line * layer + low, "grp": grp}

    def others(self, axis):
        size = self.size[axis]
        for far in range(1, size):
            index = lax.rem(self.at[axis] + far, size)
            yield far - 1, index, self.member(axis, index)


def remote(src, dst, send, recv, device):
    return pltpu.make_async_remote_copy(
        src_ref=src, dst_ref=dst, send_sem=send, recv_sem=recv, device_id=device, device_id_type=MESH
    )


def barrier(place, axes, meanwhile=None):
    sem = pltpu.get_barrier_semaphore()
    count = 0
    for axis in axes:
        for _, _, device in place.others(axis):
            pl.semaphore_signal(sem, inc=1, device_id=device, device_id_type=MESH)
            count += 1
    if meanwhile is not None:
        meanwhile()
    pl.semaphore_wait(sem, count)


def column_of(row_ref):
    row = row_ref[...].astype(F32)
    return jnp.broadcast_to(row, (128, row.shape[1])).T[:, 0:1]


def gelu(v):
    t = jnp.tanh(0.7978845608028654 * (v + 0.044715 * (v * v * v)))
    return v * (0.5 * (1.0 + t))


def gelu_and_slope(v):
    square = v * v
    t = jnp.tanh(0.7978845608028654 * (v + 0.044715 * (v * square)))
    bend = 0.7978845608028654 * (1.0 + 0.134145 * square)
    share = 0.5 * (1.0 + t)
    return v * share, share + 0.5 * v * (1.0 - t * t) * bend


def gelu_slope(v):
    square = v * v
    t = jnp.tanh(0.7978845608028654 * (v + 0.044715 * (v * square)))
    bend = 0.7978845608028654 * (1.0 + 0.134145 * square)
    return 0.5 * (1.0 + t) + 0.5 * v * (1.0 - t * t) * bend


class Share:
    def __init__(self, place, bufs, send, recv):
        self.place, self.send, self.recv = place, send, recv
        self.stages, base = [], 0
        for axis, buf in zip(("l", "z", "x"), bufs):
            self.stages.append((axis, buf, base))
            base += place.size[axis] - 1

    def start(self, stage, value):
        axis, buf, base = self.stages[stage]
        me = self.place.at[axis]
        buf[me] = value
        for far, _, device in self.place.others(axis):
            remote(
                buf.at[me], buf.at[me], self.send.at[base + far], self.recv.at[base + far], device
            ).start()

    def finish(self, stage):
        axis, buf, base = self.stages[stage]
        me = self.place.at[axis]
        for far, _, device in self.place.others(axis):
            remote(
                buf.at[me], buf.at[me], self.send.at[base + far], self.recv.at[base + far], device
            ).wait()
        total = buf[0]
        for i in range(1, self.place.size[axis]):
            total += buf[i]
        return total


def run_ticks(t, ticks):
    for at, acts in enumerate(ticks):
        if acts:

            @pl.when(t == at)
            def _(acts=acts):
                for act in acts:
                    act()


def run_order(order, letters, steps, build, act):
    ticks = None
    names = [letters[number // 1000] + str(number % 1000)[1:] for number in order]
    for name in names:
        if name[0] == "Y":
            if ticks is None:
                ticks = [[] for _ in range(steps)]
                marks = sum(other[:2] == name[:2] for other in names)
            now = (int(name[2]) + 1) * steps // marks - 1
        elif name[0] == "Z":
            build(int(name[1]), ticks)
            ticks = None
        elif ticks is not None:
            ticks[max(now, 0)].append(functools.partial(act, name))
        else:
            act(name)


def share_sems(n_nodes, n_grp):
    return (n_nodes // LINE - 1) + (LINE - 1) + max(1, n_grp - 1)


def forward_kernel(
    n_nodes,
    n_grp,
    feats_h,
    mask_ref,
    place_ref,
    child_ref,
    weight_ref,
    targets_ref,
    board_h,
    neigh_h,
    nbias_ref,
    comb_h,
    cbias_ref,
    cot_h,
    embed_h,
    hid_h,
    pre_h,
    featb_h,
    board_b_h,
    neigh_b_h,
    comb1_b_h,
    st_h,
    dnum_h,
    dz_h,
    agg_h,
    stats_ref,
    stage,
    featb,
    hid,
    pre,
    board_b,
    neigh_b,
    comb_b,
    keys,
    msg,
    acc,
    spread,
    spread_t,
    out_slots,
    in_slots,
    out_tot,
    in_tot,
    picker,
    num,
    zval,
    zpre,
    cot,
    agg,
    dz,
    dnum,
    lines,
    far_spread,
    far_picker,
    far_out,
    far_in,
    far_sum,
    end_sum,
    den_ref,
    scale_ref,
    count_l,
    count_z,
    count_x,
    load_sem,
    store_sem,
    key_send,
    key_recv,
    up_send,
    down_send,
    msg_recv,
    slot_send,
    slot_recv,
    tot_send,
    tot_recv,
    count_send,
    count_recv,
    line_send,
    line_recv,
    far_send,
    far_recv,
    sum_send,
    sum_recv,
    end_recv,
):
    place = Place(n_nodes, n_grp)
    z, low = place.at["z"], place.at["l"]
    layer = place.size["l"]
    rows, width = featb.shape
    edges = place_ref.shape[1]
    half = edges // 2
    layer_slots = spread.shape[1]
    cap = layer_slots // layer
    part = width // CHUNKS
    turn = math.gcd(half, 6400)
    steps = edges // turn

    sources = [feats_h.at[:]]
    for whole in (board_h, neigh_h, comb_h):
        for first in range(0, whole.shape[0], rows):
            sources.append(whole.at[pl.ds(first, rows)])
    n_stage = stage.shape[0]

    def load(i):
        return pltpu.make_async_copy(sources[i], stage.at[i % n_stage], load_sem.at[i % n_stage])

    for i in range(n_stage):
        load(i).start()
    load_cot = pltpu.make_async_copy(cot_h, cot, load_sem.at[n_stage])
    stores = []

    def store(src, dst):
        copy = pltpu.make_async_copy(src, dst, store_sem.at[len(stores)])
        copy.start()
        stores.append(copy)

    barrier(place, ("l", "z", "x"))
    keys[z, :, pl.ds(0, edges)] = place_ref[...] * 65536 + child_ref[...]
    keys[z, :, pl.ds(edges, half)] = (
        weight_ref[:, pl.ds(half, half)] * 65536 + weight_ref[:, pl.ds(0, half)]
    )

    def key_copy(far, device):
        return remote(keys.at[z], keys.at[z], key_send.at[far], key_recv.at[far], device)

    for far, _, device in place.others("z"):
        key_copy(far, device).start()
    inner = jnp.logical_and(z > 0, z < LINE - 1)
    outer = jnp.logical_or(z == 0, z == LINE - 1)
    half_at = z // 2
    far_end = (LINE - 1) * (1 - half_at)

    def line_copy(far, index, device):
        at = pl.ds(pl.multiple_of(index * layer_slots, layer_slots), layer_slots)
        return remote(
            targets_ref.at[:, at], lines.at[z], line_send.at[far], line_recv.at[far], device
        )

    @pl.when(outer)
    def _():
        for far, index, device in place.others("z"):
            line_copy(far, index, device).start()

    share = Share(place, (count_l, count_z, count_x), count_send, count_recv)
    mask = column_of(mask_ref)
    share.start(0, jnp.full((8, 128), jnp.sum(mask)))

    def cast(i, target, first):
        load(i).wait()
        slot = stage.at[i % n_stage]

        @pl.loop(0, rows // 32)
        def _(r):
            at = pl.ds(pl.multiple_of(r * 32, 32), 32)
            to = pl.ds(pl.multiple_of(first + r * 32, 32), 32)
            target[to, :] = slot[at, :].astype(BF16)

    cast(0, featb, 0)
    cast(1, board_b, 0)
    cast(2, board_b, rows)

    @pl.loop(0, CHUNKS)
    def _(k):
        at = pl.ds(pl.multiple_of(k * part, part), part)
        proj = jnp.dot(featb[...], board_b[:, at], preferred_element_type=F32)
        hid[:, at] = jnp.where(mask > 0.5, proj, stage[0, :, at]).astype(BF16)

    cast(3, neigh_b, 0)
    cast(4, neigh_b, rows)
    for i in range(n_stage, len(sources)):
        load(i).start()
    load_cot.start()

    def up_copy(src, k):
        piece = msg.at[src, k]
        index = src * CHUNKS + k
        return remote(
            piece, piece, up_send.at[index], msg_recv.at[index], place.member("z", z + 1)
        )

    def down_copy(src, k):
        piece = msg.at[src, k]
        index = src * CHUNKS + k
        return remote(
            piece, piece, down_send.at[index], msg_recv.at[index], place.member("z", z - 1)
        )

    def message(k):
        at = pl.ds(k * part, part)
        value = jnp.dot(hid[...], neigh_b[:, at], preferred_element_type=F32) + nbias_ref[:, at]
        pre[:, at] = value
        msg[z, k] = gelu(value).astype(BF16)

        @pl.when(z < LINE - 1)
        def _():
            up_copy(z, k).start()

        @pl.when(z > 0)
        def _():
            down_copy(z, k).start()

    def passes_up(k):
        return z < LINE - (1 if k < FAR else 2)

    def passes_down(k):
        return z > (0 if k < FAR else 1)

    def forward(j, k):
        below = z - 1 - j
        above = z + 1 + j

        comes = True if k < FAR or j == 0 else inner

        @pl.when(jnp.logical_and(below >= 0, comes))
        def _():
            up_copy(below, k).wait_recv()

            @pl.when(passes_up(k))
            def _():
                up_copy(below, k).start()

        @pl.when(jnp.logical_and(above < LINE, comes))
        def _():
            down_copy(above, k).wait_recv()

            @pl.when(passes_down(k))
            def _():
                down_copy(above, k).start()

    def tot_copy(src, far, index, device):
        at = (layer - 1) * src + far
        return remote(
            out_tot.at[src, pl.ds(pl.multiple_of(index * cap, cap), cap)],
            in_tot.at[src, pl.ds(pl.multiple_of(low * cap, cap), cap)],
            tot_send.at[at],
            tot_recv.at[at],
            device,
        )

    def finish_spread(src):
        total = acc[...]
        spread[src] = total.astype(BF16)
        spread_t[src] = total.astype(BF16).T
        sums = jnp.sum(total, axis=1, keepdims=True).astype(jnp.int32)
        lane = lax.broadcasted_iota(jnp.int32, (layer_slots, 128), 1)
        digit = jnp.where(
            lane == 0, sums & 255, jnp.where(lane == 1, (sums >> 8) & 255, jnp.where(lane == 2, sums >> 16, 0))
        )
        out_tot[src] = digit.astype(F32).astype(BF16)
        own = pl.ds(pl.multiple_of(low * cap, cap), cap)
        in_tot[src, own] = out_tot[src, own]
        for far, index, device in place.others("l"):
            tot_copy(src, far, index, device).start()

    def source(which):
        flip = z // 2
        depth = z * (1 - 2 * flip) + (LINE - 1) * flip
        index = ORDER[0][which] * (1 - depth) + ORDER[1][which] * depth
        return index * (1 - 2 * flip) + (LINE - 1) * flip

    def build(which, ticks):
        src, target = (source(which), z) if which < LINE else (z, far_end)
        acc[...] = jnp.zeros_like(acc)
        if 0 < which < LINE:
            far = lax.rem(z - src - 1 + LINE, LINE)
            remote(
                keys.at[src], keys.at[src], key_send.at[0], key_recv.at[far], place.member("z", src)
            ).wait_recv()

        @pl.loop(0, steps)
        def _(t):
            second = t // (steps // 2)
            key = keys[src, :, pl.ds(pl.multiple_of(t * turn, turn), turn)]
            start = edges + (t - second * (steps // 2)) * turn
            pair = keys[src, :, pl.ds(pl.multiple_of(start, turn), turn)]
            weight = (lax.shift_right_logical(pair, second * 16) & 65535).astype(F32).astype(F8)
            child = (key & 65535).astype(jnp.int16)
            slot = (lax.shift_right_logical(key, 16) - target * layer_slots).astype(jnp.int16)
            right = jnp.where(
                lax.broadcasted_iota(jnp.int16, (rows, turn), 0) == child, weight, jnp.zeros((), F8)
            )
            block = 256
            for first in range(0, layer_slots, block):
                ids = lax.broadcasted_iota(jnp.int16, (block, turn), 0) + jnp.asarray(
                    first, jnp.int16
                )
                left = jnp.where(ids == slot, jnp.ones((), F8), jnp.zeros((), F8))
                acc[pl.ds(first, block), :] += dot_nt(left, right)
            run_ticks(t, ticks)

        if which < LINE:
            finish_spread(src)
        else:
            far_spread[...] = acc[...].astype(BF16)

    def slot_copy(src, k, far, index, device):
        at = (src * CHUNKS + k) * (layer - 1) + far
        return remote(
            out_slots.at[src, k, pl.ds(pl.multiple_of(index * cap, cap), cap)],
            in_slots.at[src, k, pl.ds(pl.multiple_of(low * cap, cap), cap)],
            slot_send.at[at],
            slot_recv.at[at],
            device,
        )

    def piece(src, k):
        out_slots[src, k] = jnp.dot(spread[src], msg[src, k], preferred_element_type=F32).astype(BF16)
        for far, index, device in place.others("l"):
            slot_copy(src, k, far, index, device).start()
        own = pl.ds(pl.multiple_of(low * cap, cap), cap)
        in_slots[src, k, own] = out_slots[src, k, own]

    def pick(src, k):
        for far, index, device in place.others("l"):
            slot_copy(src, k, far, index, device).wait_recv()
        num[k] += jnp.dot(picker[src], in_slots[src, k], preferred_element_type=F32)

    def unless_far(which, k, act):
        if which < 2 or k < FAR:
            act(source(which), k)
        else:

            @pl.when(inner)
            def _():
                act(source(which), k)

    def far_copy(k, far, index, device):
        at = k * (layer - 1) + far
        return remote(
            far_out.at[k, pl.ds(pl.multiple_of(index * cap, cap), cap)],
            far_in.at[k, pl.ds(pl.multiple_of(low * cap, cap), cap)],
            far_send.at[at],
            far_recv.at[at],
            device,
        )

    onward = 1 - 2 * half_at

    def sum_copy(i):
        return remote(
            far_sum.at[i], far_sum.at[i], sum_send.at[i], sum_recv.at[i], place.member("z", z + onward)
        )

    def end_copy(i):
        return remote(
            far_sum.at[i],
            end_sum.at[i],
            sum_send.at[i],
            end_recv.at[i],
            place.member("z", z + 2 * onward),
        )

    def far_slots(k):
        i = k - FAR
        far_out[i] = jnp.dot(far_spread[...], msg[z, k], preferred_element_type=F32).astype(BF16)
        for far, index, device in place.others("l"):
            far_copy(i, far, index, device).start()
        own = pl.ds(pl.multiple_of(low * cap, cap), cap)
        far_in[i, own] = far_out[i, own]

    def make_far_picker():
        far = lax.rem(z - far_end - 1 + LINE, LINE)
        remote(
            lines.at[far_end],
            lines.at[far_end],
            line_send.at[0],
            line_recv.at[far],
            place.member("z", far_end),
        ).wait_recv()
        ids = lax.broadcasted_iota(jnp.int32, (rows, layer_slots), 0)
        far_picker[...] = jnp.where(ids == lines[far_end], 1.0, 0.0).astype(BF16)

        @pl.when(inner)
        def _():
            near = (LINE - 1) - far_end
            back = lax.rem(z - near - 1 + LINE, LINE)
            remote(
                lines.at[near],
                lines.at[near],
                line_send.at[0],
                line_recv.at[back],
                place.member("z", near),
            ).wait_recv()

    def far_parents(i):
        for far, index, device in place.others("l"):
            far_copy(i, far, index, device).wait_recv()
        return jnp.dot(far_picker[...], far_in[i], preferred_element_type=F32)

    def first_sum(k):
        @pl.when(outer)
        def _():
            far_sum[k - FAR] = far_parents(k - FAR).astype(BF16)
            sum_copy(k - FAR).start()

    def second_sum(k):
        @pl.when(inner)
        def _():
            i = k - FAR
            value = far_parents(i)
            sum_copy(i).wait_recv()
            far_sum[i] = (far_sum[i].astype(F32) + value).astype(BF16)
            end_copy(i).start()

    def add_far(k):
        @pl.when(outer)
        def _():
            end_copy(k - FAR).wait_recv()
            num[k] += end_sum[k - FAR].astype(F32)

    def make_picker():
        @pl.loop(0, LINE)
        def _(src):
            at = pl.ds(pl.multiple_of(src * layer_slots, layer_slots), layer_slots)
            ids = lax.broadcasted_iota(jnp.int32, (rows, layer_slots), 0)
            picker[src] = jnp.where(ids == targets_ref[:, at], 1.0, 0.0).astype(BF16)

        num[...] = jnp.zeros_like(num)

    def comb_piece(i):
        for j in range(i, 2 * width // rows, CHUNKS):
            cast(5 + j, comb_b, j * rows)

    def self_part():
        @pl.loop(0, CHUNKS)
        def _(k):
            at = pl.ds(pl.multiple_of(k * part, part), part)
            zpre[:, at] = (
                jnp.dot(hid[...], comb_b[0:width, at], preferred_element_type=F32)
                + cbias_ref[:, at]
            )

    def results():
        store(hid, hid_h)
        store(pre, pre_h)
        store(featb, featb_h)
        store(board_b, board_b_h)
        store(neigh_b, neigh_b_h)
        store(comb_b.at[pl.ds(0, width)], comb1_b_h)
        store(spread_t, st_h)

    def totals():
        digits = jnp.zeros((rows, 128), F32)
        for src in range(LINE):
            for far, index, device in place.others("l"):
                tot_copy(src, far, index, device).wait_recv()
            digits += jnp.dot(picker[src], in_tot[src], preferred_element_type=F32)
        lane = lax.broadcasted_iota(jnp.int32, (rows, 128), 1)
        worth = jnp.where(
            lane == 0, 1.0, jnp.where(lane == 1, 256.0, jnp.where(lane == 2, 65536.0, 0.0))
        )
        den_ref[...] = jnp.broadcast_to(
            1.0 + jnp.sum(digits * worth, axis=1, keepdims=True), (rows, 128)
        )

    def neighbours(k):
        at = pl.ds(k * part, part)
        agg[:, at] = (num[k] / den_ref[:, 0:1]).astype(BF16)
        if k < CHUNKS - 1:

            @pl.loop(0, CHUNKS)
            def _(n):
                to = pl.ds(pl.multiple_of(n * part, part), part)
                zpre[:, to] += jnp.dot(
                    agg[:, at], comb_b[pl.ds(width + k * part, part), to], preferred_element_type=F32
                )

    def step_share(stage):
        if stage in (1, 2):
            share.start(stage, share.finish(stage - 1))
        elif stage == 3:
            boards = share.finish(2)
            scale_ref[...] = 1.0 / (width * (1.0 + boards))

    acts = {
        "P": step_share,
        "m": message,
        "f": forward,
        "p": lambda which, k: unless_far(which, k, piece),
        "i": lambda which, k: unless_far(which, k, pick),
        "u": far_slots,
        "g": lambda _: make_far_picker(),
        "v": first_sum,
        "x": second_sum,
        "w": add_far,
        "G": lambda _: make_picker(),
        "D": comb_piece,
        "X": lambda _: self_part(),
        "R": lambda _: results(),
        "d": lambda _: totals(),
        "a": neighbours,
    }

    def act(step):
        acts[step[0]](*(int(c) for c in step[1:]))

    run_order(FORWARD, FORWARD_ACTS, steps, build, act)
    neighbours(CHUNKS - 1)
    store(agg, agg_h)
    load_cot.wait()
    den = den_ref[:, 0:1]
    scale = scale_ref[0:1, 0:1]
    last = pl.ds(width - part, part)

    def dense(k, carry):
        square, along = carry
        at = pl.ds(pl.multiple_of(k * part, part), part)
        value = zpre[:, at] + jnp.dot(
            agg[:, last], comb_b[pl.ds(2 * width - part, part), at], preferred_element_type=F32
        )
        out, slope = gelu_and_slope(value)
        zpre[:, at] = slope
        zval[:, at] = out
        square += jnp.sum(out * out, axis=1, keepdims=True)
        along += jnp.sum(out * cot[:, at], axis=1, keepdims=True)
        return square, along

    zero = jnp.zeros((rows, 1), F32)
    square, along = lax.fori_loop(0, CHUNKS, dense, (zero, zero))
    inverse = lax.rsqrt(square + 1e-06)
    along = along * inverse
    push = jnp.where(mask > 0.5, 2.0 * scale, 0.0)
    stats_ref[...] = jnp.concatenate(
        [
            jnp.full((8, 128), jnp.sum(jnp.where(mask > 0.5, square, 0.0))),
            jnp.broadcast_to(scale, (8, 128)),
        ],
        axis=0,
    )

    @pl.loop(0, CHUNKS)
    def _(k):
        at = pl.ds(pl.multiple_of(k * part, part), part)
        out = zval[:, at]
        emb = out * inverse
        grad = inverse * (cot[:, at] - emb * along) + push * out
        dz[:, at] = (grad * zpre[:, at]).astype(BF16)
        zval[:, at] = emb

    store(dz, dz_h)
    store(zval, embed_h)

    @pl.loop(0, CHUNKS)
    def _(k):
        at = pl.ds(pl.multiple_of(k * part, part), part)
        back = dot_nt(dz[...], comb_b[pl.ds(pl.multiple_of(width + k * part, part), part), :])
        dnum[:, at] = (back / den).astype(BF16)

    store(dnum, dnum_h)

    for far, _, device in place.others("z"):
        key_copy(far, device).wait_send()

    @pl.loop(0, LINE * CHUNKS)
    def _(i):
        src = i // CHUNKS
        k = lax.rem(i, CHUNKS)

        early = k < FAR

        @pl.when(
            jnp.logical_or(
                jnp.logical_and(src == z, z < LINE - 1),
                jnp.logical_and(
                    src < z, jnp.logical_or(jnp.logical_and(early, z < LINE - 1), z < LINE - 2)
                ),
            )
        )
        def _():
            up_copy(src, k).wait_send()

        @pl.when(
            jnp.logical_or(
                jnp.logical_and(src == z, z > 0),
                jnp.logical_and(src > z, jnp.logical_or(jnp.logical_and(early, z > 0), z > 1)),
            )
        )
        def _():
            down_copy(src, k).wait_send()

        near = jnp.logical_and(src - z < 2, z - src < 2)

        @pl.when(jnp.logical_or(jnp.logical_or(early, inner), near))
        def _():
            for far, index, device in place.others("l"):
                slot_copy(src, k, far, index, device).wait_send()

    for i in range(CHUNKS - FAR):
        sum_copy(i).wait_send()
        for far, index, device in place.others("l"):
            far_copy(i, far, index, device).wait_send()

    @pl.when(outer)
    def _():
        for far, index, device in place.others("z"):
            line_copy(far, index, device).wait_send()

    for src in range(LINE):
        for far, index, device in place.others("l"):
            tot_copy(src, far, index, device).wait_send()
    for copy in stores:
        copy.wait()


def forward_pass(n_nodes, n_grp, feats, mask, edges_of, targets, board, neigh, nbias, comb, cbias, cot):
    rows, width = feats.shape
    edges = edges_of[0].shape[1]
    layer = n_nodes // LINE
    layer_slots = targets.shape[1] // LINE
    part = width // CHUNKS
    dma = pltpu.SemaphoreType.DMA
    n_stage = 5
    big = pl.BlockSpec(memory_space=pl.ANY)
    small = pl.BlockSpec(memory_space=pltpu.VMEM)

    def hbm(shape, dtype):
        return jax.ShapeDtypeStruct(shape, dtype)

    return pl.pallas_call(
        functools.partial(forward_kernel, n_nodes, n_grp),
        out_shape=[
            hbm((rows, width), F32),
            hbm((rows, width), BF16),
            hbm((rows, width), F32),
            hbm((rows, width), BF16),
            hbm((width, width), BF16),
            hbm((width, width), BF16),
            hbm((width, width), BF16),
            hbm((LINE, rows, layer_slots), BF16),
            hbm((rows, width), BF16),
            hbm((rows, width), BF16),
            hbm((rows, width), BF16),
            hbm((16, 128), F32),
        ],
        in_specs=[big] + [small] * 5 + [big, big, small, big, small, big],
        out_specs=[big] * 11 + [small],
        scratch_shapes=[
            pltpu.VMEM((n_stage, rows, width), F32),
            pltpu.VMEM((rows, width), BF16),
            pltpu.VMEM((rows, width), BF16),
            pltpu.VMEM((rows, width), F32),
            pltpu.VMEM((width, width), BF16),
            pltpu.VMEM((width, width), BF16),
            pltpu.VMEM((2 * width, width), BF16),
            pltpu.VMEM((LINE, 1, edges + edges // 2), jnp.int32),
            pltpu.VMEM((LINE, CHUNKS, rows, part), BF16),
            pltpu.VMEM((layer_slots, rows), F32),
            pltpu.VMEM((LINE, layer_slots, rows), BF16),
            pltpu.VMEM((LINE, rows, layer_slots), BF16),
            pltpu.VMEM((LINE, CHUNKS, layer_slots, part), BF16),
            pltpu.VMEM((LINE, CHUNKS, layer_slots, part), BF16),
            pltpu.VMEM((LINE, layer_slots, 128), BF16),
            pltpu.VMEM((LINE, layer_slots, 128), BF16),
            pltpu.VMEM((LINE, rows, layer_slots), BF16),
            pltpu.VMEM((CHUNKS, rows, part), F32),
            pltpu.VMEM((rows, width), F32),
            pltpu.VMEM((rows, width), F32),
            pltpu.VMEM((rows, width), F32),
            pltpu.VMEM((rows, width), BF16),
            pltpu.VMEM((rows, width), BF16),
            pltpu.VMEM((rows, width), BF16),
            pltpu.VMEM((LINE, 1, layer_slots), jnp.int32),
            pltpu.VMEM((layer_slots, rows), BF16),
            pltpu.VMEM((rows, layer_slots), BF16),
            pltpu.VMEM((CHUNKS - FAR, layer_slots, part), BF16),
            pltpu.VMEM((CHUNKS - FAR, layer_slots, part), BF16),
            pltpu.VMEM((CHUNKS - FAR, rows, part), BF16),
            pltpu.VMEM((CHUNKS - FAR, rows, part), BF16),
            pltpu.VMEM((rows, 128), F32),
            pltpu.VMEM((8, 128), F32),
            pltpu.VMEM((layer, 8, 128), F32),
            pltpu.VMEM((LINE, 8, 128), F32),
            pltpu.VMEM((n_grp, 8, 128), F32),
            dma((n_stage + 1,)),
            dma((11,)),
            dma((LINE - 1,)),
            dma((LINE - 1,)),
            dma((LINE * CHUNKS,)),
            dma((LINE * CHUNKS,)),
            dma((LINE * CHUNKS,)),
            dma((LINE * CHUNKS * (layer - 1),)),
            dma((LINE * CHUNKS * (layer - 1),)),
            dma((LINE * (layer - 1),)),
            dma((LINE * (layer - 1),)),
            dma((share_sems(n_nodes, n_grp),)),
            dma((share_sems(n_nodes, n_grp),)),
            dma((LINE - 1,)),
            dma((LINE - 1,)),
            dma(((CHUNKS - FAR) * (layer - 1),)),
            dma(((CHUNKS - FAR) * (layer - 1),)),
            dma((CHUNKS - FAR,)),
            dma((CHUNKS - FAR,)),
            dma((CHUNKS - FAR,)),
        ],
        compiler_params=pltpu.CompilerParams(
            vmem_limit_bytes=63 * MIB, collective_id=2, has_side_effects=True
        ),
        name="forward_pass",
    )(feats, mask, *edges_of, targets, board, neigh, nbias, comb, cbias, cot)


def add_into(target, first, count, columns, parts, step=16):
    @pl.loop(0, count // step)
    def _(i):
        at = pl.ds(pl.multiple_of(first + i * step, step), step)
        total = target[at, columns].astype(F32)
        for part in parts:
            total += part[pl.ds(pl.multiple_of(i * step, step), step), :].astype(F32)
        target[at, columns] = total.astype(target.dtype)


def reduce_job(place, order, grad, region, arrive, land, last, send, recv, free, base):
    first, rows, left, columns = region
    half = columns // 2
    core = place.at["c"]
    mine = pl.ds(pl.multiple_of(left + core * half, half), half)
    theirs = pl.ds(pl.multiple_of(left + (1 - core) * half, half), half)
    mate = place.member("c", 1 - core)
    block = pl.ds(first, rows)
    sems = iter(range(base, base + send.shape[0]))

    def lay(src, dst, device):
        sem = next(sems)
        return remote(src, dst, send.at[sem], recv.at[sem], device)

    across = lay(grad.at[block, theirs], arrive, mate)
    down = []
    begin, length, used = first, rows, 0
    for axis in order:
        length //= place.size[axis]
        copies, parts, devices = [], [], []
        for far, index, device in place.others(axis):
            start = pl.multiple_of(begin + index * length, 16)
            slot = land.at[pl.ds(used, length)]
            used += length
            copies.append(lay(grad.at[pl.ds(start, length), mine], slot, device))
            parts.append(slot)
            devices.append(device)
        parent = begin
        begin = pl.multiple_of(begin + place.at[axis] * length, 16)
        down.append((axis, parent, begin, length, copies, parts, devices))
    axis, parent, begin, length, _, _, devices = down[-1]
    here = pl.ds(pl.multiple_of(place.at[axis] * length, 16), length)
    whole = pl.ds(pl.multiple_of(parent, 16), length * place.size[axis])
    end = [lay(last.at[here], last.at[here], device) for device in devices]
    up = []
    for stage in range(len(down) - 1, 0, -1):
        axis, _, start, piece, _, _, devices = down[stage - 1]
        own = grad.at[pl.ds(start, piece), mine]
        up.append((stage, len(devices), [lay(own, own, device) for device in devices]))
    own = grad.at[block, mine]
    back = lay(own, own, mate)
    yield

    def release(at, devices):
        for device in devices:
            pl.semaphore_signal(free.at[base + at], inc=1, device_id=device, device_id_type=MESH)

    across.start()
    yield
    across.wait()
    release(0, [mate])
    add_into(grad, first, rows, mine, [arrive])
    for stage, (_, _, begin, length, copies, parts, devices) in enumerate(down):
        for copy in copies:
            copy.start()
        yield
        for copy in copies:
            copy.wait()
        if stage < len(down) - 1:
            release(stage + 1, devices)
        add_into(grad, begin, length, mine, parts)
    last[here] = grad[pl.ds(begin, length), mine]
    for copy in end:
        copy.start()
    yield
    for copy in end:
        copy.wait()
    grad[whole, mine] = last[pl.ds(0, whole.size)]
    for stage, count, copies in up:
        pl.semaphore_wait(free.at[base + stage], count)
        for copy in copies:
            copy.start()
        yield
        for copy in copies:
            copy.wait()
    pl.semaphore_wait(free.at[base], 1)
    back.start()
    yield
    back.wait()


def job_sems(n_nodes, n_grp):
    return 2 * (1 + (n_nodes // LINE // 2 - 1) + (LINE - 1) + (n_grp - 1))


AHEAD = 2
BEHIND = CHUNKS - AHEAD
BACKWARD_ACTS = "lLAfqYZBW321OGSEHFPcnb"
BACKWARD = (
    10, 2011, 7012, 2010, 13010, 19010, 19011, 1012, 8010, 5110, 19013, 7013, 3101, 19012, 19010, 9012,
    19013, 19011, 5111, 3100, 4101, 5112, 1011, 9013, 1013, 19012, 10012, 5113, 3111, 5114, 11012, 6011,
    4111, 5120, 3110, 19010, 4100, 5121, 10013, 19011, 4110, 19012, 5122, 4120, 4121, 11013, 5123, 5124,
    19010, 14010, 6012, 12012, 19013, 3121, 19011, 3120, 20012, 12013, 20013, 19010, 5130, 20012, 4131,
    19011, 5131, 19012, 20013, 5132, 19010, 4130, 19011, 5133, 19013, 20013, 20012, 5134, 19012, 19010,
    19011, 6013, 12011, 20011, 19013, 12010, 20010, 20011, 19012, 20013, 15010, 16011, 21012, 19013, 20012,
    21013, 20010, 20013, 16010, 21011, 21012, 21013, 20011, 21010, 21011, 20010, 20013, 21010, 20011, 18010,
    21012, 19010, 17010, 21011, 20010, 20012, 19012, 21013, 20011, 21010, 21011, 19013, 21013, 20010, 21010,
    20011, 21012, 20012, 19010, 21013, 20013, 21011, 21010, 21013, 20012, 19012, 21012, 20010, 21011, 19011,
    20011, 21013, 20013, 21010, 18011, 21012, 19013, 19011, 21011, 21010, 21012, 20013, 20012, 20010, 21013,
    20011, 21010, 21011, 20010, 19012, 20012, 18012, 21012, 20010, 21011, 21012, 21010, 20011, 18013, 19013,
    21013,
)


def gradient_regions(n_nodes, n_grp, width):
    pieces = n_nodes * n_grp // 2
    x_first, y_first = ("x", "y", "z"), ("y", "x", "z")
    regions = {}
    count = max(1, min(4, 2 * width // (16 * pieces)))
    n_rows = 2 * width // count
    for j in range(count):
        regions[f"comb{j}"] = (j * n_rows, n_rows, 0, width, y_first if j % 2 else x_first)
    if width % (16 * pieces) == 0:
        part = width // CHUNKS
        for k in range(CHUNKS):
            regions[f"neigh{k}"] = (2 * width, width, k * part, part, x_first if k % 2 else y_first)
        count = max(1, min(4, width // (16 * pieces)))
        n_rows = width // count
        for j in range(count):
            order = (x_first, y_first, x_first, ("z", "y", "x"))[j]
            regions[f"board{j}"] = (3 * width + j * n_rows, n_rows, 0, width, order)
    else:
        regions["board0"] = (2 * width, 2 * width, 0, width, x_first)
    return regions


def backward_kernel(
    n_nodes,
    n_grp,
    mask_ref,
    targets_ref,
    stats_ref,
    place_h,
    child_h,
    weight_h,
    hid_h,
    pre_h,
    featb_h,
    board_b_h,
    neigh_b_h,
    comb1_b_h,
    st_h,
    dnum_h,
    dz_h,
    agg_h,
    gfeat_h,
    summed_h,
    small_ref,
    hid,
    pre,
    featb,
    board_b,
    neigh_b,
    comb1_b,
    spread_t,
    dnum,
    dz,
    agg,
    picker_t,
    picker_l,
    lines,
    edge_place,
    edge_child,
    edge_weight,
    acc,
    own_t,
    parents,
    out_slots,
    in_slots,
    chain,
    tmp,
    dpre,
    dh,
    grad,
    arrive,
    land,
    gather,
    share_l,
    share_z,
    share_x,
    small,
    load_sem,
    store_sem,
    slot_send,
    slot_recv,
    up_send,
    down_send,
    chain_recv,
    line_send,
    line_recv,
    parent_up,
    parent_down,
    parent_recv,
    job_send,
    job_recv,
    job_free,
    share_send,
    share_recv,
):
    place = Place(n_nodes, n_grp)
    z, low = place.at["z"], place.at["l"]
    layer = place.size["l"]
    rows, width = hid.shape
    layer_slots = spread_t.shape[2]
    cap = layer_slots // layer
    part = width // CHUNKS

    loads = {}
    for i, (name, src, dst) in enumerate(
        (
            ("dnum", dnum_h, dnum),
            ("hid", hid_h, hid),
            ("agg", agg_h, agg),
            ("dz", dz_h, dz),
            ("spread_t", st_h, spread_t),
            ("comb1_b", comb1_b_h, comb1_b),
            ("pre", pre_h, pre),
            ("neigh_b", neigh_b_h, neigh_b),
            ("featb", featb_h, featb),
            ("board_b", board_b_h, board_b),
            ("place", place_h, edge_place),
            ("child", child_h, edge_child),
            ("weight", weight_h, edge_weight),
        )
    ):
        loads[name] = pltpu.make_async_copy(src, dst, load_sem.at[i])
        loads[name].start()
    def make_pickers():
        @pl.loop(0, LINE)
        def _(src):
            at = pl.ds(pl.multiple_of(src * layer_slots, layer_slots), layer_slots)
            ids = lax.broadcasted_iota(jnp.int32, (rows, layer_slots), 0)
            picker_t[src] = jnp.where(ids == targets_ref[:, at], 1.0, 0.0).astype(BF16).T

    barrier(place, ("l", "z", "x"), make_pickers)
    stores = []

    def store(src, dst):
        copy = pltpu.make_async_copy(src, dst, store_sem.at[len(stores)])
        copy.start()
        stores.append(copy)

    mask = column_of(mask_ref) > 0.5

    def source(which):
        flip = z // 2
        inner = z * (1 - 2 * flip) + (LINE - 1) * flip
        index = ORDER[0][which] * (1 - inner) + ORDER[1][which] * inner
        return index * (1 - 2 * flip) + (LINE - 1) * flip

    def cols(k):
        return pl.ds(pl.multiple_of(k * part, part), part)

    def slot_copy(dst, k, far, index, device):
        at = (dst * CHUNKS + k) * (layer - 1) + far
        return remote(
            out_slots.at[dst, k, pl.ds(pl.multiple_of(index * cap, cap), cap)],
            in_slots.at[dst, k, pl.ds(pl.multiple_of(low * cap, cap), cap)],
            slot_send.at[at],
            slot_recv.at[at],
            device,
        )

    def back(dst, k):
        out_slots[dst, k] = jnp.dot(
            picker_t[dst], dnum[:, cols(k)], preferred_element_type=F32
        ).astype(BF16)
        for far, index, device in place.others("l"):
            slot_copy(dst, k, far, index, device).start()
        own = pl.ds(pl.multiple_of(low * cap, cap), cap)
        in_slots[dst, k, own] = out_slots[dst, k, own]

    def child_sums(dst, k):
        for far, index, device in place.others("l"):
            slot_copy(dst, k, far, index, device).wait_recv()
        tmp[...] = jnp.dot(spread_t[dst], in_slots[dst, k], preferred_element_type=F32)

    def up_copy(dst, k):
        k = k - AHEAD
        at = dst * BEHIND + k
        return remote(
            chain.at[dst, k],
            chain.at[dst, k],
            up_send.at[at],
            chain_recv.at[at],
            place.member("z", z + 1),
        )

    def down_copy(dst, k, last):
        slot = LINE if last else dst
        k = k - AHEAD
        return remote(
            chain.at[dst, k],
            chain.at[slot, k],
            down_send.at[dst * BEHIND + k],
            chain_recv.at[slot * BEHIND + k],
            place.member("z", z - 1),
        )

    def arrived(slot, k):
        k = k - AHEAD
        remote(
            chain.at[slot, k],
            chain.at[slot, k],
            up_send.at[0],
            chain_recv.at[slot * BEHIND + k],
            place.member("z", lax.rem(z + 1, LINE)),
        ).wait_recv()

    def hand_on(dst, k):
        child_sums(dst, k)

        @pl.when(dst > z)
        def _():
            @pl.when(z > 0)
            def _():
                up_copy(dst, k).wait_recv()
                chain[dst, k - AHEAD] = (chain[dst, k - AHEAD].astype(F32) + tmp[...]).astype(BF16)

            @pl.when(z == 0)
            def _():
                chain[dst, k - AHEAD] = tmp[...].astype(BF16)

            up_copy(dst, k).start()

        @pl.when(dst < z)
        def _():
            @pl.when(z < LINE - 1)
            def _():
                down_copy(dst, k, False).wait_recv()
                chain[dst, k - AHEAD] = (chain[dst, k - AHEAD].astype(F32) + tmp[...]).astype(BF16)

            @pl.when(z == LINE - 1)
            def _():
                chain[dst, k - AHEAD] = tmp[...].astype(BF16)

            @pl.when(dst == z - 1)
            def _():
                down_copy(dst, k, True).start()

            @pl.when(dst < z - 1)
            def _():
                down_copy(dst, k, False).start()

    regions = gradient_regions(n_nodes, n_grp, width)
    per_job = job_sems(n_nodes, n_grp)

    def job(name):
        first, n_rows, left, columns, order = regions[name]
        rows_at, cols_at = pl.ds(first, n_rows), pl.ds(left, columns)
        land_at = pl.ds(left // 2, columns // 2)
        yield from reduce_job(
            place,
            order,
            grad,
            (first, n_rows, left, columns),
            arrive.at[rows_at, land_at],
            land.at[rows_at, land_at],
            gather.at[pl.ds(first // 4, n_rows // 4), land_at],
            job_send,
            job_recv,
            job_free,
            list(regions).index(name) * per_job,
        )
        store(grad.at[rows_at, cols_at], summed_h.at[rows_at, cols_at])

    jobs = {name: job(name) for name in regions}
    for lay_out in jobs.values():
        next(lay_out)

    def step_job(name, last=False):
        if name in jobs and (last or name != "board0" or "board3" in regions):
            try:
                next(jobs[name])
            except StopIteration:
                del jobs[name]

    loads["dnum"].wait()

    def back_all(k):
        for which in (3, 2, 1, 0):
            back(source(which), k)

    def comb_grad(left, first):
        @pl.loop(0, CHUNKS)
        def _(k):
            grad[pl.ds(first, width), cols(k)] = dot_tn(left[...], dz[:, cols(k)]).astype(BF16)

    def line_targets():
        lines[z] = targets_ref[:, pl.ds(pl.multiple_of(z * layer_slots, layer_slots), layer_slots)]
        for far, index, device in place.others("z"):
            at = pl.ds(pl.multiple_of(index * layer_slots, layer_slots), layer_slots)
            remote(
                targets_ref.at[:, at], lines.at[z], line_send.at[far], line_recv.at[far], device
            ).start()

    def line_picker(which):
        src = source(which)
        far = lax.rem(z - src - 1 + LINE, LINE)
        remote(
            lines.at[src], lines.at[src], line_send.at[0], line_recv.at[far], place.member("z", src)
        ).wait_recv()
        ids = lax.broadcasted_iota(jnp.int32, (rows, layer_slots), 0)
        picker_l[src] = jnp.where(ids == lines[src], 1.0, 0.0).astype(BF16).T

    def parent_copy(src, k, sems, to):
        piece = parents.at[src, k]
        at = src * AHEAD + k
        return remote(piece, piece, sems.at[at], parent_recv.at[at], place.member("z", to))

    def parent_send(k):
        parents[z, k] = dnum[:, cols(k)]

        @pl.when(z < LINE - 1)
        def _():
            parent_copy(z, k, parent_up, z + 1).start()

        @pl.when(z > 0)
        def _():
            parent_copy(z, k, parent_down, z - 1).start()

    def parent_forward(j, k):
        below = z - 1 - j
        above = z + 1 + j

        @pl.when(below >= 0)
        def _():
            parent_copy(below, k, parent_up, z + 1).wait_recv()

            @pl.when(z < LINE - 1)
            def _():
                parent_copy(below, k, parent_up, z + 1).start()

        @pl.when(above < LINE)
        def _():
            parent_copy(above, k, parent_down, z - 1).wait_recv()

            @pl.when(z > 0)
            def _():
                parent_copy(above, k, parent_down, z - 1).start()

    def parent_slots(which, k):
        src = source(which)
        choose = picker_t[z] if which == 0 else picker_l[src]
        out_slots[src, k] = jnp.dot(choose, parents[src, k], preferred_element_type=F32).astype(
            BF16
        )
        for far, index, device in place.others("l"):
            slot_copy(src, k, far, index, device).start()
        own = pl.ds(pl.multiple_of(low * cap, cap), cap)
        in_slots[src, k, own] = out_slots[src, k, own]

    edges = edge_place.shape[1]
    turn = math.gcd(edges, 2560)
    steps = edges // turn

    def build_own(which, ticks):
        src = source(which)
        if which == 1:
            for name in ("place", "child", "weight"):
                loads[name].wait()
        acc[...] = jnp.zeros_like(acc)

        @pl.loop(0, steps)
        def _(t):
            at = pl.ds(pl.multiple_of(t * turn, turn), turn)
            slot = (edge_place[:, at] - src * layer_slots).astype(jnp.int16)
            child = edge_child[:, at].astype(jnp.int16)
            weight = edge_weight[:, at].astype(F32).astype(F8)
            right = jnp.where(
                lax.broadcasted_iota(jnp.int16, (layer_slots, turn), 0) == slot,
                jnp.ones((), F8),
                jnp.zeros((), F8),
            )
            block = 256
            for first in range(0, rows, block):
                ids = lax.broadcasted_iota(jnp.int16, (block, turn), 0) + jnp.asarray(
                    first, jnp.int16
                )
                left = jnp.where(ids == child, weight, jnp.zeros((), F8))
                acc[pl.ds(first, block), :] += dot_nt(left, right)
            run_ticks(t, ticks)

        own_t[src] = acc[...].astype(BF16)

    def own(k):
        if k < AHEAD:
            for which in range(LINE):
                src = source(which)
                for far, index, device in place.others("l"):
                    slot_copy(src, k, far, index, device).wait_recv()
                weights = spread_t[z] if which == 0 else own_t[src]
                value = jnp.dot(weights, in_slots[src, k], preferred_element_type=F32)
                if which == 0:
                    tmp[...] = value
                else:
                    tmp[...] += value
        else:
            child_sums(z, k)

            @pl.when(z > 0)
            def _():
                arrived(z, k)
                tmp[...] += chain[z, k - AHEAD].astype(F32)

            @pl.when(z < LINE - 1)
            def _():
                arrived(LINE, k)
                tmp[...] += chain[LINE, k - AHEAD].astype(F32)

        down = (tmp[...] * gelu_slope(pre[:, cols(k)])).astype(BF16)
        dpre[:, cols(k)] = down
        small[0:1, cols(k)] = jnp.sum(down.astype(F32), axis=0, keepdims=True)
        dh[...] += dot_nt(down, neigh_b[:, cols(k)])

    def neigh_grad(k):
        grad[pl.ds(2 * width, width), cols(k)] = dot_tn(hid[...], dpre[:, cols(k)]).astype(BF16)

    def comb_grads():
        for name in ("hid", "agg", "dz", "comb1_b"):
            loads[name].wait()
        comb_grad(hid, 0)
        comb_grad(agg, width)

    def self_part():
        small[...] = jnp.zeros_like(small)
        small[1:2, :] = jnp.sum(dz[...].astype(F32), axis=0, keepdims=True)
        small[2:3, :] = jnp.broadcast_to(stats_ref[0:1, 0:1], (1, width))

        @pl.loop(0, CHUNKS)
        def _(k):
            dh[:, cols(k)] = dot_nt(dz[...], comb1_b[cols(k), :])

        for name in ("pre", "neigh_b", "featb", "board_b"):
            loads[name].wait()

    def own_and_grad(k):
        own(k)
        neigh_grad(k)

    def end_of_line():
        last = dh[...].astype(BF16)
        dpre[...] = jnp.where(mask, last, jnp.zeros_like(last))
        pre[...] = last.astype(F32)

    def board_grad(i):
        half = width // 2
        grad[pl.ds(3 * width + i * half, half), :] = dot_tn(
            featb[:, i * half : (i + 1) * half], dpre[...]
        ).astype(BF16)

    def feature_grad():
        @pl.loop(0, CHUNKS)
        def _(k):
            pre[:, cols(k)] = jnp.where(
                mask, dot_nt(dpre[...], board_b[cols(k), :]), pre[:, cols(k)]
            )

        store(pre, gfeat_h)

    share = Share(place, (share_l, share_z, share_x), share_send, share_recv)

    def step_share(stage):
        if stage == 0:
            share.start(0, small[...])
        elif stage < 3:
            share.start(stage, share.finish(stage - 1))
        else:
            row = lax.broadcasted_iota(jnp.int32, small_ref.shape, 0)
            small_ref[...] = share.finish(2) * jnp.where(row == 2, stats_ref[8:9, 0:1], 1.0)

    acts = {
        "l": lambda _: line_targets(),
        "L": line_picker,
        "A": parent_send,
        "f": parent_forward,
        "q": parent_slots,
        "B": back_all,
        "W": lambda _: loads["spread_t"].wait(),
        "G": lambda _: comb_grads(),
        "S": lambda _: self_part(),
        "O": own_and_grad,
        "E": lambda _: end_of_line(),
        "H": board_grad,
        "F": lambda _: feature_grad(),
        "P": step_share,
        "c": lambda j: step_job(f"comb{j}"),
        "n": lambda j: step_job(f"neigh{j}"),
        "b": lambda j: step_job(f"board{j}"),
        "3": lambda k: hand_on(source(3), k),
        "2": lambda k: hand_on(source(2), k),
        "1": lambda k: hand_on(source(1), k),
    }
    def act(name):
        acts[name[0]](*(int(c) for c in name[1:]))

    run_order(BACKWARD, BACKWARD_ACTS, steps, build_own, act)
    while jobs:
        for name in list(jobs):
            step_job(name, last=True)

    for far, index, device in place.others("z"):
        remote(lines.at[z], lines.at[z], line_send.at[far], line_recv.at[far], device).wait_send()

    @pl.loop(0, LINE * CHUNKS)
    def _(i):
        dst = i // CHUNKS
        k = lax.rem(i, CHUNKS)

        @pl.when(k < AHEAD)
        def _():
            @pl.when(jnp.logical_and(dst <= z, z < LINE - 1))
            def _():
                parent_copy(dst, k, parent_up, z + 1).wait_send()

            @pl.when(jnp.logical_and(dst >= z, z > 0))
            def _():
                parent_copy(dst, k, parent_down, z - 1).wait_send()

        @pl.when(k >= AHEAD)
        def _():
            @pl.when(dst > z)
            def _():
                up_copy(dst, k).wait_send()

            @pl.when(dst < z)
            def _():
                down_copy(dst, k, False).wait_send()

        for far, index, device in place.others("l"):
            slot_copy(dst, k, far, index, device).wait_send()

    for copy in stores:
        copy.wait()


def backward_pass(n_nodes, n_grp, mask, targets, stats, edges_of, hid, pre, featb, board_b, neigh_b, comb1_b, st, dnum, dz, agg):
    rows, width = hid.shape
    edges = edges_of[0].shape[1]
    layer = n_nodes // LINE
    layer_slots = st.shape[2]
    part = width // CHUNKS
    n_rows = 4 * width
    count = len(gradient_regions(n_nodes, n_grp, width))
    dma = pltpu.SemaphoreType.DMA
    big = pl.BlockSpec(memory_space=pl.ANY)
    vmem = pl.BlockSpec(memory_space=pltpu.VMEM)
    sems = count * job_sems(n_nodes, n_grp)
    pieces = LINE * CHUNKS
    return pl.pallas_call(
        functools.partial(backward_kernel, n_nodes, n_grp),
        out_shape=[
            jax.ShapeDtypeStruct((rows, width), F32),
            jax.ShapeDtypeStruct((n_rows, width), BF16),
            jax.ShapeDtypeStruct((8, width), F32),
        ],
        in_specs=[vmem, vmem, vmem] + [big] * 13,
        out_specs=[big, big, vmem],
        scratch_shapes=[
            pltpu.VMEM((rows, width), BF16),
            pltpu.VMEM((rows, width), F32),
            pltpu.VMEM((rows, width), BF16),
            pltpu.VMEM((width, width), BF16),
            pltpu.VMEM((width, width), BF16),
            pltpu.VMEM((width, width), BF16),
            pltpu.VMEM((LINE, rows, layer_slots), BF16),
            pltpu.VMEM((rows, width), BF16),
            pltpu.VMEM((rows, width), BF16),
            pltpu.VMEM((rows, width), BF16),
            pltpu.VMEM((LINE, layer_slots, rows), BF16),
            pltpu.VMEM((LINE, layer_slots, rows), BF16),
            pltpu.VMEM((LINE, 1, layer_slots), jnp.int32),
            pltpu.VMEM((1, edges), jnp.int32),
            pltpu.VMEM((1, edges), jnp.int32),
            pltpu.VMEM((1, edges), jnp.int32),
            pltpu.VMEM((rows, layer_slots), F32),
            pltpu.VMEM((LINE, rows, layer_slots), BF16),
            pltpu.VMEM((LINE, AHEAD, rows, part), BF16),
            pltpu.VMEM((LINE, CHUNKS, layer_slots, part), BF16),
            pltpu.VMEM((LINE, CHUNKS, layer_slots, part), BF16),
            pltpu.VMEM((LINE + 1, BEHIND, rows, part), BF16),
            pltpu.VMEM((rows, part), F32),
            pltpu.VMEM((rows, width), BF16),
            pltpu.VMEM((rows, width), F32),
            pltpu.VMEM((n_rows, width), BF16),
            pltpu.VMEM((n_rows, width // 2), BF16),
            pltpu.VMEM((n_rows, width // 2), BF16),
            pltpu.VMEM((n_rows // 4, width // 2), BF16),
            pltpu.VMEM((layer, 8, width), F32),
            pltpu.VMEM((LINE, 8, width), F32),
            pltpu.VMEM((n_grp, 8, width), F32),
            pltpu.VMEM((8, width), F32),
            dma((13,)),
            dma((count + 1,)),
            dma((pieces * (layer - 1),)),
            dma((pieces * (layer - 1),)),
            dma((LINE * BEHIND,)),
            dma((LINE * BEHIND,)),
            dma(((LINE + 1) * BEHIND,)),
            dma((LINE - 1,)),
            dma((LINE - 1,)),
            dma((LINE * AHEAD,)),
            dma((LINE * AHEAD,)),
            dma((LINE * AHEAD,)),
            dma((sems,)),
            dma((sems,)),
            pltpu.SemaphoreType.REGULAR((sems,)),
            dma((share_sems(n_nodes, n_grp),)),
            dma((share_sems(n_nodes, n_grp),)),
        ],
        compiler_params=pltpu.CompilerParams(
            vmem_limit_bytes=63 * MIB, collective_id=3, has_side_effects=True
        ),
        name="backward_pass",
    )(mask, targets, stats, *edges_of, hid, pre, featb, board_b, neigh_b, comb1_b, st, dnum, dz, agg)


def unpack_kernel(
    rows,
    joined,
    small_ref,
    embed_in,
    gfeat_in,
    comb,
    neigh,
    board,
    nbias_ref,
    cbias_ref,
    penalty_ref,
    embed,
    gfeat,
    low,
    wide,
    held,
    load_sem,
    store_sem,
):
    width = joined.shape[1]
    blocks = joined.shape[0] // rows

    def load(i):
        at = pl.ds(i * rows, rows)
        return pltpu.make_async_copy(joined.at[at], low.at[at], load_sem.at[i])

    def store(i):
        first = i * rows
        if first < 2 * width:
            target = comb.at[pl.ds(first, rows)]
        elif first < 3 * width:
            target = neigh.at[pl.ds(first - 2 * width, rows)]
        else:
            target = board.at[pl.ds(first - 3 * width, rows)]
        return pltpu.make_async_copy(wide.at[pl.ds(first, rows)], target, store_sem.at[i])

    through = (embed_in, embed), (gfeat_in, gfeat)

    def load_whole(j):
        return pltpu.make_async_copy(through[j][0], held.at[j], load_sem.at[blocks + j])

    def store_whole(j):
        return pltpu.make_async_copy(held.at[j], through[j][1], store_sem.at[blocks + j])

    for i in range(blocks):
        if i % 4 == 2 and i // 4 < 2:
            load_whole(i // 4).start()
        load(i).start()
    nbias_ref[...] = small_ref[0:1, :]
    cbias_ref[...] = small_ref[1:2, :]
    penalty_ref[...] = small_ref[2:3, 0:1]
    for i in range(blocks):
        load(i).wait()

        @pl.loop(0, rows // 32)
        def _(r, i=i):
            at = pl.ds(pl.multiple_of(i * rows + r * 32, 32), 32)
            wide[at, :] = low[at, :].astype(F32)

        store(i).start()
        if i % 4 == 3 and i // 4 < 2:
            load_whole(i // 4).wait()
            store_whole(i // 4).start()
    for i in range(blocks):
        store(i).wait()
    for j in range(2):
        store_whole(j).wait()


def unpack(joined, small, embed, gfeat):
    n_rows, width = joined.shape
    rows = math.gcd(width, 256)
    big = pl.BlockSpec(memory_space=pl.ANY)
    vmem = pl.BlockSpec(memory_space=pltpu.VMEM)
    dma = pltpu.SemaphoreType.DMA
    return pl.pallas_call(
        functools.partial(unpack_kernel, rows),
        out_shape=[
            jax.ShapeDtypeStruct((2 * width, width), F32),
            jax.ShapeDtypeStruct((width, width), F32),
            jax.ShapeDtypeStruct((width, width), F32),
            jax.ShapeDtypeStruct((1, width), F32),
            jax.ShapeDtypeStruct((1, width), F32),
            jax.ShapeDtypeStruct((1, 1), F32),
            jax.ShapeDtypeStruct(embed.shape, F32),
            jax.ShapeDtypeStruct(gfeat.shape, F32),
        ],
        in_specs=[big, vmem, big, big],
        out_specs=[big] * 3 + [vmem] * 3 + [big] * 2,
        scratch_shapes=[
            pltpu.VMEM((n_rows, width), BF16),
            pltpu.VMEM((n_rows, width), F32),
            pltpu.VMEM((2, *embed.shape), F32),
            dma((n_rows // rows + 2,)),
            dma((n_rows // rows + 2,)),
        ],
        compiler_params=pltpu.CompilerParams(vmem_limit_bytes=60 * MIB),
        name="unpack",
    )(joined, small, embed, gfeat)


def on_device(
    n_nodes,
    n_grp,
    features,
    type_mask,
    edge_child,
    edge_slot,
    edge_weight,
    recv_rows,
    board_proj,
    neigh_proj,
    neigh_bias,
    combine_proj,
    combine_bias,
    out_cot,
):
    feats = features[0]
    rows, width = feats.shape
    peers = recv_rows.shape[2]
    cap = recv_rows.shape[3]
    slots = peers * cap
    targets = recv_rows[0, 0].reshape(1, slots)
    embed, hidden, pre, featb, pbl, qwl, cwl1, spread_t, dnum, dzb, aggb, stats = forward_pass(
        n_nodes,
        n_grp,
        feats,
        type_mask,
        (edge_slot, edge_child, edge_weight),
        targets,
        board_proj,
        neigh_proj,
        neigh_bias.reshape(1, width),
        combine_proj,
        combine_bias.reshape(1, width),
        out_cot[0],
    )
    grad_feats, summed, small = backward_pass(
        n_nodes,
        n_grp,
        type_mask,
        targets,
        stats,
        (edge_slot, edge_child, edge_weight),
        hidden,
        pre,
        featb,
        pbl,
        qwl,
        cwl1,
        spread_t,
        dnum,
        dzb,
        aggb,
    )
    grad_comb, grad_neigh, grad_board, grad_nbias, grad_cbias, penalty, embed, grad_feats = unpack(
        summed, small, embed, grad_feats
    )
    return (
        embed[None],
        penalty[0, 0],
        grad_feats[None],
        grad_board,
        grad_neigh,
        grad_nbias[0],
        grad_comb,
        grad_cbias[0],
    )


def solution(mesh):
    in_specs = (
        P("grp", "nodes", None),
        P("grp", "nodes"),
        P("grp", "nodes"),
        P("grp", "nodes"),
        P("grp", "nodes"),
        P("grp", "nodes", None, None),
        P(),
        P(),
        P(),
        P(),
        P(),
        P("grp", "nodes", None),
    )
    out_specs = (P("grp", "nodes", None), P(), P("grp", "nodes", None), P(), P(), P(), P(), P())
    return jax.shard_map(
        functools.partial(on_device, mesh.shape["nodes"], mesh.shape["grp"]),
        mesh=mesh,
        in_specs=in_specs,
        out_specs=out_specs,
        check_vma=False,
    )
```
